32 devices in a mesh: head: 2 (over y), blk: 16 (over z, x, core).
Axes of the slice: x: 2, y: 2, z: 4, core: 2. Of those that a mesh axis runs over, the one named last changes fastest.
Arguments:
- tokens: bfloat16 [4096, 768], P(('head', 'blk')), may hold values from -6 to 6
- segments: int32 [2, 2048], P(None, 'blk'), may hold values from 0 to 98, as said below
- routes: int32 [2, 4096, 2], P(None, ('head', 'blk')), may hold values from 0 to 11, all different within a row; in each aligned block of 128 rows (0 to 127, 128 to 255, ..., all dimensions but the last counted through in order) at most 40 rows name the same one
- gates: float32 [2, 4096, 2], P(None, ('head', 'blk')), may hold values from 0.2 to 1
- w_qkv: bfloat16 [2, 768, 2304], P(None, ('head', 'blk')), may hold values from -0.21875 to 0.21875
- w_out: bfloat16 [2, 768, 768], P(None, ('head', 'blk')), may hold values from -0.625 to 0.625
- gain_attn: bfloat16 [2, 768], P(None, ('head', 'blk')), may hold values from 0.5 to 1.5
- gain_moe: bfloat16 [2, 768], P(None, ('head', 'blk')), may hold values from 0.5 to 1.5
- const_gate: bfloat16 [2, 768, 4], P(None, ('head', 'blk')), may hold values from -0.21875 to 0.21875
- const_vec: bfloat16 [2, 768, 2], P(None, ('head', 'blk')), may hold values from -6 to 6
- w_gate: bfloat16 [2, 16384, 768], P(None, 'blk', 'head'), may hold values from -0.21875 to 0.21875
- w_up: bfloat16 [2, 16384, 768], P(None, 'blk', 'head'), may hold values from -0.21875 to 0.21875
- w_down: bfloat16 [2, 16384, 768], P(None, 'blk', 'head'), may hold values from -0.125 to 0.125
- cotangent: bfloat16 [4096, 768], P(('head', 'blk')), may hold values from -6 to 6
Outputs:
- output: float32 [4096, 768], P(('head', 'blk'))
- input_grad: float32 [4096, 768], P(('head', 'blk'))
- grad_qkv: float32 [2, 768, 2304], P(None, ('head', 'blk'))
- grad_out: float32 [2, 768, 768], P(None, ('head', 'blk'))
- grad_gain_attn: float32 [2, 768], P(None, ('head', 'blk'))
- grad_gain_moe: float32 [2, 768], P(None, ('head', 'blk'))
- grad_const_gate: float32 [2, 768, 4], P(None, ('head', 'blk'))
- grad_const_vec: float32 [2, 768, 2], P(None, ('head', 'blk'))
- grad_gate: float32 [2, 16384, 768], P(None, 'blk', 'head')
- grad_up: float32 [2, 16384, 768], P(None, 'blk', 'head')
- grad_down: float32 [2, 16384, 768], P(None, 'blk', 'head')
The draws below stay inside these ranges and needn't reach their ends.
Inputs may be any that keep to these rules, and one draw needn't show every extreme that they name: `routes`: each row names two different experts; in the 128 rows of one device no number is named by more than 40 rows. `segments`: never falling along the positions taken row after row; the first position holds 0 and the last the largest number.
All inputs are finite; a program needn't handle non-finite values.
Results may differ from the reference program's by a relative error of at most 0.04.
Values may be sent and summed in bfloat16 or wider, within the bound.
A program may use at most 384 MiB of HBM per device.

```python
import math
import jax
import jax.numpy as jnp
import numpy as np
from jax import lax

D = 768
HEADS = 12
FF = 2048
NE = 8
LAYERS = 2
TOK_DEV = 128
CAP = 40
TOKENS = 4096
N_HEAD = 2
N_BLK = 16


def draw_segments(key, part):
    key = jax.random.fold_in(key, 17)
    total_rows = TOK_DEV * N_HEAD * N_BLK
    key_list = jax.random.split(key, 5)
    centers = jax.random.randint(key_list[0], (24, 1), 0, total_rows)
    reach_len = jnp.left_shift(jnp.int32(1), jax.random.randint(key_list[1], (24, 1), 2, 12))
    offsets = jax.random.randint(key_list[2], (24, 4), 0, 4096) % reach_len
    cut_rows = jnp.clip((centers + offsets).reshape(-1), 1, total_rows - 1)
    first_row = 1 + jax.random.randint(key_list[3], (), 0, TOK_DEV - 1)
    last_row = N_BLK * TOK_DEV + N_BLK // 2 * TOK_DEV + jax.random.randint(key_list[4], (), 0, TOK_DEV)
    cut_rows = jnp.where((cut_rows > first_row) & (cut_rows <= last_row), first_row, cut_rows)
    cut_rows = jnp.concatenate([cut_rows, jnp.stack([first_row, last_row + 1])])
    positions = jnp.arange(total_rows, dtype=jnp.int32)
    seg_ids = jnp.sum((cut_rows[None, :] <= positions[:, None]).astype(jnp.int32), axis=1)
    return seg_ids.reshape((N_HEAD, TOK_DEV * N_BLK)).astype(jnp.int32)


def shard_levels(rng, dims, pieces, low, largest):
    factor_of = 1.0
    for axis_at, shards_of in pieces:
        draws = jax.random.uniform(jax.random.fold_in(jax.random.fold_in(rng, 6), axis_at), (shards_of,), jnp.float32, low / len(pieces), largest / len(pieces))
        factor_of = factor_of * jnp.repeat(jnp.exp(draws), dims[axis_at] // shards_of).reshape((-1,) + (1,) * (len(dims) - 1 - axis_at))
    return factor_of


def assign_block(key, own, number, rows, count, top, bound, skew):
    ranking = jax.random.permutation(key, count)
    packed, common = load_shares(count, rows * top, bound, skew, True), load_shares(count, rows * top, bound, skew, False)
    places = jnp.arange(count)

    def named(sizes, turn):
        used = int((sizes > 0).sum())
        fixed = max(1, used // 4)
        passed = fixed + (places - fixed + turn * (used - fixed)) % max(1, count - fixed)
        return jnp.zeros((count,), jnp.int32).at[ranking[jnp.where(places < fixed, places, passed)]].set(jnp.asarray(sizes, jnp.int32))

    sizes = jnp.where(number % 4 == 0, named(packed, number // 4), named(common, number - number // 4 - 1))
    mixed = jax.random.permutation(jax.random.fold_in(own, 3), count)
    source_of, taker = mixed[0:count // 2 * 2:2], mixed[1:count // 2 * 2:2]
    room = jnp.minimum(sizes[source_of] - 1, bound - sizes[taker]) // 2
    room = jnp.where((source_of == ranking[0]) | (taker == ranking[0]) | (sizes[taker] == 0), 0, jnp.maximum(room, 0))
    passed = jax.random.randint(jax.random.fold_in(own, 4), (count // 2,), 0, 1 << 20) % (room + 1)
    sizes = sizes.at[source_of].add(-passed).at[taker].add(passed)
    items = jnp.searchsorted(jnp.cumsum(sizes), jnp.arange(rows * top), side="right").astype(jnp.int32)
    table = items.reshape(top, rows).T
    table = table[jax.random.permutation(jax.random.fold_in(own, 1), rows)]
    turn = jax.random.randint(jax.random.fold_in(own, 2), (rows, 1), 0, top)
    return jnp.take_along_axis(table, (jnp.arange(top)[None, :] + turn) % top, axis=1)


def load_shares(number_of, total, limit, slope, full):
    weights = [(1 << 20) // math.isqrt(rank ** slope) + 1 for rank in range(1, number_of + 1)]
    largest = limit if full else min(limit, max(-(-total // number_of), total * weights[0] // sum(weights)))
    least = 1 if total - largest >= number_of - 1 else 0
    holding, rest = [largest] + [least] * (number_of - 1), total - largest - least * (number_of - 1)
    while rest > 0:
        candidates = [i for i in range(1, number_of) if holding[i] < largest] or [i for i in range(1, number_of) if holding[i] < limit]
        pool, budget = sum([weights[i] for i in candidates]), rest
        for i in candidates:
            more = min(limit - holding[i], max(1, budget * weights[i] // pool), rest)
            holding[i] = holding[i] + more
            rest = rest - more
    return np.array(holding)


def noise(stream_key, extent, spread, limit, shards=(), kind=jnp.bfloat16):
    drawn = spread * jax.random.normal(stream_key, extent, jnp.float32)
    if shards:
        drawn = drawn * shard_levels(stream_key, extent, shards, -0.22, 0.18)
    return jnp.clip(drawn, -limit, limit).astype(kind)


def setup_inputs(seed: int = 0) -> dict:
    key_of = jax.random.split(jax.random.key(seed), 15)
    tokens = noise(key_of[0], (TOKENS, D), 1.0, 6.0, ((0, 32),))
    segments = draw_segments(jax.random.fold_in(key_of[14], 71), 0)
    routes_keys = jax.random.split(jax.random.fold_in(key_of[2], 1), LAYERS * TOKENS // TOK_DEV)
    routes_turns = jax.random.permutation(jax.random.fold_in(key_of[2], 3), LAYERS * TOKENS // TOK_DEV)
    routes = jax.vmap(lambda own, number: assign_block(jax.random.fold_in(key_of[2], 2), own, number, TOK_DEV, NE + 4, 2, CAP, 1))(routes_keys, routes_turns).reshape((LAYERS, TOKENS, 2))
    gates = jnp.clip(0.2 + 0.8 * jax.random.uniform(key_of[3], (LAYERS, TOKENS, 2), jnp.float32) ** shard_levels(key_of[3], (LAYERS, TOKENS, 2), ((1, 32),), -0.2, 0.2), 0.2, 1.0)
    w_qkv = noise(key_of[4], (LAYERS, D, 3 * D), D ** -0.5, 0.21875, ((1, 32),))
    w_out = noise(key_of[5], (LAYERS, D, D), (D // 8) ** -0.5, 0.625, ((1, 32),))
    gain_attn = jnp.clip(1.0 + 0.1 * jax.random.normal(key_of[6], (LAYERS, D), jnp.float32), 0.5, 1.5).astype(jnp.bfloat16)
    gain_moe = jnp.clip(1.0 + 0.1 * jax.random.normal(key_of[7], (LAYERS, D), jnp.float32), 0.5, 1.5).astype(jnp.bfloat16)
    const_gate = noise(key_of[8], (LAYERS, D, 4), D ** -0.5, 0.21875, ((1, 32),))
    const_vec = noise(key_of[9], (LAYERS, D, 2), 1.0, 6.0, ((1, 32),))
    w_gate = noise(key_of[10], (LAYERS, NE * FF, D), D ** -0.5, 0.21875, ((1, 16), (2, 2)))
    w_up = noise(key_of[11], (LAYERS, NE * FF, D), D ** -0.5, 0.21875, ((1, 16), (2, 2)))
    w_down = noise(key_of[12], (LAYERS, NE * FF, D), FF ** -0.5, 0.125, ((1, 16), (2, 2)))
    cotangent = noise(key_of[13], (TOKENS, D), 1.0, 6.0, ((0, 32),))
    return dict(tokens=tokens, segments=segments, routes=routes, gates=gates, w_qkv=w_qkv, w_out=w_out, gain_attn=gain_attn, gain_moe=gain_moe, const_gate=const_gate, const_vec=const_vec, w_gate=w_gate, w_up=w_up, w_down=w_down, cotangent=cotangent)


NEGATIVE = -1e+30
EPSILON = 1e-06
HIGHEST_PRECISION = lax.Precision.HIGHEST

@jax.custom_vjp
def low(v):
    return lax.optimization_barrier(v.astype(jnp.bfloat16)).astype(jnp.float32)

@jax.custom_vjp
def low_back(v):
    return v

def low_keep(v):
    return (low(v), None)

def low_pass(kept, grad):
    return (grad,)

def back_keep(v):
    return (v, None)

def back_low(kept, grad):
    return (low(grad),)
low.defvjp(low_keep, low_pass)
low_back.defvjp(back_keep, back_low)

def rms_scaled(values, gain_vec):
    return values * lax.rsqrt(lax.optimization_barrier(jnp.mean(values * values, axis=-1, keepdims=True)) + EPSILON) * gain_vec

def attention(query_all, key_all, value_all, seg_flat, score_scale):
    total_rows = query_all.shape[0]
    positions = jnp.arange(total_rows, dtype=jnp.int32)

    def one_block(block_args):
        query_block, query_pos, query_seg = block_args
        scores = low_back(jnp.einsum('qhd,khd->hqk', query_block, key_all, precision=HIGHEST_PRECISION) * score_scale)
        allowed = (positions[None, :] <= query_pos[:, None]) & (seg_flat[None, :] == query_seg[:, None])
        probability = low(jax.nn.softmax(jnp.where(allowed[None], scores, NEGATIVE), axis=-1))
        return jnp.einsum('hqk,khd->qhd', probability, value_all, precision=HIGHEST_PRECISION)
    block_count = total_rows // 512
    heads_out = lax.map(jax.checkpoint(one_block), (query_all.reshape((block_count, 512) + query_all.shape[1:]), positions.reshape((block_count, 512)), seg_flat.reshape((block_count, 512))))
    return heads_out.reshape((total_rows, -1))

def expert_mixture(moe_in, gate_w, up_w, down_w, route_ids, gate_vals):
    slices = N_BLK // NE
    slice_width = FF // slices
    expert_ids = jnp.arange(NE, dtype=jnp.int32)
    coefficient = lax.optimization_barrier(jnp.sum(jnp.where(route_ids[None, :, :] == expert_ids[:, None, None], gate_vals[None], 0.0), axis=-1))

    def one_expert(carry_sum, expert_args):
        gate_e, up_e, down_e, coef_e = expert_args
        branch = jnp.zeros_like(moe_in)
        for slice_index in range(slices):
            shared_in = low_back(moe_in)
            gate_pre = low_back(jnp.dot(shared_in, gate_e[slice_index].T, precision=HIGHEST_PRECISION))
            up_pre = low_back(jnp.dot(shared_in, up_e[slice_index].T, precision=HIGHEST_PRECISION))
            hidden = low(jax.nn.silu(gate_pre) * up_pre)
            branch = branch + low(jnp.dot(hidden, down_e[slice_index], precision=HIGHEST_PRECISION))
        return (carry_sum + coef_e[:, None] * low_back(branch), None)
    model_width = moe_in.shape[1]
    stacked = (gate_w.reshape((NE, slices, slice_width, model_width)), up_w.reshape((NE, slices, slice_width, model_width)), down_w.reshape((NE, slices, slice_width, model_width)), coefficient)
    return lax.scan(jax.checkpoint(one_expert), jnp.zeros_like(moe_in), stacked)[0]

def layer_block(residual_state, layer_params, route_ids, gate_vals, seg_flat):
    qkv_w, out_w, attention_norm_gain, mixture_norm_gain, cgate_w, cvec_w, gate_w, up_w, down_w = layer_params
    total_rows, model_width = residual_state.shape
    head_dim = model_width // HEADS
    attn_in = low(rms_scaled(residual_state, attention_norm_gain))
    projected = low_back(low(jnp.dot(attn_in, qkv_w, precision=HIGHEST_PRECISION)))
    head_parts = projected.reshape((total_rows, 3, HEADS, head_dim))
    attended = attention(head_parts[:, 0], head_parts[:, 1], head_parts[:, 2], seg_flat, head_dim ** (-0.5))
    attended = low_back(low(attended))
    residual_between = residual_state + low_back(jnp.dot(attended, out_w, precision=HIGHEST_PRECISION))
    moe_in = low(rms_scaled(residual_between, mixture_norm_gain))
    ffn_out = expert_mixture(moe_in, gate_w, up_w, down_w, route_ids, gate_vals)
    copy_weight = lax.optimization_barrier(jnp.sum(jnp.where(route_ids == NE + 1, gate_vals, 0.0), axis=1))
    const_weight = jnp.stack([lax.optimization_barrier(jnp.sum(jnp.where(route_ids == NE + 2 + const_idx, gate_vals, 0.0), axis=1)) for const_idx in range(2)], axis=1)
    mixing = jax.nn.softmax(jnp.dot(moe_in, cgate_w, precision=HIGHEST_PRECISION).reshape((total_rows, 2, 2)), axis=-1)
    const_out = lax.optimization_barrier(jnp.sum(const_weight[:, :, None] * (mixing[:, :, 0:1] * moe_in[:, None, :] + mixing[:, :, 1:2] * cvec_w.T[None]), axis=1))
    return residual_between + ffn_out + copy_weight[:, None] * moe_in + const_out

def reference(tokens, segments, routes, gates, w_qkv, w_out, gain_attn, gain_moe, const_gate, const_vec, w_gate, w_up, w_down, cotangent):
    seg_flat = segments.reshape(-1)
    params = tuple((weight_item.astype(jnp.float32) for weight_item in (w_qkv, w_out, gain_attn, gain_moe, const_gate, const_vec, w_gate, w_up, w_down)))

    def forward(residual_state, *weight_list):
        for layer_index in range(LAYERS):
            residual_state = layer_block(residual_state, tuple((weight_item[layer_index] for weight_item in weight_list)), routes[layer_index], gates[layer_index], seg_flat)
        return residual_state
    output, pullback = jax.vjp(forward, tokens.astype(jnp.float32), *params)
    gradients = pullback(cotangent.astype(jnp.float32))
    return (output, gradients[0], gradients[1], gradients[2], gradients[3], gradients[4], gradients[5], gradients[6], gradients[7], gradients[8], gradients[9])
```

```python
from functools import partial

import jax
import jax.numpy as jnp
from jax import lax
from jax.experimental import pallas as pl
from jax.experimental.pallas import tpu as pltpu
from jax.sharding import PartitionSpec as P

HEADS = 12
NE = 8
LAYERS = 2
CAP = 40
COLUMNS = 4
MESH = pl.DeviceIdType.MESH
ANY = pl.BlockSpec(memory_space=pl.ANY)
VMEM = pl.BlockSpec(memory_space=pltpu.VMEM)
DMA = pltpu.SemaphoreType.DMA
VMEM_BYTES = 48 * 1024 * 1024


def greet(peers):
    barrier = pltpu.get_barrier_semaphore()
    for peer in peers:
        pl.semaphore_signal(barrier, inc=1, device_id=peer, device_id_type=MESH)
    pl.semaphore_wait(barrier, len(peers))


def remote(src, dst, send_sem, recv_sem, peer):
    return pltpu.make_async_remote_copy(
        src_ref=src,
        dst_ref=dst,
        send_sem=send_sem,
        recv_sem=recv_sem,
        device_id=peer,
        device_id_type=MESH,
    )


def comm_params(collective_id):
    return pltpu.CompilerParams(
        collective_id=collective_id, has_side_effects=True, vmem_limit_bytes=VMEM_BYTES
    )


def column_exchange(values, blocks, gather, collective_id):
    span = blocks // COLUMNS
    slab = values.shape if gather else values.shape[1:]

    def body(src, dst, own_sem, send_sems, recv_sems):
        head, blk = lax.axis_index("head"), lax.axis_index("blk")
        plane, rest = lax.div(blk, span), lax.rem(blk, span)
        planes = [lax.rem(plane + d, COLUMNS) for d in range(COLUMNS)]
        peers = [(head, p * span + rest) for p in planes]
        greet(peers[1:])
        own = pltpu.make_async_copy(src if gather else src.at[plane], dst.at[plane], own_sem)
        own.start()
        copies = []
        for d in (2, 1, 3):
            copy = remote(
                src if gather else src.at[planes[d]],
                dst.at[plane],
                send_sems.at[d],
                recv_sems.at[d],
                peers[d],
            )
            copy.start()
            copies.append(copy)
        own.wait()
        for copy in copies:
            copy.wait()

    return pl.pallas_call(
        body,
        out_shape=jax.ShapeDtypeStruct((COLUMNS,) + tuple(slab), values.dtype),
        in_specs=[ANY],
        out_specs=ANY,
        scratch_shapes=[DMA, DMA((COLUMNS,)), DMA((COLUMNS,))],
        compiler_params=comm_params(collective_id),
    )(values)


def plane_gather(values, blocks, collective_id):
    span = blocks // COLUMNS
    width = span // 2
    half = values.shape[0] // 2
    links = 4 * (width - 1) + 2

    def body(src, dst, own_sem, send_sems, recv_sems, pass_sems, land_sems):
        head, blk = lax.axis_index("head"), lax.axis_index("blk")
        plane, rest = lax.div(blk, span), lax.rem(blk, span)
        x, core = lax.div(rest, 2), lax.rem(rest, 2)
        first = plane * span
        right = [lax.rem(x + d, width) for d in range(width)]
        left = [lax.rem(x - d + width, width) for d in range(width)]
        x_peers = [(head, first + right[d] * 2 + core) for d in range(width)]
        y_peer = (1 - head, blk)
        core_peer = (head, first + x * 2 + 1 - core)
        greet(x_peers[1:] + [y_peer, core_peer])

        def part(h):
            return src.at[pl.ds(h * half, half)]

        def place(h, dy, d):
            row = head if dy == 0 else 1 - head
            return dst.at[row, pl.ds(h * half, half), left[d] * 2 + core]

        sends = []

        def send(h, dy, d, peer, to_dy, to_d):
            copy = remote(
                part(h) if dy == 0 and d == 0 else place(h, dy, d),
                place(h, dy, d),
                send_sems.at[len(sends)],
                recv_sems.at[h, to_dy, to_d],
                peer,
            )
            copy.start()
            sends.append(copy)

        passes = []

        def hand_over(h, dy, d):
            copy = remote(
                part(h) if dy == 0 and d == 0 else place(h, dy, d),
                place(h, dy, d),
                pass_sems.at[h, dy, d],
                land_sems.at[h, dy, d],
                core_peer,
            )
            copy.start()
            passes.append(copy)

        def arrived(h, dy, d):
            remote(
                place(h, dy, d), place(h, dy, d), send_sems.at[0], recv_sems.at[h, dy, d], y_peer
            ).wait_recv()

        own = pltpu.make_async_copy(src, dst.at[head, :, rest], own_sem)
        own.start()
        for d in range(1, width):
            send(0, 0, 0, x_peers[d], 0, d)
        send(1, 0, 0, y_peer, 1, 0)
        send(0, 0, 0, y_peer, 1, 0)
        for d in range(1, width):
            send(1, 0, 0, x_peers[d], 0, d)
        hand_over(0, 0, 0)
        hand_over(1, 0, 0)
        for d in range(1, width):
            arrived(0, 0, d)
            send(0, 0, d, y_peer, 1, d)
            hand_over(0, 0, d)
        arrived(1, 1, 0)
        for d in range(1, width):
            send(1, 1, 0, x_peers[d], 1, d)
        hand_over(1, 1, 0)
        arrived(0, 1, 0)
        hand_over(0, 1, 0)
        for d in range(1, width):
            arrived(1, 0, d)
            hand_over(1, 0, d)
        for d in range(1, width):
            arrived(0, 1, d)
            hand_over(0, 1, d)
            arrived(1, 1, d)
            hand_over(1, 1, d)
        own.wait()
        for copy in passes:
            copy.wait()
        for copy in sends:
            copy.wait_send()

    return pl.pallas_call(
        body,
        out_shape=jax.ShapeDtypeStruct(
            (2, values.shape[0], span) + tuple(values.shape[1:]), values.dtype
        ),
        in_specs=[ANY],
        out_specs=ANY,
        scratch_shapes=[
            DMA,
            DMA((links,)),
            DMA((2, 2, width)),
            DMA((2, 2, width)),
            DMA((2, 2, width)),
        ],
        compiler_params=comm_params(collective_id),
    )(values)


def plane_reduce(values, blocks, collective_id):
    span = blocks // COLUMNS
    width = span // 2
    slabs, rows, cols = values.shape[1], values.shape[3], values.shape[4]
    half = slabs // 2
    kind = values.dtype

    def body(
        src,
        out,
        core_in,
        summed,
        xa_in,
        ya_out,
        ya_in,
        yb_in,
        xb_out,
        xb_in,
        core_send,
        core_recv,
        link_send,
        link_recv,
    ):
        head, blk = lax.axis_index("head"), lax.axis_index("blk")
        plane, rest = lax.div(blk, span), lax.rem(blk, span)
        x, core = lax.div(rest, 2), lax.rem(rest, 2)
        first = plane * span
        right = [lax.rem(x + d, width) for d in range(width)]
        x_peers = [(head, first + right[d] * 2 + core) for d in range(width)]
        y_peer = (1 - head, blk)
        core_peer = (head, first + x * 2 + 1 - core)
        greet(x_peers[1:] + [y_peer, core_peer])

        def wide(ref, *at):
            return ref[at].astype(jnp.float32)

        starts = []
        for h in range(2):
            copy = remote(
                src.at[:, pl.ds(h * half, half), :, 1 - core],
                core_in.at[:, pl.ds(h * half, half)],
                core_send.at[h],
                core_recv.at[h],
                core_peer,
            )
            copy.start()
            starts.append(copy)

        def core_sum(h):
            def step(i, _):
                yy = lax.div(i, half * width)
                zz = lax.div(lax.rem(i, half * width), width) + h * half
                xx = lax.rem(i, width)
                total = wide(src, yy, zz, xx, core) + wide(core_in, yy, zz, xx)
                summed[yy, zz, xx] = total.astype(kind)
                return 0

            lax.fori_loop(0, 2 * half * width, step, 0)

        sends = []
        starts[0].wait_recv()
        core_sum(0)
        for d in range(1, width):
            copy = remote(
                summed.at[:, pl.ds(0, half), right[d]],
                xa_in.at[d],
                link_send.at[0, d],
                link_recv.at[0, d],
                x_peers[d],
            )
            copy.start()
            sends.append(copy)
        starts[1].wait_recv()
        core_sum(1)
        yb = remote(
            summed.at[1 - head, pl.ds(half, half)],
            yb_in,
            link_send.at[1, 0],
            link_recv.at[1, 0],
            y_peer,
        )
        yb.start()
        for copy in sends:
            copy.wait_recv()

        def a_step(zz, _):
            total = wide(summed, 1 - head, zz, x)
            for d in range(1, width):
                total = total + wide(xa_in, d, 1 - head, zz)
            ya_out[zz] = total.astype(kind)
            return 0

        lax.fori_loop(0, half, a_step, 0)
        ya = remote(ya_out, ya_in, link_send.at[0, 0], link_recv.at[0, 0], y_peer)
        ya.start()
        yb.wait_recv()
        xb_sends = []
        for d in range(1, width):

            def b_step(zz, _):
                total = wide(summed, head, half + zz, right[d]) + wide(yb_in, zz, right[d])
                xb_out[d, zz] = total.astype(kind)
                return 0

            lax.fori_loop(0, half, b_step, 0)
            copy = remote(
                xb_out.at[d], xb_in.at[d], link_send.at[1, d], link_recv.at[1, d], x_peers[d]
            )
            copy.start()
            xb_sends.append(copy)
        ya.wait_recv()

        def a_last(zz, _):
            total = wide(summed, head, zz, x) + wide(ya_in, zz)
            for d in range(1, width):
                total = total + wide(xa_in, d, head, zz)
            out[zz] = total.astype(kind)
            return 0

        lax.fori_loop(0, half, a_last, 0)
        for copy in xb_sends:
            copy.wait_recv()

        def b_last(zz, _):
            total = wide(summed, head, half + zz, x) + wide(yb_in, zz, x)
            for d in range(1, width):
                total = total + wide(xb_in, d, zz)
            out[half + zz] = total.astype(kind)
            return 0

        lax.fori_loop(0, half, b_last, 0)
        for copy in starts + sends + [yb, ya] + xb_sends:
            copy.wait_send()

    tile = (rows, cols)
    return pl.pallas_call(
        body,
        out_shape=jax.ShapeDtypeStruct((slabs,) + tile, kind),
        in_specs=[VMEM],
        out_specs=VMEM,
        scratch_shapes=[
            pltpu.VMEM((2, slabs, width) + tile, kind),
            pltpu.VMEM((2, slabs, width) + tile, kind),
            pltpu.VMEM((width, 2, half) + tile, kind),
            pltpu.VMEM((half,) + tile, kind),
            pltpu.VMEM((half,) + tile, kind),
            pltpu.VMEM((half, width) + tile, kind),
            pltpu.VMEM((width, half) + tile, kind),
            pltpu.VMEM((width, half) + tile, kind),
            DMA((2,)),
            DMA((2,)),
            DMA((2, width)),
            DMA((2, width)),
        ],
        compiler_params=comm_params(collective_id),
    )(values.reshape((2, slabs, width, 2) + tile))


def expert_dispatch(buffer, blocks, collective_id):
    copies = blocks // NE
    tile = tuple(buffer.shape[1:])

    def body(src, dst, own_sem, send_sems, recv_sems, pass_sems, land_sems):
        head, blk = lax.axis_index("head"), lax.axis_index("blk")
        expert, piece = lax.div(blk, copies), lax.rem(blk, copies)
        ahead = [lax.rem(expert + d, NE) for d in range(NE)]
        behind = [lax.rem(expert - d + NE, NE) for d in range(NE)]
        peers = [(head, ahead[d] * copies + piece) for d in range(NE)]
        siblings = [
            (head, expert * copies + lax.rem(piece + k, copies)) for k in range(copies)
        ]
        greet(peers[1:] + siblings[1:])
        own = pltpu.make_async_copy(src.at[expert], dst.at[piece, expert], own_sem)
        own.start()
        sends, passes = [], []
        for d in (4, 3, 5, 2, 6, 1, 7):
            copy = remote(
                src.at[ahead[d]],
                dst.at[piece, expert],
                send_sems.at[d],
                recv_sems.at[d],
                peers[d],
            )
            copy.start()
            sends.append(copy)
        for d in (0, 1, 7, 2, 6, 3, 5, 4):
            place = dst.at[piece, behind[d]]
            if d > 0:
                remote(place, place, send_sems.at[d], recv_sems.at[d], peers[d]).wait_recv()
            for k in range(1, copies):
                copy = remote(
                    place if d > 0 else src.at[expert],
                    place,
                    pass_sems.at[k, d],
                    land_sems.at[k, d],
                    siblings[k],
                )
                copy.start()
                passes.append(copy)
        own.wait()
        for copy in passes:
            copy.wait()
        for copy in sends:
            copy.wait_send()

    return pl.pallas_call(
        body,
        out_shape=jax.ShapeDtypeStruct((copies, NE) + tile, buffer.dtype),
        in_specs=[ANY],
        out_specs=ANY,
        scratch_shapes=[DMA, DMA((NE,)), DMA((NE,)), DMA((copies, NE)), DMA((copies, NE))],
        compiler_params=comm_params(collective_id),
    )(buffer)


def expert_return(parts, blocks, collective_id):
    copies = blocks // NE
    tile = tuple(parts.shape[2:])
    kind = parts.dtype

    def body(src, dst, sib_in, total, own_sem, send_sems, recv_sems, pass_sems, land_sems):
        head, blk = lax.axis_index("head"), lax.axis_index("blk")
        expert, piece = lax.div(blk, copies), lax.rem(blk, copies)
        ahead = [lax.rem(expert + d, NE) for d in range(NE)]
        peers = [(head, ahead[d] * copies + piece) for d in range(NE)]
        places = [lax.rem(piece + k, copies) for k in range(copies)]
        siblings = [(head, expert * copies + places[k]) for k in range(copies)]
        greet(peers[1:] + siblings[1:])
        order = (4, 3, 5, 2, 6, 1, 7, 0)
        passes, sends = {}, []
        for d in order:
            for k in range(1, copies):
                copy = remote(
                    src.at[places[k], ahead[d]],
                    sib_in.at[k, ahead[d]],
                    pass_sems.at[k, d],
                    land_sems.at[k, d],
                    siblings[k],
                )
                copy.start()
                passes[k, d] = copy
        for d in order:
            value = src[piece, ahead[d]].astype(jnp.float32)
            for k in range(1, copies):
                passes[k, d].wait_recv()
                value = value + sib_in[k, ahead[d]].astype(jnp.float32)
            total[ahead[d]] = value.astype(kind)
            if d > 0:
                copy = remote(
                    total.at[ahead[d]],
                    dst.at[expert],
                    send_sems.at[d],
                    recv_sems.at[d],
                    peers[d],
                )
                copy.start()
                sends.append(copy)
        own = pltpu.make_async_copy(total.at[expert], dst.at[expert], own_sem)
        own.start()
        own.wait()
        for copy in sends:
            copy.wait()
        for copy in passes.values():
            copy.wait_send()

    return pl.pallas_call(
        body,
        out_shape=jax.ShapeDtypeStruct((NE,) + tile, kind),
        in_specs=[VMEM],
        out_specs=ANY,
        scratch_shapes=[
            pltpu.VMEM((copies, NE) + tile, kind),
            pltpu.VMEM((NE,) + tile, kind),
            DMA,
            DMA((NE,)),
            DMA((NE,)),
            DMA((copies, NE)),
            DMA((copies, NE)),
        ],
        compiler_params=comm_params(collective_id),
    )(parts)


NEGATIVE = -1e30
EPSILON = 1e-06
HIGHEST = lax.Precision.HIGHEST
KEYS = 512
LANES = 128
LAST = (((1,), (1,)), ((), ()))
FIRST = (((0,), (0,)), ((), ()))


def dot32(a, b, dims=(((1,), (0,)), ((), ()))):
    return lax.dot_general(a, b, dims, preferred_element_type=jnp.float32)


def visible(key_base, query_base, keys, queries, starts):
    key_pos = key_base + lax.broadcasted_iota(jnp.int32, (keys, queries), 0)
    query_pos = query_base + lax.broadcasted_iota(jnp.int32, (keys, queries), 1)
    return (key_pos <= query_pos) & (key_pos >= starts)


def attend(bounds, queries, kv_all, starts):
    count, rows, width = queries.shape
    heads = width // LANES

    def body(bounds_ref, q_ref, kv_ref, start_ref, out_ref):
        i = pl.program_id(0)
        low, high, base = bounds_ref[i, 0], bounds_ref[i, 1], bounds_ref[i, 2]
        start_row = start_ref[0]
        q = [q_ref[0, :, h * LANES : (h + 1) * LANES] for h in range(heads)]

        def step(t, carry):
            chunk = high - t
            at = pl.multiple_of(chunk * KEYS, KEYS)
            ok = visible(chunk * KEYS, base, KEYS, rows, start_row)
            new = []
            for h in range(heads):
                top, total, acc = carry[h]
                kv = kv_ref[pl.ds(at, KEYS), h * LANES : (h + 1) * LANES]
                score = jnp.where(ok, dot32(kv, q[h], LAST), NEGATIVE)
                new_top = jnp.maximum(top, jnp.max(score, axis=0, keepdims=True))
                weight = jnp.exp(score - new_top)
                shrink = jnp.exp(top - new_top)
                total = total * shrink + jnp.sum(weight, axis=0, keepdims=True)
                acc = acc * shrink + dot32(kv, weight.astype(jnp.bfloat16), FIRST)
                new.append((new_top, total, acc))
            return tuple(new)

        empty = tuple(
            (
                jnp.full((1, rows), NEGATIVE, jnp.float32),
                jnp.zeros((1, rows), jnp.float32),
                jnp.zeros((LANES, rows), jnp.float32),
            )
            for h in range(heads)
        )
        done = lax.fori_loop(0, high - low + 1, step, empty)
        lane = lax.broadcasted_iota(jnp.int32, (LANES, rows), 0)
        for h in range(heads):
            top, total, acc = done[h]
            value = jnp.where(lane < LANES // 2, top + jnp.log(total), acc / total)
            out_ref[0, :, h * LANES : (h + 1) * LANES] = value.T

    return pl.pallas_call(
        body,
        out_shape=jax.ShapeDtypeStruct((count, rows, width), jnp.float32),
        grid_spec=pltpu.PrefetchScalarGridSpec(
            num_scalar_prefetch=1,
            grid=(count,),
            in_specs=[
                pl.BlockSpec((1, rows, width), lambda i, b: (i, 0, 0)),
                pl.BlockSpec(kv_all.shape, lambda i, b: (0, 0)),
                pl.BlockSpec((1, 1, rows), lambda i, b: (i, 0, 0)),
            ],
            out_specs=pl.BlockSpec((1, rows, width), lambda i, b: (i, 0, 0)),
        ),
        compiler_params=pltpu.CompilerParams(vmem_limit_bytes=VMEM_BYTES),
        cost_estimate=pl.CostEstimate(
            flops=2 * count * rows * kv_all.shape[0] * width,
            bytes_accessed=kv_all.size * 2,
            transcendentals=count * rows * kv_all.shape[0],
        ),
    )(bounds, queries, kv_all, starts)


def attend_back(bounds, queries, grads, kept, kv_all, starts, scale):
    count, rows, width = queries.shape
    total_keys = kv_all.shape[0]
    heads = width // LANES
    if total_keys * width * 14 > VMEM_BYTES:
        heads = 1
    wide = heads * LANES

    def body(bounds_ref, q_ref, g_ref, kept_ref, kv_ref, start_ref, dq_ref, dkv_ref, acc_ref):
        i = pl.program_id(1)
        low, high, base = bounds_ref[i, 0], bounds_ref[i, 1], bounds_ref[i, 2]
        start_row = start_ref[0]

        @pl.when(i == 0)
        def _():
            def clear(c, _):
                acc_ref[pl.ds(pl.multiple_of(c * KEYS, KEYS), KEYS), :] = jnp.zeros(
                    (KEYS, wide), jnp.float32
                )
                return 0

            lax.fori_loop(0, total_keys // KEYS, clear, 0)

        q = [q_ref[0, :, h * LANES : (h + 1) * LANES] for h in range(heads)]
        g = [g_ref[0, :, h * LANES : (h + 1) * LANES] for h in range(heads)]
        lse, delta = [], []
        for h in range(heads):
            kept_t = kept_ref[0, :, h * LANES : (h + 1) * LANES].T
            lse.append(kept_t[0:1])
            delta.append(jnp.sum(kept_t * g[h].astype(jnp.float32).T, axis=0, keepdims=True))

        def step(t, carry):
            chunk = high - t
            at = pl.multiple_of(chunk * KEYS, KEYS)
            ok = visible(chunk * KEYS, base, KEYS, rows, start_row)
            new = []
            for h in range(heads):
                lanes = slice(h * LANES, (h + 1) * LANES)
                kv = kv_ref[pl.ds(at, KEYS), lanes]
                score = jnp.where(ok, dot32(kv, q[h], LAST), NEGATIVE)
                prob = jnp.exp(score - lse[h])
                dscore = (prob * (dot32(kv, g[h], LAST) - delta[h])).astype(jnp.bfloat16)
                acc_ref[pl.ds(at, KEYS), lanes] += dot32(dscore, q[h]) + dot32(
                    prob.astype(jnp.bfloat16), g[h]
                )
                new.append(carry[h] + dot32(kv, dscore, FIRST))
            return tuple(new)

        done = lax.fori_loop(
            0,
            high - low + 1,
            step,
            tuple(jnp.zeros((LANES, rows), jnp.float32) for h in range(heads)),
        )
        lane = lax.broadcasted_iota(jnp.int32, (LANES, rows), 0)
        for h in range(heads):
            value = jnp.where(lane < LANES // 2, done[h] * scale, 0.0)
            dq_ref[0, :, h * LANES : (h + 1) * LANES] = value.T.astype(jnp.bfloat16)

        @pl.when(i == count - 1)
        def _():
            def store(c, _):
                at = pl.ds(pl.multiple_of(c * KEYS, KEYS), KEYS)
                dkv_ref[at, :] = acc_ref[at, :].astype(jnp.bfloat16)
                return 0

            lax.fori_loop(0, total_keys // KEYS, store, 0)

    block = pl.BlockSpec((1, rows, wide), lambda h, i, b: (i, 0, h))
    whole = pl.BlockSpec((total_keys, wide), lambda h, i, b: (0, h))
    return pl.pallas_call(
        body,
        out_shape=(
            jax.ShapeDtypeStruct((count, rows, width), jnp.bfloat16),
            jax.ShapeDtypeStruct(kv_all.shape, jnp.bfloat16),
        ),
        grid_spec=pltpu.PrefetchScalarGridSpec(
            num_scalar_prefetch=1,
            grid=(width // wide, count),
            in_specs=[
                block,
                block,
                block,
                whole,
                pl.BlockSpec((1, 1, rows), lambda h, i, b: (i, 0, 0)),
            ],
            out_specs=(block, whole),
            scratch_shapes=[pltpu.VMEM((total_keys, wide), jnp.float32)],
        ),
        compiler_params=pltpu.CompilerParams(vmem_limit_bytes=VMEM_BYTES),
        cost_estimate=pl.CostEstimate(
            flops=5 * count * rows * total_keys * width,
            bytes_accessed=kv_all.size * 4,
            transcendentals=count * rows * total_keys,
        ),
    )(bounds, queries, grads, kept, kv_all, starts)


def norm_forward(values, gain_vec):
    row_scale = lax.rsqrt(jnp.mean(values * values, axis=-1, keepdims=True) + EPSILON)
    normed = values * row_scale
    return normed * gain_vec, normed, row_scale


def norm_backward(upstream, normed, row_scale, gain_vec):
    through = upstream * gain_vec
    gain_grad = jnp.sum(upstream * normed, axis=0)
    inner_mean = jnp.mean(through * normed, axis=-1, keepdims=True)
    return row_scale * (through - normed * inner_mean), gain_grad


def slot_index(route_ids):
    token_rows = route_ids.shape[0]
    expert_ids = jnp.arange(NE, dtype=jnp.int32)
    matches = (
        (route_ids[:, :, None] == expert_ids[None, None, :])
        .astype(jnp.int32)
        .reshape((token_rows * 2, NE))
    )
    before = jnp.cumsum(matches, axis=0) - 1
    slot_pos = jnp.sum(matches * before, axis=1).reshape((token_rows, 2))
    return jnp.where(route_ids < NE, route_ids * CAP + slot_pos, NE * CAP)


def per_device(
    tokens,
    segments,
    routes,
    gates,
    w_qkv,
    w_out,
    gain_attn,
    gain_moe,
    const_gate,
    const_vec,
    w_gate,
    w_up,
    w_down,
    cotangent,
):
    blocks = lax.axis_size("blk")
    head_index, blk_index = lax.axis_index("head"), lax.axis_index("blk")
    span = blocks // COLUMNS
    plane, rest = lax.div(blk_index, span), lax.rem(blk_index, span)
    shards = 2 * blocks
    token_rows, width = tokens.shape
    shard_rows = width // shards
    head_dim = width // HEADS
    heads = HEADS // COLUMNS
    scale = head_dim ** (-0.5)
    half_length = blocks * token_rows
    positions = 2 * half_length
    features = w_gate.shape[2]
    hidden_rows = w_gate.shape[1]
    copies = blocks // NE
    own_qkv = heads * 3 * head_dim
    own_out = heads * head_dim

    swap = [(0, 1), (1, 0)]
    ready = [
        [lax.ppermute(w[layer], "head", swap) for w in (w_gate, w_up, w_down)]
        for layer in range(LAYERS)
    ]

    def whole_features(own, other):
        return jnp.concatenate(
            [
                jnp.where(head_index == 0, own, other),
                jnp.where(head_index == 0, other, own),
            ],
            axis=1,
        )

    qkv_slabs = w_qkv.reshape((LAYERS, shard_rows, 3, COLUMNS, heads, head_dim))
    qkv_slabs = qkv_slabs.transpose((3, 0, 1, 4, 2, 5)).reshape(
        (COLUMNS, LAYERS, shard_rows, own_qkv)
    )
    small = jnp.concatenate(
        [gain_attn[..., None], gain_moe[..., None], const_gate, const_vec], axis=2
    )
    seg_own = lax.dynamic_index_in_dim(segments, head_index, 0, keepdims=False)
    seg_parts = jnp.concatenate([lax.rem(seg_own, 128), lax.div(seg_own, 128)]).astype(
        jnp.bfloat16
    )
    seg_columns = -(-seg_parts.shape[0] // shard_rows)
    seg_parts = jnp.pad(seg_parts, (0, seg_columns * shard_rows - seg_parts.shape[0]))
    seg_parts = jnp.broadcast_to(
        seg_parts.reshape((1, shard_rows, seg_columns)), (LAYERS, shard_rows, seg_columns)
    )
    side = jnp.concatenate([w_out, small, seg_parts], axis=2)
    side = jnp.pad(side, ((0, 0), (0, 0), (0, -(own_qkv + side.shape[2]) % LANES)))
    slabs = jnp.concatenate(
        [qkv_slabs, jnp.broadcast_to(side[None], (COLUMNS,) + side.shape)], axis=3
    )
    weights = plane_gather(column_exchange(slabs, blocks, False, 1), blocks, 2)
    weights = weights.reshape((shards, LAYERS, shard_rows, -1))

    seg_all = weights[:, 0, :, own_qkv + width + 8 : own_qkv + width + 8 + seg_columns]
    seg_all = seg_all.reshape((shards, -1))[:, : 2 * token_rows].astype(jnp.int32)
    seg_all = seg_all[:, :token_rows] + 128 * seg_all[:, token_rows:]
    seg_query = lax.dynamic_index_in_dim(
        seg_all.reshape((2, COLUMNS, span, token_rows)), head_index, 0, keepdims=False
    )
    seg_query = lax.dynamic_index_in_dim(seg_query, rest, 1, keepdims=False)
    starts = jnp.sum(
        (seg_all.reshape((1, 1, -1)) < seg_query[:, :, None]).astype(jnp.int32), axis=2
    )
    bases = (
        head_index * half_length
        + (jnp.arange(COLUMNS, dtype=jnp.int32) * span + rest) * token_rows
    )
    bounds = jnp.stack(
        [lax.div(starts[:, 0], KEYS), lax.div(bases + token_rows - 1, KEYS), bases], axis=1
    )
    starts = starts[:, None, :]

    layers = []
    for layer in range(LAYERS):
        rows = weights[:, layer]
        qkv = rows[:, :, :own_qkv].reshape((width, heads, 3, head_dim))
        query_w = jnp.pad(qkv[:, :, 0], ((0, 0), (0, 0), (0, LANES - head_dim)))
        query_w = query_w.reshape((width, heads * LANES))
        kv_w = qkv[:, :, 1:].reshape((width, heads * LANES))
        out_w = rows[:, :, own_qkv : own_qkv + width].reshape((width, width))
        small_w = rows[:, :, own_qkv + width : own_qkv + width + 8].reshape((width, 8))
        layers.append((query_w, kv_w, out_w, small_w))

    residual = tokens.astype(jnp.float32)
    kept = []
    for layer in range(LAYERS):
        query_w, kv_w, out_w, small_w = layers[layer]
        attn_gain = small_w[:, 0].astype(jnp.float32)
        moe_gain = small_w[:, 1].astype(jnp.float32)
        gate_w = small_w[:, 2:6]
        vectors = small_w[:, 6:8].astype(jnp.float32).T
        normed_in, unit_in, scale_in = norm_forward(residual, attn_gain)
        column = column_exchange(normed_in.astype(jnp.bfloat16), blocks, True, 3)
        column = column.reshape((COLUMNS * token_rows, width))
        queries = (
            dot32(column, query_w).astype(jnp.bfloat16).astype(jnp.float32) * scale
        ).astype(jnp.bfloat16)
        queries = queries.reshape((COLUMNS, token_rows, heads * LANES))
        kv_own = dot32(column, kv_w).astype(jnp.bfloat16)
        kv_all = plane_gather(kv_own.reshape((COLUMNS, token_rows, heads * LANES)), blocks, 4)
        kv_all = kv_all.reshape((positions, heads * LANES))
        attended = attend(bounds, queries, kv_all, starts)
        attn_col = (
            attended.reshape((COLUMNS, token_rows, heads, LANES))[..., head_dim:]
            .reshape((COLUMNS, token_rows, own_out))
            .astype(jnp.bfloat16)
        )
        attn = column_exchange(attn_col, blocks, False, 5)
        attn = attn.transpose((1, 0, 2)).reshape((token_rows, width))
        middle = residual + dot32(attn, out_w)
        normed_mid, unit_mid, scale_mid = norm_forward(middle, moe_gain)
        moe_in = normed_mid.astype(jnp.bfloat16)
        moe_float = moe_in.astype(jnp.float32)
        route_ids, gate_vals = routes[layer], gates[layer]
        slots = slot_index(route_ids)
        named = slots[:, :, None] == jnp.arange(NE * CAP, dtype=jnp.int32)[None, None, :]
        picks = jnp.any(named, axis=1)
        pick_gates = jnp.sum(jnp.where(named, gate_vals[:, :, None], 0.0), axis=1)
        sent = dot32(picks.astype(jnp.bfloat16), moe_in, FIRST).astype(jnp.bfloat16)
        arrived = expert_dispatch(sent.reshape((NE, CAP, width)), blocks, 6)
        flat_in = arrived.reshape((-1, width))
        expert_w = [
            whole_features(w[layer], other)
            for w, other in zip((w_gate, w_up, w_down), ready[layer])
        ]
        gate_pre = dot32(flat_in, expert_w[0], LAST)
        up_pre = dot32(flat_in, expert_w[1], LAST)
        hidden = (jax.nn.silu(gate_pre) * up_pre).astype(jnp.bfloat16)
        parts = dot32(hidden, expert_w[2]).astype(jnp.bfloat16)
        back = expert_return(parts.reshape((copies, NE, CAP, width)), blocks, 7)
        back = back.reshape((NE * CAP, width)).astype(jnp.float32)
        ffn_out = jnp.dot(pick_gates, back, precision=HIGHEST)
        copy_weight = jnp.sum(jnp.where(route_ids == NE + 1, gate_vals, 0.0), axis=1)
        const_weight = jnp.stack(
            [
                jnp.sum(jnp.where(route_ids == NE + 2 + c, gate_vals, 0.0), axis=1)
                for c in range(2)
            ],
            axis=1,
        )
        mixing = jax.nn.softmax(dot32(moe_in, gate_w).reshape((token_rows, 2, 2)), axis=-1)
        const_out = jnp.sum(
            const_weight[:, :, None]
            * (mixing[:, :, 0:1] * moe_float[:, None, :] + mixing[:, :, 1:2] * vectors[None]),
            axis=1,
        )
        residual = middle + ffn_out + copy_weight[:, None] * moe_float + const_out
        kept.append(
            (
                unit_in,
                scale_in,
                column,
                queries,
                kv_all,
                attended,
                attn_col,
                unit_mid,
                scale_mid,
                moe_float,
                picks,
                pick_gates,
                flat_in,
                expert_w,
                gate_pre,
                up_pre,
                hidden,
                copy_weight,
                const_weight,
                mixing,
            )
        )
    output = residual

    upstream = cotangent.astype(jnp.float32)
    shared_grads = [None] * LAYERS
    expert_grads = [None] * LAYERS
    for layer in reversed(range(LAYERS)):
        query_w, kv_w, out_w, small_w = layers[layer]
        attn_gain = small_w[:, 0].astype(jnp.float32)
        moe_gain = small_w[:, 1].astype(jnp.float32)
        gate_w = small_w[:, 2:6].astype(jnp.float32)
        vectors = small_w[:, 6:8].astype(jnp.float32).T
        (
            unit_in,
            scale_in,
            column,
            queries,
            kv_all,
            attended,
            attn_col,
            unit_mid,
            scale_mid,
            moe_float,
            picks,
            pick_gates,
            flat_in,
            expert_w,
            gate_pre,
            up_pre,
            hidden,
            copy_weight,
            const_weight,
            mixing,
        ) = kept[layer]
        picked = jnp.dot(picks.astype(jnp.float32).T, upstream, precision=HIGHEST)
        dz = (jnp.sum(pick_gates, axis=0)[:, None] * picked).astype(jnp.bfloat16)
        dz_in = expert_dispatch(dz.reshape((NE, CAP, width)), blocks, 6).reshape((-1, width))

        mix_grad = const_weight[:, :, None] * upstream[:, None, :]
        alpha_grad = jnp.stack(
            [
                jnp.sum(mix_grad * moe_float[:, None, :], axis=-1),
                jnp.sum(mix_grad * vectors[None], axis=-1),
            ],
            axis=-1,
        )
        logit_grad = (
            mixing * (alpha_grad - jnp.sum(mixing * alpha_grad, axis=-1, keepdims=True))
        ).reshape((token_rows, 4))
        hn_grad = (
            copy_weight[:, None] * upstream
            + jnp.sum(mixing[:, :, 0:1] * mix_grad, axis=1)
            + jnp.dot(logit_grad, gate_w.T, precision=HIGHEST)
        )
        cgate_grad = jnp.dot(moe_float.T, logit_grad, precision=HIGHEST)
        cvec_grad = jnp.sum(mixing[:, :, 1:2] * mix_grad, axis=0).T

        sigmoid = jax.nn.sigmoid(gate_pre)
        silu = gate_pre * sigmoid
        hidden_grad = dot32(dz_in, expert_w[2], LAST)
        dgate = (hidden_grad * up_pre * sigmoid * (1.0 + gate_pre * (1.0 - sigmoid))).astype(
            jnp.bfloat16
        )
        dup = (hidden_grad * silu).astype(jnp.bfloat16)
        dparts = (dot32(dgate, expert_w[0]) + dot32(dup, expert_w[1])).astype(jnp.bfloat16)
        dback = expert_return(dparts.reshape((copies, NE, CAP, width)), blocks, 7)
        weight_grads = [dot32(a, b, FIRST) for a, b in ((dgate, flat_in), (dup, flat_in), (hidden, dz_in))]
        summed = []
        for grad in weight_grads:
            away = lax.dynamic_slice_in_dim(grad, (1 - head_index) * features, features, 1)
            own = lax.dynamic_slice_in_dim(grad, head_index * features, features, 1)
            got = lax.ppermute(away.astype(jnp.bfloat16), "head", swap)
            summed.append(own + got.astype(jnp.float32))
        expert_grads[layer] = summed

        hn_grad = hn_grad + dot32(
            picks.astype(jnp.bfloat16), dback.reshape((NE * CAP, width))
        )
        middle_grad, moe_gain_grad = norm_backward(hn_grad, unit_mid, scale_mid, moe_gain)
        middle_grad = middle_grad + upstream
        dy = column_exchange(middle_grad.astype(jnp.bfloat16), blocks, True, 3)
        dy = dy.reshape((COLUMNS * token_rows, width))
        out_rows = lax.dynamic_slice_in_dim(out_w, plane * own_out, own_out, 0)
        out_rows = jnp.pad(
            out_rows.reshape((heads, head_dim, width)), ((0, 0), (LANES - head_dim, 0), (0, 0))
        ).reshape((heads * LANES, width))
        dattn = dot32(dy, out_rows, LAST).astype(jnp.bfloat16)
        dattn = dattn.reshape((COLUMNS, token_rows, heads * LANES))
        out_grad = dot32(attn_col.reshape((-1, own_out)), dy, FIRST)
        dq, dkv_all = attend_back(bounds, queries, dattn, attended, kv_all, starts, scale)
        dkv = plane_reduce(
            dkv_all.reshape((2, COLUMNS, span, token_rows, heads * LANES)), blocks, 8
        )
        dq = dq.reshape((-1, heads * LANES))
        dkv = dkv.reshape((-1, heads * LANES))
        dxn = (dot32(dq, query_w, LAST) + dot32(dkv, kv_w, LAST)).astype(jnp.bfloat16)
        dxn = column_exchange(dxn.reshape((COLUMNS, token_rows, width)), blocks, False, 9)
        dxn = jnp.sum(dxn.astype(jnp.float32), axis=0)
        query_grad = dot32(column, dq, FIRST).reshape((width, heads, LANES))[:, :, :head_dim]
        kv_grad = dot32(column, dkv, FIRST).reshape((width, heads, LANES))
        lead_grad, attn_gain_grad = norm_backward(dxn, unit_in, scale_in, attn_gain)
        upstream = middle_grad + lead_grad

        qkv_part = jnp.concatenate([query_grad, kv_grad], axis=2).reshape(
            (2, COLUMNS, span, shard_rows, own_qkv)
        )
        out_part = out_grad.reshape((2, span, shard_rows, COLUMNS, own_out)).transpose(
            (0, 3, 1, 2, 4)
        )
        small_part = jnp.concatenate(
            [attn_gain_grad[:, None], moe_gain_grad[:, None], cgate_grad, cvec_grad], axis=1
        ).reshape((2, COLUMNS, span, shard_rows, 8))
        shared_grads[layer] = jnp.concatenate(
            [
                qkv_part.astype(jnp.bfloat16),
                out_part.astype(jnp.bfloat16),
                small_part.astype(jnp.bfloat16),
            ],
            axis=4,
        )

    packed = jnp.concatenate(shared_grads, axis=3)
    packed = jnp.pad(packed, ((0, 0),) * 4 + ((0, -packed.shape[4] % LANES),))
    reduced = plane_reduce(packed, blocks, 10)
    from_planes = column_exchange(reduced, blocks, False, 11).astype(jnp.float32)
    from_planes = from_planes.reshape((COLUMNS, LAYERS, shard_rows, -1))
    qkv_out = from_planes[..., :own_qkv].reshape(
        (COLUMNS, LAYERS, shard_rows, heads, 3, head_dim)
    )
    qkv_out = qkv_out.transpose((1, 2, 4, 0, 3, 5)).reshape((LAYERS, shard_rows, 3 * width))
    small_out = jnp.sum(from_planes[..., own_qkv + own_out : own_qkv + own_out + 8], axis=0)
    out_rows = reduced[..., own_qkv : own_qkv + own_out].reshape(
        (COLUMNS, LAYERS, shard_rows, own_out)
    )
    out_rows = out_rows.transpose((1, 2, 0, 3)).reshape((LAYERS, shard_rows, width))
    owners = [
        (y * blocks + z * span + r, (z * 2 + y) * span + r)
        for y in range(2)
        for z in range(COLUMNS)
        for r in range(span)
    ]
    out_rows = lax.ppermute(out_rows, ("head", "blk"), owners).astype(jnp.float32)
    stacked = [jnp.stack(group) for group in zip(*expert_grads)]
    return (
        output,
        upstream,
        qkv_out,
        out_rows,
        small_out[..., 0],
        small_out[..., 1],
        small_out[..., 2:6],
        small_out[..., 6:8],
        stacked[0],
        stacked[1],
        stacked[2],
    )


def solution(mesh):
    tokens = P(("head", "blk"), None)
    by_layer = P(None, ("head", "blk"), None)
    gains = P(None, ("head", "blk"))
    experts = P(None, "blk", "head")
    return jax.shard_map(
        per_device,
        mesh=mesh,
        in_specs=(
            tokens,
            P(None, "blk"),
            by_layer,
            by_layer,
            by_layer,
            by_layer,
            gains,
            gains,
            by_layer,
            by_layer,
            experts,
            experts,
            experts,
            tokens,
        ),
        out_specs=(
            tokens,
            tokens,
            by_layer,
            by_layer,
            gains,
            gains,
            by_layer,
            by_layer,
            experts,
            experts,
            experts,
        ),
        check_vma=False,
    )
```

```python
from functools import partial

import jax
import jax.numpy as jnp
from jax import lax
from jax.experimental import pallas as pl
from jax.experimental.pallas import tpu as pltpu
from jax.sharding import PartitionSpec as P

HEADS = 12
NE = 8
LAYERS = 2
CAP = 40
COLUMNS = 4
MESH = pl.DeviceIdType.MESH
ANY = pl.BlockSpec(memory_space=pl.ANY)
VMEM = pl.BlockSpec(memory_space=pltpu.VMEM)
DMA = pltpu.SemaphoreType.DMA
VMEM_BYTES = 48 * 1024 * 1024


def greet(peers):
    barrier = pltpu.get_barrier_semaphore()
    for peer in peers:
        pl.semaphore_signal(barrier, inc=1, device_id=peer, device_id_type=MESH)
    pl.semaphore_wait(barrier, len(peers))


def remote(src, dst, send_sem, recv_sem, peer):
    return pltpu.make_async_remote_copy(
        src_ref=src,
        dst_ref=dst,
        send_sem=send_sem,
        recv_sem=recv_sem,
        device_id=peer,
        device_id_type=MESH,
    )


def comm_params(collective_id):
    return pltpu.CompilerParams(
        collective_id=collective_id, has_side_effects=True, vmem_limit_bytes=VMEM_BYTES
    )


def lasting(microseconds):
    return pl.CostEstimate(
        flops=0, bytes_accessed=int(microseconds * 3_500_000), transcendentals=0
    )


def column_exchange(arrays, gathers, blocks, collective_id, cost=16):
    span = blocks // COLUMNS
    count = len(arrays)
    slabs = [
        tuple(values.shape if gather else values.shape[1:])
        for values, gather in zip(arrays, gathers)
    ]

    def body(*refs):
        srcs, dsts = refs[:count], refs[count : 2 * count]
        own_sems, send_sems, recv_sems = refs[2 * count :]
        head, blk = lax.axis_index("head"), lax.axis_index("blk")
        plane, rest = lax.div(blk, span), lax.rem(blk, span)
        planes = [lax.rem(plane + d, COLUMNS) for d in range(COLUMNS)]
        peers = [(head, p * span + rest) for p in planes]
        greet(peers[1:])
        waits, copies = [], []
        for n in range(count):
            own = pltpu.make_async_copy(
                srcs[n] if gathers[n] else srcs[n].at[plane], dsts[n].at[plane], own_sems.at[n]
            )
            own.start()
            waits.append(own)
        for n in range(count):
            for d in (2, 1, 3):
                copy = remote(
                    srcs[n] if gathers[n] else srcs[n].at[planes[d]],
                    dsts[n].at[plane],
                    send_sems.at[n, d],
                    recv_sems.at[n, d],
                    peers[d],
                )
                copy.start()
                copies.append(copy)
        for own in waits:
            own.wait()
        for copy in copies:
            copy.wait()

    return pl.pallas_call(
        body,
        out_shape=[
            jax.ShapeDtypeStruct((COLUMNS,) + slab, values.dtype)
            for values, slab in zip(arrays, slabs)
        ],
        in_specs=[ANY] * count,
        out_specs=[ANY] * count,
        scratch_shapes=[DMA((count,)), DMA((count, COLUMNS)), DMA((count, COLUMNS))],
        compiler_params=comm_params(collective_id),
        cost_estimate=lasting(cost),
    )(*arrays)


def plane_gather(arrays, blocks, collective_id, cost=16):
    span = blocks // COLUMNS
    width = span // 2
    count = len(arrays)
    links = 4 * (width - 1) + 2

    def body(*refs):
        srcs, dsts = refs[:count], refs[count : 2 * count]
        own_sems, send_sems, recv_sems, pass_sems, land_sems = refs[2 * count :]
        head, blk = lax.axis_index("head"), lax.axis_index("blk")
        plane, rest = lax.div(blk, span), lax.rem(blk, span)
        x, core = lax.div(rest, 2), lax.rem(rest, 2)
        first = plane * span
        right = [lax.rem(x + d, width) for d in range(width)]
        left = [lax.rem(x - d + width, width) for d in range(width)]
        x_peers = [(head, first + right[d] * 2 + core) for d in range(width)]
        y_peer = (1 - head, blk)
        core_peer = (head, first + x * 2 + 1 - core)
        greet(x_peers[1:] + [y_peer, core_peer])
        sends, passes = [], []

        def place(n, h, dy, d):
            half = srcs[n].shape[0] // 2
            row = head if dy == 0 else 1 - head
            return dsts[n].at[row, pl.ds(h * half, half), left[d] * 2 + core]

        def held(n, h, dy, d):
            half = srcs[n].shape[0] // 2
            return srcs[n].at[pl.ds(h * half, half)] if dy == 0 and d == 0 else place(n, h, dy, d)

        def send(n, h, dy, d, peer, to_dy, to_d):
            copy = remote(
                held(n, h, dy, d),
                place(n, h, dy, d),
                send_sems.at[len(sends)],
                recv_sems.at[n, h, to_dy, to_d],
                peer,
            )
            copy.start()
            sends.append(copy)

        def hand_over(n, h, dy, d):
            copy = remote(
                held(n, h, dy, d),
                place(n, h, dy, d),
                pass_sems.at[n, h, dy, d],
                land_sems.at[n, h, dy, d],
                core_peer,
            )
            copy.start()
            passes.append(copy)

        def arrived(n, h, dy, d):
            at = place(n, h, dy, d)
            remote(at, at, send_sems.at[0], recv_sems.at[n, h, dy, d], y_peer).wait_recv()

        owns = []
        for n in range(count):
            own = pltpu.make_async_copy(srcs[n], dsts[n].at[head, :, rest], own_sems.at[n])
            own.start()
            owns.append(own)
        for n in range(count):
            for d in range(1, width):
                send(n, 0, 0, 0, x_peers[d], 0, d)
            send(n, 1, 0, 0, y_peer, 1, 0)
            send(n, 0, 0, 0, y_peer, 1, 0)
            for d in range(1, width):
                send(n, 1, 0, 0, x_peers[d], 0, d)
            hand_over(n, 0, 0, 0)
            hand_over(n, 1, 0, 0)
        for n in range(count):
            for d in range(1, width):
                arrived(n, 0, 0, d)
                send(n, 0, 0, d, y_peer, 1, d)
                hand_over(n, 0, 0, d)
            arrived(n, 1, 1, 0)
            for d in range(1, width):
                send(n, 1, 1, 0, x_peers[d], 1, d)
            hand_over(n, 1, 1, 0)
        for n in range(count):
            arrived(n, 0, 1, 0)
            hand_over(n, 0, 1, 0)
            for d in range(1, width):
                arrived(n, 1, 0, d)
                hand_over(n, 1, 0, d)
            for d in range(1, width):
                arrived(n, 0, 1, d)
                hand_over(n, 0, 1, d)
                arrived(n, 1, 1, d)
                hand_over(n, 1, 1, d)
        for own in owns:
            own.wait()
        for copy in passes:
            copy.wait()
        for copy in sends:
            copy.wait_send()

    return pl.pallas_call(
        body,
        out_shape=[
            jax.ShapeDtypeStruct(
                (2, values.shape[0], span) + tuple(values.shape[1:]), values.dtype
            )
            for values in arrays
        ],
        in_specs=[ANY] * count,
        out_specs=[ANY] * count,
        scratch_shapes=[
            DMA((count,)),
            DMA((count * links,)),
            DMA((count, 2, 2, width)),
            DMA((count, 2, 2, width)),
            DMA((count, 2, 2, width)),
        ],
        compiler_params=comm_params(collective_id),
        cost_estimate=lasting(cost),
    )(*arrays)


def plane_reduce(values, blocks, collective_id):
    span = blocks // COLUMNS
    width = span // 2
    slabs, rows, cols = values.shape[1], values.shape[3], values.shape[4]
    half = slabs // 2
    kind = values.dtype

    def body(
        src,
        out,
        core_in,
        summed,
        xa_in,
        ya_out,
        ya_in,
        yb_in,
        xb_out,
        xb_in,
        core_send,
        core_recv,
        link_send,
        link_recv,
    ):
        head, blk = lax.axis_index("head"), lax.axis_index("blk")
        plane, rest = lax.div(blk, span), lax.rem(blk, span)
        x, core = lax.div(rest, 2), lax.rem(rest, 2)
        first = plane * span
        right = [lax.rem(x + d, width) for d in range(width)]
        x_peers = [(head, first + right[d] * 2 + core) for d in range(width)]
        y_peer = (1 - head, blk)
        core_peer = (head, first + x * 2 + 1 - core)
        greet(x_peers[1:] + [y_peer, core_peer])

        def wide(ref, *at):
            return ref[at].astype(jnp.float32)

        starts = []
        for h in range(2):
            copy = remote(
                src.at[:, pl.ds(h * half, half), :, 1 - core],
                core_in.at[:, pl.ds(h * half, half)],
                core_send.at[h],
                core_recv.at[h],
                core_peer,
            )
            copy.start()
            starts.append(copy)

        def core_sum(h):
            def step(i, _):
                yy = lax.div(i, half * width)
                zz = lax.div(lax.rem(i, half * width), width) + h * half
                xx = lax.rem(i, width)
                total = wide(src, yy, zz, xx, core) + wide(core_in, yy, zz, xx)
                summed[yy, zz, xx] = total.astype(kind)
                return 0

            lax.fori_loop(0, 2 * half * width, step, 0)

        sends = []
        starts[0].wait_recv()
        core_sum(0)
        for d in range(1, width):
            copy = remote(
                summed.at[:, pl.ds(0, half), right[d]],
                xa_in.at[d],
                link_send.at[0, d],
                link_recv.at[0, d],
                x_peers[d],
            )
            copy.start()
            sends.append(copy)
        starts[1].wait_recv()
        core_sum(1)
        yb = remote(
            summed.at[1 - head, pl.ds(half, half)],
            yb_in,
            link_send.at[1, 0],
            link_recv.at[1, 0],
            y_peer,
        )
        yb.start()
        for copy in sends:
            copy.wait_recv()

        def a_step(zz, _):
            total = wide(summed, 1 - head, zz, x)
            for d in range(1, width):
                total = total + wide(xa_in, d, 1 - head, zz)
            ya_out[zz] = total.astype(kind)
            return 0

        lax.fori_loop(0, half, a_step, 0)
        ya = remote(ya_out, ya_in, link_send.at[0, 0], link_recv.at[0, 0], y_peer)
        ya.start()
        yb.wait_recv()
        xb_sends = []
        for d in range(1, width):

            def b_step(zz, _):
                total = wide(summed, head, half + zz, right[d]) + wide(yb_in, zz, right[d])
                xb_out[d, zz] = total.astype(kind)
                return 0

            lax.fori_loop(0, half, b_step, 0)
            copy = remote(
                xb_out.at[d], xb_in.at[d], link_send.at[1, d], link_recv.at[1, d], x_peers[d]
            )
            copy.start()
            xb_sends.append(copy)
        ya.wait_recv()

        def a_last(zz, _):
            total = wide(summed, head, zz, x) + wide(ya_in, zz)
            for d in range(1, width):
                total = total + wide(xa_in, d, head, zz)
            out[zz] = total.astype(kind)
            return 0

        lax.fori_loop(0, half, a_last, 0)
        for copy in xb_sends:
            copy.wait_recv()

        def b_last(zz, _):
            total = wide(summed, head, half + zz, x) + wide(yb_in, zz, x)
            for d in range(1, width):
                total = total + wide(xb_in, d, zz)
            out[half + zz] = total.astype(kind)
            return 0

        lax.fori_loop(0, half, b_last, 0)
        for copy in starts + sends + [yb, ya] + xb_sends:
            copy.wait_send()

    tile = (rows, cols)
    return pl.pallas_call(
        body,
        out_shape=jax.ShapeDtypeStruct((slabs,) + tile, kind),
        in_specs=[VMEM],
        out_specs=VMEM,
        scratch_shapes=[
            pltpu.VMEM((2, slabs, width) + tile, kind),
            pltpu.VMEM((2, slabs, width) + tile, kind),
            pltpu.VMEM((width, 2, half) + tile, kind),
            pltpu.VMEM((half,) + tile, kind),
            pltpu.VMEM((half,) + tile, kind),
            pltpu.VMEM((half, width) + tile, kind),
            pltpu.VMEM((width, half) + tile, kind),
            pltpu.VMEM((width, half) + tile, kind),
            DMA((2,)),
            DMA((2,)),
            DMA((2, width)),
            DMA((2, width)),
        ],
        compiler_params=comm_params(collective_id),
        cost_estimate=lasting(25),
    )(values.reshape((2, slabs, width, 2) + tile))


def expert_dispatch(buffer, blocks, collective_id):
    copies = blocks // NE
    tile = tuple(buffer.shape[1:])

    def body(src, dst, own_sem, send_sems, recv_sems, pass_sems, land_sems):
        head, blk = lax.axis_index("head"), lax.axis_index("blk")
        expert, piece = lax.div(blk, copies), lax.rem(blk, copies)
        ahead = [lax.rem(expert + d, NE) for d in range(NE)]
        behind = [lax.rem(expert - d + NE, NE) for d in range(NE)]
        peers = [(head, ahead[d] * copies + piece) for d in range(NE)]
        siblings = [
            (head, expert * copies + lax.rem(piece + k, copies)) for k in range(copies)
        ]
        greet(peers[1:] + siblings[1:])
        own = pltpu.make_async_copy(src.at[expert], dst.at[piece, expert], own_sem)
        own.start()
        sends, passes = [], []
        for d in (4, 3, 5, 2, 6, 1, 7):
            copy = remote(
                src.at[ahead[d]],
                dst.at[piece, expert],
                send_sems.at[d],
                recv_sems.at[d],
                peers[d],
            )
            copy.start()
            sends.append(copy)
        for d in (0, 1, 7, 2, 6, 3, 5, 4):
            place = dst.at[piece, behind[d]]
            if d > 0:
                remote(place, place, send_sems.at[d], recv_sems.at[d], peers[d]).wait_recv()
            for k in range(1, copies):
                copy = remote(
                    place if d > 0 else src.at[expert],
                    place,
                    pass_sems.at[k, d],
                    land_sems.at[k, d],
                    siblings[k],
                )
                copy.start()
                passes.append(copy)
        own.wait()
        for copy in passes:
            copy.wait()
        for copy in sends:
            copy.wait_send()

    return pl.pallas_call(
        body,
        out_shape=jax.ShapeDtypeStruct((copies, NE) + tile, buffer.dtype),
        in_specs=[ANY],
        out_specs=ANY,
        scratch_shapes=[DMA, DMA((NE,)), DMA((NE,)), DMA((copies, NE)), DMA((copies, NE))],
        compiler_params=comm_params(collective_id),
        cost_estimate=lasting(15),
    )(buffer)


def expert_return(parts, blocks, collective_id):
    copies = blocks // NE
    tile = tuple(parts.shape[2:])
    kind = parts.dtype

    def body(src, dst, sib_in, total, own_sem, send_sems, recv_sems, pass_sems, land_sems):
        head, blk = lax.axis_index("head"), lax.axis_index("blk")
        expert, piece = lax.div(blk, copies), lax.rem(blk, copies)
        ahead = [lax.rem(expert + d, NE) for d in range(NE)]
        peers = [(head, ahead[d] * copies + piece) for d in range(NE)]
        places = [lax.rem(piece + k, copies) for k in range(copies)]
        siblings = [(head, expert * copies + places[k]) for k in range(copies)]
        greet(peers[1:] + siblings[1:])
        order = (4, 3, 5, 2, 6, 1, 7, 0)
        passes, sends = {}, []
        for d in order:
            for k in range(1, copies):
                copy = remote(
                    src.at[places[k], ahead[d]],
                    sib_in.at[k, ahead[d]],
                    pass_sems.at[k, d],
                    land_sems.at[k, d],
                    siblings[k],
                )
                copy.start()
                passes[k, d] = copy
        for d in order:
            value = src[piece, ahead[d]].astype(jnp.float32)
            for k in range(1, copies):
                passes[k, d].wait_recv()
                value = value + sib_in[k, ahead[d]].astype(jnp.float32)
            total[ahead[d]] = value.astype(kind)
            if d > 0:
                copy = remote(
                    total.at[ahead[d]],
                    dst.at[expert],
                    send_sems.at[d],
                    recv_sems.at[d],
                    peers[d],
                )
                copy.start()
                sends.append(copy)
        own = pltpu.make_async_copy(total.at[expert], dst.at[expert], own_sem)
        own.start()
        own.wait()
        for copy in sends:
            copy.wait()
        for copy in passes.values():
            copy.wait_send()

    return pl.pallas_call(
        body,
        out_shape=jax.ShapeDtypeStruct((NE,) + tile, kind),
        in_specs=[VMEM],
        out_specs=ANY,
        scratch_shapes=[
            pltpu.VMEM((copies, NE) + tile, kind),
            pltpu.VMEM((NE,) + tile, kind),
            DMA,
            DMA((NE,)),
            DMA((NE,)),
            DMA((copies, NE)),
            DMA((copies, NE)),
        ],
        compiler_params=comm_params(collective_id),
        cost_estimate=lasting(15),
    )(parts)


NEGATIVE = -1e30
EPSILON = 1e-06
HIGHEST = lax.Precision.HIGHEST
KEYS = 512
LANES = 128
LAST = (((1,), (1,)), ((), ()))
FIRST = (((0,), (0,)), ((), ()))


def dot32(a, b, dims=(((1,), (0,)), ((), ()))):
    return lax.dot_general(a, b, dims, preferred_element_type=jnp.float32)


def visible(key_base, query_base, keys, queries, starts):
    key_pos = key_base + lax.broadcasted_iota(jnp.int32, (keys, queries), 0)
    query_pos = query_base + lax.broadcasted_iota(jnp.int32, (keys, queries), 1)
    return (key_pos <= query_pos) & (key_pos >= starts)


def attend(bounds, queries, kv_all, starts):
    count, rows, width = queries.shape
    heads = width // LANES

    def body(bounds_ref, q_ref, kv_ref, start_ref, out_ref):
        i = pl.program_id(0)
        low, high, base = bounds_ref[i, 0], bounds_ref[i, 1], bounds_ref[i, 2]
        start_row = start_ref[0]
        q = [q_ref[0, :, h * LANES : (h + 1) * LANES] for h in range(heads)]

        def step(t, carry):
            chunk = high - t
            at = pl.multiple_of(chunk * KEYS, KEYS)
            ok = visible(chunk * KEYS, base, KEYS, rows, start_row)
            new = []
            for h in range(heads):
                top, total, acc = carry[h]
                kv = kv_ref[pl.ds(at, KEYS), h * LANES : (h + 1) * LANES]
                score = jnp.where(ok, dot32(kv, q[h], LAST), NEGATIVE)
                new_top = jnp.maximum(top, jnp.max(score, axis=0, keepdims=True))
                weight = jnp.exp(score - new_top)
                shrink = jnp.exp(top - new_top)
                total = total * shrink + jnp.sum(weight, axis=0, keepdims=True)
                acc = acc * shrink + dot32(kv, weight.astype(jnp.bfloat16), FIRST)
                new.append((new_top, total, acc))
            return tuple(new)

        empty = tuple(
            (
                jnp.full((1, rows), NEGATIVE, jnp.float32),
                jnp.zeros((1, rows), jnp.float32),
                jnp.zeros((LANES, rows), jnp.float32),
            )
            for h in range(heads)
        )
        done = lax.fori_loop(0, high - low + 1, step, empty)
        lane = lax.broadcasted_iota(jnp.int32, (LANES, rows), 0)
        for h in range(heads):
            top, total, acc = done[h]
            value = jnp.where(lane < LANES // 2, top + jnp.log(total), acc / total)
            out_ref[0, :, h * LANES : (h + 1) * LANES] = value.T

    return pl.pallas_call(
        body,
        out_shape=jax.ShapeDtypeStruct((count, rows, width), jnp.float32),
        grid_spec=pltpu.PrefetchScalarGridSpec(
            num_scalar_prefetch=1,
            grid=(count,),
            in_specs=[
                pl.BlockSpec((1, rows, width), lambda i, b: (i, 0, 0)),
                pl.BlockSpec(kv_all.shape, lambda i, b: (0, 0)),
                pl.BlockSpec((1, 1, rows), lambda i, b: (i, 0, 0)),
            ],
            out_specs=pl.BlockSpec((1, rows, width), lambda i, b: (i, 0, 0)),
        ),
        compiler_params=pltpu.CompilerParams(vmem_limit_bytes=VMEM_BYTES),
        cost_estimate=pl.CostEstimate(
            flops=2 * count * rows * kv_all.shape[0] * width,
            bytes_accessed=kv_all.size * 2,
            transcendentals=count * rows * kv_all.shape[0],
        ),
    )(bounds, queries, kv_all, starts)


def attend_back(bounds, queries, grads, kept, kv_all, starts, scale):
    count, rows, width = queries.shape
    total_keys = kv_all.shape[0]
    heads = width // LANES
    if total_keys * width * 14 > VMEM_BYTES:
        heads = 1
    wide = heads * LANES

    def body(bounds_ref, q_ref, g_ref, kept_ref, kv_ref, start_ref, dq_ref, dkv_ref, acc_ref):
        i = pl.program_id(1)
        low, high, base = bounds_ref[i, 0], bounds_ref[i, 1], bounds_ref[i, 2]
        start_row = start_ref[0]

        @pl.when(i == 0)
        def _():
            def clear(c, _):
                acc_ref[pl.ds(pl.multiple_of(c * KEYS, KEYS), KEYS), :] = jnp.zeros(
                    (KEYS, wide), jnp.float32
                )
                return 0

            lax.fori_loop(0, total_keys // KEYS, clear, 0)

        q = [q_ref[0, :, h * LANES : (h + 1) * LANES] for h in range(heads)]
        g = [g_ref[0, :, h * LANES : (h + 1) * LANES] for h in range(heads)]
        lse, delta = [], []
        for h in range(heads):
            kept_t = kept_ref[0, :, h * LANES : (h + 1) * LANES].T
            lse.append(kept_t[0:1])
            delta.append(jnp.sum(kept_t * g[h].astype(jnp.float32).T, axis=0, keepdims=True))

        def step(t, carry):
            chunk = high - t
            at = pl.multiple_of(chunk * KEYS, KEYS)
            ok = visible(chunk * KEYS, base, KEYS, rows, start_row)
            new = []
            for h in range(heads):
                lanes = slice(h * LANES, (h + 1) * LANES)
                kv = kv_ref[pl.ds(at, KEYS), lanes]
                score = jnp.where(ok, dot32(kv, q[h], LAST), NEGATIVE)
                prob = jnp.exp(score - lse[h])
                dscore = (prob * (dot32(kv, g[h], LAST) - delta[h])).astype(jnp.bfloat16)
                acc_ref[pl.ds(at, KEYS), lanes] += dot32(dscore, q[h]) + dot32(
                    prob.astype(jnp.bfloat16), g[h]
                )
                new.append(carry[h] + dot32(kv, dscore, FIRST))
            return tuple(new)

        done = lax.fori_loop(
            0,
            high - low + 1,
            step,
            tuple(jnp.zeros((LANES, rows), jnp.float32) for h in range(heads)),
        )
        lane = lax.broadcasted_iota(jnp.int32, (LANES, rows), 0)
        for h in range(heads):
            value = jnp.where(lane < LANES // 2, done[h] * scale, 0.0)
            dq_ref[0, :, h * LANES : (h + 1) * LANES] = value.T.astype(jnp.bfloat16)

        @pl.when(i == count - 1)
        def _():
            def store(c, _):
                at = pl.ds(pl.multiple_of(c * KEYS, KEYS), KEYS)
                dkv_ref[at, :] = acc_ref[at, :].astype(jnp.bfloat16)
                return 0

            lax.fori_loop(0, total_keys // KEYS, store, 0)

    block = pl.BlockSpec((1, rows, wide), lambda h, i, b: (i, 0, h))
    whole = pl.BlockSpec((total_keys, wide), lambda h, i, b: (0, h))
    return pl.pallas_call(
        body,
        out_shape=(
            jax.ShapeDtypeStruct((count, rows, width), jnp.bfloat16),
            jax.ShapeDtypeStruct(kv_all.shape, jnp.bfloat16),
        ),
        grid_spec=pltpu.PrefetchScalarGridSpec(
            num_scalar_prefetch=1,
            grid=(width // wide, count),
            in_specs=[
                block,
                block,
                block,
                whole,
                pl.BlockSpec((1, 1, rows), lambda h, i, b: (i, 0, 0)),
            ],
            out_specs=(block, whole),
            scratch_shapes=[pltpu.VMEM((total_keys, wide), jnp.float32)],
        ),
        compiler_params=pltpu.CompilerParams(vmem_limit_bytes=VMEM_BYTES),
        cost_estimate=pl.CostEstimate(
            flops=5 * count * rows * total_keys * width,
            bytes_accessed=kv_all.size * 4,
            transcendentals=count * rows * total_keys,
        ),
    )(bounds, queries, grads, kept, kv_all, starts)


def expert_forward(head, rows_in, own, other):
    count, width = rows_in.shape
    hidden, features = own[0].shape
    tile = min(hidden, 256)
    steps = hidden // tile

    def body(head_ref, x_ref, go, gx, uo, ux, do, dx, out_ref, acc_ref):
        i = pl.program_id(0)
        mine = pl.ds(pl.multiple_of(head_ref[0] * features, LANES), features)
        rest = pl.ds(pl.multiple_of((1 - head_ref[0]) * features, LANES), features)
        xo, xx = x_ref[:, mine], x_ref[:, rest]
        gate = dot32(xo, go[...], LAST) + dot32(xx, gx[...], LAST)
        up = dot32(xo, uo[...], LAST) + dot32(xx, ux[...], LAST)
        act = (jax.nn.silu(gate) * up).astype(jnp.bfloat16)

        @pl.when(i == 0)
        def _():
            acc_ref[...] = jnp.zeros_like(acc_ref)

        acc_ref[:, mine] += dot32(act, do[...])
        acc_ref[:, rest] += dot32(act, dx[...])

        @pl.when(i == steps - 1)
        def _():
            out_ref[...] = acc_ref[...].astype(jnp.bfloat16)

    whole = pl.BlockSpec((count, width), lambda i, h: (0, 0))
    piece = pl.BlockSpec((tile, features), lambda i, h: (i, 0))
    weights = [w for pair in zip(own, other) for w in pair]
    return pl.pallas_call(
        body,
        out_shape=jax.ShapeDtypeStruct((count, width), jnp.bfloat16),
        grid_spec=pltpu.PrefetchScalarGridSpec(
            num_scalar_prefetch=1,
            grid=(steps,),
            in_specs=[whole] + [piece] * 6,
            out_specs=whole,
            scratch_shapes=[pltpu.VMEM((count, width), jnp.float32)],
        ),
        compiler_params=pltpu.CompilerParams(vmem_limit_bytes=VMEM_BYTES),
        cost_estimate=pl.CostEstimate(
            flops=6 * count * width * hidden,
            bytes_accessed=6 * hidden * features * 2 + 4 * count * width,
            transcendentals=count * hidden,
        ),
    )(head, rows_in, *weights)


def expert_backward(head, rows_in, grads_in, own, other):
    count, width = rows_in.shape
    hidden, features = own[0].shape
    tile = min(hidden, 256)
    steps = hidden // tile

    def body(head_ref, x_ref, z_ref, go, gx, uo, ux, do, dx, *outs):
        keeps, sends, out_ref, acc_ref = outs[:3], outs[3:6], outs[6], outs[7]
        i = pl.program_id(0)
        mine = pl.ds(pl.multiple_of(head_ref[0] * features, LANES), features)
        rest = pl.ds(pl.multiple_of((1 - head_ref[0]) * features, LANES), features)
        xo, xx = x_ref[:, mine], x_ref[:, rest]
        zo, zx = z_ref[:, mine], z_ref[:, rest]
        gate = dot32(xo, go[...], LAST) + dot32(xx, gx[...], LAST)
        up = dot32(xo, uo[...], LAST) + dot32(xx, ux[...], LAST)
        dact = dot32(zo, do[...], LAST) + dot32(zx, dx[...], LAST)
        sigmoid = jax.nn.sigmoid(gate)
        silu = gate * sigmoid
        act = (silu * up).astype(jnp.bfloat16)
        dgate = (dact * up * sigmoid * (1.0 + gate * (1.0 - sigmoid))).astype(jnp.bfloat16)
        dup = (dact * silu).astype(jnp.bfloat16)

        @pl.when(i == 0)
        def _():
            acc_ref[...] = jnp.zeros_like(acc_ref)

        acc_ref[:, mine] += dot32(dgate, go[...]) + dot32(dup, uo[...])
        acc_ref[:, rest] += dot32(dgate, gx[...]) + dot32(dup, ux[...])
        for n, (left, mine_in, rest_in) in enumerate(((dgate, xo, xx), (dup, xo, xx), (act, zo, zx))):
            keeps[n][...] = dot32(left, mine_in, FIRST)
            sends[n][...] = dot32(left, rest_in, FIRST).astype(jnp.bfloat16)

        @pl.when(i == steps - 1)
        def _():
            out_ref[...] = acc_ref[...].astype(jnp.bfloat16)

    whole = pl.BlockSpec((count, width), lambda i, h: (0, 0))
    piece = pl.BlockSpec((tile, features), lambda i, h: (i, 0))
    weights = [w for pair in zip(own, other) for w in pair]
    return pl.pallas_call(
        body,
        out_shape=[jax.ShapeDtypeStruct((hidden, features), jnp.float32)] * 3
        + [jax.ShapeDtypeStruct((hidden, features), jnp.bfloat16)] * 3
        + [jax.ShapeDtypeStruct((count, width), jnp.bfloat16)],
        grid_spec=pltpu.PrefetchScalarGridSpec(
            num_scalar_prefetch=1,
            grid=(steps,),
            in_specs=[whole, whole] + [piece] * 6,
            out_specs=[piece] * 6 + [whole],
            scratch_shapes=[pltpu.VMEM((count, width), jnp.float32)],
        ),
        compiler_params=pltpu.CompilerParams(vmem_limit_bytes=VMEM_BYTES),
        cost_estimate=pl.CostEstimate(
            flops=22 * count * width * hidden,
            bytes_accessed=15 * hidden * features * 2 + 8 * count * width,
            transcendentals=count * hidden,
        ),
    )(head, rows_in, grads_in, *weights)


def norm_forward(values, gain_vec):
    row_scale = lax.rsqrt(jnp.mean(values * values, axis=-1, keepdims=True) + EPSILON)
    normed = values * row_scale
    return normed * gain_vec, normed, row_scale


def norm_backward(upstream, normed, row_scale, gain_vec):
    through = upstream * gain_vec
    gain_grad = jnp.sum(upstream * normed, axis=0)
    inner_mean = jnp.mean(through * normed, axis=-1, keepdims=True)
    return row_scale * (through - normed * inner_mean), gain_grad


def slot_index(route_ids):
    token_rows = route_ids.shape[0]
    expert_ids = jnp.arange(NE, dtype=jnp.int32)
    matches = (
        (route_ids[:, :, None] == expert_ids[None, None, :])
        .astype(jnp.int32)
        .reshape((token_rows * 2, NE))
    )
    before = jnp.cumsum(matches, axis=0) - 1
    slot_pos = jnp.sum(matches * before, axis=1).reshape((token_rows, 2))
    return jnp.where(route_ids < NE, route_ids * CAP + slot_pos, NE * CAP)


def per_device(
    tokens,
    segments,
    routes,
    gates,
    w_qkv,
    w_out,
    gain_attn,
    gain_moe,
    const_gate,
    const_vec,
    w_gate,
    w_up,
    w_down,
    cotangent,
):
    blocks = lax.axis_size("blk")
    head_index, blk_index = lax.axis_index("head"), lax.axis_index("blk")
    span = blocks // COLUMNS
    plane, rest = lax.div(blk_index, span), lax.rem(blk_index, span)
    shards = 2 * blocks
    token_rows, width = tokens.shape
    shard_rows = width // shards
    head_dim = width // HEADS
    heads = HEADS // COLUMNS
    scale = head_dim ** (-0.5)
    half_length = blocks * token_rows
    positions = 2 * half_length
    features = w_gate.shape[2]
    hidden_rows = w_gate.shape[1]
    copies = blocks // NE
    own_qkv = heads * 3 * head_dim
    own_out = heads * head_dim

    swap = [(0, 1), (1, 0)]
    head_scalar = head_index.reshape((1,)).astype(jnp.int32)

    seg_own = lax.dynamic_index_in_dim(segments, head_index, 0, keepdims=False)
    seg_parts = jnp.concatenate([lax.rem(seg_own, 128), lax.div(seg_own, 128)]).astype(
        jnp.bfloat16
    )
    seg_columns = -(-seg_parts.shape[0] // shard_rows)
    seg_parts = jnp.pad(seg_parts, (0, seg_columns * shard_rows - seg_parts.shape[0]))
    seg_parts = seg_parts.reshape((shard_rows, seg_columns))
    packs = []
    for layer in range(LAYERS):
        split = w_qkv[layer].reshape((shard_rows, 3, COLUMNS, heads, head_dim))
        query_part = jnp.pad(split[:, 0], ((0, 0),) * 3 + ((0, LANES - head_dim),))
        kv_part = jnp.concatenate([split[:, 1], split[:, 2]], axis=3)
        side = jnp.concatenate(
            [
                w_out[layer],
                gain_attn[layer][:, None],
                gain_moe[layer][:, None],
                const_gate[layer],
                const_vec[layer],
                seg_parts,
            ],
            axis=1,
        )
        side = jnp.pad(side, ((0, 0), (0, -side.shape[1] % LANES)))
        pack = jnp.concatenate(
            [
                query_part.transpose((1, 0, 2, 3)).reshape((COLUMNS, shard_rows, heads * LANES)),
                kv_part.transpose((1, 0, 2, 3)).reshape((COLUMNS, shard_rows, heads * LANES)),
                jnp.broadcast_to(side[None], (COLUMNS,) + side.shape),
            ],
            axis=2,
        )
        packs.append(pack)
    *packs, column_tokens = column_exchange(
        packs + [tokens], [False] * LAYERS + [True], blocks, 1, 14
    )
    weights = plane_gather(packs, blocks, 2, 24)
    weights = [pack.reshape((shards, shard_rows, -1)) for pack in weights]
    out_at = 2 * heads * LANES
    small_at = out_at + width

    def send_experts(layer, after):
        held = lax.optimization_barrier(
            tuple(w[layer] for w in (w_gate, w_up, w_down)) + (after,)
        )[:3]
        return held, [lax.ppermute(w, "head", swap) for w in held]

    own_experts, other_experts = [None] * LAYERS, [None] * LAYERS
    own_experts[0], other_experts[0] = send_experts(0, weights[0])

    seg_all = weights[0][:, :, small_at + 8 : small_at + 8 + seg_columns]
    seg_all = seg_all.reshape((shards, -1))[:, : 2 * token_rows].astype(jnp.int32)
    seg_all = seg_all[:, :token_rows] + 128 * seg_all[:, token_rows:]
    seg_query = lax.dynamic_index_in_dim(
        seg_all.reshape((2, COLUMNS, span, token_rows)), head_index, 0, keepdims=False
    )
    seg_query = lax.dynamic_index_in_dim(seg_query, rest, 1, keepdims=False)
    starts = jnp.sum(
        (seg_all.reshape((1, 1, -1)) < seg_query[:, :, None]).astype(jnp.int32), axis=2
    )
    bases = (
        head_index * half_length
        + (jnp.arange(COLUMNS, dtype=jnp.int32) * span + rest) * token_rows
    )
    bounds = jnp.stack(
        [lax.div(starts[:, 0], KEYS), lax.div(bases + token_rows - 1, KEYS), bases], axis=1
    )
    starts = starts[:, None, :]

    layers = []
    for pack in weights:
        rows = pack.reshape((width, -1))
        query_w = rows[:, : heads * LANES]
        kv_w = rows[:, heads * LANES : out_at]
        out_w = rows[:, out_at:small_at]
        small_w = rows[:, small_at : small_at + 8]
        layers.append((query_w, kv_w, out_w, small_w))

    residual = tokens.astype(jnp.float32)
    kept = []
    for layer in range(LAYERS):
        query_w, kv_w, out_w, small_w = layers[layer]
        attn_gain = small_w[:, 0].astype(jnp.float32)
        moe_gain = small_w[:, 1].astype(jnp.float32)
        gate_w = small_w[:, 2:6]
        vectors = small_w[:, 6:8].astype(jnp.float32).T
        normed_in, unit_in, scale_in = norm_forward(residual, attn_gain)
        if layer == 0:
            column = norm_forward(column_tokens.astype(jnp.float32), attn_gain)[0]
            column = column.astype(jnp.bfloat16)
        else:
            (column,) = column_exchange([normed_in.astype(jnp.bfloat16)], [True], blocks, 3)
        column = column.reshape((COLUMNS * token_rows, width))
        queries = (
            dot32(column, query_w).astype(jnp.bfloat16).astype(jnp.float32) * scale
        ).astype(jnp.bfloat16)
        queries = queries.reshape((COLUMNS, token_rows, heads * LANES))
        kv_own = dot32(column, kv_w).astype(jnp.bfloat16)
        (kv_all,) = plane_gather(
            [kv_own.reshape((COLUMNS, token_rows, heads * LANES))], blocks, 4
        )
        kv_all = kv_all.reshape((positions, heads * LANES))
        attended = attend(bounds, queries, kv_all, starts)
        attn_col = (
            attended.reshape((COLUMNS, token_rows, heads, LANES))[..., head_dim:]
            .reshape((COLUMNS, token_rows, own_out))
            .astype(jnp.bfloat16)
        )
        (attn,) = column_exchange([attn_col], [False], blocks, 5, 9)
        attn = attn.transpose((1, 0, 2)).reshape((token_rows, width))
        middle = residual + dot32(attn, out_w)
        normed_mid, unit_mid, scale_mid = norm_forward(middle, moe_gain)
        moe_in = normed_mid.astype(jnp.bfloat16)
        moe_float = moe_in.astype(jnp.float32)
        route_ids, gate_vals = routes[layer], gates[layer]
        slots = slot_index(route_ids)
        named = slots[:, :, None] == jnp.arange(NE * CAP, dtype=jnp.int32)[None, None, :]
        picks = jnp.any(named, axis=1)
        pick_gates = jnp.sum(jnp.where(named, gate_vals[:, :, None], 0.0), axis=1)
        sent = dot32(picks.astype(jnp.bfloat16), moe_in, FIRST).astype(jnp.bfloat16)
        arrived = expert_dispatch(sent.reshape((NE, CAP, width)), blocks, 6)
        flat_in = arrived.reshape((-1, width))
        if layer + 1 < LAYERS:
            own_experts[layer + 1], other_experts[layer + 1] = send_experts(layer + 1, flat_in)
        parts = expert_forward(head_scalar, flat_in, own_experts[layer], other_experts[layer])
        back = expert_return(parts.reshape((copies, NE, CAP, width)), blocks, 7)
        back = back.reshape((NE * CAP, width)).astype(jnp.float32)
        ffn_out = jnp.dot(pick_gates, back, precision=HIGHEST)
        copy_weight = jnp.sum(jnp.where(route_ids == NE + 1, gate_vals, 0.0), axis=1)
        const_weight = jnp.stack(
            [
                jnp.sum(jnp.where(route_ids == NE + 2 + c, gate_vals, 0.0), axis=1)
                for c in range(2)
            ],
            axis=1,
        )
        mixing = jax.nn.softmax(dot32(moe_in, gate_w).reshape((token_rows, 2, 2)), axis=-1)
        const_out = jnp.sum(
            const_weight[:, :, None]
            * (mixing[:, :, 0:1] * moe_float[:, None, :] + mixing[:, :, 1:2] * vectors[None]),
            axis=1,
        )
        residual = middle + ffn_out + copy_weight[:, None] * moe_float + const_out
        kept.append(
            (
                unit_in,
                scale_in,
                column,
                queries,
                kv_all,
                attended,
                attn_col,
                unit_mid,
                scale_mid,
                moe_float,
                picks,
                pick_gates,
                flat_in,
                copy_weight,
                const_weight,
                mixing,
            )
        )
    output = residual

    upstream = cotangent.astype(jnp.float32)
    shared_grads = [None] * LAYERS
    expert_grads = [None] * LAYERS
    for layer in reversed(range(LAYERS)):
        query_w, kv_w, out_w, small_w = layers[layer]
        attn_gain = small_w[:, 0].astype(jnp.float32)
        moe_gain = small_w[:, 1].astype(jnp.float32)
        gate_w = small_w[:, 2:6].astype(jnp.float32)
        vectors = small_w[:, 6:8].astype(jnp.float32).T
        (
            unit_in,
            scale_in,
            column,
            queries,
            kv_all,
            attended,
            attn_col,
            unit_mid,
            scale_mid,
            moe_float,
            picks,
            pick_gates,
            flat_in,
            copy_weight,
            const_weight,
            mixing,
        ) = kept[layer]
        picked = jnp.dot(picks.astype(jnp.float32).T, upstream, precision=HIGHEST)
        dz = (jnp.sum(pick_gates, axis=0)[:, None] * picked).astype(jnp.bfloat16)
        dz_in = expert_dispatch(dz.reshape((NE, CAP, width)), blocks, 6).reshape((-1, width))

        mix_grad = const_weight[:, :, None] * upstream[:, None, :]
        alpha_grad = jnp.stack(
            [
                jnp.sum(mix_grad * moe_float[:, None, :], axis=-1),
                jnp.sum(mix_grad * vectors[None], axis=-1),
            ],
            axis=-1,
        )
        logit_grad = (
            mixing * (alpha_grad - jnp.sum(mixing * alpha_grad, axis=-1, keepdims=True))
        ).reshape((token_rows, 4))
        hn_grad = (
            copy_weight[:, None] * upstream
            + jnp.sum(mixing[:, :, 0:1] * mix_grad, axis=1)
            + jnp.dot(logit_grad, gate_w.T, precision=HIGHEST)
        )
        cgate_grad = jnp.dot(moe_float.T, logit_grad, precision=HIGHEST)
        cvec_grad = jnp.sum(mixing[:, :, 1:2] * mix_grad, axis=0).T

        *wgrads, dparts = expert_backward(
            head_scalar, flat_in, dz_in, own_experts[layer], other_experts[layer]
        )
        dback = expert_return(dparts.reshape((copies, NE, CAP, width)), blocks, 7)
        got = [lax.ppermute(away, "head", swap) for away in wgrads[3:]]

        hn_grad = hn_grad + dot32(
            picks.astype(jnp.bfloat16), dback.reshape((NE * CAP, width))
        )
        middle_grad, moe_gain_grad = norm_backward(hn_grad, unit_mid, scale_mid, moe_gain)
        middle_grad = middle_grad + upstream
        (dy,) = column_exchange([middle_grad.astype(jnp.bfloat16)], [True], blocks, 3)
        dy = dy.reshape((COLUMNS * token_rows, width))
        out_rows = lax.dynamic_slice_in_dim(out_w, plane * own_out, own_out, 0)
        out_rows = jnp.pad(
            out_rows.reshape((heads, head_dim, width)), ((0, 0), (LANES - head_dim, 0), (0, 0))
        ).reshape((heads * LANES, width))
        dattn = dot32(dy, out_rows, LAST).astype(jnp.bfloat16)
        dattn = dattn.reshape((COLUMNS, token_rows, heads * LANES))
        out_grad = dot32(attn_col.reshape((-1, own_out)), dy, FIRST)
        dq, dkv_all = attend_back(bounds, queries, dattn, attended, kv_all, starts, scale)
        dkv = plane_reduce(
            dkv_all.reshape((2, COLUMNS, span, token_rows, heads * LANES)), blocks, 8
        )
        dq = dq.reshape((-1, heads * LANES))
        dkv = dkv.reshape((-1, heads * LANES))
        dxn = (dot32(dq, query_w, LAST) + dot32(dkv, kv_w, LAST)).astype(jnp.bfloat16)
        (dxn,) = column_exchange(
            [dxn.reshape((COLUMNS, token_rows, width))], [False], blocks, 9
        )
        dxn = jnp.sum(dxn.astype(jnp.float32), axis=0)
        query_grad = dot32(column, dq, FIRST).reshape((width, heads, LANES))[:, :, :head_dim]
        kv_grad = dot32(column, dkv, FIRST).reshape((width, heads, LANES))
        lead_grad, attn_gain_grad = norm_backward(dxn, unit_in, scale_in, attn_gain)
        upstream = middle_grad + lead_grad
        if layer > 0:
            upstream, *got = lax.optimization_barrier((upstream, *got))
        expert_grads[layer] = [
            own + other.astype(jnp.float32) for own, other in zip(wgrads[:3], got)
        ]

        qkv_part = jnp.concatenate([query_grad, kv_grad], axis=2).reshape(
            (2, COLUMNS, span, shard_rows, own_qkv)
        )
        out_part = out_grad.reshape((2, span, shard_rows, COLUMNS, own_out)).transpose(
            (0, 3, 1, 2, 4)
        )
        small_part = jnp.concatenate(
            [attn_gain_grad[:, None], moe_gain_grad[:, None], cgate_grad, cvec_grad], axis=1
        ).reshape((2, COLUMNS, span, shard_rows, 8))
        shared_grads[layer] = jnp.concatenate(
            [
                qkv_part.astype(jnp.bfloat16),
                out_part.astype(jnp.bfloat16),
                small_part.astype(jnp.bfloat16),
            ],
            axis=4,
        )

    packed = jnp.concatenate(shared_grads, axis=3)
    packed = jnp.pad(packed, ((0, 0),) * 4 + ((0, -packed.shape[4] % LANES),))
    reduced = plane_reduce(packed, blocks, 10)
    (from_planes,) = column_exchange([reduced], [False], blocks, 11, 10)
    from_planes = from_planes.astype(jnp.float32)
    from_planes = from_planes.reshape((COLUMNS, LAYERS, shard_rows, -1))
    qkv_out = from_planes[..., :own_qkv].reshape(
        (COLUMNS, LAYERS, shard_rows, heads, 3, head_dim)
    )
    qkv_out = qkv_out.transpose((1, 2, 4, 0, 3, 5)).reshape((LAYERS, shard_rows, 3 * width))
    small_out = jnp.sum(from_planes[..., own_qkv + own_out : own_qkv + own_out + 8], axis=0)
    out_rows = reduced[..., own_qkv : own_qkv + own_out].reshape(
        (COLUMNS, LAYERS, shard_rows, own_out)
    )
    out_rows = out_rows.transpose((1, 2, 0, 3)).reshape((LAYERS, shard_rows, width))
    owners = [
        (y * blocks + z * span + r, (z * 2 + y) * span + r)
        for y in range(2)
        for z in range(COLUMNS)
        for r in range(span)
    ]
    out_rows = lax.ppermute(out_rows, ("head", "blk"), owners).astype(jnp.float32)
    stacked = [jnp.stack(group) for group in zip(*expert_grads)]
    return (
        output,
        upstream,
        qkv_out,
        out_rows,
        small_out[..., 0],
        small_out[..., 1],
        small_out[..., 2:6],
        small_out[..., 6:8],
        stacked[0],
        stacked[1],
        stacked[2],
    )


def solution(mesh):
    tokens = P(("head", "blk"), None)
    by_layer = P(None, ("head", "blk"), None)
    gains = P(None, ("head", "blk"))
    experts = P(None, "blk", "head")
    return jax.shard_map(
        per_device,
        mesh=mesh,
        in_specs=(
            tokens,
            P(None, "blk"),
            by_layer,
            by_layer,
            by_layer,
            by_layer,
            gains,
            gains,
            by_layer,
            by_layer,
            experts,
            experts,
            experts,
            tokens,
        ),
        out_specs=(
            tokens,
            tokens,
            by_layer,
            by_layer,
            gains,
            gains,
            by_layer,
            by_layer,
            experts,
            experts,
            experts,
        ),
        check_vma=False,
    )
```

```python
from functools import partial

import jax
import jax.numpy as jnp
from jax import lax
from jax.experimental import pallas as pl
from jax.experimental.pallas import tpu as pltpu
from jax.sharding import PartitionSpec as P

HEADS = 12
NE = 8
LAYERS = 2
CAP = 40
COLUMNS = 4
MESH = pl.DeviceIdType.MESH
ANY = pl.BlockSpec(memory_space=pl.ANY)
VMEM = pl.BlockSpec(memory_space=pltpu.VMEM)
DMA = pltpu.SemaphoreType.DMA
VMEM_BYTES = 48 * 1024 * 1024


def greet(peers):
    barrier = pltpu.get_barrier_semaphore()
    for peer in peers:
        pl.semaphore_signal(barrier, inc=1, device_id=peer, device_id_type=MESH)
    pl.semaphore_wait(barrier, len(peers))


def remote(src, dst, send_sem, recv_sem, peer):
    return pltpu.make_async_remote_copy(
        src_ref=src,
        dst_ref=dst,
        send_sem=send_sem,
        recv_sem=recv_sem,
        device_id=peer,
        device_id_type=MESH,
    )


def comm_params(collective_id):
    return pltpu.CompilerParams(
        collective_id=collective_id, has_side_effects=True, vmem_limit_bytes=VMEM_BYTES
    )


def lasting(microseconds):
    return pl.CostEstimate(
        flops=0, bytes_accessed=int(microseconds * 3_500_000), transcendentals=0
    )


def column_place(blocks):
    span = blocks // COLUMNS
    head, blk = lax.axis_index("head"), lax.axis_index("blk")
    plane, rest = lax.div(blk, span), lax.rem(blk, span)
    planes = [lax.rem(plane + d, COLUMNS) for d in range(COLUMNS)]
    return plane, planes, [(head, p * span + rest) for p in planes]


def column_start(src, gather, dst, own_sem, send_sems, recv_sems, where):
    plane, planes, peers = where
    own = pltpu.make_async_copy(src if gather else src.at[plane], dst.at[plane], own_sem)
    own.start()
    copies = [own]
    for d in (2, 1, 3):
        copy = remote(
            src if gather else src.at[planes[d]],
            dst.at[plane],
            send_sems.at[d],
            recv_sems.at[d],
            peers[d],
        )
        copy.start()
        copies.append(copy)
    return copies


def column_exchange(arrays, gathers, blocks, collective_id, cost=16):
    count = len(arrays)
    slabs = [
        tuple(values.shape if gather else values.shape[1:])
        for values, gather in zip(arrays, gathers)
    ]

    def body(*refs):
        srcs, dsts = refs[:count], refs[count : 2 * count]
        own_sems, send_sems, recv_sems = refs[2 * count :]
        where = column_place(blocks)
        greet(where[2][1:])
        copies = []
        for n in range(count):
            copies += column_start(
                srcs[n],
                gathers[n],
                dsts[n],
                own_sems.at[n],
                send_sems.at[n],
                recv_sems.at[n],
                where,
            )
        for copy in copies:
            copy.wait()

    return pl.pallas_call(
        body,
        out_shape=[
            jax.ShapeDtypeStruct((COLUMNS,) + slab, values.dtype)
            for values, slab in zip(arrays, slabs)
        ],
        in_specs=[ANY] * count,
        out_specs=[ANY] * count,
        scratch_shapes=[DMA((count,)), DMA((count, COLUMNS)), DMA((count, COLUMNS))],
        compiler_params=comm_params(collective_id),
        cost_estimate=lasting(cost),
    )(*arrays)


def plane_place(blocks):
    span = blocks // COLUMNS
    width = span // 2
    head, blk = lax.axis_index("head"), lax.axis_index("blk")
    plane, rest = lax.div(blk, span), lax.rem(blk, span)
    x, core = lax.div(rest, 2), lax.rem(rest, 2)
    first = plane * span
    right = [lax.rem(x + d, width) for d in range(width)]
    left = [lax.rem(x - d + width, width) for d in range(width)]
    x_peers = [(head, first + right[d] * 2 + core) for d in range(width)]
    y_peer = (1 - head, blk)
    core_peer = (head, first + x * 2 + 1 - core)
    return head, rest, core, left, x_peers, y_peer, core_peer


def plane_run(srcs, dsts, own_sems, send_sems, recv_sems, pass_sems, land_sems, where):
    head, rest, core, left, x_peers, y_peer, core_peer = where
    width, count = len(x_peers), len(srcs)
    sends, passes = [], []

    def place(n, h, dy, d):
        half = srcs[n].shape[0] // 2
        row = head if dy == 0 else 1 - head
        return dsts[n].at[row, pl.ds(h * half, half), left[d] * 2 + core]

    def held(n, h, dy, d):
        half = srcs[n].shape[0] // 2
        return srcs[n].at[pl.ds(h * half, half)] if dy == 0 and d == 0 else place(n, h, dy, d)

    def send(n, h, dy, d, peer, to_dy, to_d):
        copy = remote(
            held(n, h, dy, d),
            place(n, h, dy, d),
            send_sems.at[len(sends)],
            recv_sems.at[n, h, to_dy, to_d],
            peer,
        )
        copy.start()
        sends.append(copy)

    def hand_over(n, h, dy, d):
        copy = remote(
            held(n, h, dy, d),
            place(n, h, dy, d),
            pass_sems.at[n, h, dy, d],
            land_sems.at[n, h, dy, d],
            core_peer,
        )
        copy.start()
        passes.append(copy)

    def arrived(n, h, dy, d):
        at = place(n, h, dy, d)
        remote(at, at, send_sems.at[0], recv_sems.at[n, h, dy, d], y_peer).wait_recv()

    owns = []
    for n in range(count):
        own = pltpu.make_async_copy(srcs[n], dsts[n].at[head, :, rest], own_sems.at[n])
        own.start()
        owns.append(own)
    for n in range(count):
        for d in range(1, width):
            send(n, 0, 0, 0, x_peers[d], 0, d)
        send(n, 1, 0, 0, y_peer, 1, 0)
        send(n, 0, 0, 0, y_peer, 1, 0)
        for d in range(1, width):
            send(n, 1, 0, 0, x_peers[d], 0, d)
        hand_over(n, 0, 0, 0)
        hand_over(n, 1, 0, 0)
    for n in range(count):
        for d in range(1, width):
            arrived(n, 0, 0, d)
            send(n, 0, 0, d, y_peer, 1, d)
            hand_over(n, 0, 0, d)
        arrived(n, 1, 1, 0)
        for d in range(1, width):
            send(n, 1, 1, 0, x_peers[d], 1, d)
        hand_over(n, 1, 1, 0)
    for n in range(count):
        arrived(n, 0, 1, 0)
        hand_over(n, 0, 1, 0)
        for d in range(1, width):
            arrived(n, 1, 0, d)
            hand_over(n, 1, 0, d)
        for d in range(1, width):
            arrived(n, 0, 1, d)
            hand_over(n, 0, 1, d)
            arrived(n, 1, 1, d)
            hand_over(n, 1, 1, d)
    for own in owns:
        own.wait()
    for copy in passes:
        copy.wait()
    for copy in sends:
        copy.wait_send()


def plane_scratch(count, blocks):
    width = blocks // COLUMNS // 2
    links = 4 * (width - 1) + 2
    return [DMA((count,)), DMA((count * links,))] + [DMA((count, 2, 2, width))] * 3


def plane_shapes(arrays, blocks):
    return [
        jax.ShapeDtypeStruct(
            (2, values.shape[0], blocks // COLUMNS) + tuple(values.shape[1:]), values.dtype
        )
        for values in arrays
    ]


def plane_gather(arrays, blocks, collective_id, cost=16):
    count = len(arrays)

    def body(*refs):
        srcs, dsts, sems = refs[:count], refs[count : 2 * count], refs[2 * count :]
        where = plane_place(blocks)
        greet(where[4][1:] + [where[5], where[6]])
        plane_run(srcs, dsts, *sems, where)

    return pl.pallas_call(
        body,
        out_shape=plane_shapes(arrays, blocks),
        in_specs=[ANY] * count,
        out_specs=[ANY] * count,
        scratch_shapes=plane_scratch(count, blocks),
        compiler_params=comm_params(collective_id),
        cost_estimate=lasting(cost),
    )(*arrays)


def start_gather(packs, tokens, blocks, collective_id, cost=35):
    count = len(packs)

    def body(*refs):
        srcs, refs = refs[: count + 1], refs[count + 1 :]
        wholes, refs = refs[:count], refs[count:]
        columns, refs = refs[: count + 1], refs[count + 1 :]
        own_sems, send_sems, recv_sems, *plane_sems = refs
        column, plane = column_place(blocks), plane_place(blocks)
        greet(column[2][1:] + plane[4][1:] + [plane[5], plane[6]])
        waits = [
            column_start(
                srcs[n],
                n == count,
                columns[n],
                own_sems.at[n],
                send_sems.at[n],
                recv_sems.at[n],
                column,
            )
            for n in range(count + 1)
        ]
        for n in range(count):
            for copy in waits[n]:
                copy.wait()
        plane_run(columns[:count], wholes, *plane_sems, plane)
        for copy in waits[count]:
            copy.wait()

    results = pl.pallas_call(
        body,
        out_shape=plane_shapes(packs, blocks)
        + [jax.ShapeDtypeStruct(pack.shape, pack.dtype) for pack in packs]
        + [jax.ShapeDtypeStruct((COLUMNS,) + tokens.shape, tokens.dtype)],
        in_specs=[ANY] * (count + 1),
        out_specs=[ANY] * (2 * count + 1),
        scratch_shapes=[
            DMA((count + 1,)),
            DMA((count + 1, COLUMNS)),
            DMA((count + 1, COLUMNS)),
        ]
        + plane_scratch(count, blocks),
        compiler_params=comm_params(collective_id),
        cost_estimate=lasting(cost),
    )(*packs, tokens)
    return results[:count], results[-1]


def plane_reduce(arrays, blocks, collective_id, cost=25):
    span = blocks // COLUMNS
    width = span // 2
    count = len(arrays)
    shapes = [(values.shape[1],) + tuple(values.shape[3:]) for values in arrays]

    def body(*refs):
        srcs, outs, refs = refs[:count], refs[count : 2 * count], refs[2 * count :]
        scratch = [refs[8 * n : 8 * n + 8] for n in range(count)]
        core_send, core_recv, link_send, link_recv = refs[8 * count :]
        head, blk = lax.axis_index("head"), lax.axis_index("blk")
        plane, rest = lax.div(blk, span), lax.rem(blk, span)
        x, core = lax.div(rest, 2), lax.rem(rest, 2)
        first = plane * span
        right = [lax.rem(x + d, width) for d in range(width)]
        x_peers = [(head, first + right[d] * 2 + core) for d in range(width)]
        y_peer = (1 - head, blk)
        core_peer = (head, first + x * 2 + 1 - core)
        greet(x_peers[1:] + [y_peer, core_peer])

        def wide(ref, *at):
            return ref[at].astype(jnp.float32)

        starts = {}
        for n in range(count):
            half = shapes[n][0] // 2
            for h in range(2):
                copy = remote(
                    srcs[n].at[:, pl.ds(h * half, half), :, 1 - core],
                    scratch[n][0].at[:, pl.ds(h * half, half)],
                    core_send.at[n, h],
                    core_recv.at[n, h],
                    core_peer,
                )
                copy.start()
                starts[n, h] = copy

        sends, yas, ybs, xbs = {}, {}, {}, {}
        for n in range(count):
            src, half, kind = srcs[n], shapes[n][0] // 2, arrays[n].dtype
            core_in, summed, xa_in, _, _, yb_in, _, _ = scratch[n]

            def core_sum(h):
                def step(i, _):
                    yy = lax.div(i, half * width)
                    zz = lax.div(lax.rem(i, half * width), width) + h * half
                    xx = lax.rem(i, width)
                    total = wide(src, yy, zz, xx, core) + wide(core_in, yy, zz, xx)
                    summed[yy, zz, xx] = total.astype(kind)
                    return 0

                lax.fori_loop(0, 2 * half * width, step, 0)

            starts[n, 0].wait_recv()
            core_sum(0)
            for d in range(1, width):
                copy = remote(
                    summed.at[:, pl.ds(0, half), right[d]],
                    xa_in.at[d],
                    link_send.at[n, 0, d],
                    link_recv.at[n, 0, d],
                    x_peers[d],
                )
                copy.start()
                sends[n, d] = copy
            starts[n, 1].wait_recv()
            core_sum(1)
            ybs[n] = remote(
                summed.at[1 - head, pl.ds(half, half)],
                yb_in,
                link_send.at[n, 1, 0],
                link_recv.at[n, 1, 0],
                y_peer,
            )
            ybs[n].start()
        for n in range(count):
            half, kind = shapes[n][0] // 2, arrays[n].dtype
            _, summed, xa_in, ya_out, ya_in, yb_in, xb_out, xb_in = scratch[n]
            for d in range(1, width):
                sends[n, d].wait_recv()

            def a_step(zz, _):
                total = wide(summed, 1 - head, zz, x)
                for d in range(1, width):
                    total = total + wide(xa_in, d, 1 - head, zz)
                ya_out[zz] = total.astype(kind)
                return 0

            lax.fori_loop(0, half, a_step, 0)
            yas[n] = remote(
                ya_out, ya_in, link_send.at[n, 0, 0], link_recv.at[n, 0, 0], y_peer
            )
            yas[n].start()
            ybs[n].wait_recv()
            for d in range(1, width):

                def b_step(zz, _):
                    total = wide(summed, head, half + zz, right[d]) + wide(yb_in, zz, right[d])
                    xb_out[d, zz] = total.astype(kind)
                    return 0

                lax.fori_loop(0, half, b_step, 0)
                xbs[n, d] = remote(
                    xb_out.at[d],
                    xb_in.at[d],
                    link_send.at[n, 1, d],
                    link_recv.at[n, 1, d],
                    x_peers[d],
                )
                xbs[n, d].start()
        for n in range(count):
            out, half, kind = outs[n], shapes[n][0] // 2, arrays[n].dtype
            _, summed, xa_in, _, ya_in, yb_in, _, xb_in = scratch[n]
            yas[n].wait_recv()

            def a_last(zz, _):
                total = wide(summed, head, zz, x) + wide(ya_in, zz)
                for d in range(1, width):
                    total = total + wide(xa_in, d, head, zz)
                out[zz] = total.astype(kind)
                return 0

            lax.fori_loop(0, half, a_last, 0)
            for d in range(1, width):
                xbs[n, d].wait_recv()

            def b_last(zz, _):
                total = wide(summed, head, half + zz, x) + wide(yb_in, zz, x)
                for d in range(1, width):
                    total = total + wide(xb_in, d, zz)
                out[half + zz] = total.astype(kind)
                return 0

            lax.fori_loop(0, half, b_last, 0)
        for group in (starts, sends, yas, ybs, xbs):
            for copy in group.values():
                copy.wait_send()

    scratch = []
    for (slabs, *tile), values in zip(shapes, arrays):
        tile, half, kind = tuple(tile), slabs // 2, values.dtype
        scratch += [
            pltpu.VMEM((2, slabs, width) + tile, kind),
            pltpu.VMEM((2, slabs, width) + tile, kind),
            pltpu.VMEM((width, 2, half) + tile, kind),
            pltpu.VMEM((half,) + tile, kind),
            pltpu.VMEM((half,) + tile, kind),
            pltpu.VMEM((half, width) + tile, kind),
            pltpu.VMEM((width, half) + tile, kind),
            pltpu.VMEM((width, half) + tile, kind),
        ]
    return pl.pallas_call(
        body,
        out_shape=[
            jax.ShapeDtypeStruct(shape, values.dtype) for shape, values in zip(shapes, arrays)
        ],
        in_specs=[VMEM] * count,
        out_specs=[VMEM] * count,
        scratch_shapes=scratch
        + [DMA((count, 2)), DMA((count, 2)), DMA((count, 2, width)), DMA((count, 2, width))],
        compiler_params=comm_params(collective_id),
        cost_estimate=lasting(cost),
    )(
        *[
            values.reshape((2, values.shape[1], width, 2) + tuple(values.shape[3:]))
            for values in arrays
        ]
    )


def expert_dispatch(buffers, blocks, collective_id, cost=15):
    copies = blocks // NE
    count = len(buffers)

    def body(*refs):
        srcs, dsts = refs[:count], refs[count : 2 * count]
        own_sems, send_sems, recv_sems, pass_sems, land_sems = refs[2 * count :]
        head, blk = lax.axis_index("head"), lax.axis_index("blk")
        expert, piece = lax.div(blk, copies), lax.rem(blk, copies)
        ahead = [lax.rem(expert + d, NE) for d in range(NE)]
        behind = [lax.rem(expert - d + NE, NE) for d in range(NE)]
        peers = [(head, ahead[d] * copies + piece) for d in range(NE)]
        siblings = [(head, expert * copies + lax.rem(piece + k, copies)) for k in range(copies)]
        greet(peers[1:] + siblings[1:])
        sends, passes = [], []
        for n in range(count):
            own = pltpu.make_async_copy(
                srcs[n].at[expert], dsts[n].at[piece, expert], own_sems.at[n]
            )
            own.start()
            passes.append(own)
        for n in range(count):
            for d in (4, 3, 5, 2, 6, 1, 7):
                copy = remote(
                    srcs[n].at[ahead[d]],
                    dsts[n].at[piece, expert],
                    send_sems.at[n, d],
                    recv_sems.at[n, d],
                    peers[d],
                )
                copy.start()
                sends.append(copy)
        for n in range(count):
            for d in (0, 1, 7, 2, 6, 3, 5, 4):
                place = dsts[n].at[piece, behind[d]]
                if d > 0:
                    remote(
                        place, place, send_sems.at[n, d], recv_sems.at[n, d], peers[d]
                    ).wait_recv()
                for k in range(1, copies):
                    copy = remote(
                        place if d > 0 else srcs[n].at[expert],
                        place,
                        pass_sems.at[n, k, d],
                        land_sems.at[n, k, d],
                        siblings[k],
                    )
                    copy.start()
                    passes.append(copy)
        for copy in passes:
            copy.wait()
        for copy in sends:
            copy.wait_send()

    return pl.pallas_call(
        body,
        out_shape=[
            jax.ShapeDtypeStruct((copies,) + tuple(b.shape), b.dtype) for b in buffers
        ],
        in_specs=[ANY] * count,
        out_specs=[ANY] * count,
        scratch_shapes=[DMA((count,))]
        + [DMA((count, NE))] * 2
        + [DMA((count, copies, NE))] * 2,
        compiler_params=comm_params(collective_id),
        cost_estimate=lasting(cost),
    )(*buffers)


def expert_return(arrays, blocks, collective_id, cost=15):
    copies = blocks // NE
    count = len(arrays)

    def body(*refs):
        srcs, dsts = refs[:count], refs[count : 2 * count]
        sib_ins, totals = refs[2 * count : 3 * count], refs[3 * count : 4 * count]
        own_sems, send_sems, recv_sems, pass_sems, land_sems = refs[4 * count :]
        head, blk = lax.axis_index("head"), lax.axis_index("blk")
        expert, piece = lax.div(blk, copies), lax.rem(blk, copies)
        ahead = [lax.rem(expert + d, NE) for d in range(NE)]
        peers = [(head, ahead[d] * copies + piece) for d in range(NE)]
        places = [lax.rem(piece + k, copies) for k in range(copies)]
        siblings = [(head, expert * copies + places[k]) for k in range(copies)]
        greet(peers[1:] + siblings[1:])
        order = (4, 3, 5, 2, 6, 1, 7, 0)
        passes, sends = {}, []
        for n in range(count):
            for d in order:
                for k in range(1, copies):
                    copy = remote(
                        srcs[n].at[places[k], ahead[d]],
                        sib_ins[n].at[k, ahead[d]],
                        pass_sems.at[n, k, d],
                        land_sems.at[n, k, d],
                        siblings[k],
                    )
                    copy.start()
                    passes[n, k, d] = copy
        for n in range(count):
            for d in order:
                value = srcs[n][piece, ahead[d]].astype(jnp.float32)
                for k in range(1, copies):
                    passes[n, k, d].wait_recv()
                    value = value + sib_ins[n][k, ahead[d]].astype(jnp.float32)
                totals[n][ahead[d]] = value.astype(arrays[n].dtype)
                if d > 0:
                    copy = remote(
                        totals[n].at[ahead[d]],
                        dsts[n].at[expert],
                        send_sems.at[n, d],
                        recv_sems.at[n, d],
                        peers[d],
                    )
                else:
                    copy = pltpu.make_async_copy(
                        totals[n].at[expert], dsts[n].at[expert], own_sems.at[n]
                    )
                copy.start()
                sends.append(copy)
        for copy in sends:
            copy.wait()
        for copy in passes.values():
            copy.wait_send()

    return pl.pallas_call(
        body,
        out_shape=[jax.ShapeDtypeStruct(a.shape[1:], a.dtype) for a in arrays],
        in_specs=[VMEM] * count,
        out_specs=[ANY] * count,
        scratch_shapes=[pltpu.VMEM(a.shape, a.dtype) for a in arrays]
        + [pltpu.VMEM(a.shape[1:], a.dtype) for a in arrays]
        + [DMA((count,))]
        + [DMA((count, NE))] * 2
        + [DMA((count, copies, NE))] * 2,
        compiler_params=comm_params(collective_id),
        cost_estimate=lasting(cost),
    )(*arrays)


NEGATIVE = -1e30
EPSILON = 1e-06
HIGHEST = lax.Precision.HIGHEST
KEYS = 512
LANES = 128
LAST = (((1,), (1,)), ((), ()))
FIRST = (((0,), (0,)), ((), ()))


def dot32(a, b, dims=(((1,), (0,)), ((), ()))):
    return lax.dot_general(a, b, dims, preferred_element_type=jnp.float32)


def visible(key_base, query_base, keys, queries, starts):
    key_pos = key_base + lax.broadcasted_iota(jnp.int32, (keys, queries), 0)
    query_pos = query_base + lax.broadcasted_iota(jnp.int32, (keys, queries), 1)
    return (key_pos <= query_pos) & (key_pos >= starts)


def attend(bounds, queries, kv_all, starts):
    count, rows, width = queries.shape
    heads = width // LANES

    def body(bounds_ref, q_ref, kv_ref, start_ref, out_ref):
        i = pl.program_id(0)
        low, high, base = bounds_ref[i, 0], bounds_ref[i, 1], bounds_ref[i, 2]
        start_row = start_ref[0]
        q = [q_ref[0, :, h * LANES : (h + 1) * LANES] for h in range(heads)]

        def step(t, carry):
            chunk = high - t
            at = pl.multiple_of(chunk * KEYS, KEYS)
            ok = visible(chunk * KEYS, base, KEYS, rows, start_row)
            new = []
            for h in range(heads):
                top, total, acc = carry[h]
                kv = kv_ref[pl.ds(at, KEYS), h * LANES : (h + 1) * LANES]
                score = jnp.where(ok, dot32(kv, q[h], LAST), NEGATIVE)
                new_top = jnp.maximum(top, jnp.max(score, axis=0, keepdims=True))
                weight = jnp.exp(score - new_top)
                shrink = jnp.exp(top - new_top)
                total = total * shrink + jnp.sum(weight, axis=0, keepdims=True)
                acc = acc * shrink + dot32(kv, weight.astype(jnp.bfloat16), FIRST)
                new.append((new_top, total, acc))
            return tuple(new)

        empty = tuple(
            (
                jnp.full((1, rows), NEGATIVE, jnp.float32),
                jnp.zeros((1, rows), jnp.float32),
                jnp.zeros((LANES, rows), jnp.float32),
            )
            for h in range(heads)
        )
        done = lax.fori_loop(0, high - low + 1, step, empty)
        lane = lax.broadcasted_iota(jnp.int32, (LANES, rows), 0)
        for h in range(heads):
            top, total, acc = done[h]
            value = jnp.where(lane < LANES // 2, top + jnp.log(total), acc / total)
            out_ref[0, :, h * LANES : (h + 1) * LANES] = value.T

    return pl.pallas_call(
        body,
        out_shape=jax.ShapeDtypeStruct((count, rows, width), jnp.float32),
        grid_spec=pltpu.PrefetchScalarGridSpec(
            num_scalar_prefetch=1,
            grid=(count,),
            in_specs=[
                pl.BlockSpec((1, rows, width), lambda i, b: (i, 0, 0)),
                pl.BlockSpec(kv_all.shape, lambda i, b: (0, 0)),
                pl.BlockSpec((1, 1, rows), lambda i, b: (i, 0, 0)),
            ],
            out_specs=pl.BlockSpec((1, rows, width), lambda i, b: (i, 0, 0)),
        ),
        compiler_params=pltpu.CompilerParams(vmem_limit_bytes=VMEM_BYTES),
        cost_estimate=pl.CostEstimate(
            flops=2 * count * rows * kv_all.shape[0] * width,
            bytes_accessed=kv_all.size * 2,
            transcendentals=count * rows * kv_all.shape[0],
        ),
    )(bounds, queries, kv_all, starts)


def attend_back(bounds, queries, grads, kept, kv_all, starts, scale):
    count, rows, width = queries.shape
    total_keys = kv_all.shape[0]
    heads = width // LANES
    if total_keys * width * 14 > VMEM_BYTES:
        heads = 1
    wide = heads * LANES

    def body(bounds_ref, q_ref, g_ref, kept_ref, kv_ref, start_ref, dq_ref, dkv_ref, acc_ref):
        i = pl.program_id(1)
        low, high, base = bounds_ref[i, 0], bounds_ref[i, 1], bounds_ref[i, 2]
        start_row = start_ref[0]

        @pl.when(i == 0)
        def _():
            def clear(c, _):
                acc_ref[pl.ds(pl.multiple_of(c * KEYS, KEYS), KEYS), :] = jnp.zeros(
                    (KEYS, wide), jnp.float32
                )
                return 0

            lax.fori_loop(0, total_keys // KEYS, clear, 0)

        q = [q_ref[0, :, h * LANES : (h + 1) * LANES] for h in range(heads)]
        g = [g_ref[0, :, h * LANES : (h + 1) * LANES] for h in range(heads)]
        lse, delta = [], []
        for h in range(heads):
            kept_t = kept_ref[0, :, h * LANES : (h + 1) * LANES].T
            lse.append(kept_t[0:1])
            delta.append(jnp.sum(kept_t * g[h].astype(jnp.float32).T, axis=0, keepdims=True))

        def step(t, carry):
            chunk = high - t
            at = pl.multiple_of(chunk * KEYS, KEYS)
            ok = visible(chunk * KEYS, base, KEYS, rows, start_row)
            new = []
            for h in range(heads):
                lanes = slice(h * LANES, (h + 1) * LANES)
                kv = kv_ref[pl.ds(at, KEYS), lanes]
                score = jnp.where(ok, dot32(kv, q[h], LAST), NEGATIVE)
                prob = jnp.exp(score - lse[h])
                dscore = (prob * (dot32(kv, g[h], LAST) - delta[h])).astype(jnp.bfloat16)
                acc_ref[pl.ds(at, KEYS), lanes] += dot32(dscore, q[h]) + dot32(
                    prob.astype(jnp.bfloat16), g[h]
                )
                new.append(carry[h] + dot32(kv, dscore, FIRST))
            return tuple(new)

        done = lax.fori_loop(
            0,
            high - low + 1,
            step,
            tuple(jnp.zeros((LANES, rows), jnp.float32) for h in range(heads)),
        )
        lane = lax.broadcasted_iota(jnp.int32, (LANES, rows), 0)
        for h in range(heads):
            value = jnp.where(lane < LANES // 2, done[h] * scale, 0.0)
            dq_ref[0, :, h * LANES : (h + 1) * LANES] = value.T.astype(jnp.bfloat16)

        @pl.when(i == count - 1)
        def _():
            def store(c, _):
                at = pl.ds(pl.multiple_of(c * KEYS, KEYS), KEYS)
                dkv_ref[at, :] = acc_ref[at, :].astype(jnp.bfloat16)
                return 0

            lax.fori_loop(0, total_keys // KEYS, store, 0)

    block = pl.BlockSpec((1, rows, wide), lambda h, i, b: (i, 0, h))
    whole = pl.BlockSpec((total_keys, wide), lambda h, i, b: (0, h))
    return pl.pallas_call(
        body,
        out_shape=(
            jax.ShapeDtypeStruct((count, rows, width), jnp.bfloat16),
            jax.ShapeDtypeStruct(kv_all.shape, jnp.bfloat16),
        ),
        grid_spec=pltpu.PrefetchScalarGridSpec(
            num_scalar_prefetch=1,
            grid=(width // wide, count),
            in_specs=[
                block,
                block,
                block,
                whole,
                pl.BlockSpec((1, 1, rows), lambda h, i, b: (i, 0, 0)),
            ],
            out_specs=(block, whole),
            scratch_shapes=[pltpu.VMEM((total_keys, wide), jnp.float32)],
        ),
        compiler_params=pltpu.CompilerParams(vmem_limit_bytes=VMEM_BYTES),
        cost_estimate=pl.CostEstimate(
            flops=5 * count * rows * total_keys * width,
            bytes_accessed=kv_all.size * 4,
            transcendentals=count * rows * total_keys,
        ),
    )(bounds, queries, grads, kept, kv_all, starts)


def expert_forward(head, rows_in, own, other):
    count, width = rows_in.shape
    hidden, features = own[0].shape
    tile = min(hidden, 256)
    steps = hidden // tile

    def body(head_ref, x_ref, go, gx, uo, ux, do, dx, out_ref, acc_ref):
        i = pl.program_id(0)
        mine = pl.ds(pl.multiple_of(head_ref[0] * features, LANES), features)
        rest = pl.ds(pl.multiple_of((1 - head_ref[0]) * features, LANES), features)
        xo, xx = x_ref[:, mine], x_ref[:, rest]
        gate = dot32(xo, go[...], LAST) + dot32(xx, gx[...], LAST)
        up = dot32(xo, uo[...], LAST) + dot32(xx, ux[...], LAST)
        act = (jax.nn.silu(gate) * up).astype(jnp.bfloat16)

        @pl.when(i == 0)
        def _():
            acc_ref[...] = jnp.zeros_like(acc_ref)

        acc_ref[:, mine] += dot32(act, do[...])
        acc_ref[:, rest] += dot32(act, dx[...])

        @pl.when(i == steps - 1)
        def _():
            out_ref[...] = acc_ref[...].astype(jnp.bfloat16)

    whole = pl.BlockSpec((count, width), lambda i, h: (0, 0))
    piece = pl.BlockSpec((tile, features), lambda i, h: (i, 0))
    weights = [w for pair in zip(own, other) for w in pair]
    return pl.pallas_call(
        body,
        out_shape=jax.ShapeDtypeStruct((count, width), jnp.bfloat16),
        grid_spec=pltpu.PrefetchScalarGridSpec(
            num_scalar_prefetch=1,
            grid=(steps,),
            in_specs=[whole] + [piece] * 6,
            out_specs=whole,
            scratch_shapes=[pltpu.VMEM((count, width), jnp.float32)],
        ),
        compiler_params=pltpu.CompilerParams(vmem_limit_bytes=VMEM_BYTES),
        cost_estimate=pl.CostEstimate(
            flops=6 * count * width * hidden,
            bytes_accessed=6 * hidden * features * 2 + 4 * count * width,
            transcendentals=count * hidden,
        ),
    )(head, rows_in, *weights)


def expert_backward(head, rows_in, grads_in, own, other, with_parts):
    count, width = rows_in.shape
    hidden, features = own[0].shape
    tile = min(hidden, 256)
    steps = hidden // tile
    sums = 2 if with_parts else 1

    def body(head_ref, x_ref, z_ref, go, gx, uo, ux, do, dx, *outs):
        keeps, sends, totals, accs = outs[:3], outs[3:6], outs[6 : 6 + sums], outs[6 + sums :]
        i = pl.program_id(0)
        mine = pl.ds(pl.multiple_of(head_ref[0] * features, LANES), features)
        rest = pl.ds(pl.multiple_of((1 - head_ref[0]) * features, LANES), features)
        xo, xx = x_ref[:, mine], x_ref[:, rest]
        zo, zx = z_ref[:, mine], z_ref[:, rest]
        gate = dot32(xo, go[...], LAST) + dot32(xx, gx[...], LAST)
        up = dot32(xo, uo[...], LAST) + dot32(xx, ux[...], LAST)
        dact = dot32(zo, do[...], LAST) + dot32(zx, dx[...], LAST)
        sigmoid = jax.nn.sigmoid(gate)
        silu = gate * sigmoid
        act = (silu * up).astype(jnp.bfloat16)
        dgate = (dact * up * sigmoid * (1.0 + gate * (1.0 - sigmoid))).astype(jnp.bfloat16)
        dup = (dact * silu).astype(jnp.bfloat16)

        @pl.when(i == 0)
        def _():
            for acc in accs:
                acc[...] = jnp.zeros_like(acc)

        accs[0][:, mine] += dot32(dgate, go[...]) + dot32(dup, uo[...])
        accs[0][:, rest] += dot32(dgate, gx[...]) + dot32(dup, ux[...])
        if with_parts:
            accs[1][:, mine] += dot32(act, do[...])
            accs[1][:, rest] += dot32(act, dx[...])
        for n, (left, mine_in, rest_in) in enumerate(
            ((dgate, xo, xx), (dup, xo, xx), (act, zo, zx))
        ):
            keeps[n][...] = dot32(left, mine_in, FIRST)
            sends[n][...] = dot32(left, rest_in, FIRST).astype(jnp.bfloat16)

        @pl.when(i == steps - 1)
        def _():
            for total, acc in zip(totals, accs):
                total[...] = acc[...].astype(jnp.bfloat16)

    whole = pl.BlockSpec((count, width), lambda i, h: (0, 0))
    piece = pl.BlockSpec((tile, features), lambda i, h: (i, 0))
    weights = [w for pair in zip(own, other) for w in pair]
    return pl.pallas_call(
        body,
        out_shape=[jax.ShapeDtypeStruct((hidden, features), jnp.float32)] * 3
        + [jax.ShapeDtypeStruct((hidden, features), jnp.bfloat16)] * 3
        + [jax.ShapeDtypeStruct((count, width), jnp.bfloat16)] * sums,
        grid_spec=pltpu.PrefetchScalarGridSpec(
            num_scalar_prefetch=1,
            grid=(steps,),
            in_specs=[whole, whole] + [piece] * 6,
            out_specs=[piece] * 6 + [whole] * sums,
            scratch_shapes=[pltpu.VMEM((count, width), jnp.float32)] * sums,
        ),
        compiler_params=pltpu.CompilerParams(vmem_limit_bytes=VMEM_BYTES),
        cost_estimate=pl.CostEstimate(
            flops=22 * count * width * hidden,
            bytes_accessed=15 * hidden * features * 2 + 8 * count * width,
            transcendentals=count * hidden,
        ),
    )(head, rows_in, grads_in, *weights)


def pack_grads(column, dq, dkv, attn, dy, small, compact):
    width = column.shape[1]
    kv_cols, own_out = dkv.shape[1], attn.shape[1]
    small_cols = small.shape[1]
    rows, cols = own_out // 2, width // 2

    def body(column_ref, dq_ref, dkv_ref, attn_ref, dy_ref, small_ref, compact_ref, one, two):
        one[:, :kv_cols] = dot32(column_ref[...], dkv_ref[...], FIRST).astype(jnp.bfloat16)
        narrow = dot32(dq_ref[...], compact_ref[...]).astype(jnp.bfloat16)
        one[:, kv_cols:] = (
            dot32(column_ref[...], narrow, FIRST) + small_ref[...]
        ).astype(jnp.bfloat16)
        out = dot32(attn_ref[...], dy_ref[...], FIRST).astype(jnp.bfloat16)
        for a in range(2):
            for b in range(2):
                two[a, b] = out[a * rows : (a + 1) * rows, b * cols : (b + 1) * cols]

    return pl.pallas_call(
        body,
        out_shape=[
            jax.ShapeDtypeStruct((width, kv_cols + small_cols), jnp.bfloat16),
            jax.ShapeDtypeStruct((2, 2, rows, cols), jnp.bfloat16),
        ],
        compiler_params=pltpu.CompilerParams(vmem_limit_bytes=VMEM_BYTES),
        cost_estimate=lasting(4),
    )(column, dq, dkv, attn, dy, small, compact)


def norm_forward(values, gain_vec):
    row_scale = lax.rsqrt(jnp.mean(values * values, axis=-1, keepdims=True) + EPSILON)
    normed = values * row_scale
    return normed * gain_vec, normed, row_scale


def norm_backward(upstream, normed, row_scale, gain_vec):
    through = upstream * gain_vec
    gain_grad = jnp.sum(upstream * normed, axis=0)
    inner_mean = jnp.mean(through * normed, axis=-1, keepdims=True)
    return row_scale * (through - normed * inner_mean), gain_grad


def slot_index(route_ids):
    token_rows = route_ids.shape[0]
    expert_ids = jnp.arange(NE, dtype=jnp.int32)
    matches = (
        (route_ids[:, :, None] == expert_ids[None, None, :])
        .astype(jnp.int32)
        .reshape((token_rows * 2, NE))
    )
    before = jnp.cumsum(matches, axis=0) - 1
    slot_pos = jnp.sum(matches * before, axis=1).reshape((token_rows, 2))
    return jnp.where(route_ids < NE, route_ids * CAP + slot_pos, NE * CAP)


def per_device(
    tokens,
    segments,
    routes,
    gates,
    w_qkv,
    w_out,
    gain_attn,
    gain_moe,
    const_gate,
    const_vec,
    w_gate,
    w_up,
    w_down,
    cotangent,
):
    blocks = lax.axis_size("blk")
    head_index, blk_index = lax.axis_index("head"), lax.axis_index("blk")
    span = blocks // COLUMNS
    plane, rest = lax.div(blk_index, span), lax.rem(blk_index, span)
    shards = 2 * blocks
    token_rows, width = tokens.shape
    shard_rows = width // shards
    head_dim = width // HEADS
    heads = HEADS // COLUMNS
    scale = head_dim ** (-0.5)
    half_length = blocks * token_rows
    positions = 2 * half_length
    features = w_gate.shape[2]
    hidden_rows = w_gate.shape[1]
    copies = blocks // NE
    own_out = heads * head_dim

    swap = [(0, 1), (1, 0)]
    head_scalar = head_index.reshape((1,)).astype(jnp.int32)

    seg_own = lax.dynamic_index_in_dim(segments, head_index, 0, keepdims=False)
    seg_parts = jnp.concatenate([lax.rem(seg_own, 128), lax.div(seg_own, 128)]).astype(
        jnp.bfloat16
    )
    seg_columns = -(-seg_parts.shape[0] // shard_rows)
    seg_parts = jnp.pad(seg_parts, (0, seg_columns * shard_rows - seg_parts.shape[0]))
    seg_parts = seg_parts.reshape((shard_rows, seg_columns))
    packs = []
    for layer in range(LAYERS):
        split = w_qkv[layer].reshape((shard_rows, 3, COLUMNS, heads, head_dim))
        kv_part = jnp.concatenate([split[:, 1], split[:, 2]], axis=3)
        kv_part = kv_part.transpose((1, 0, 2, 3)).reshape((COLUMNS, shard_rows, heads * LANES))
        query_part = split[:, 0].transpose((1, 0, 2, 3)).reshape((COLUMNS, shard_rows, own_out))
        side = [
            gain_attn[layer][:, None],
            gain_moe[layer][:, None],
            const_gate[layer],
            const_vec[layer],
            seg_parts,
        ]
        filled = own_out + 8 + seg_columns
        side.append(jnp.zeros((shard_rows, -filled % LANES), jnp.bfloat16))
        side = jnp.concatenate(side, axis=1)
        packs.append(
            jnp.concatenate(
                [
                    kv_part,
                    jnp.broadcast_to(w_out[layer][None], (COLUMNS, shard_rows, width)),
                    query_part,
                    jnp.broadcast_to(side[None], (COLUMNS,) + side.shape),
                ],
                axis=2,
            )
        )
    weights, column_tokens = start_gather(packs, tokens, blocks, 1)
    weights = [pack.reshape((shards, shard_rows, -1)) for pack in weights]
    out_at = heads * LANES
    query_at = out_at + width
    small_at = query_at + own_out

    place = jnp.arange(own_out, dtype=jnp.int32)
    place = lax.div(place, head_dim) * LANES + lax.rem(place, head_dim)
    wide_place = jnp.arange(heads * LANES, dtype=jnp.int32)
    to_low = (place[:, None] == wide_place[None, :]).astype(jnp.bfloat16)
    to_high = (place[:, None] + head_dim == wide_place[None, :]).astype(jnp.bfloat16)
    small_cols = own_out + LANES - own_out % LANES
    compact = jnp.pad(to_low.T, ((0, 0), (0, small_cols - own_out)))

    def send_experts(layer, after):
        held = lax.optimization_barrier(
            tuple(w[layer] for w in (w_gate, w_up, w_down)) + (after,)
        )[:3]
        return held, [lax.ppermute(w, "head", swap) for w in held]

    own_experts, other_experts = [None] * LAYERS, [None] * LAYERS

    seg_all = weights[0][:, :, small_at + 8 : small_at + 8 + seg_columns]
    seg_all = seg_all.reshape((shards, -1))[:, : 2 * token_rows].astype(jnp.int32)
    seg_all = seg_all[:, :token_rows] + 128 * seg_all[:, token_rows:]
    seg_query = lax.dynamic_index_in_dim(
        seg_all.reshape((2, COLUMNS, span, token_rows)), head_index, 0, keepdims=False
    )
    seg_query = lax.dynamic_index_in_dim(seg_query, rest, 1, keepdims=False)
    starts = jnp.sum(
        (seg_all.reshape((1, 1, -1)) < seg_query[:, :, None]).astype(jnp.int32), axis=2
    )
    bases = (
        head_index * half_length
        + (jnp.arange(COLUMNS, dtype=jnp.int32) * span + rest) * token_rows
    )
    bounds = jnp.stack(
        [lax.div(starts[:, 0], KEYS), lax.div(bases + token_rows - 1, KEYS), bases], axis=1
    )
    starts = starts[:, None, :]

    layers = []
    for pack in weights:
        rows = pack.reshape((width, -1))
        kv_w = rows[:, :out_at]
        out_w = rows[:, out_at:query_at]
        query_w = dot32(rows[:, query_at:small_at], to_low).astype(jnp.bfloat16)
        small_w = rows[:, small_at : small_at + 8]
        out_rows = lax.dynamic_slice_in_dim(out_w, plane * own_out, own_out, 0)
        out_rows = dot32(to_high, out_rows, FIRST).astype(jnp.bfloat16)
        layers.append((query_w, kv_w, out_w, small_w, out_rows))

    def expert_buffers(layer):
        route_ids, gate_vals = routes[layer], gates[layer]
        slots = slot_index(route_ids)
        named = slots[:, :, None] == jnp.arange(NE * CAP, dtype=jnp.int32)[None, None, :]
        picks = jnp.any(named, axis=1)
        pick_gates = jnp.sum(jnp.where(named, gate_vals[:, :, None], 0.0), axis=1)
        return picks, pick_gates

    def gated_rows(picks, pick_gates, upstream):
        picked = jnp.dot(picks.astype(jnp.float32).T, upstream, precision=HIGHEST)
        dz = (jnp.sum(pick_gates, axis=0)[:, None] * picked).astype(jnp.bfloat16)
        return dz.reshape((NE, CAP, width))

    upstream = cotangent.astype(jnp.float32)
    residual = tokens.astype(jnp.float32)
    kept = []
    for layer in range(LAYERS):
        query_w, kv_w, out_w, small_w, out_rows = layers[layer]
        attn_gain = small_w[:, 0].astype(jnp.float32)
        moe_gain = small_w[:, 1].astype(jnp.float32)
        gate_w = small_w[:, 2:6]
        vectors = small_w[:, 6:8].astype(jnp.float32).T
        normed_in, unit_in, scale_in = norm_forward(residual, attn_gain)
        if layer == 0:
            column = norm_forward(column_tokens.astype(jnp.float32), attn_gain)[0]
            column = column.astype(jnp.bfloat16)
        else:
            (column,) = column_exchange([normed_in.astype(jnp.bfloat16)], [True], blocks, 3)
        column = column.reshape((COLUMNS * token_rows, width))
        queries = (
            dot32(column, query_w).astype(jnp.bfloat16).astype(jnp.float32) * scale
        ).astype(jnp.bfloat16)
        queries = queries.reshape((COLUMNS, token_rows, heads * LANES))
        kv_own = dot32(column, kv_w).astype(jnp.bfloat16)
        (kv_all,) = plane_gather(
            [kv_own.reshape((COLUMNS, token_rows, heads * LANES))], blocks, 4
        )
        kv_all = kv_all.reshape((positions, heads * LANES))
        if layer == 0:
            own_experts[0], other_experts[0] = send_experts(0, kv_all)
        attended = attend(bounds, queries, kv_all, starts)
        attn_col = dot32(
            attended.astype(jnp.bfloat16).reshape((-1, heads * LANES)), to_high, LAST
        ).astype(jnp.bfloat16)
        (attn,) = column_exchange(
            [attn_col.reshape((COLUMNS, token_rows, own_out))], [False], blocks, 5, 9
        )
        attn = attn.transpose((1, 0, 2)).reshape((token_rows, width))
        middle = residual + dot32(attn, out_w)
        normed_mid, unit_mid, scale_mid = norm_forward(middle, moe_gain)
        moe_in = normed_mid.astype(jnp.bfloat16)
        moe_float = moe_in.astype(jnp.float32)
        route_ids, gate_vals = routes[layer], gates[layer]
        picks, pick_gates = expert_buffers(layer)
        sent = dot32(picks.astype(jnp.bfloat16), moe_in, FIRST).astype(jnp.bfloat16)
        sent = [sent.reshape((NE, CAP, width))]
        last = layer + 1 == LAYERS
        if last:
            sent.append(gated_rows(picks, pick_gates, upstream))
        arrived = expert_dispatch(sent, blocks, 7 if last else 6, 24 if last else 15)
        flat_in, *dz_in = [rows.reshape((-1, width)) for rows in arrived]
        if last:
            *wgrads, dparts, parts = expert_backward(
                head_scalar, flat_in, dz_in[0], own_experts[layer], other_experts[layer], True
            )
            back, dback = expert_return(
                [rows.reshape((copies, NE, CAP, width)) for rows in (parts, dparts)],
                blocks,
                9,
                24,
            )
            last_grads = wgrads, dback
        else:
            own_experts[layer + 1], other_experts[layer + 1] = send_experts(layer + 1, flat_in)
            parts = expert_forward(
                head_scalar, flat_in, own_experts[layer], other_experts[layer]
            )
            (back,) = expert_return([parts.reshape((copies, NE, CAP, width))], blocks, 8)
        back = back.reshape((NE * CAP, width)).astype(jnp.float32)
        ffn_out = jnp.dot(pick_gates, back, precision=HIGHEST)
        copy_weight = jnp.sum(jnp.where(route_ids == NE + 1, gate_vals, 0.0), axis=1)
        const_weight = jnp.stack(
            [
                jnp.sum(jnp.where(route_ids == NE + 2 + c, gate_vals, 0.0), axis=1)
                for c in range(2)
            ],
            axis=1,
        )
        mixing = jax.nn.softmax(dot32(moe_in, gate_w).reshape((token_rows, 2, 2)), axis=-1)
        const_out = jnp.sum(
            const_weight[:, :, None]
            * (mixing[:, :, 0:1] * moe_float[:, None, :] + mixing[:, :, 1:2] * vectors[None]),
            axis=1,
        )
        residual = middle + ffn_out + copy_weight[:, None] * moe_float + const_out
        kept.append(
            (
                unit_in,
                scale_in,
                column,
                queries,
                kv_all,
                attended,
                attn_col,
                unit_mid,
                scale_mid,
                moe_float,
                picks,
                pick_gates,
                flat_in,
                copy_weight,
                const_weight,
                mixing,
            )
        )
    output = residual

    shared_grads = [None] * LAYERS
    expert_grads = [None] * LAYERS
    for layer in reversed(range(LAYERS)):
        query_w, kv_w, out_w, small_w, out_rows = layers[layer]
        attn_gain = small_w[:, 0].astype(jnp.float32)
        moe_gain = small_w[:, 1].astype(jnp.float32)
        gate_w = small_w[:, 2:6].astype(jnp.float32)
        vectors = small_w[:, 6:8].astype(jnp.float32).T
        (
            unit_in,
            scale_in,
            column,
            queries,
            kv_all,
            attended,
            attn_col,
            unit_mid,
            scale_mid,
            moe_float,
            picks,
            pick_gates,
            flat_in,
            copy_weight,
            const_weight,
            mixing,
        ) = kept[layer]
        mix_grad = const_weight[:, :, None] * upstream[:, None, :]
        alpha_grad = jnp.stack(
            [
                jnp.sum(mix_grad * moe_float[:, None, :], axis=-1),
                jnp.sum(mix_grad * vectors[None], axis=-1),
            ],
            axis=-1,
        )
        logit_grad = (
            mixing * (alpha_grad - jnp.sum(mixing * alpha_grad, axis=-1, keepdims=True))
        ).reshape((token_rows, 4))
        hn_grad = (
            copy_weight[:, None] * upstream
            + jnp.sum(mixing[:, :, 0:1] * mix_grad, axis=1)
            + jnp.dot(logit_grad, gate_w.T, precision=HIGHEST)
        )
        cgate_grad = jnp.dot(moe_float.T, logit_grad, precision=HIGHEST)
        cvec_grad = jnp.sum(mixing[:, :, 1:2] * mix_grad, axis=0).T

        if layer + 1 == LAYERS:
            wgrads, dback = last_grads
        else:
            (dz_in,) = expert_dispatch([gated_rows(picks, pick_gates, upstream)], blocks, 6)
            *wgrads, dparts = expert_backward(
                head_scalar,
                flat_in,
                dz_in.reshape((-1, width)),
                own_experts[layer],
                other_experts[layer],
                False,
            )
            (dback,) = expert_return([dparts.reshape((copies, NE, CAP, width))], blocks, 8)
        got = [lax.ppermute(away, "head", swap) for away in wgrads[3:]]
        dback, got[0] = lax.optimization_barrier((dback, got[0]))
        hn_grad = hn_grad + dot32(
            picks.astype(jnp.bfloat16), dback.reshape((NE * CAP, width))
        )
        middle_grad, moe_gain_grad = norm_backward(hn_grad, unit_mid, scale_mid, moe_gain)
        middle_grad = middle_grad + upstream
        (dy,) = column_exchange([middle_grad.astype(jnp.bfloat16)], [True], blocks, 3)
        dy, got[1] = lax.optimization_barrier((dy, got[1]))
        dy = dy.reshape((COLUMNS * token_rows, width))
        dattn = dot32(dy, out_rows, LAST).astype(jnp.bfloat16)
        dattn = dattn.reshape((COLUMNS, token_rows, heads * LANES))
        dq, dkv_all = attend_back(bounds, queries, dattn, attended, kv_all, starts, scale)
        dkv_all, got[2] = lax.optimization_barrier((dkv_all, got[2]))
        (dkv,) = plane_reduce(
            [dkv_all.reshape((2, COLUMNS, span, token_rows, heads * LANES))], blocks, 10
        )
        dq = dq.reshape((-1, heads * LANES))
        dkv = dkv.reshape((-1, heads * LANES))
        dxn = (dot32(dq, query_w, LAST) + dot32(dkv, kv_w, LAST)).astype(jnp.bfloat16)
        (dxn,) = column_exchange(
            [dxn.reshape((COLUMNS, token_rows, width))], [False], blocks, 11
        )
        dxn = jnp.sum(dxn.astype(jnp.float32), axis=0)
        lead_grad, attn_gain_grad = norm_backward(dxn, unit_in, scale_in, attn_gain)
        upstream = middle_grad + lead_grad
        expert_grads[layer] = [
            own + other.astype(jnp.float32) for own, other in zip(wgrads[:3], got)
        ]

        small_part = jnp.concatenate(
            [
                jnp.zeros((width, own_out), jnp.float32),
                attn_gain_grad[:, None],
                moe_gain_grad[:, None],
                cgate_grad,
                cvec_grad,
                jnp.zeros((width, small_cols - own_out - 8), jnp.float32),
            ],
            axis=1,
        )
        qkv_part, out_part = pack_grads(column, dq, dkv, attn_col, dy, small_part, compact)
        shared_grads[layer] = [
            qkv_part.reshape((2, COLUMNS, span, shard_rows, -1)),
            out_part.reshape((2, 2, span, shard_rows, width // 2)),
        ]

    packed = [part for layer in range(LAYERS) for part in shared_grads[layer]]
    reduced = plane_reduce(packed, blocks, 12, 20)
    from_planes = column_exchange(reduced[::2], [False] * LAYERS, blocks, 13, 10)
    from_planes = jnp.stack(from_planes, axis=1).astype(jnp.float32)
    kv_out = from_planes[..., : heads * LANES].reshape(
        (COLUMNS, LAYERS, shard_rows, heads, 2, head_dim)
    )
    query_out = from_planes[..., heads * LANES : heads * LANES + own_out].reshape(
        (COLUMNS, LAYERS, shard_rows, heads, 1, head_dim)
    )
    qkv_out = jnp.concatenate([query_out, kv_out], axis=4)
    qkv_out = qkv_out.transpose((1, 2, 4, 0, 3, 5)).reshape((LAYERS, shard_rows, 3 * width))
    small_out = heads * LANES + own_out
    small_out = jnp.sum(from_planes[..., small_out : small_out + 8], axis=0)
    out_grads = jnp.stack(reduced[1::2]).transpose((0, 2, 1, 3))
    out_grads = out_grads.reshape((LAYERS, shard_rows, width))
    owners = [
        (y * blocks + z * span + r, (z * 2 + y) * span + r)
        for y in range(2)
        for z in range(COLUMNS)
        for r in range(span)
    ]
    out_grads = lax.ppermute(out_grads, ("head", "blk"), owners).astype(jnp.float32)
    stacked = [jnp.stack(group) for group in zip(*expert_grads)]
    return (
        output,
        upstream,
        qkv_out,
        out_grads,
        small_out[..., 0],
        small_out[..., 1],
        small_out[..., 2:6],
        small_out[..., 6:8],
        stacked[0],
        stacked[1],
        stacked[2],
    )


def solution(mesh):
    tokens = P(("head", "blk"), None)
    by_layer = P(None, ("head", "blk"), None)
    gains = P(None, ("head", "blk"))
    experts = P(None, "blk", "head")
    return jax.shard_map(
        per_device,
        mesh=mesh,
        in_specs=(
            tokens,
            P(None, "blk"),
            by_layer,
            by_layer,
            by_layer,
            by_layer,
            gains,
            gains,
            by_layer,
            by_layer,
            experts,
            experts,
            experts,
            tokens,
        ),
        out_specs=(
            tokens,
            tokens,
            by_layer,
            by_layer,
            gains,
            gains,
            by_layer,
            by_layer,
            experts,
            experts,
            experts,
        ),
        check_vma=False,
    )
```

```python
import jax
import jax.numpy as jnp
from jax import lax
from jax.experimental import pallas as pl
from jax.experimental.pallas import tpu as pltpu
from jax.sharding import PartitionSpec as P

HEADS = 12
NE = 8
LAYERS = 2
CAP = 40
COLUMNS = 4
MESH = pl.DeviceIdType.MESH
ANY = pl.BlockSpec(memory_space=pl.ANY)
VMEM = pl.BlockSpec(memory_space=pltpu.VMEM)
DMA = pltpu.SemaphoreType.DMA
VMEM_BYTES = 48 * 1024 * 1024


def greet(peers):
    barrier = pltpu.get_barrier_semaphore()
    for peer in peers:
        pl.semaphore_signal(barrier, inc=1, device_id=peer, device_id_type=MESH)
    pl.semaphore_wait(barrier, len(peers))


def remote(src, dst, send_sem, recv_sem, peer):
    return pltpu.make_async_remote_copy(
        src_ref=src,
        dst_ref=dst,
        send_sem=send_sem,
        recv_sem=recv_sem,
        device_id=peer,
        device_id_type=MESH,
    )


def comm_params(collective_id):
    return pltpu.CompilerParams(
        collective_id=collective_id, has_side_effects=True, vmem_limit_bytes=VMEM_BYTES
    )


def lasting(microseconds):
    return pl.CostEstimate(
        flops=0, bytes_accessed=int(microseconds * 3_500_000), transcendentals=0
    )


def column_place(blocks):
    span = blocks // COLUMNS
    head, blk = lax.axis_index("head"), lax.axis_index("blk")
    plane, rest = lax.div(blk, span), lax.rem(blk, span)
    planes = [lax.rem(plane + d, COLUMNS) for d in range(COLUMNS)]
    return plane, planes, [(head, p * span + rest) for p in planes]


def column_start(src, gather, dst, own_sem, send_sems, recv_sems, where):
    plane, planes, peers = where
    own = pltpu.make_async_copy(src if gather else src.at[plane], dst.at[plane], own_sem)
    own.start()
    copies = [own]
    for d in (2, 1, 3):
        copy = remote(
            src if gather else src.at[planes[d]],
            dst.at[plane],
            send_sems.at[d],
            recv_sems.at[d],
            peers[d],
        )
        copy.start()
        copies.append(copy)
    return copies


def column_exchange(arrays, gathers, blocks, collective_id, cost=16):
    count = len(arrays)
    slabs = [
        tuple(values.shape if gather else values.shape[1:])
        for values, gather in zip(arrays, gathers)
    ]

    def body(*refs):
        srcs, dsts = refs[:count], refs[count : 2 * count]
        own_sems, send_sems, recv_sems = refs[2 * count :]
        where = column_place(blocks)
        greet(where[2][1:])
        copies = []
        for n in range(count):
            copies += column_start(
                srcs[n],
                gathers[n],
                dsts[n],
                own_sems.at[n],
                send_sems.at[n],
                recv_sems.at[n],
                where,
            )
        for copy in copies:
            copy.wait()

    return pl.pallas_call(
        body,
        out_shape=[
            jax.ShapeDtypeStruct((COLUMNS,) + slab, values.dtype)
            for values, slab in zip(arrays, slabs)
        ],
        in_specs=[ANY] * count,
        out_specs=[ANY] * count,
        scratch_shapes=[DMA((count,)), DMA((count, COLUMNS)), DMA((count, COLUMNS))],
        compiler_params=comm_params(collective_id),
        cost_estimate=lasting(cost),
    )(*arrays)


def plane_place(blocks):
    span = blocks // COLUMNS
    width = span // 2
    head, blk = lax.axis_index("head"), lax.axis_index("blk")
    plane, rest = lax.div(blk, span), lax.rem(blk, span)
    x, core = lax.div(rest, 2), lax.rem(rest, 2)
    first = plane * span
    right = [lax.rem(x + d, width) for d in range(width)]
    left = [lax.rem(x - d + width, width) for d in range(width)]
    x_peers = [(head, first + right[d] * 2 + core) for d in range(width)]
    y_peer = (1 - head, blk)
    core_peer = (head, first + x * 2 + 1 - core)
    return head, rest, core, left, x_peers, y_peer, core_peer


def plane_run(srcs, dsts, own_sems, send_sems, recv_sems, pass_sems, land_sems, where):
    head, rest, core, left, x_peers, y_peer, core_peer = where
    width, count = len(x_peers), len(srcs)
    sends, passes = [], []

    def place(n, h, dy, d):
        half = srcs[n].shape[0] // 2
        row = head if dy == 0 else 1 - head
        return dsts[n].at[row, pl.ds(h * half, half), left[d] * 2 + core]

    def held(n, h, dy, d):
        half = srcs[n].shape[0] // 2
        return srcs[n].at[pl.ds(h * half, half)] if dy == 0 and d == 0 else place(n, h, dy, d)

    def send(n, h, dy, d, peer, to_dy, to_d):
        copy = remote(
            held(n, h, dy, d),
            place(n, h, dy, d),
            send_sems.at[len(sends)],
            recv_sems.at[n, h, to_dy, to_d],
            peer,
        )
        copy.start()
        sends.append(copy)

    def hand_over(n, h, dy, d):
        copy = remote(
            held(n, h, dy, d),
            place(n, h, dy, d),
            pass_sems.at[n, h, dy, d],
            land_sems.at[n, h, dy, d],
            core_peer,
        )
        copy.start()
        passes.append(copy)

    def arrived(n, h, dy, d):
        at = place(n, h, dy, d)
        remote(at, at, send_sems.at[0], recv_sems.at[n, h, dy, d], y_peer).wait_recv()

    owns = []
    for n in range(count):
        own = pltpu.make_async_copy(srcs[n], dsts[n].at[head, :, rest], own_sems.at[n])
        own.start()
        owns.append(own)
    for n in range(count):
        for d in range(1, width):
            send(n, 0, 0, 0, x_peers[d], 0, d)
        send(n, 1, 0, 0, y_peer, 1, 0)
        send(n, 0, 0, 0, y_peer, 1, 0)
        for d in range(1, width):
            send(n, 1, 0, 0, x_peers[d], 0, d)
        hand_over(n, 0, 0, 0)
        hand_over(n, 1, 0, 0)
    for n in range(count):
        for d in range(1, width):
            arrived(n, 0, 0, d)
            send(n, 0, 0, d, y_peer, 1, d)
            hand_over(n, 0, 0, d)
        arrived(n, 1, 1, 0)
        for d in range(1, width):
            send(n, 1, 1, 0, x_peers[d], 1, d)
        hand_over(n, 1, 1, 0)
    for n in range(count):
        arrived(n, 0, 1, 0)
        hand_over(n, 0, 1, 0)
        for d in range(1, width):
            arrived(n, 1, 0, d)
            hand_over(n, 1, 0, d)
        for d in range(1, width):
            arrived(n, 0, 1, d)
            hand_over(n, 0, 1, d)
            arrived(n, 1, 1, d)
            hand_over(n, 1, 1, d)
    for own in owns:
        own.wait()
    for copy in passes:
        copy.wait()
    for copy in sends:
        copy.wait_send()


def plane_scratch(count, blocks):
    width = blocks // COLUMNS // 2
    links = 4 * (width - 1) + 2
    return [DMA((count,)), DMA((count * links,))] + [DMA((count, 2, 2, width))] * 3


def plane_shapes(arrays, blocks):
    return [
        jax.ShapeDtypeStruct(
            (2, values.shape[0], blocks // COLUMNS) + tuple(values.shape[1:]), values.dtype
        )
        for values in arrays
    ]


def plane_gather(arrays, blocks, collective_id, cost=16):
    count = len(arrays)

    def body(*refs):
        srcs, dsts, sems = refs[:count], refs[count : 2 * count], refs[2 * count :]
        where = plane_place(blocks)
        greet(where[4][1:] + [where[5], where[6]])
        plane_run(srcs, dsts, *sems, where)

    return pl.pallas_call(
        body,
        out_shape=plane_shapes(arrays, blocks),
        in_specs=[ANY] * count,
        out_specs=[ANY] * count,
        scratch_shapes=plane_scratch(count, blocks),
        compiler_params=comm_params(collective_id),
        cost_estimate=lasting(cost),
    )(*arrays)


def start_gather(packs, tokens, blocks, collective_id, cost=35):
    count = len(packs)

    def body(*refs):
        srcs, refs = refs[: count + 1], refs[count + 1 :]
        wholes, refs = refs[:count], refs[count:]
        columns, refs = refs[: count + 1], refs[count + 1 :]
        own_sems, send_sems, recv_sems, *plane_sems = refs
        column, plane = column_place(blocks), plane_place(blocks)
        greet(column[2][1:] + plane[4][1:] + [plane[5], plane[6]])
        waits = [
            column_start(
                srcs[n],
                n == count,
                columns[n],
                own_sems.at[n],
                send_sems.at[n],
                recv_sems.at[n],
                column,
            )
            for n in range(count + 1)
        ]
        for n in range(count):
            for copy in waits[n]:
                copy.wait()
        plane_run(columns[:count], wholes, *plane_sems, plane)
        for copy in waits[count]:
            copy.wait()

    results = pl.pallas_call(
        body,
        out_shape=plane_shapes(packs, blocks)
        + [jax.ShapeDtypeStruct(pack.shape, pack.dtype) for pack in packs]
        + [jax.ShapeDtypeStruct((COLUMNS,) + tokens.shape, tokens.dtype)],
        in_specs=[ANY] * (count + 1),
        out_specs=[ANY] * (2 * count + 1),
        scratch_shapes=[
            DMA((count + 1,)),
            DMA((count + 1, COLUMNS)),
            DMA((count + 1, COLUMNS)),
        ]
        + plane_scratch(count, blocks),
        compiler_params=comm_params(collective_id),
        cost_estimate=lasting(cost),
    )(*packs, tokens)
    return results[:count], results[-1]


def plane_reduce(arrays, blocks, collective_id, cost=25):
    span = blocks // COLUMNS
    width = span // 2
    count = len(arrays)
    shapes = [(values.shape[1],) + tuple(values.shape[3:]) for values in arrays]

    def body(*refs):
        srcs, outs, refs = refs[:count], refs[count : 2 * count], refs[2 * count :]
        scratch = [refs[8 * n : 8 * n + 8] for n in range(count)]
        core_send, core_recv, link_send, link_recv = refs[8 * count :]
        head, blk = lax.axis_index("head"), lax.axis_index("blk")
        plane, rest = lax.div(blk, span), lax.rem(blk, span)
        x, core = lax.div(rest, 2), lax.rem(rest, 2)
        first = plane * span
        right = [lax.rem(x + d, width) for d in range(width)]
        x_peers = [(head, first + right[d] * 2 + core) for d in range(width)]
        y_peer = (1 - head, blk)
        core_peer = (head, first + x * 2 + 1 - core)
        greet(x_peers[1:] + [y_peer, core_peer])

        def wide(ref, *at):
            return ref[at].astype(jnp.float32)

        starts = {}
        for n in range(count):
            half = shapes[n][0] // 2
            for h in range(2):
                copy = remote(
                    srcs[n].at[:, pl.ds(h * half, half), :, 1 - core],
                    scratch[n][0].at[:, pl.ds(h * half, half)],
                    core_send.at[n, h],
                    core_recv.at[n, h],
                    core_peer,
                )
                copy.start()
                starts[n, h] = copy

        sends, yas, ybs, xbs = {}, {}, {}, {}
        for n in range(count):
            src, half, kind = srcs[n], shapes[n][0] // 2, arrays[n].dtype
            core_in, summed, xa_in, _, _, yb_in, _, _ = scratch[n]

            def core_sum(h):
                def step(i, _):
                    yy = lax.div(i, half * width)
                    zz = lax.div(lax.rem(i, half * width), width) + h * half
                    xx = lax.rem(i, width)
                    total = wide(src, yy, zz, xx, core) + wide(core_in, yy, zz, xx)
                    summed[yy, zz, xx] = total.astype(kind)
                    return 0

                lax.fori_loop(0, 2 * half * width, step, 0)

            starts[n, 0].wait_recv()
            core_sum(0)
            for d in range(1, width):
                copy = remote(
                    summed.at[:, pl.ds(0, half), right[d]],
                    xa_in.at[d],
                    link_send.at[n, 0, d],
                    link_recv.at[n, 0, d],
                    x_peers[d],
                )
                copy.start()
                sends[n, d] = copy
            starts[n, 1].wait_recv()
            core_sum(1)
            ybs[n] = remote(
                summed.at[1 - head, pl.ds(half, half)],
                yb_in,
                link_send.at[n, 1, 0],
                link_recv.at[n, 1, 0],
                y_peer,
            )
            ybs[n].start()
        for n in range(count):
            half, kind = shapes[n][0] // 2, arrays[n].dtype
            _, summed, xa_in, ya_out, ya_in, yb_in, xb_out, xb_in = scratch[n]
            for d in range(1, width):
                sends[n, d].wait_recv()

            def a_step(zz, _):
                total = wide(summed, 1 - head, zz, x)
                for d in range(1, width):
                    total = total + wide(xa_in, d, 1 - head, zz)
                ya_out[zz] = total.astype(kind)
                return 0

            lax.fori_loop(0, half, a_step, 0)
            yas[n] = remote(
                ya_out, ya_in, link_send.at[n, 0, 0], link_recv.at[n, 0, 0], y_peer
            )
            yas[n].start()
            ybs[n].wait_recv()
            for d in range(1, width):

                def b_step(zz, _):
                    total = wide(summed, head, half + zz, right[d]) + wide(yb_in, zz, right[d])
                    xb_out[d, zz] = total.astype(kind)
                    return 0

                lax.fori_loop(0, half, b_step, 0)
                xbs[n, d] = remote(
                    xb_out.at[d],
                    xb_in.at[d],
                    link_send.at[n, 1, d],
                    link_recv.at[n, 1, d],
                    x_peers[d],
                )
                xbs[n, d].start()
        for n in range(count):
            out, half, kind = outs[n], shapes[n][0] // 2, arrays[n].dtype
            _, summed, xa_in, _, ya_in, yb_in, _, xb_in = scratch[n]
            yas[n].wait_recv()

            def a_last(zz, _):
                total = wide(summed, head, zz, x) + wide(ya_in, zz)
                for d in range(1, width):
                    total = total + wide(xa_in, d, head, zz)
                out[zz] = total.astype(kind)
                return 0

            lax.fori_loop(0, half, a_last, 0)
            for d in range(1, width):
                xbs[n, d].wait_recv()

            def b_last(zz, _):
                total = wide(summed, head, half + zz, x) + wide(yb_in, zz, x)
                for d in range(1, width):
                    total = total + wide(xb_in, d, zz)
                out[half + zz] = total.astype(kind)
                return 0

            lax.fori_loop(0, half, b_last, 0)
        for group in (starts, sends, yas, ybs, xbs):
            for copy in group.values():
                copy.wait_send()

    scratch = []
    for (slabs, *tile), values in zip(shapes, arrays):
        tile, half, kind = tuple(tile), slabs // 2, values.dtype
        scratch += [
            pltpu.VMEM((2, slabs, width) + tile, kind),
            pltpu.VMEM((2, slabs, width) + tile, kind),
            pltpu.VMEM((width, 2, half) + tile, kind),
            pltpu.VMEM((half,) + tile, kind),
            pltpu.VMEM((half,) + tile, kind),
            pltpu.VMEM((half, width) + tile, kind),
            pltpu.VMEM((width, half) + tile, kind),
            pltpu.VMEM((width, half) + tile, kind),
        ]
    return pl.pallas_call(
        body,
        out_shape=[
            jax.ShapeDtypeStruct(shape, values.dtype) for shape, values in zip(shapes, arrays)
        ],
        in_specs=[VMEM] * count,
        out_specs=[VMEM] * count,
        scratch_shapes=scratch
        + [DMA((count, 2)), DMA((count, 2)), DMA((count, 2, width)), DMA((count, 2, width))],
        compiler_params=comm_params(collective_id),
        cost_estimate=lasting(cost),
    )(
        *[
            values.reshape((2, values.shape[1], width, 2) + tuple(values.shape[3:]))
            for values in arrays
        ]
    )


def expert_dispatch(buffers, blocks, collective_id, cost=15):
    copies = blocks // NE
    count = len(buffers)

    def body(*refs):
        srcs, dsts = refs[:count], refs[count : 2 * count]
        own_sems, send_sems, recv_sems, pass_sems, land_sems = refs[2 * count :]
        head, blk = lax.axis_index("head"), lax.axis_index("blk")
        expert, piece = lax.div(blk, copies), lax.rem(blk, copies)
        ahead = [lax.rem(expert + d, NE) for d in range(NE)]
        behind = [lax.rem(expert - d + NE, NE) for d in range(NE)]
        peers = [(head, ahead[d] * copies + piece) for d in range(NE)]
        siblings = [(head, expert * copies + lax.rem(piece + k, copies)) for k in range(copies)]
        greet(peers[1:] + siblings[1:])
        sends, passes = [], []
        for n in range(count):
            own = pltpu.make_async_copy(
                srcs[n].at[expert], dsts[n].at[piece, expert], own_sems.at[n]
            )
            own.start()
            passes.append(own)
        for n in range(count):
            for d in (4, 3, 5, 2, 6, 1, 7):
                copy = remote(
                    srcs[n].at[ahead[d]],
                    dsts[n].at[piece, expert],
                    send_sems.at[n, d],
                    recv_sems.at[n, d],
                    peers[d],
                )
                copy.start()
                sends.append(copy)
        for n in range(count):
            for d in (0, 1, 7, 2, 6, 3, 5, 4):
                place = dsts[n].at[piece, behind[d]]
                if d > 0:
                    remote(
                        place, place, send_sems.at[n, d], recv_sems.at[n, d], peers[d]
                    ).wait_recv()
                for k in range(1, copies):
                    copy = remote(
                        place if d > 0 else srcs[n].at[expert],
                        place,
                        pass_sems.at[n, k, d],
                        land_sems.at[n, k, d],
                        siblings[k],
                    )
                    copy.start()
                    passes.append(copy)
        for copy in passes:
            copy.wait()
        for copy in sends:
            copy.wait_send()

    return pl.pallas_call(
        body,
        out_shape=[
            jax.ShapeDtypeStruct((copies,) + tuple(b.shape), b.dtype) for b in buffers
        ],
        in_specs=[ANY] * count,
        out_specs=[ANY] * count,
        scratch_shapes=[DMA((count,))]
        + [DMA((count, NE))] * 2
        + [DMA((count, copies, NE))] * 2,
        compiler_params=comm_params(collective_id),
        cost_estimate=lasting(cost),
    )(*buffers)


def expert_return(arrays, blocks, collective_id, cost=15):
    copies = blocks // NE
    count = len(arrays)

    def body(*refs):
        srcs, dsts = refs[:count], refs[count : 2 * count]
        sib_ins, totals = refs[2 * count : 3 * count], refs[3 * count : 4 * count]
        own_sems, send_sems, recv_sems, pass_sems, land_sems = refs[4 * count :]
        head, blk = lax.axis_index("head"), lax.axis_index("blk")
        expert, piece = lax.div(blk, copies), lax.rem(blk, copies)
        ahead = [lax.rem(expert + d, NE) for d in range(NE)]
        peers = [(head, ahead[d] * copies + piece) for d in range(NE)]
        places = [lax.rem(piece + k, copies) for k in range(copies)]
        siblings = [(head, expert * copies + places[k]) for k in range(copies)]
        greet(peers[1:] + siblings[1:])
        order = (4, 3, 5, 2, 6, 1, 7, 0)
        passes, sends = {}, []
        for n in range(count):
            for d in order:
                for k in range(1, copies):
                    copy = remote(
                        srcs[n].at[places[k], ahead[d]],
                        sib_ins[n].at[k, ahead[d]],
                        pass_sems.at[n, k, d],
                        land_sems.at[n, k, d],
                        siblings[k],
                    )
                    copy.start()
                    passes[n, k, d] = copy
        for n in range(count):
            for d in order:
                value = srcs[n][piece, ahead[d]].astype(jnp.float32)
                for k in range(1, copies):
                    passes[n, k, d].wait_recv()
                    value = value + sib_ins[n][k, ahead[d]].astype(jnp.float32)
                totals[n][ahead[d]] = value.astype(arrays[n].dtype)
                if d > 0:
                    copy = remote(
                        totals[n].at[ahead[d]],
                        dsts[n].at[expert],
                        send_sems.at[n, d],
                        recv_sems.at[n, d],
                        peers[d],
                    )
                else:
                    copy = pltpu.make_async_copy(
                        totals[n].at[expert], dsts[n].at[expert], own_sems.at[n]
                    )
                copy.start()
                sends.append(copy)
        for copy in sends:
            copy.wait()
        for copy in passes.values():
            copy.wait_send()

    return pl.pallas_call(
        body,
        out_shape=[jax.ShapeDtypeStruct(a.shape[1:], a.dtype) for a in arrays],
        in_specs=[VMEM] * count,
        out_specs=[ANY] * count,
        scratch_shapes=[pltpu.VMEM(a.shape, a.dtype) for a in arrays]
        + [pltpu.VMEM(a.shape[1:], a.dtype) for a in arrays]
        + [DMA((count,))]
        + [DMA((count, NE))] * 2
        + [DMA((count, copies, NE))] * 2,
        compiler_params=comm_params(collective_id),
        cost_estimate=lasting(cost),
    )(*arrays)


NEGATIVE = -1e30
EPSILON = 1e-06
KEYS = 1024
LANES = 128
LAST = (((1,), (1,)), ((), ()))
FIRST = (((0,), (0,)), ((), ()))


def dot32(a, b, dims=(((1,), (0,)), ((), ()))):
    return lax.dot_general(a, b, dims, preferred_element_type=jnp.float32)


def visible(key_base, query_base, keys, queries, starts):
    key_pos = key_base + lax.broadcasted_iota(jnp.int32, (keys, queries), 0)
    query_pos = query_base + lax.broadcasted_iota(jnp.int32, (keys, queries), 1)
    return (key_pos <= query_pos) & (key_pos >= starts)


def block_bounds(starts, bases, rows):
    return jnp.stack(
        [
            lax.div(starts[:, 0], KEYS),
            lax.div(bases + rows - 1, KEYS),
            bases,
            lax.div(starts[:, rows - 1], KEYS),
        ],
        axis=1,
    )


def over_chunks(bounds_ref, i, step, carry):
    low, high, edge = bounds_ref[i, 0], bounds_ref[i, 1], bounds_ref[i, 3]
    carry = step(high, True, carry)
    inner = jnp.maximum(high - 1 - edge, 0)
    carry = lax.fori_loop(0, inner, lambda t, c: step(high - 1 - t, False, c), carry)
    below = high - 1 - inner
    return lax.fori_loop(0, below - low + 1, lambda t, c: step(below - t, True, c), carry)


def attend(bounds, queries, kv_all, starts):
    count, rows, width = queries.shape
    heads = width // LANES

    def body(bounds_ref, q_ref, kv_ref, start_ref, out_ref, attn_ref):
        i = pl.program_id(0)
        base = bounds_ref[i, 2]
        start_row = start_ref[0]
        q = [q_ref[0, :, h * LANES : (h + 1) * LANES] for h in range(heads)]

        def step(chunk, masked, carry):
            at = pl.multiple_of(chunk * KEYS, KEYS)
            if masked:
                ok = visible(chunk * KEYS, base, KEYS, rows, start_row)
            kvs = [kv_ref[pl.ds(at, KEYS), h * LANES : (h + 1) * LANES] for h in range(heads)]
            scores = [dot32(kvs[h], q[h], LAST) for h in range(heads)]
            if masked:
                scores = [jnp.where(ok, s, NEGATIVE) for s in scores]
            tops = [
                jnp.maximum(carry[h][0], jnp.max(scores[h], axis=0, keepdims=True))
                for h in range(heads)
            ]
            weights = [jnp.exp(scores[h] - tops[h]) for h in range(heads)]
            shrinks = [jnp.exp(carry[h][0] - tops[h]) for h in range(heads)]
            totals = [
                carry[h][1] * shrinks[h] + jnp.sum(weights[h], axis=0, keepdims=True)
                for h in range(heads)
            ]
            accs = [
                carry[h][2] * shrinks[h] + dot32(kvs[h], weights[h].astype(jnp.bfloat16), FIRST)
                for h in range(heads)
            ]
            return tuple(zip(tops, totals, accs))

        empty = tuple(
            (
                jnp.full((1, rows), NEGATIVE, jnp.float32),
                jnp.zeros((1, rows), jnp.float32),
                jnp.zeros((LANES, rows), jnp.float32),
            )
            for h in range(heads)
        )
        done = over_chunks(bounds_ref, i, step, empty)
        lane = lax.broadcasted_iota(jnp.int32, (LANES, rows), 0)
        narrow = []
        for h in range(heads):
            top, total, acc = done[h]
            value = jnp.where(lane < LANES // 2, top + jnp.log(total), acc / total)
            out_ref[0, :, h * LANES : (h + 1) * LANES] = value.T
            narrow.append(value[LANES // 2 :])
        attn_ref[0] = jnp.concatenate(narrow, axis=0).T.astype(jnp.bfloat16)

    return pl.pallas_call(
        body,
        out_shape=(
            jax.ShapeDtypeStruct((count, rows, width), jnp.float32),
            jax.ShapeDtypeStruct((count, rows, width // 2), jnp.bfloat16),
        ),
        grid_spec=pltpu.PrefetchScalarGridSpec(
            num_scalar_prefetch=1,
            grid=(count,),
            in_specs=[
                pl.BlockSpec((1, rows, width), lambda i, b: (i, 0, 0)),
                pl.BlockSpec(kv_all.shape, lambda i, b: (0, 0)),
                pl.BlockSpec((1, 1, rows), lambda i, b: (i, 0, 0)),
            ],
            out_specs=(
                pl.BlockSpec((1, rows, width), lambda i, b: (i, 0, 0)),
                pl.BlockSpec((1, rows, width // 2), lambda i, b: (i, 0, 0)),
            ),
        ),
        compiler_params=pltpu.CompilerParams(vmem_limit_bytes=VMEM_BYTES),
        cost_estimate=lasting(13),
    )(bounds, queries, kv_all, starts)


def attend_back(bounds, queries, dy, out_rows, kept, kv_all, starts, scale):
    count, rows, width = queries.shape
    total_keys = kv_all.shape[0]
    heads = width // LANES
    if total_keys * width * 14 > VMEM_BYTES:
        heads = 1
    wide = heads * LANES

    def body(bounds_ref, q_ref, dy_ref, w_ref, kept_ref, kv_ref, start_ref, dq_ref, dkv_ref, acc_ref):
        i = pl.program_id(1)
        base = bounds_ref[i, 2]
        start_row = start_ref[0]

        @pl.when(i == 0)
        def _():
            def clear(c, _):
                acc_ref[pl.ds(pl.multiple_of(c * KEYS, KEYS), KEYS), :] = jnp.zeros(
                    (KEYS, wide), jnp.float32
                )
                return 0

            lax.fori_loop(0, total_keys // KEYS, clear, 0)

        q = [q_ref[0, :, h * LANES : (h + 1) * LANES] for h in range(heads)]
        grads = dot32(dy_ref[0], w_ref[...], LAST).astype(jnp.bfloat16)
        g = [grads[:, h * LANES : (h + 1) * LANES] for h in range(heads)]
        qg = [jnp.concatenate([q[h], g[h]], axis=0) for h in range(heads)]
        lse, delta = [], []
        for h in range(heads):
            kept_t = kept_ref[0, :, h * LANES : (h + 1) * LANES].T
            lse.append(kept_t[0:1])
            delta.append(jnp.sum(kept_t * g[h].astype(jnp.float32).T, axis=0, keepdims=True))

        def step(chunk, masked, carry):
            at = pl.multiple_of(chunk * KEYS, KEYS)
            if masked:
                ok = visible(chunk * KEYS, base, KEYS, rows, start_row)
            lanes = [slice(h * LANES, (h + 1) * LANES) for h in range(heads)]
            kvs = [kv_ref[pl.ds(at, KEYS), lanes[h]] for h in range(heads)]
            pairs = [dot32(kvs[h], qg[h], LAST) for h in range(heads)]
            scores = [p[:, :rows] for p in pairs]
            dprobs = [p[:, rows:] for p in pairs]
            if masked:
                scores = [jnp.where(ok, s, NEGATIVE) for s in scores]
            probs = [jnp.exp(scores[h] - lse[h]) for h in range(heads)]
            dscores = [
                (probs[h] * (dprobs[h] - delta[h])).astype(jnp.bfloat16) for h in range(heads)
            ]
            both = [
                jnp.concatenate([dscores[h], probs[h].astype(jnp.bfloat16)], axis=1)
                for h in range(heads)
            ]
            for h in range(heads):
                acc_ref[pl.ds(at, KEYS), lanes[h]] += dot32(both[h], qg[h])
            return tuple(carry[h] + dot32(kvs[h], dscores[h], FIRST) for h in range(heads))

        done = over_chunks(
            bounds_ref,
            i,
            step,
            tuple(jnp.zeros((LANES, rows), jnp.float32) for h in range(heads)),
        )
        lane = lax.broadcasted_iota(jnp.int32, (LANES, rows), 0)
        for h in range(heads):
            value = jnp.where(lane < LANES // 2, done[h] * scale, 0.0)
            dq_ref[0, :, h * LANES : (h + 1) * LANES] = value.T.astype(jnp.bfloat16)

        @pl.when(i == count - 1)
        def _():
            def store(c, _):
                at = pl.ds(pl.multiple_of(c * KEYS, KEYS), KEYS)
                dkv_ref[at, :] = acc_ref[at, :].astype(jnp.bfloat16)
                return 0

            lax.fori_loop(0, total_keys // KEYS, store, 0)

    block = pl.BlockSpec((1, rows, wide), lambda h, i, b: (i, 0, h))
    whole = pl.BlockSpec((total_keys, wide), lambda h, i, b: (0, h))
    return pl.pallas_call(
        body,
        out_shape=(
            jax.ShapeDtypeStruct((count, rows, width), jnp.bfloat16),
            jax.ShapeDtypeStruct(kv_all.shape, jnp.bfloat16),
        ),
        grid_spec=pltpu.PrefetchScalarGridSpec(
            num_scalar_prefetch=1,
            grid=(width // wide, count),
            in_specs=[
                block,
                pl.BlockSpec((1,) + tuple(dy.shape[1:]), lambda h, i, b: (i, 0, 0)),
                pl.BlockSpec((wide, out_rows.shape[1]), lambda h, i, b: (h, 0)),
                block,
                whole,
                pl.BlockSpec((1, 1, rows), lambda h, i, b: (i, 0, 0)),
            ],
            out_specs=(block, whole),
            scratch_shapes=[pltpu.VMEM((total_keys, wide), jnp.float32)],
        ),
        compiler_params=pltpu.CompilerParams(vmem_limit_bytes=VMEM_BYTES),
        cost_estimate=lasting(20),
    )(bounds, queries, dy, out_rows, kept, kv_all, starts)


def expert_forward(head, rows_in, own, other):
    count, width = rows_in.shape
    hidden, features = own[0].shape
    tile = min(hidden, 256)
    steps = hidden // tile

    def body(head_ref, x_ref, go, gx, uo, ux, do, dx, out_ref, acc_ref):
        i = pl.program_id(0)
        mine = pl.ds(pl.multiple_of(head_ref[0] * features, LANES), features)
        rest = pl.ds(pl.multiple_of((1 - head_ref[0]) * features, LANES), features)
        xo, xx = x_ref[:, mine], x_ref[:, rest]
        gate = dot32(xo, go[...], LAST) + dot32(xx, gx[...], LAST)
        up = dot32(xo, uo[...], LAST) + dot32(xx, ux[...], LAST)
        act = (jax.nn.silu(gate) * up).astype(jnp.bfloat16)

        @pl.when(i == 0)
        def _():
            acc_ref[...] = jnp.zeros_like(acc_ref)

        acc_ref[:, mine] += dot32(act, do[...])
        acc_ref[:, rest] += dot32(act, dx[...])

        @pl.when(i == steps - 1)
        def _():
            out_ref[...] = acc_ref[...].astype(jnp.bfloat16)

    whole = pl.BlockSpec((count, width), lambda i, h: (0, 0))
    piece = pl.BlockSpec((tile, features), lambda i, h: (i, 0))
    weights = [w for pair in zip(own, other) for w in pair]
    return pl.pallas_call(
        body,
        out_shape=jax.ShapeDtypeStruct((count, width), jnp.bfloat16),
        grid_spec=pltpu.PrefetchScalarGridSpec(
            num_scalar_prefetch=1,
            grid=(steps,),
            in_specs=[whole] + [piece] * 6,
            out_specs=whole,
            scratch_shapes=[pltpu.VMEM((count, width), jnp.float32)],
        ),
        compiler_params=pltpu.CompilerParams(vmem_limit_bytes=VMEM_BYTES),
        cost_estimate=pl.CostEstimate(
            flops=6 * count * width * hidden,
            bytes_accessed=6 * hidden * features * 2 + 4 * count * width,
            transcendentals=count * hidden,
        ),
    )(head, rows_in, *weights)


def expert_backward(head, rows_in, grads_in, own, other, with_parts):
    count, width = rows_in.shape
    hidden, features = own[0].shape
    tile = min(hidden, 256)
    steps = hidden // tile
    sums = 2 if with_parts else 1

    def body(head_ref, x_ref, z_ref, go, gx, uo, ux, do, dx, *outs):
        keeps, sends, totals, accs = outs[:3], outs[3:6], outs[6 : 6 + sums], outs[6 + sums :]
        i = pl.program_id(0)
        mine = pl.ds(pl.multiple_of(head_ref[0] * features, LANES), features)
        rest = pl.ds(pl.multiple_of((1 - head_ref[0]) * features, LANES), features)
        xo, xx = x_ref[:, mine], x_ref[:, rest]
        zo, zx = z_ref[:, mine], z_ref[:, rest]
        gate = dot32(xo, go[...], LAST) + dot32(xx, gx[...], LAST)
        up = dot32(xo, uo[...], LAST) + dot32(xx, ux[...], LAST)
        dact = dot32(zo, do[...], LAST) + dot32(zx, dx[...], LAST)
        sigmoid = jax.nn.sigmoid(gate)
        silu = gate * sigmoid
        act = (silu * up).astype(jnp.bfloat16)
        dgate = (dact * up * sigmoid * (1.0 + gate * (1.0 - sigmoid))).astype(jnp.bfloat16)
        dup = (dact * silu).astype(jnp.bfloat16)

        @pl.when(i == 0)
        def _():
            for acc in accs:
                acc[...] = jnp.zeros_like(acc)

        accs[0][:, mine] += dot32(dgate, go[...]) + dot32(dup, uo[...])
        accs[0][:, rest] += dot32(dgate, gx[...]) + dot32(dup, ux[...])
        if with_parts:
            accs[1][:, mine] += dot32(act, do[...])
            accs[1][:, rest] += dot32(act, dx[...])
        for n, (left, mine_in, rest_in) in enumerate(
            ((dgate, xo, xx), (dup, xo, xx), (act, zo, zx))
        ):
            keeps[n][...] = dot32(left, mine_in, FIRST)
            sends[n][...] = dot32(left, rest_in, FIRST).astype(jnp.bfloat16)

        @pl.when(i == steps - 1)
        def _():
            for total, acc in zip(totals, accs):
                total[...] = acc[...].astype(jnp.bfloat16)

    whole = pl.BlockSpec((count, width), lambda i, h: (0, 0))
    piece = pl.BlockSpec((tile, features), lambda i, h: (i, 0))
    weights = [w for pair in zip(own, other) for w in pair]
    return pl.pallas_call(
        body,
        out_shape=[jax.ShapeDtypeStruct((hidden, features), jnp.float32)] * 3
        + [jax.ShapeDtypeStruct((hidden, features), jnp.bfloat16)] * 3
        + [jax.ShapeDtypeStruct((count, width), jnp.bfloat16)] * sums,
        grid_spec=pltpu.PrefetchScalarGridSpec(
            num_scalar_prefetch=1,
            grid=(steps,),
            in_specs=[whole, whole] + [piece] * 6,
            out_specs=[piece] * 6 + [whole] * sums,
            scratch_shapes=[pltpu.VMEM((count, width), jnp.float32)] * sums,
        ),
        compiler_params=pltpu.CompilerParams(vmem_limit_bytes=VMEM_BYTES),
        cost_estimate=pl.CostEstimate(
            flops=22 * count * width * hidden,
            bytes_accessed=15 * hidden * features * 2 + 8 * count * width,
            transcendentals=count * hidden,
        ),
    )(head, rows_in, grads_in, *weights)


def split(values, terms=2):
    parts = []
    for _ in range(terms):
        part = values.astype(jnp.bfloat16)
        parts.append(part)
        values = values - part.astype(jnp.float32)
    return parts


def exact_dot(pieces, values, dims):
    total = dot32(pieces[0], values, dims)
    for piece in pieces[1:]:
        total = total + dot32(piece, values, dims)
    return total


def unit_scale(values):
    return lax.rsqrt(jnp.mean(values * values, axis=-1, keepdims=True) + EPSILON)


def alone(body, out_shape, cost, *operands, scalars=0):
    specs = [pl.BlockSpec(memory_space=pltpu.SMEM)] * scalars + [VMEM] * (len(operands) - scalars)
    results = pl.pallas_call(
        body,
        out_shape=out_shape,
        in_specs=specs,
        out_specs=jax.tree.map(lambda _: VMEM, out_shape),
        compiler_params=pltpu.CompilerParams(vmem_limit_bytes=VMEM_BYTES),
        cost_estimate=lasting(cost),
    )(*operands)
    return list(results) if isinstance(out_shape, (list, tuple)) else results


def make(shape, kind=jnp.float32):
    return jax.ShapeDtypeStruct(tuple(shape), kind)


def route_tables(routes, gates):
    count, rows, _ = routes.shape
    slots = NE * CAP

    def body(routes_ref, gates_ref, picks_ref, weights_ref, slot_ref, other_ref):
        row = lax.broadcasted_iota(jnp.int32, (rows, rows), 0)
        col = lax.broadcasted_iota(jnp.int32, (rows, rows), 1)
        before = (col < row).astype(jnp.bfloat16)
        expert = lax.broadcasted_iota(jnp.int32, (rows, LANES), 1)
        slot = lax.broadcasted_iota(jnp.int32, (rows, slots), 1)
        source = lax.broadcasted_iota(jnp.int32, (LANES, slots), 0)
        target = lax.broadcasted_iota(jnp.int32, (LANES, slots), 1)
        spread = (
            (target >= source * CAP) & (target < source * CAP + CAP) & (source < NE)
        ).astype(jnp.bfloat16)
        ones = jnp.ones((rows, LANES), jnp.bfloat16)
        for n in range(count):
            gate = jnp.zeros((rows, LANES), jnp.float32)
            named = jnp.zeros((rows, LANES), jnp.float32)
            for k in range(2):
                hit = routes_ref[n, :, k : k + 1] == expert
                named = named + jnp.where(hit, 1.0, 0.0)
                gate = gate + jnp.where(hit, gates_ref[n, :, k : k + 1], 0.0)
            rank = dot32(before, named.astype(jnp.bfloat16)) + expert.astype(jnp.float32) * CAP
            rank = jnp.where(expert < NE, rank, 0.0)
            goal = exact_dot(split(rank, 2), spread, (((1,), (0,)), ((), ())))
            member = dot32(named.astype(jnp.bfloat16), spread)
            pick = jnp.where(goal == slot.astype(jnp.float32), member, 0.0)
            weight = pick * exact_dot(split(gate, 3), spread, (((1,), (0,)), ((), ())))
            picks_ref[n] = pick.astype(jnp.bfloat16)
            weights_ref[n] = weight
            slot_ref[n] = exact_dot(split(weight, 3), ones, FIRST)
            other_ref[n] = gate

    return alone(
        body,
        (
            make((count, rows, slots), jnp.bfloat16),
            make((count, rows, slots)),
            make((count, slots, LANES)),
            make((count, rows, LANES)),
        ),
        3,
        routes,
        gates,
    )


def gate_slots(slot_gates, picks, grads):
    picked = dot32(picks, grads[0], FIRST)
    for part in grads[1:]:
        picked = picked + dot32(picks, part, FIRST)
    lanes = [
        (picked[:, at : at + LANES] * slot_gates).astype(jnp.bfloat16)
        for at in range(0, picked.shape[1], LANES)
    ]
    return jnp.concatenate(lanes, axis=1)


def const_alphas(hn, smalls, base):
    logits = dot32(hn, smalls[base + 2 : base + 6].astype(jnp.bfloat16), LAST)
    alphas = []
    for c in range(2):
        first, second = logits[:, 2 * c : 2 * c + 1], logits[:, 2 * c + 1 : 2 * c + 2]
        top = jnp.maximum(first, second)
        first, second = jnp.exp(first - top), jnp.exp(second - top)
        total = first + second
        alphas.append((first / total, second / total))
    return alphas


def project(column, pack, smalls, plane, heads, scale, normed):
    count, rows, width = column.shape
    own_out = pack.shape[1] - width - heads * LANES - LANES + LANES // 2
    kv_at, tail_at = width, width + heads * LANES
    wide = heads * LANES
    small_rows = 8 * LAYERS

    def body(plane_ref, column_ref, pack_ref, *refs):
        if normed:
            smalls_in, query_ref, kv_ref, query_w_ref, out_w_ref = refs
        else:
            xn_ref, query_ref, kv_ref, query_w_ref, out_w_ref, small_ref = refs
        tail = pack_ref[:, tail_at:]
        source = lax.broadcasted_iota(jnp.int32, (tail.shape[1], wide), 0)
        target = lax.broadcasted_iota(jnp.int32, (tail.shape[1], wide), 1)
        dim = LANES // 2
        goal = lax.div(source, dim) * LANES + lax.rem(source, dim)
        to_low = ((goal == target) & (source < own_out)).astype(jnp.bfloat16)
        query_w = dot32(tail, to_low).astype(jnp.bfloat16)
        query_w_ref[...] = query_w
        out_rows = pack_ref[pl.ds(pl.multiple_of(plane_ref[0] * own_out, 64), own_out), :width]
        pieces = []
        for h in range(heads):
            pieces += [jnp.zeros((dim, width), jnp.bfloat16), out_rows[h * dim : (h + 1) * dim]]
        out_w_ref[...] = jnp.concatenate(pieces, axis=0)
        if normed:
            xn = column_ref[...].reshape((count * rows, width))
        else:
            small = tail[:, tail.shape[1] - LANES :].astype(jnp.float32).T
            first = own_out - (tail.shape[1] - LANES)
            small = small[first : first + small_rows]
            small_ref[...] = small
            x = column_ref[...].reshape((count * rows, width)).astype(jnp.float32)
            xn = (x * unit_scale(x) * small[0:1]).astype(jnp.bfloat16)
            xn_ref[...] = xn.reshape((count, rows, width))
        query = dot32(xn, query_w).astype(jnp.bfloat16).astype(jnp.float32) * scale
        query_ref[...] = query.astype(jnp.bfloat16).reshape((count, rows, wide))
        kv = dot32(xn, pack_ref[:, kv_at:tail_at]).astype(jnp.bfloat16)
        kv_ref[...] = kv.reshape((count, rows, wide))

    outs = [
        make((count, rows, wide), jnp.bfloat16),
        make((count, rows, wide), jnp.bfloat16),
        make((width, wide), jnp.bfloat16),
        make((wide, width), jnp.bfloat16),
    ]
    if normed:
        return [column] + alone(body, outs, 4, plane, column, pack, smalls, scalars=1) + [smalls]
    outs = [make(column.shape, jnp.bfloat16)] + outs + [make((small_rows, width))]
    return alone(body, outs, 4, plane, column, pack, scalars=1)


def middle(attn, x, pack, smalls, base, picks, slot_gates, grads):
    planes, rows, part = attn.shape
    width = x.shape[1]
    slots = picks.shape[1]

    def body(attn_ref, x_ref, w_ref, small_ref, picks_ref, gates_ref, *refs):
        total = x_ref[...].astype(jnp.float32)
        for z in range(planes):
            total = total + dot32(attn_ref[z], w_ref[z * part : (z + 1) * part, :width])
        mid_ref, sent_ref = refs[-2:] if grads is None else refs[-3:-1]
        mid_ref[...] = total
        hn = (total * unit_scale(total) * small_ref[base + 1 : base + 2]).astype(jnp.bfloat16)
        sent_ref[...] = dot32(picks_ref[...], hn, FIRST).astype(jnp.bfloat16)
        if grads is not None:
            refs[-1][...] = gate_slots(gates_ref[...], picks_ref[...], [refs[0][...]])

    outs = [make((rows, width)), make((slots, width), jnp.bfloat16)]
    more = []
    if grads is not None:
        outs.append(make((slots, width), jnp.bfloat16))
        more.append(grads)
    return alone(body, outs, 3, attn, x, pack, smalls, picks, slot_gates, *more)


def combine(back, weights, mid, other, smalls, base, following):
    rows, width = mid.shape

    def body(back_ref, weights_ref, mid_ref, other_ref, small_ref, x_ref, *refs):
        mid_value, gate = mid_ref[...], other_ref[...]
        hn = (mid_value * unit_scale(mid_value) * small_ref[base + 1 : base + 2]).astype(
            jnp.bfloat16
        )
        alphas = const_alphas(hn, small_ref, base)
        wide = hn.astype(jnp.float32)
        total = mid_value + exact_dot(
            split(weights_ref[...]), back_ref[...], (((1,), (0,)), ((), ()))
        )
        factor = gate[:, NE + 1 : NE + 2]
        for c in range(2):
            weight = gate[:, NE + 2 + c : NE + 3 + c]
            factor = factor + weight * alphas[c][0]
            total = total + (weight * alphas[c][1]) * small_ref[base + 6 + c : base + 7 + c]
        total = total + factor * wide
        x_ref[...] = total
        if following:
            refs[0][...] = (total * unit_scale(total) * small_ref[base + 8 : base + 9]).astype(
                jnp.bfloat16
            )

    outs = [make((rows, width))]
    if following:
        outs.append(make((rows, width), jnp.bfloat16))
    return alone(body, outs, 3, back, weights, mid, other, smalls)


def experts_back(dback, picks, upstream, mid, other, smalls, base):
    rows, width = mid.shape

    def body(dback_ref, picks_ref, up_ref, mid_ref, other_ref, small_ref, dmid_ref, dy_ref, row_ref):
        mid_value, gate = mid_ref[...], other_ref[...]
        g = up_ref[...].astype(jnp.float32)
        scale = unit_scale(mid_value)
        unit = mid_value * scale
        gain = small_ref[base + 1 : base + 2]
        hn = (unit * gain).astype(jnp.bfloat16)
        alphas = const_alphas(hn, small_ref, base)
        wide = hn.astype(jnp.float32)
        dhn = dot32(picks_ref[...], dback_ref[...])
        g_hn = jnp.sum(g * wide, axis=1, keepdims=True)
        factor = gate[:, NE + 1 : NE + 2]
        row_ref[0:1] = jnp.zeros((1, width), jnp.float32)
        for c in range(2):
            weight = gate[:, NE + 2 + c : NE + 3 + c]
            vector = small_ref[base + 6 + c : base + 7 + c]
            first, second = alphas[c]
            factor = factor + weight * first
            row_ref[6 + c : 7 + c] = jnp.sum((weight * second) * g, axis=0, keepdims=True)
            da_first = weight * g_hn
            da_second = weight * jnp.sum(g * vector, axis=1, keepdims=True)
            mean = first * da_first + second * da_second
            for j, dlog in enumerate((first * (da_first - mean), second * (da_second - mean))):
                at = 2 + 2 * c + j
                dhn = dhn + dlog * small_ref[base + at : base + at + 1]
                row_ref[at : at + 1] = jnp.sum(dlog * wide, axis=0, keepdims=True)
        dhn = dhn + factor * g
        row_ref[1:2] = jnp.sum(dhn * unit, axis=0, keepdims=True)
        through = dhn * gain
        inner = jnp.mean(through * unit, axis=1, keepdims=True)
        dmid = g + scale * (through - unit * inner)
        dmid_ref[...] = dmid
        dy_ref[...] = dmid.astype(jnp.bfloat16)

    return alone(
        body,
        [make((rows, width)), make((rows, width), jnp.bfloat16), make((8, width))],
        4,
        dback,
        picks,
        upstream,
        mid,
        other,
        smalls,
    )


def finish(dxn, x, dmid, rows_in, smalls, base, picks, slot_gates):
    planes, rows, width = dxn.shape

    def body(dxn_ref, x_ref, dmid_ref, row_ref, small_ref, *refs):
        grad = dxn_ref[0].astype(jnp.float32)
        for z in range(1, planes):
            grad = grad + dxn_ref[z].astype(jnp.float32)
        value = x_ref[...].astype(jnp.float32)
        scale = unit_scale(value)
        unit = value * scale
        out_rows = refs[-1 if picks is None else -2]
        out_rows[...] = row_ref[...]
        out_rows[0:1] = jnp.sum(grad * unit, axis=0, keepdims=True)
        through = grad * small_ref[base : base + 1]
        inner = jnp.mean(through * unit, axis=1, keepdims=True)
        g = dmid_ref[...] + scale * (through - unit * inner)
        refs[-2 if picks is None else -3][...] = g
        if picks is not None:
            refs[-1][...] = gate_slots(refs[1][...], refs[0][...], split(g))

    outs = [make((rows, width)), make((8, width))]
    more = []
    if picks is not None:
        outs.append(make((picks.shape[1], width), jnp.bfloat16))
        more = [picks, slot_gates]
    return alone(body, outs, 3, dxn, x, dmid, rows_in, smalls, *more)


def column_parts(dq, dkv, query_w, pack, width):
    rows, wide = dq.shape

    def body(dq_ref, dkv_ref, w_ref, pack_ref, out_ref):
        out_ref[...] = (
            dot32(dq_ref[...], w_ref[...], LAST)
            + dot32(dkv_ref[...], pack_ref[:, width : width + wide], LAST)
        ).astype(jnp.bfloat16)

    return alone(body, make((rows, width), jnp.bfloat16), 2, dq, dkv, query_w, pack)


def pack_grads(column, dq, dkv, attn, dy, small):
    width = column.shape[1]
    kv_cols, own_out = dkv.shape[1], attn.shape[1]
    tail = own_out + LANES // 2
    rows, cols = own_out // 2, width // 2

    def body(column_ref, dq_ref, dkv_ref, attn_ref, dy_ref, small_ref, one, two):
        one[:, :kv_cols] = dot32(column_ref[...], dkv_ref[...], FIRST).astype(jnp.bfloat16)
        source = lax.broadcasted_iota(jnp.int32, (kv_cols, tail), 0)
        target = lax.broadcasted_iota(jnp.int32, (kv_cols, tail), 1)
        dim = LANES // 2
        goal = lax.div(target, dim) * LANES + lax.rem(target, dim)
        compact = ((goal == source) & (target < own_out)).astype(jnp.bfloat16)
        narrow = dot32(dq_ref[...], compact).astype(jnp.bfloat16)
        placed = jnp.concatenate(
            [
                jnp.zeros((own_out, width), jnp.float32),
                small_ref[...],
                jnp.zeros((tail - own_out - 8, width), jnp.float32),
            ],
            axis=0,
        ).T
        one[:, kv_cols:] = (dot32(column_ref[...], narrow, FIRST) + placed).astype(jnp.bfloat16)
        out = dot32(attn_ref[...], dy_ref[...], FIRST).astype(jnp.bfloat16)
        for a in range(2):
            for b in range(2):
                two[a, b] = out[a * rows : (a + 1) * rows, b * cols : (b + 1) * cols]

    return alone(
        body,
        [make((width, kv_cols + tail), jnp.bfloat16), make((2, 2, rows, cols), jnp.bfloat16)],
        4,
        column,
        dq,
        dkv,
        attn,
        dy,
        small,
    )


def per_device(
    tokens,
    segments,
    routes,
    gates,
    w_qkv,
    w_out,
    gain_attn,
    gain_moe,
    const_gate,
    const_vec,
    w_gate,
    w_up,
    w_down,
    cotangent,
):
    blocks = lax.axis_size("blk")
    head_index, blk_index = lax.axis_index("head"), lax.axis_index("blk")
    span = blocks // COLUMNS
    plane, rest = lax.div(blk_index, span), lax.rem(blk_index, span)
    shards = 2 * blocks
    token_rows, width = tokens.shape
    shard_rows = width // shards
    head_dim = width // HEADS
    heads = HEADS // COLUMNS
    scale = head_dim ** (-0.5)
    half_length = blocks * token_rows
    positions = 2 * half_length
    copies = blocks // NE
    own_out = heads * head_dim
    wide = heads * LANES

    swap = [(0, 1), (1, 0)]
    head_scalar = head_index.reshape((1,)).astype(jnp.int32)
    plane_scalar = plane.reshape((1,)).astype(jnp.int32)

    seg_own = lax.dynamic_index_in_dim(segments, head_index, 0, keepdims=True)
    seg_rows = jnp.concatenate([lax.rem(seg_own, 128), lax.div(seg_own, 128)], axis=0)
    seg_rows = jnp.pad(seg_rows, ((0, 14), (0, 0))).astype(jnp.bfloat16)
    seg_rows = jnp.broadcast_to(seg_rows[None], (COLUMNS,) + seg_rows.shape)
    smalls = [
        jnp.concatenate(
            [gain_attn[n][:, None], gain_moe[n][:, None], const_gate[n], const_vec[n]], axis=1
        )
        for n in range(LAYERS)
    ]
    smalls.append(jnp.zeros((shard_rows, LANES // 2 - 8 * LAYERS), jnp.bfloat16))
    smalls = jnp.concatenate(smalls, axis=1)
    packs = []
    for layer in range(LAYERS):
        parts = w_qkv[layer].reshape((shard_rows, 3, COLUMNS, heads, head_dim))
        kv_part = jnp.concatenate([parts[:, 1], parts[:, 2]], axis=3)
        kv_part = kv_part.transpose((1, 0, 2, 3)).reshape((COLUMNS, shard_rows, wide))
        query_part = parts[:, 0].transpose((1, 0, 2, 3)).reshape((COLUMNS, shard_rows, own_out))
        packs.append(
            jnp.concatenate(
                [
                    jnp.broadcast_to(w_out[layer][None], (COLUMNS, shard_rows, width)),
                    kv_part,
                    query_part,
                    jnp.broadcast_to(smalls[None], (COLUMNS,) + smalls.shape),
                ],
                axis=2,
            )
        )
    weights, column_tokens = start_gather(packs + [seg_rows], tokens, blocks, 1)
    packs = [pack.reshape((width, -1)) for pack in weights[:LAYERS]]
    picks, pick_gates, slot_gates, other_gates = route_tables(routes, gates)

    def send_experts(layer, after):
        held = lax.optimization_barrier(
            tuple(w[layer] for w in (w_gate, w_up, w_down)) + (after,)
        )[:3]
        return held, [lax.ppermute(w, "head", swap) for w in held]

    own_experts, other_experts = [None] * LAYERS, [None] * LAYERS
    seg_all = weights[LAYERS][..., :2, :].astype(jnp.int32)
    seg_all = seg_all[..., 0, :] + 128 * seg_all[..., 1, :]
    seg_query = lax.dynamic_index_in_dim(seg_all, head_index, 0, keepdims=False)
    seg_query = lax.dynamic_index_in_dim(seg_query, rest, 1, keepdims=False)
    starts = jnp.sum(
        (seg_all.reshape((1, 1, -1)) < seg_query[:, :, None]).astype(jnp.int32), axis=2
    )
    bases = (
        head_index * half_length
        + (jnp.arange(COLUMNS, dtype=jnp.int32) * span + rest) * token_rows
    )
    bounds = block_bounds(starts, bases, token_rows)
    starts = starts[:, None, :]

    values = tokens
    column, small_rows = column_tokens, None
    kept = []
    for layer in range(LAYERS):
        base = 8 * layer
        last = layer + 1 == LAYERS
        column, queries, kv_own, query_w, out_rows, small_rows = project(
            column, packs[layer], small_rows, plane_scalar, heads, scale, layer > 0
        )
        (kv_all,) = plane_gather([kv_own], blocks, 4)
        kv_all = kv_all.reshape((positions, wide))
        if layer == 0:
            own_experts[0], other_experts[0] = send_experts(0, kv_all)
        attended, attn_col = attend(bounds, queries, kv_all, starts)
        (attn,) = column_exchange([attn_col], [False], blocks, 5, 9)
        mid, *sent = middle(
            attn,
            values,
            packs[layer],
            small_rows,
            base,
            picks[layer],
            slot_gates[layer],
            cotangent if last else None,
        )
        sent = [rows.reshape((NE, CAP, width)) for rows in sent]
        arrived = expert_dispatch(sent, blocks, 7 if last else 6, 24 if last else 15)
        flat_in, *dz_in = [rows.reshape((-1, width)) for rows in arrived]
        if last:
            *wgrads, dparts, parts = expert_backward(
                head_scalar, flat_in, dz_in[0], own_experts[layer], other_experts[layer], True
            )
            back, dback = expert_return(
                [rows.reshape((copies, NE, CAP, width)) for rows in (parts, dparts)],
                blocks,
                9,
                24,
            )
        else:
            own_experts[layer + 1], other_experts[layer + 1] = send_experts(layer + 1, flat_in)
            parts = expert_forward(
                head_scalar, flat_in, own_experts[layer], other_experts[layer]
            )
            (back,) = expert_return([parts.reshape((copies, NE, CAP, width))], blocks, 8)
        kept.append(
            (values, column, queries, kv_all, attended, attn_col, query_w, out_rows, mid, flat_in)
        )
        values, *normed = combine(
            back.reshape((NE * CAP, width)),
            pick_gates[layer],
            mid,
            other_gates[layer],
            small_rows,
            base,
            not last,
        )
        if not last:
            (column,) = column_exchange(normed, [True], blocks, 3)
    output = values

    upstream = cotangent
    shared_grads = [None] * LAYERS
    expert_grads = [None] * LAYERS
    for layer in reversed(range(LAYERS)):
        base = 8 * layer
        values, column, queries, kv_all, attended, attn_col, query_w, out_rows, mid, flat_in = (
            kept[layer]
        )
        if layer + 1 < LAYERS:
            (dz_in,) = expert_dispatch([dz.reshape((NE, CAP, width))], blocks, 6)
            *wgrads, dparts = expert_backward(
                head_scalar,
                flat_in,
                dz_in.reshape((-1, width)),
                own_experts[layer],
                other_experts[layer],
                False,
            )
            (dback,) = expert_return([dparts.reshape((copies, NE, CAP, width))], blocks, 8)
        got = [lax.ppermute(away, "head", swap) for away in wgrads[3:]]
        dback, got[0] = lax.optimization_barrier((dback, got[0]))
        dmid, dy, rows = experts_back(
            dback.reshape((NE * CAP, width)),
            picks[layer],
            upstream,
            mid,
            other_gates[layer],
            small_rows,
            base,
        )
        (dy,) = column_exchange([dy], [True], blocks, 3)
        dy, got[1] = lax.optimization_barrier((dy, got[1]))
        dq, dkv_all = attend_back(
            bounds, queries, dy, out_rows, attended, kv_all, starts, scale
        )
        dkv_all, got[2] = lax.optimization_barrier((dkv_all, got[2]))
        (dkv,) = plane_reduce([dkv_all.reshape((2, COLUMNS, span, token_rows, wide))], blocks, 10)
        dq = dq.reshape((-1, wide))
        dkv = dkv.reshape((-1, wide))
        dxn = column_parts(dq, dkv, query_w, packs[layer], width)
        (dxn,) = column_exchange(
            [dxn.reshape((COLUMNS, token_rows, width))], [False], blocks, 11
        )
        before = layer > 0
        upstream, rows, *dz = finish(
            dxn,
            values,
            dmid,
            rows,
            small_rows,
            base,
            picks[layer - 1] if before else None,
            slot_gates[layer - 1] if before else None,
        )
        if before:
            (dz,) = dz
        expert_grads[layer] = [
            own + other.astype(jnp.float32) for own, other in zip(wgrads[:3], got)
        ]
        qkv_part, out_part = pack_grads(
            column.reshape((-1, width)),
            dq,
            dkv,
            attn_col.reshape((-1, own_out)),
            dy.reshape((-1, width)),
            rows,
        )
        shared_grads[layer] = [
            qkv_part.reshape((2, COLUMNS, span, shard_rows, -1)),
            out_part.reshape((2, 2, span, shard_rows, width // 2)),
        ]

    packed = [part for layer in range(LAYERS) for part in shared_grads[layer]]
    reduced = plane_reduce(packed, blocks, 12, 20)
    from_planes = column_exchange(reduced[::2], [False] * LAYERS, blocks, 13, 10)
    from_planes = jnp.stack(from_planes, axis=1).astype(jnp.float32)
    kv_out = from_planes[..., :wide].reshape((COLUMNS, LAYERS, shard_rows, heads, 2, head_dim))
    query_out = from_planes[..., wide : wide + own_out].reshape(
        (COLUMNS, LAYERS, shard_rows, heads, 1, head_dim)
    )
    qkv_out = jnp.concatenate([query_out, kv_out], axis=4)
    qkv_out = qkv_out.transpose((1, 2, 4, 0, 3, 5)).reshape((LAYERS, shard_rows, 3 * width))
    small_out = jnp.sum(from_planes[..., wide + own_out : wide + own_out + 8], axis=0)
    out_grads = jnp.stack(reduced[1::2]).transpose((0, 2, 1, 3))
    out_grads = out_grads.reshape((LAYERS, shard_rows, width))
    owners = [
        (y * blocks + z * span + r, (z * 2 + y) * span + r)
        for y in range(2)
        for z in range(COLUMNS)
        for r in range(span)
    ]
    out_grads = lax.ppermute(out_grads, ("head", "blk"), owners).astype(jnp.float32)
    stacked = [jnp.stack(group) for group in zip(*expert_grads)]
    return (
        output,
        upstream,
        qkv_out,
        out_grads,
        small_out[..., 0],
        small_out[..., 1],
        small_out[..., 2:6],
        small_out[..., 6:8],
        stacked[0],
        stacked[1],
        stacked[2],
    )


def solution(mesh):
    tokens = P(("head", "blk"), None)
    by_layer = P(None, ("head", "blk"), None)
    gains = P(None, ("head", "blk"))
    experts = P(None, "blk", "head")
    return jax.shard_map(
        per_device,
        mesh=mesh,
        in_specs=(
            tokens,
            P(None, "blk"),
            by_layer,
            by_layer,
            by_layer,
            by_layer,
            gains,
            gains,
            by_layer,
            by_layer,
            experts,
            experts,
            experts,
            tokens,
        ),
        out_specs=(
            tokens,
            tokens,
            by_layer,
            by_layer,
            gains,
            gains,
            by_layer,
            by_layer,
            experts,
            experts,
            experts,
        ),
        check_vma=False,
    )
```

```python
import jax
import jax.numpy as jnp
from jax import lax
from jax.experimental import pallas as pl
from jax.experimental.pallas import tpu as pltpu
from jax.sharding import PartitionSpec as P

HEADS = 12
NE = 8
LAYERS = 2
CAP = 40
COLUMNS = 4
MESH = pl.DeviceIdType.MESH
ANY = pl.BlockSpec(memory_space=pl.ANY)
VMEM = pl.BlockSpec(memory_space=pltpu.VMEM)
DMA = pltpu.SemaphoreType.DMA
VMEM_BYTES = 48 * 1024 * 1024


def greet(peers, line=()):
    barrier = pltpu.get_barrier_semaphore()
    count = len(peers)
    for peer in peers:
        pl.semaphore_signal(barrier, inc=1, device_id=peer, device_id_type=MESH)
    for there, peer in line:

        @pl.when(there)
        def _():
            pl.semaphore_signal(barrier, inc=1, device_id=peer, device_id_type=MESH)

        count = count + there.astype(jnp.int32)
    pl.semaphore_wait(barrier, count)


def remote(src, dst, send_sem, recv_sem, peer):
    return pltpu.make_async_remote_copy(
        src_ref=src,
        dst_ref=dst,
        send_sem=send_sem,
        recv_sem=recv_sem,
        device_id=peer,
        device_id_type=MESH,
    )


def comm_params(collective_id):
    return pltpu.CompilerParams(
        collective_id=collective_id, has_side_effects=True, vmem_limit_bytes=VMEM_BYTES
    )


def lasting(microseconds):
    return pl.CostEstimate(
        flops=0, bytes_accessed=int(microseconds * 3_500_000), transcendentals=0
    )


def column_place(blocks):
    span = blocks // COLUMNS
    head, blk = lax.axis_index("head"), lax.axis_index("blk")
    plane, rest = lax.div(blk, span), lax.rem(blk, span)
    planes = [lax.rem(plane + d, COLUMNS) for d in range(COLUMNS)]
    return plane, planes, [(head, p * span + rest) for p in planes]


class Chain:
    def __init__(self, source, dst, send_sems, recv_sems, blocks):
        span = blocks // COLUMNS
        head, blk = lax.axis_index("head"), lax.axis_index("blk")
        plane, rest = lax.div(blk, span), lax.rem(blk, span)
        self.source, self.dst, self.plane = source, dst, plane
        self.send_sems, self.recv_sems = send_sems, recv_sems
        after = jnp.minimum(plane + 1, COLUMNS - 1)
        before = jnp.maximum(plane - 1, 0)
        self.line = [
            (plane < COLUMNS - 1, (head, after * span + rest)),
            (plane > 0, (head, before * span + rest)),
        ]
        lower = plane < COLUMNS // 2
        self.slabs = [
            plane,
            plane + 1 - 2 * lax.rem(plane, 2),
            jnp.where(lower, 2, 1),
            jnp.where(lower, 3, 0),
        ]

    def copy(self, k, way):
        slab = self.slabs[k]
        place = self.dst.at[slab]
        return remote(
            self.source if k == 0 else place,
            place,
            self.send_sems.at[k, way],
            self.recv_sems.at[slab],
            self.line[way][1],
        )

    def onward(self, k):
        if k == 0:
            return [self.line[0][0], self.line[1][0]]
        from_before = self.slabs[k] < self.plane
        return [
            from_before & self.line[0][0],
            jnp.logical_not(from_before) & self.line[1][0],
        ]

    def pass_on(self, k):
        for way, there in enumerate(self.onward(k)):

            @pl.when(there)
            def _():
                self.copy(k, way).start()

    def arrive(self, k):
        self.copy(k, 0).wait_recv()
        self.pass_on(k)

    def finish(self):
        for k in range(COLUMNS):
            for way, there in enumerate(self.onward(k)):

                @pl.when(there)
                def _():
                    self.copy(k, way).wait_send()


def column_start(src, gather, dst, own_sem, send_sems, recv_sems, where):
    plane, planes, peers = where
    own = pltpu.make_async_copy(src if gather else src.at[plane], dst.at[plane], own_sem)
    own.start()
    copies = [own]
    for d in (2, 1, 3):
        copy = remote(
            src if gather else src.at[planes[d]],
            dst.at[plane],
            send_sems.at[d],
            recv_sems.at[d],
            peers[d],
        )
        copy.start()
        copies.append(copy)
    return copies


def column_exchange(arrays, gathers, blocks, collective_id, cost=16):
    count = len(arrays)
    slabs = [
        tuple(values.shape if gather else values.shape[1:])
        for values, gather in zip(arrays, gathers)
    ]

    def body(*refs):
        srcs, dsts = refs[:count], refs[count : 2 * count]
        own_sems, send_sems, recv_sems = refs[2 * count :]
        where = column_place(blocks)
        greet(where[2][1:])
        copies = []
        for n in range(count):
            copies += column_start(
                srcs[n],
                gathers[n],
                dsts[n],
                own_sems.at[n],
                send_sems.at[n],
                recv_sems.at[n],
                where,
            )
        for copy in copies:
            copy.wait()

    return pl.pallas_call(
        body,
        out_shape=[
            jax.ShapeDtypeStruct((COLUMNS,) + slab, values.dtype)
            for values, slab in zip(arrays, slabs)
        ],
        in_specs=[ANY] * count,
        out_specs=[ANY] * count,
        scratch_shapes=[DMA((count,)), DMA((count, COLUMNS)), DMA((count, COLUMNS))],
        compiler_params=comm_params(collective_id),
        cost_estimate=lasting(cost),
    )(*arrays)


def column_gather(values, blocks, collective_id, cost=14):
    def body(src, dst, own_sem, send_sems, recv_sems):
        chain = Chain(src, dst, send_sems, recv_sems, blocks)
        greet([], chain.line)
        chain.pass_on(0)
        own = pltpu.make_async_copy(src, dst.at[chain.plane], own_sem)
        own.start()
        for k in range(1, COLUMNS):
            chain.arrive(k)
        own.wait()
        chain.finish()

    return pl.pallas_call(
        body,
        out_shape=jax.ShapeDtypeStruct((COLUMNS,) + tuple(values.shape), values.dtype),
        in_specs=[ANY],
        out_specs=ANY,
        scratch_shapes=[DMA, DMA((COLUMNS, 2)), DMA((COLUMNS,))],
        compiler_params=comm_params(collective_id),
        cost_estimate=lasting(cost),
    )(values)


def plane_place(blocks):
    span = blocks // COLUMNS
    width = span // 2
    head, blk = lax.axis_index("head"), lax.axis_index("blk")
    plane, rest = lax.div(blk, span), lax.rem(blk, span)
    x, core = lax.div(rest, 2), lax.rem(rest, 2)
    first = plane * span
    right = [lax.rem(x + d, width) for d in range(width)]
    left = [lax.rem(x - d + width, width) for d in range(width)]
    x_peers = [(head, first + right[d] * 2 + core) for d in range(width)]
    y_peer = (1 - head, blk)
    core_peer = (head, first + x * 2 + 1 - core)
    return head, rest, core, left, x_peers, y_peer, core_peer


class PlaneRun:
    def __init__(self, srcs, dsts, own_sems, send_sems, recv_sems, pass_sems, land_sems, where):
        self.srcs, self.dsts = srcs, dsts
        self.own_sems, self.send_sems, self.recv_sems = own_sems, send_sems, recv_sems
        self.pass_sems, self.land_sems = pass_sems, land_sems
        self.head, self.rest, self.core, self.left, self.x_peers, self.y_peer, self.core_peer = (
            where
        )
        self.width = len(self.x_peers)
        self.sends, self.passes, self.owns = [], [], []

    def place(self, n, h, dy, d):
        half = self.srcs[n].shape[0] // 2
        row = self.head if dy == 0 else 1 - self.head
        return self.dsts[n].at[row, pl.ds(h * half, half), self.left[d] * 2 + self.core]

    def held(self, n, h, dy, d):
        half = self.srcs[n].shape[0] // 2
        if dy == 0 and d == 0:
            return self.srcs[n].at[pl.ds(h * half, half)]
        return self.place(n, h, dy, d)

    def send(self, n, h, dy, d, peer, to_dy, to_d):
        copy = remote(
            self.held(n, h, dy, d),
            self.place(n, h, dy, d),
            self.send_sems.at[len(self.sends)],
            self.recv_sems.at[n, h, to_dy, to_d],
            peer,
        )
        copy.start()
        self.sends.append(copy)

    def hand_over(self, n, h, dy, d):
        copy = remote(
            self.held(n, h, dy, d),
            self.place(n, h, dy, d),
            self.pass_sems.at[n, h, dy, d],
            self.land_sems.at[n, h, dy, d],
            self.core_peer,
        )
        copy.start()
        self.passes.append(copy)

    def arrived(self, n, h, dy, d):
        at = self.place(n, h, dy, d)
        remote(
            at, at, self.send_sems.at[0], self.recv_sems.at[n, h, dy, d], self.y_peer
        ).wait_recv()

    def first(self, n):
        own = pltpu.make_async_copy(
            self.srcs[n], self.dsts[n].at[self.head, :, self.rest], self.own_sems.at[n]
        )
        own.start()
        self.owns.append(own)
        for d in range(1, self.width):
            self.send(n, 0, 0, 0, self.x_peers[d], 0, d)
        self.send(n, 1, 0, 0, self.y_peer, 1, 0)
        self.send(n, 0, 0, 0, self.y_peer, 1, 0)
        for d in range(1, self.width):
            self.send(n, 1, 0, 0, self.x_peers[d], 0, d)
        self.hand_over(n, 0, 0, 0)
        self.hand_over(n, 1, 0, 0)

    def second(self, n):
        for d in range(1, self.width):
            self.arrived(n, 0, 0, d)
            self.send(n, 0, 0, d, self.y_peer, 1, d)
            self.hand_over(n, 0, 0, d)
        self.arrived(n, 1, 1, 0)
        for d in range(1, self.width):
            self.send(n, 1, 1, 0, self.x_peers[d], 1, d)
        self.hand_over(n, 1, 1, 0)

    def third(self, n):
        self.arrived(n, 0, 1, 0)
        self.hand_over(n, 0, 1, 0)
        for d in range(1, self.width):
            self.arrived(n, 1, 0, d)
            self.hand_over(n, 1, 0, d)
        for d in range(1, self.width):
            self.arrived(n, 0, 1, d)
            self.hand_over(n, 0, 1, d)
            self.arrived(n, 1, 1, d)
            self.hand_over(n, 1, 1, d)

    def last(self):
        for own in self.owns:
            own.wait()
        for copy in self.passes:
            copy.wait()
        for copy in self.sends:
            copy.wait_send()


def plane_scratch(count, blocks):
    width = blocks // COLUMNS // 2
    links = 4 * (width - 1) + 2
    return [DMA((count,)), DMA((count * links,))] + [DMA((count, 2, 2, width))] * 3


def plane_shapes(arrays, blocks):
    return [
        jax.ShapeDtypeStruct(
            (2, values.shape[0], blocks // COLUMNS) + tuple(values.shape[1:]), values.dtype
        )
        for values in arrays
    ]


def start_gather(packs, tokens, blocks, collective_id, cost=28):
    count = len(packs)

    def body(*refs):
        srcs, refs = refs[: count + 1], refs[count + 1 :]
        wholes, refs = refs[:count], refs[count:]
        columns, refs = refs[: count + 1], refs[count + 1 :]
        own_sems, send_sems, recv_sems, *plane_sems = refs
        column, plane = column_place(blocks), plane_place(blocks)
        greet(column[2][1:] + plane[4][1:] + [plane[5], plane[6]])
        run = PlaneRun(columns[:count], wholes, *plane_sems, plane)

        def begin(n):
            return column_start(
                srcs[n],
                n == count,
                columns[n],
                own_sems.at[n],
                send_sems.at[n],
                recv_sems.at[n],
                column,
            )

        waits = [begin(0), begin(1)]
        for n in range(count):
            for copy in waits[n]:
                copy.wait()
            if n + 2 <= count:
                waits.append(begin(n + 2))
            run.first(n)
        for n in range(count):
            run.second(n)
        for n in range(count):
            run.third(n)
        run.last()
        for copy in waits[count]:
            copy.wait()

    results = pl.pallas_call(
        body,
        out_shape=plane_shapes(packs, blocks)
        + [jax.ShapeDtypeStruct(pack.shape, pack.dtype) for pack in packs]
        + [jax.ShapeDtypeStruct((COLUMNS,) + tokens.shape, tokens.dtype)],
        in_specs=[ANY] * (count + 1),
        out_specs=[ANY] * (2 * count + 1),
        scratch_shapes=[
            DMA((count + 1,)),
            DMA((count + 1, COLUMNS)),
            DMA((count + 1, COLUMNS)),
        ]
        + plane_scratch(count, blocks),
        compiler_params=comm_params(collective_id),
        cost_estimate=lasting(cost),
    )(*packs, tokens)
    return results[:count], results[-1]


def project_gather(source, pack, smalls, heads, scale, blocks, collective_id, cost=22):
    span = blocks // COLUMNS
    width = span // 2
    chained = smalls is not None
    rows, features = source.shape[-2:]
    wide = heads * LANES
    kv_at, tail_at = features, features + wide
    tail_cols = pack.shape[1] - tail_at
    own_out = tail_cols - LANES // 2
    dim = LANES // 2
    half = rows // 2
    small_rows = 8 * LAYERS
    links = 4 * (width - 1) + 2

    def body(*refs):
        if chained:
            source_ref, pack_ref, small_ref = refs[:3]
            refs = refs[3:]
            small_out = None
        else:
            source_ref, pack_ref = refs[:2]
            small_out, refs = refs[2], refs[3:]
        column_ref, query_ref, query_w_ref, out_w_ref, kv_ref = refs[:5]
        kv_own, own_sems, send_sems, recv_sems, pass_sems, land_sems, z_send, z_recv = refs[5:]
        head, rest, core, left, x_peers, y_peer, core_peer = plane_place(blocks)
        plane = lax.div(lax.axis_index("blk"), span)
        sends, passes, owns = [], [], []
        near = x_peers[1:] + [y_peer, core_peer]
        if chained:
            chain = Chain(source_ref, column_ref, z_send, z_recv, blocks)
            slabs = chain.slabs
            greet(near, chain.line)
            chain.pass_on(0)
        else:
            slabs = list(range(COLUMNS))
            greet(near)

        tail = pack_ref[:, tail_at:]
        low = lax.broadcasted_iota(jnp.int32, (tail_cols, wide), 0)
        target = lax.broadcasted_iota(jnp.int32, (tail_cols, wide), 1)
        goal = lax.div(low, dim) * LANES + lax.rem(low, dim)
        to_low = ((goal == target) & (low < own_out)).astype(jnp.bfloat16)
        query_w = dot32(tail, to_low).astype(jnp.bfloat16)
        query_w_ref[...] = query_w
        out_rows = pack_ref[pl.ds(pl.multiple_of(plane * own_out, 64), own_out), :features]
        pieces = []
        for h in range(heads):
            pieces += [jnp.zeros((dim, features), jnp.bfloat16), out_rows[h * dim : (h + 1) * dim]]
        out_w_ref[...] = jnp.concatenate(pieces, axis=0)
        if not chained:
            small = tail[:, tail_cols - LANES :].astype(jnp.float32).T
            at = own_out - (tail_cols - LANES)
            small = small[at : at + small_rows]
            small_out[...] = small

        def place(k, h, dy, d):
            row = head if dy == 0 else 1 - head
            return kv_ref.at[row, slabs[k], left[d] * 2 + core, pl.ds(h * half, half)]

        def held(k, h, dy, d):
            if dy == 0 and d == 0:
                return kv_own.at[k, pl.ds(h * half, half)]
            return place(k, h, dy, d)

        def send(k, h, dy, d, peer, to_dy, to_d):
            copy = remote(
                held(k, h, dy, d),
                place(k, h, dy, d),
                send_sems.at[len(sends)],
                recv_sems.at[k, h, to_dy, to_d],
                peer,
            )
            copy.start()
            sends.append(copy)

        def hand_over(k, h, dy, d):
            copy = remote(
                held(k, h, dy, d),
                place(k, h, dy, d),
                pass_sems.at[k, h, dy, d],
                land_sems.at[k, h, dy, d],
                core_peer,
            )
            copy.start()
            passes.append(copy)

        def arrived(k, h, dy, d):
            at = place(k, h, dy, d)
            remote(at, at, send_sems.at[0], recv_sems.at[k, h, dy, d], y_peer).wait_recv()

        def first(k):
            slab = slabs[k]
            if not chained:
                x = source_ref[slab].astype(jnp.float32)
                xn = (x * unit_scale(x) * small[0:1]).astype(jnp.bfloat16)
                column_ref[slab] = xn
            elif k == 0:
                xn = source_ref[...]
                column_ref[slab] = xn
            else:
                chain.arrive(k)
                xn = column_ref[slab]
            kv = dot32(xn, pack_ref[:, kv_at:tail_at])
            kv_own[k] = kv.astype(jnp.bfloat16)
            own = pltpu.make_async_copy(
                kv_own.at[k], kv_ref.at[head, slab, rest], own_sems.at[k]
            )
            own.start()
            owns.append(own)
            for d in range(1, width):
                send(k, 0, 0, 0, x_peers[d], 0, d)
            send(k, 1, 0, 0, y_peer, 1, 0)
            send(k, 0, 0, 0, y_peer, 1, 0)
            for d in range(1, width):
                send(k, 1, 0, 0, x_peers[d], 0, d)
            hand_over(k, 0, 0, 0)
            hand_over(k, 1, 0, 0)
            query = dot32(xn, query_w).astype(jnp.bfloat16).astype(jnp.float32) * scale
            query_ref[slab] = query.astype(jnp.bfloat16)

        def second(k):
            for d in range(1, width):
                arrived(k, 0, 0, d)
                send(k, 0, 0, d, y_peer, 1, d)
                hand_over(k, 0, 0, d)
            arrived(k, 1, 1, 0)
            for d in range(1, width):
                send(k, 1, 1, 0, x_peers[d], 1, d)
            hand_over(k, 1, 1, 0)

        def third(k):
            arrived(k, 0, 1, 0)
            hand_over(k, 0, 1, 0)
            for d in range(1, width):
                arrived(k, 1, 0, d)
                hand_over(k, 1, 0, d)
            for d in range(1, width):
                arrived(k, 0, 1, d)
                hand_over(k, 0, 1, d)
                arrived(k, 1, 1, d)
                hand_over(k, 1, 1, d)

        for t in range(COLUMNS + 2):
            if t < COLUMNS:
                first(t)
            if 0 <= t - 1 < COLUMNS:
                second(t - 1)
            if 0 <= t - 2 < COLUMNS:
                third(t - 2)
        for copy in owns + passes:
            copy.wait()
        for copy in sends:
            copy.wait_send()
        if chained:
            chain.finish()

    shapes = [
        jax.ShapeDtypeStruct((COLUMNS, rows, features), jnp.bfloat16),
        jax.ShapeDtypeStruct((COLUMNS, rows, wide), jnp.bfloat16),
        jax.ShapeDtypeStruct((features, wide), jnp.bfloat16),
        jax.ShapeDtypeStruct((wide, features), jnp.bfloat16),
        jax.ShapeDtypeStruct((2, COLUMNS, span, rows, wide), jnp.bfloat16),
    ]
    operands = [source, pack]
    if chained:
        operands.append(smalls)
    else:
        shapes = [jax.ShapeDtypeStruct((small_rows, features), jnp.float32)] + shapes
    results = pl.pallas_call(
        body,
        out_shape=shapes,
        in_specs=[VMEM] * len(operands),
        out_specs=[VMEM] * (len(shapes) - 1) + [ANY],
        scratch_shapes=[
            pltpu.VMEM((COLUMNS, rows, wide), jnp.bfloat16),
            DMA((COLUMNS,)),
            DMA((COLUMNS * links,)),
            DMA((COLUMNS, 2, 2, width)),
            DMA((COLUMNS, 2, 2, width)),
            DMA((COLUMNS, 2, 2, width)),
            DMA((COLUMNS, 2)),
            DMA((COLUMNS,)),
        ],
        compiler_params=comm_params(collective_id),
        cost_estimate=lasting(cost),
    )(*operands)
    return list(results) + [smalls] if chained else list(results[1:]) + [results[0]]


def plane_reduce(arrays, blocks, collective_id, cost=25):
    span = blocks // COLUMNS
    width = span // 2
    count = len(arrays)
    shapes = [(values.shape[1],) + tuple(values.shape[3:]) for values in arrays]

    def body(*refs):
        srcs, outs, refs = refs[:count], refs[count : 2 * count], refs[2 * count :]
        scratch = [refs[8 * n : 8 * n + 8] for n in range(count)]
        core_send, core_recv, link_send, link_recv = refs[8 * count :]
        head, blk = lax.axis_index("head"), lax.axis_index("blk")
        plane, rest = lax.div(blk, span), lax.rem(blk, span)
        x, core = lax.div(rest, 2), lax.rem(rest, 2)
        first = plane * span
        right = [lax.rem(x + d, width) for d in range(width)]
        x_peers = [(head, first + right[d] * 2 + core) for d in range(width)]
        y_peer = (1 - head, blk)
        core_peer = (head, first + x * 2 + 1 - core)
        greet(x_peers[1:] + [y_peer, core_peer])

        def wide(ref, *at):
            return ref[at].astype(jnp.float32)

        starts = {}
        for n in range(count):
            half = shapes[n][0] // 2
            for h in range(2):
                copy = remote(
                    srcs[n].at[:, pl.ds(h * half, half), :, 1 - core],
                    scratch[n][0].at[:, pl.ds(h * half, half)],
                    core_send.at[n, h],
                    core_recv.at[n, h],
                    core_peer,
                )
                copy.start()
                starts[n, h] = copy

        sends, yas, ybs, xbs = {}, {}, {}, {}
        for n in range(count):
            src, half, kind = srcs[n], shapes[n][0] // 2, arrays[n].dtype
            core_in, summed, xa_in, _, _, yb_in, _, _ = scratch[n]

            def core_sum(h):
                def step(i, _):
                    yy = lax.div(i, half * width)
                    zz = lax.div(lax.rem(i, half * width), width) + h * half
                    xx = lax.rem(i, width)
                    total = wide(src, yy, zz, xx, core) + wide(core_in, yy, zz, xx)
                    summed[yy, zz, xx] = total.astype(kind)
                    return 0

                lax.fori_loop(0, 2 * half * width, step, 0)

            starts[n, 0].wait_recv()
            core_sum(0)
            for d in range(1, width):
                copy = remote(
                    summed.at[:, pl.ds(0, half), right[d]],
                    xa_in.at[d],
                    link_send.at[n, 0, d],
                    link_recv.at[n, 0, d],
                    x_peers[d],
                )
                copy.start()
                sends[n, d] = copy
            starts[n, 1].wait_recv()
            core_sum(1)
            ybs[n] = remote(
                summed.at[1 - head, pl.ds(half, half)],
                yb_in,
                link_send.at[n, 1, 0],
                link_recv.at[n, 1, 0],
                y_peer,
            )
            ybs[n].start()
        for n in range(count):
            half, kind = shapes[n][0] // 2, arrays[n].dtype
            _, summed, xa_in, ya_out, ya_in, yb_in, xb_out, xb_in = scratch[n]
            for d in range(1, width):
                sends[n, d].wait_recv()

            def a_step(zz, _):
                total = wide(summed, 1 - head, zz, x)
                for d in range(1, width):
                    total = total + wide(xa_in, d, 1 - head, zz)
                ya_out[zz] = total.astype(kind)
                return 0

            lax.fori_loop(0, half, a_step, 0)
            yas[n] = remote(
                ya_out, ya_in, link_send.at[n, 0, 0], link_recv.at[n, 0, 0], y_peer
            )
            yas[n].start()
            ybs[n].wait_recv()
            for d in range(1, width):

                def b_step(zz, _):
                    total = wide(summed, head, half + zz, right[d]) + wide(yb_in, zz, right[d])
                    xb_out[d, zz] = total.astype(kind)
                    return 0

                lax.fori_loop(0, half, b_step, 0)
                xbs[n, d] = remote(
                    xb_out.at[d],
                    xb_in.at[d],
                    link_send.at[n, 1, d],
                    link_recv.at[n, 1, d],
                    x_peers[d],
                )
                xbs[n, d].start()
        for n in range(count):
            out, half, kind = outs[n], shapes[n][0] // 2, arrays[n].dtype
            _, summed, xa_in, _, ya_in, yb_in, _, xb_in = scratch[n]
            yas[n].wait_recv()

            def a_last(zz, _):
                total = wide(summed, head, zz, x) + wide(ya_in, zz)
                for d in range(1, width):
                    total = total + wide(xa_in, d, head, zz)
                out[zz] = total.astype(kind)
                return 0

            lax.fori_loop(0, half, a_last, 0)
            for d in range(1, width):
                xbs[n, d].wait_recv()

            def b_last(zz, _):
                total = wide(summed, head, half + zz, x) + wide(yb_in, zz, x)
                for d in range(1, width):
                    total = total + wide(xb_in, d, zz)
                out[half + zz] = total.astype(kind)
                return 0

            lax.fori_loop(0, half, b_last, 0)
        for group in (starts, sends, yas, ybs, xbs):
            for copy in group.values():
                copy.wait_send()

    scratch = []
    for (slabs, *tile), values in zip(shapes, arrays):
        tile, half, kind = tuple(tile), slabs // 2, values.dtype
        scratch += [
            pltpu.VMEM((2, slabs, width) + tile, kind),
            pltpu.VMEM((2, slabs, width) + tile, kind),
            pltpu.VMEM((width, 2, half) + tile, kind),
            pltpu.VMEM((half,) + tile, kind),
            pltpu.VMEM((half,) + tile, kind),
            pltpu.VMEM((half, width) + tile, kind),
            pltpu.VMEM((width, half) + tile, kind),
            pltpu.VMEM((width, half) + tile, kind),
        ]
    return pl.pallas_call(
        body,
        out_shape=[
            jax.ShapeDtypeStruct(shape, values.dtype) for shape, values in zip(shapes, arrays)
        ],
        in_specs=[VMEM] * count,
        out_specs=[VMEM] * count,
        scratch_shapes=scratch
        + [DMA((count, 2)), DMA((count, 2)), DMA((count, 2, width)), DMA((count, 2, width))],
        compiler_params=comm_params(collective_id),
        cost_estimate=lasting(cost),
    )(
        *[
            values.reshape((2, values.shape[1], width, 2) + tuple(values.shape[3:]))
            for values in arrays
        ]
    )


def reduce_project(dkv_all, dq, query_w, pack, blocks, collective_id, cost=26):
    span = blocks // COLUMNS
    width = span // 2
    rows, wide = dkv_all.shape[3:]
    half = rows // 2
    features = query_w.shape[0]
    kind = dkv_all.dtype

    def body(
        src,
        dq_ref,
        w_ref,
        pack_ref,
        dkv_ref,
        dxn_ref,
        core_in,
        summed,
        xa_in,
        ya_out,
        ya_in,
        yb_in,
        xb_out,
        xb_in,
        share,
        core_send,
        core_recv,
        link_send,
        link_recv,
        z_send,
        z_recv,
    ):
        head, _, core, _, x_peers, y_peer, core_peer = plane_place(blocks)
        plane, planes, z_peers = column_place(blocks)
        x = lax.div(lax.rem(lax.axis_index("blk"), span), 2)
        right = [lax.rem(x + d, width) for d in range(width)]
        greet(x_peers[1:] + [y_peer, core_peer] + z_peers[1:])
        order = (2, 1, 3, 0)
        copies = []

        def begin(copy):
            copy.start()
            copies.append(copy)
            return copy

        def wide_of(ref, *at):
            return ref[at].astype(jnp.float32)

        top, low = pl.ds(0, half), pl.ds(half, half)
        starts = [
            begin(
                remote(
                    src.at[:, planes[d], :, 1 - core],
                    core_in.at[k],
                    core_send.at[k],
                    core_recv.at[k],
                    core_peer,
                )
            )
            for k, d in enumerate(order)
        ]
        xas, yas, ybs, xbs, z_copies = {}, {}, {}, {}, []

        def first(k):
            starts[k].wait_recv()

            def step(i, _):
                yy, xx = lax.div(i, width), lax.rem(i, width)
                total = wide_of(src, yy, planes[order[k]], xx, core) + wide_of(core_in, k, yy, xx)
                summed[k, yy, xx] = total.astype(kind)
                return 0

            lax.fori_loop(0, 2 * width, step, 0)
            for d in range(1, width):
                xas[k, d] = begin(
                    remote(
                        summed.at[k, :, right[d], top],
                        xa_in.at[k, d],
                        link_send.at[k, 0, d],
                        link_recv.at[k, 0, d],
                        x_peers[d],
                    )
                )
            ybs[k] = begin(
                remote(
                    summed.at[k, 1 - head, :, low],
                    yb_in.at[k],
                    link_send.at[k, 1, 0],
                    link_recv.at[k, 1, 0],
                    y_peer,
                )
            )

        def second(k):
            total = wide_of(summed, k, 1 - head, x, top)
            for d in range(1, width):
                xas[k, d].wait_recv()
                total = total + wide_of(xa_in, k, d, 1 - head)
            ya_out[k] = total.astype(kind)
            yas[k] = begin(
                remote(
                    ya_out.at[k],
                    ya_in.at[k],
                    link_send.at[k, 0, 0],
                    link_recv.at[k, 0, 0],
                    y_peer,
                )
            )
            ybs[k].wait_recv()
            for d in range(1, width):
                total = wide_of(summed, k, head, right[d], low) + wide_of(yb_in, k, right[d])
                xb_out[k, d] = total.astype(kind)
                xbs[k, d] = begin(
                    remote(
                        xb_out.at[k, d],
                        xb_in.at[k, d],
                        link_send.at[k, 1, d],
                        link_recv.at[k, 1, d],
                        x_peers[d],
                    )
                )

        def third(k):
            slab = planes[order[k]]
            yas[k].wait_recv()
            total = wide_of(summed, k, head, x, top) + wide_of(ya_in, k)
            for d in range(1, width):
                total = total + wide_of(xa_in, k, d, head)
            dkv_ref[slab, top] = total.astype(kind)
            total = wide_of(summed, k, head, x, low) + wide_of(yb_in, k, x)
            for d in range(1, width):
                xbs[k, d].wait_recv()
                total = total + wide_of(xb_in, k, d)
            dkv_ref[slab, low] = total.astype(kind)
            part = (
                dot32(dq_ref[slab], w_ref[...], LAST)
                + dot32(dkv_ref[slab], pack_ref[:, features : features + wide], LAST)
            ).astype(kind)
            if order[k] == 0:
                dxn_ref[plane] = part
            else:
                share[k] = part
                z_copies.append(
                    begin(
                        remote(
                            share.at[k],
                            dxn_ref.at[plane],
                            z_send.at[order[k]],
                            z_recv.at[order[k]],
                            z_peers[order[k]],
                        )
                    )
                )

        for t in range(COLUMNS + 2):
            if t < COLUMNS:
                first(t)
            if 0 <= t - 1 < COLUMNS:
                second(t - 1)
            if 0 <= t - 2 < COLUMNS:
                third(t - 2)
        for copy in z_copies:
            copy.wait_recv()
        for copy in copies:
            copy.wait_send()

    tile = (rows, wide)
    part = (half, wide)
    return pl.pallas_call(
        body,
        out_shape=[
            jax.ShapeDtypeStruct((COLUMNS,) + tile, kind),
            jax.ShapeDtypeStruct((COLUMNS, rows, features), kind),
        ],
        in_specs=[VMEM] * 4,
        out_specs=[VMEM] * 2,
        scratch_shapes=[
            pltpu.VMEM((COLUMNS, 2, width) + tile, kind),
            pltpu.VMEM((COLUMNS, 2, width) + tile, kind),
            pltpu.VMEM((COLUMNS, width, 2) + part, kind),
            pltpu.VMEM((COLUMNS,) + part, kind),
            pltpu.VMEM((COLUMNS,) + part, kind),
            pltpu.VMEM((COLUMNS, width) + part, kind),
            pltpu.VMEM((COLUMNS, width) + part, kind),
            pltpu.VMEM((COLUMNS, width) + part, kind),
            pltpu.VMEM((COLUMNS, rows, features), kind),
            DMA((COLUMNS,)),
            DMA((COLUMNS,)),
            DMA((COLUMNS, 2, width)),
            DMA((COLUMNS, 2, width)),
            DMA((COLUMNS,)),
            DMA((COLUMNS,)),
        ],
        compiler_params=comm_params(collective_id),
        cost_estimate=lasting(cost),
    )(dkv_all.reshape((2, COLUMNS, width, 2) + tile), dq, query_w, pack)


def expert_dispatch(buffers, blocks, collective_id, cost=15):
    copies = blocks // NE
    count = len(buffers)

    def body(*refs):
        srcs, dsts = refs[:count], refs[count : 2 * count]
        own_sems, send_sems, recv_sems, pass_sems, land_sems = refs[2 * count :]
        head, blk = lax.axis_index("head"), lax.axis_index("blk")
        expert, piece = lax.div(blk, copies), lax.rem(blk, copies)
        ahead = [lax.rem(expert + d, NE) for d in range(NE)]
        behind = [lax.rem(expert - d + NE, NE) for d in range(NE)]
        peers = [(head, ahead[d] * copies + piece) for d in range(NE)]
        siblings = [(head, expert * copies + lax.rem(piece + k, copies)) for k in range(copies)]
        greet(peers[1:] + siblings[1:])
        sends, passes = [], []
        for n in range(count):
            own = pltpu.make_async_copy(
                srcs[n].at[expert], dsts[n].at[piece, expert], own_sems.at[n]
            )
            own.start()
            passes.append(own)
        for n in range(count):
            for d in (4, 3, 5, 2, 6, 1, 7):
                copy = remote(
                    srcs[n].at[ahead[d]],
                    dsts[n].at[piece, expert],
                    send_sems.at[n, d],
                    recv_sems.at[n, d],
                    peers[d],
                )
                copy.start()
                sends.append(copy)
        for n in range(count):
            for d in (0, 1, 7, 2, 6, 3, 5, 4):
                place = dsts[n].at[piece, behind[d]]
                if d > 0:
                    remote(
                        place, place, send_sems.at[n, d], recv_sems.at[n, d], peers[d]
                    ).wait_recv()
                for k in range(1, copies):
                    copy = remote(
                        place if d > 0 else srcs[n].at[expert],
                        place,
                        pass_sems.at[n, k, d],
                        land_sems.at[n, k, d],
                        siblings[k],
                    )
                    copy.start()
                    passes.append(copy)
        for copy in passes:
            copy.wait()
        for copy in sends:
            copy.wait_send()

    return pl.pallas_call(
        body,
        out_shape=[
            jax.ShapeDtypeStruct((copies,) + tuple(b.shape), b.dtype) for b in buffers
        ],
        in_specs=[ANY] * count,
        out_specs=[ANY] * count,
        scratch_shapes=[DMA((count,))]
        + [DMA((count, NE))] * 2
        + [DMA((count, copies, NE))] * 2,
        compiler_params=comm_params(collective_id),
        cost_estimate=lasting(cost),
    )(*buffers)


def expert_return(arrays, blocks, collective_id, cost=15):
    copies = blocks // NE
    count = len(arrays)

    def body(*refs):
        srcs, dsts = refs[:count], refs[count : 2 * count]
        sib_ins, totals = refs[2 * count : 3 * count], refs[3 * count : 4 * count]
        own_sems, send_sems, recv_sems, pass_sems, land_sems = refs[4 * count :]
        head, blk = lax.axis_index("head"), lax.axis_index("blk")
        expert, piece = lax.div(blk, copies), lax.rem(blk, copies)
        ahead = [lax.rem(expert + d, NE) for d in range(NE)]
        peers = [(head, ahead[d] * copies + piece) for d in range(NE)]
        places = [lax.rem(piece + k, copies) for k in range(copies)]
        siblings = [(head, expert * copies + places[k]) for k in range(copies)]
        greet(peers[1:] + siblings[1:])
        order = (4, 3, 5, 2, 6, 1, 7, 0)
        passes, sends = {}, []
        for n in range(count):
            for d in order:
                for k in range(1, copies):
                    copy = remote(
                        srcs[n].at[places[k], ahead[d]],
                        sib_ins[n].at[k, ahead[d]],
                        pass_sems.at[n, k, d],
                        land_sems.at[n, k, d],
                        siblings[k],
                    )
                    copy.start()
                    passes[n, k, d] = copy
        for n in range(count):
            for d in order:
                value = srcs[n][piece, ahead[d]].astype(jnp.float32)
                for k in range(1, copies):
                    passes[n, k, d].wait_recv()
                    value = value + sib_ins[n][k, ahead[d]].astype(jnp.float32)
                totals[n][ahead[d]] = value.astype(arrays[n].dtype)
                if d > 0:
                    copy = remote(
                        totals[n].at[ahead[d]],
                        dsts[n].at[expert],
                        send_sems.at[n, d],
                        recv_sems.at[n, d],
                        peers[d],
                    )
                else:
                    copy = pltpu.make_async_copy(
                        totals[n].at[expert], dsts[n].at[expert], own_sems.at[n]
                    )
                copy.start()
                sends.append(copy)
        for copy in sends:
            copy.wait()
        for copy in passes.values():
            copy.wait_send()

    return pl.pallas_call(
        body,
        out_shape=[jax.ShapeDtypeStruct(a.shape[1:], a.dtype) for a in arrays],
        in_specs=[VMEM] * count,
        out_specs=[ANY] * count,
        scratch_shapes=[pltpu.VMEM(a.shape, a.dtype) for a in arrays]
        + [pltpu.VMEM(a.shape[1:], a.dtype) for a in arrays]
        + [DMA((count,))]
        + [DMA((count, NE))] * 2
        + [DMA((count, copies, NE))] * 2,
        compiler_params=comm_params(collective_id),
        cost_estimate=lasting(cost),
    )(*arrays)


NEGATIVE = -1e30
EPSILON = 1e-06
KEYS = 1024
LANES = 128
LAST = (((1,), (1,)), ((), ()))
FIRST = (((0,), (0,)), ((), ()))


def dot32(a, b, dims=(((1,), (0,)), ((), ()))):
    return lax.dot_general(a, b, dims, preferred_element_type=jnp.float32)


def visible(key_base, query_base, keys, queries, starts):
    key_pos = key_base + lax.broadcasted_iota(jnp.int32, (keys, queries), 0)
    query_pos = query_base + lax.broadcasted_iota(jnp.int32, (keys, queries), 1)
    return (key_pos <= query_pos) & (key_pos >= starts)


def block_bounds(starts, bases, rows):
    return jnp.stack(
        [
            lax.div(starts[:, 0], KEYS),
            lax.div(bases + rows - 1, KEYS),
            bases,
            lax.div(starts[:, rows - 1], KEYS),
        ],
        axis=1,
    )


def over_chunks(bounds_ref, i, step, carry):
    low, high, edge = bounds_ref[i, 0], bounds_ref[i, 1], bounds_ref[i, 3]
    carry = step(high, True, carry)
    inner = jnp.maximum(high - 1 - edge, 0)
    carry = lax.fori_loop(0, inner, lambda t, c: step(high - 1 - t, False, c), carry)
    below = high - 1 - inner
    return lax.fori_loop(0, below - low + 1, lambda t, c: step(below - t, True, c), carry)


def attend(bounds, queries, kv_all, starts):
    count, rows, width = queries.shape
    heads = width // LANES

    def body(bounds_ref, q_ref, kv_ref, start_ref, out_ref, attn_ref):
        i = pl.program_id(0)
        base = bounds_ref[i, 2]
        start_row = start_ref[0]
        q = [q_ref[0, :, h * LANES : (h + 1) * LANES] for h in range(heads)]

        def step(chunk, masked, carry):
            at = pl.multiple_of(chunk * KEYS, KEYS)
            if masked:
                ok = visible(chunk * KEYS, base, KEYS, rows, start_row)
            kvs = [kv_ref[pl.ds(at, KEYS), h * LANES : (h + 1) * LANES] for h in range(heads)]
            scores = [dot32(kvs[h], q[h], LAST) for h in range(heads)]
            if masked:
                scores = [jnp.where(ok, s, NEGATIVE) for s in scores]
            tops = [
                jnp.maximum(carry[h][0], jnp.max(scores[h], axis=0, keepdims=True))
                for h in range(heads)
            ]
            weights = [jnp.exp(scores[h] - tops[h]) for h in range(heads)]
            shrinks = [jnp.exp(carry[h][0] - tops[h]) for h in range(heads)]
            totals = [
                carry[h][1] * shrinks[h] + jnp.sum(weights[h], axis=0, keepdims=True)
                for h in range(heads)
            ]
            accs = [
                carry[h][2] * shrinks[h] + dot32(kvs[h], weights[h].astype(jnp.bfloat16), FIRST)
                for h in range(heads)
            ]
            return tuple(zip(tops, totals, accs))

        empty = tuple(
            (
                jnp.full((1, rows), NEGATIVE, jnp.float32),
                jnp.zeros((1, rows), jnp.float32),
                jnp.zeros((LANES, rows), jnp.float32),
            )
            for h in range(heads)
        )
        done = over_chunks(bounds_ref, i, step, empty)
        lane = lax.broadcasted_iota(jnp.int32, (LANES, rows), 0)
        narrow = []
        for h in range(heads):
            top, total, acc = done[h]
            value = jnp.where(lane < LANES // 2, top + jnp.log(total), acc / total)
            out_ref[0, :, h * LANES : (h + 1) * LANES] = value.T
            narrow.append(value[LANES // 2 :])
        attn_ref[0] = jnp.concatenate(narrow, axis=0).T.astype(jnp.bfloat16)

    return pl.pallas_call(
        body,
        out_shape=(
            jax.ShapeDtypeStruct((count, rows, width), jnp.float32),
            jax.ShapeDtypeStruct((count, rows, width // 2), jnp.bfloat16),
        ),
        grid_spec=pltpu.PrefetchScalarGridSpec(
            num_scalar_prefetch=1,
            grid=(count,),
            in_specs=[
                pl.BlockSpec((1, rows, width), lambda i, b: (i, 0, 0)),
                pl.BlockSpec(kv_all.shape, lambda i, b: (0, 0)),
                pl.BlockSpec((1, 1, rows), lambda i, b: (i, 0, 0)),
            ],
            out_specs=(
                pl.BlockSpec((1, rows, width), lambda i, b: (i, 0, 0)),
                pl.BlockSpec((1, rows, width // 2), lambda i, b: (i, 0, 0)),
            ),
        ),
        compiler_params=pltpu.CompilerParams(vmem_limit_bytes=VMEM_BYTES),
        cost_estimate=lasting(13),
    )(bounds, queries, kv_all, starts)


def attend_back(bounds, queries, dy, out_rows, kept, kv_all, starts, scale):
    count, rows, width = queries.shape
    total_keys = kv_all.shape[0]
    heads = width // LANES
    if total_keys * width * 14 > VMEM_BYTES:
        heads = 1
    wide = heads * LANES

    def body(bounds_ref, q_ref, dy_ref, w_ref, kept_ref, kv_ref, start_ref, dq_ref, dkv_ref, acc_ref):
        i = pl.program_id(1)
        base = bounds_ref[i, 2]
        start_row = start_ref[0]

        @pl.when(i == 0)
        def _():
            def clear(c, _):
                acc_ref[pl.ds(pl.multiple_of(c * KEYS, KEYS), KEYS), :] = jnp.zeros(
                    (KEYS, wide), jnp.float32
                )
                return 0

            lax.fori_loop(0, total_keys // KEYS, clear, 0)

        q = [q_ref[0, :, h * LANES : (h + 1) * LANES] for h in range(heads)]
        grads = dot32(dy_ref[0], w_ref[...], LAST).astype(jnp.bfloat16)
        g = [grads[:, h * LANES : (h + 1) * LANES] for h in range(heads)]
        qg = [jnp.concatenate([q[h], g[h]], axis=0) for h in range(heads)]
        lse, delta = [], []
        for h in range(heads):
            kept_t = kept_ref[0, :, h * LANES : (h + 1) * LANES].T
            lse.append(kept_t[0:1])
            delta.append(jnp.sum(kept_t * g[h].astype(jnp.float32).T, axis=0, keepdims=True))

        def step(chunk, masked, carry):
            at = pl.multiple_of(chunk * KEYS, KEYS)
            if masked:
                ok = visible(chunk * KEYS, base, KEYS, rows, start_row)
            lanes = [slice(h * LANES, (h + 1) * LANES) for h in range(heads)]
            kvs = [kv_ref[pl.ds(at, KEYS), lanes[h]] for h in range(heads)]
            pairs = [dot32(kvs[h], qg[h], LAST) for h in range(heads)]
            scores = [p[:, :rows] for p in pairs]
            dprobs = [p[:, rows:] for p in pairs]
            if masked:
                scores = [jnp.where(ok, s, NEGATIVE) for s in scores]
            probs = [jnp.exp(scores[h] - lse[h]) for h in range(heads)]
            dscores = [
                (probs[h] * (dprobs[h] - delta[h])).astype(jnp.bfloat16) for h in range(heads)
            ]
            both = [
                jnp.concatenate([dscores[h], probs[h].astype(jnp.bfloat16)], axis=1)
                for h in range(heads)
            ]
            for h in range(heads):
                acc_ref[pl.ds(at, KEYS), lanes[h]] += dot32(both[h], qg[h])
            return tuple(carry[h] + dot32(kvs[h], dscores[h], FIRST) for h in range(heads))

        done = over_chunks(
            bounds_ref,
            i,
            step,
            tuple(jnp.zeros((LANES, rows), jnp.float32) for h in range(heads)),
        )
        lane = lax.broadcasted_iota(jnp.int32, (LANES, rows), 0)
        for h in range(heads):
            value = jnp.where(lane < LANES // 2, done[h] * scale, 0.0)
            dq_ref[0, :, h * LANES : (h + 1) * LANES] = value.T.astype(jnp.bfloat16)

        @pl.when(i == count - 1)
        def _():
            def store(c, _):
                at = pl.ds(pl.multiple_of(c * KEYS, KEYS), KEYS)
                dkv_ref[at, :] = acc_ref[at, :].astype(jnp.bfloat16)
                return 0

            lax.fori_loop(0, total_keys // KEYS, store, 0)

    block = pl.BlockSpec((1, rows, wide), lambda h, i, b: (i, 0, h))
    whole = pl.BlockSpec((total_keys, wide), lambda h, i, b: (0, h))
    return pl.pallas_call(
        body,
        out_shape=(
            jax.ShapeDtypeStruct((count, rows, width), jnp.bfloat16),
            jax.ShapeDtypeStruct(kv_all.shape, jnp.bfloat16),
        ),
        grid_spec=pltpu.PrefetchScalarGridSpec(
            num_scalar_prefetch=1,
            grid=(width // wide, count),
            in_specs=[
                block,
                pl.BlockSpec((1,) + tuple(dy.shape[1:]), lambda h, i, b: (i, 0, 0)),
                pl.BlockSpec((wide, out_rows.shape[1]), lambda h, i, b: (h, 0)),
                block,
                whole,
                pl.BlockSpec((1, 1, rows), lambda h, i, b: (i, 0, 0)),
            ],
            out_specs=(block, whole),
            scratch_shapes=[pltpu.VMEM((total_keys, wide), jnp.float32)],
        ),
        compiler_params=pltpu.CompilerParams(vmem_limit_bytes=VMEM_BYTES),
        cost_estimate=lasting(20),
    )(bounds, queries, dy, out_rows, kept, kv_all, starts)


def expert_forward(head, rows_in, own, other):
    count, width = rows_in.shape
    hidden, features = own[0].shape
    tile = min(hidden, 256)
    steps = hidden // tile

    def body(head_ref, x_ref, go, gx, uo, ux, do, dx, out_ref, acc_ref):
        i = pl.program_id(0)
        mine = pl.ds(pl.multiple_of(head_ref[0] * features, LANES), features)
        rest = pl.ds(pl.multiple_of((1 - head_ref[0]) * features, LANES), features)
        xo, xx = x_ref[:, mine], x_ref[:, rest]
        gate = dot32(xo, go[...], LAST) + dot32(xx, gx[...], LAST)
        up = dot32(xo, uo[...], LAST) + dot32(xx, ux[...], LAST)
        act = (jax.nn.silu(gate) * up).astype(jnp.bfloat16)

        @pl.when(i == 0)
        def _():
            acc_ref[...] = jnp.zeros_like(acc_ref)

        acc_ref[:, mine] += dot32(act, do[...])
        acc_ref[:, rest] += dot32(act, dx[...])

        @pl.when(i == steps - 1)
        def _():
            out_ref[...] = acc_ref[...].astype(jnp.bfloat16)

    whole = pl.BlockSpec((count, width), lambda i, h: (0, 0))
    piece = pl.BlockSpec((tile, features), lambda i, h: (i, 0))
    weights = [w for pair in zip(own, other) for w in pair]
    return pl.pallas_call(
        body,
        out_shape=jax.ShapeDtypeStruct((count, width), jnp.bfloat16),
        grid_spec=pltpu.PrefetchScalarGridSpec(
            num_scalar_prefetch=1,
            grid=(steps,),
            in_specs=[whole] + [piece] * 6,
            out_specs=whole,
            scratch_shapes=[pltpu.VMEM((count, width), jnp.float32)],
        ),
        compiler_params=pltpu.CompilerParams(vmem_limit_bytes=VMEM_BYTES),
        cost_estimate=pl.CostEstimate(
            flops=6 * count * width * hidden,
            bytes_accessed=6 * hidden * features * 2 + 4 * count * width,
            transcendentals=count * hidden,
        ),
    )(head, rows_in, *weights)


def expert_backward(head, rows_in, grads_in, own, other, with_parts):
    count, width = rows_in.shape
    hidden, features = own[0].shape
    tile = min(hidden, 256)
    steps = hidden // tile
    sums = 2 if with_parts else 1

    def body(head_ref, x_ref, z_ref, go, gx, uo, ux, do, dx, *outs):
        keeps, sends, totals, accs = outs[:3], outs[3:6], outs[6 : 6 + sums], outs[6 + sums :]
        i = pl.program_id(0)
        mine = pl.ds(pl.multiple_of(head_ref[0] * features, LANES), features)
        rest = pl.ds(pl.multiple_of((1 - head_ref[0]) * features, LANES), features)
        xo, xx = x_ref[:, mine], x_ref[:, rest]
        zo, zx = z_ref[:, mine], z_ref[:, rest]
        gate = dot32(xo, go[...], LAST) + dot32(xx, gx[...], LAST)
        up = dot32(xo, uo[...], LAST) + dot32(xx, ux[...], LAST)
        dact = dot32(zo, do[...], LAST) + dot32(zx, dx[...], LAST)
        sigmoid = jax.nn.sigmoid(gate)
        silu = gate * sigmoid
        act = (silu * up).astype(jnp.bfloat16)
        dgate = (dact * up * sigmoid * (1.0 + gate * (1.0 - sigmoid))).astype(jnp.bfloat16)
        dup = (dact * silu).astype(jnp.bfloat16)

        @pl.when(i == 0)
        def _():
            for acc in accs:
                acc[...] = jnp.zeros_like(acc)

        accs[0][:, mine] += dot32(dgate, go[...]) + dot32(dup, uo[...])
        accs[0][:, rest] += dot32(dgate, gx[...]) + dot32(dup, ux[...])
        if with_parts:
            accs[1][:, mine] += dot32(act, do[...])
            accs[1][:, rest] += dot32(act, dx[...])
        for n, (left, mine_in, rest_in) in enumerate(
            ((dgate, xo, xx), (dup, xo, xx), (act, zo, zx))
        ):
            keeps[n][...] = dot32(left, mine_in, FIRST)
            sends[n][...] = dot32(left, rest_in, FIRST).astype(jnp.bfloat16)

        @pl.when(i == steps - 1)
        def _():
            for total, acc in zip(totals, accs):
                total[...] = acc[...].astype(jnp.bfloat16)

    whole = pl.BlockSpec((count, width), lambda i, h: (0, 0))
    piece = pl.BlockSpec((tile, features), lambda i, h: (i, 0))
    weights = [w for pair in zip(own, other) for w in pair]
    return pl.pallas_call(
        body,
        out_shape=[jax.ShapeDtypeStruct((hidden, features), jnp.float32)] * 3
        + [jax.ShapeDtypeStruct((hidden, features), jnp.bfloat16)] * 3
        + [jax.ShapeDtypeStruct((count, width), jnp.bfloat16)] * sums,
        grid_spec=pltpu.PrefetchScalarGridSpec(
            num_scalar_prefetch=1,
            grid=(steps,),
            in_specs=[whole, whole] + [piece] * 6,
            out_specs=[piece] * 6 + [whole] * sums,
            scratch_shapes=[pltpu.VMEM((count, width), jnp.float32)] * sums,
        ),
        compiler_params=pltpu.CompilerParams(vmem_limit_bytes=VMEM_BYTES),
        cost_estimate=pl.CostEstimate(
            flops=22 * count * width * hidden,
            bytes_accessed=15 * hidden * features * 2 + 8 * count * width,
            transcendentals=count * hidden,
        ),
    )(head, rows_in, grads_in, *weights)


def split(values, terms=2):
    parts = []
    for _ in range(terms):
        part = values.astype(jnp.bfloat16)
        parts.append(part)
        values = values - part.astype(jnp.float32)
    return parts


def exact_dot(pieces, values, dims):
    total = dot32(pieces[0], values, dims)
    for piece in pieces[1:]:
        total = total + dot32(piece, values, dims)
    return total


def unit_scale(values):
    return lax.rsqrt(jnp.mean(values * values, axis=-1, keepdims=True) + EPSILON)


def alone(body, out_shape, cost, *operands, scalars=0):
    specs = [pl.BlockSpec(memory_space=pltpu.SMEM)] * scalars + [VMEM] * (len(operands) - scalars)
    results = pl.pallas_call(
        body,
        out_shape=out_shape,
        in_specs=specs,
        out_specs=jax.tree.map(lambda _: VMEM, out_shape),
        compiler_params=pltpu.CompilerParams(vmem_limit_bytes=VMEM_BYTES),
        cost_estimate=lasting(cost),
    )(*operands)
    return list(results) if isinstance(out_shape, (list, tuple)) else results


def make(shape, kind=jnp.float32):
    return jax.ShapeDtypeStruct(tuple(shape), kind)


def route_tables(routes, gates):
    count, rows, _ = routes.shape
    slots = NE * CAP

    def body(routes_ref, gates_ref, picks_ref, weights_ref, slot_ref, other_ref):
        row = lax.broadcasted_iota(jnp.int32, (rows, rows), 0)
        col = lax.broadcasted_iota(jnp.int32, (rows, rows), 1)
        before = (col < row).astype(jnp.bfloat16)
        expert = lax.broadcasted_iota(jnp.int32, (rows, LANES), 1)
        slot = lax.broadcasted_iota(jnp.int32, (rows, slots), 1)
        source = lax.broadcasted_iota(jnp.int32, (LANES, slots), 0)
        target = lax.broadcasted_iota(jnp.int32, (LANES, slots), 1)
        spread = (
            (target >= source * CAP) & (target < source * CAP + CAP) & (source < NE)
        ).astype(jnp.bfloat16)
        ones = jnp.ones((rows, LANES), jnp.bfloat16)
        for n in range(count):
            gate = jnp.zeros((rows, LANES), jnp.float32)
            named = jnp.zeros((rows, LANES), jnp.float32)
            for k in range(2):
                hit = routes_ref[n, :, k : k + 1] == expert
                named = named + jnp.where(hit, 1.0, 0.0)
                gate = gate + jnp.where(hit, gates_ref[n, :, k : k + 1], 0.0)
            rank = dot32(before, named.astype(jnp.bfloat16)) + expert.astype(jnp.float32) * CAP
            rank = jnp.where(expert < NE, rank, 0.0)
            goal = exact_dot(split(rank, 2), spread, (((1,), (0,)), ((), ())))
            member = dot32(named.astype(jnp.bfloat16), spread)
            pick = jnp.where(goal == slot.astype(jnp.float32), member, 0.0)
            weight = pick * exact_dot(split(gate, 3), spread, (((1,), (0,)), ((), ())))
            picks_ref[n] = pick.astype(jnp.bfloat16)
            weights_ref[n] = weight
            slot_ref[n] = exact_dot(split(weight, 3), ones, FIRST)
            other_ref[n] = gate

    return alone(
        body,
        (
            make((count, rows, slots), jnp.bfloat16),
            make((count, rows, slots)),
            make((count, slots, LANES)),
            make((count, rows, LANES)),
        ),
        3,
        routes,
        gates,
    )


def gate_slots(slot_gates, picks, grads):
    picked = dot32(picks, grads[0], FIRST)
    for part in grads[1:]:
        picked = picked + dot32(picks, part, FIRST)
    lanes = [
        (picked[:, at : at + LANES] * slot_gates).astype(jnp.bfloat16)
        for at in range(0, picked.shape[1], LANES)
    ]
    return jnp.concatenate(lanes, axis=1)


def const_alphas(hn, smalls, base):
    logits = dot32(hn, smalls[base + 2 : base + 6].astype(jnp.bfloat16), LAST)
    alphas = []
    for c in range(2):
        first, second = logits[:, 2 * c : 2 * c + 1], logits[:, 2 * c + 1 : 2 * c + 2]
        top = jnp.maximum(first, second)
        first, second = jnp.exp(first - top), jnp.exp(second - top)
        total = first + second
        alphas.append((first / total, second / total))
    return alphas


def middle(attn, x, pack, smalls, base, picks, slot_gates, grads):
    planes, rows, part = attn.shape
    width = x.shape[1]
    slots = picks.shape[1]

    def body(attn_ref, x_ref, w_ref, small_ref, picks_ref, gates_ref, *refs):
        total = x_ref[...].astype(jnp.float32)
        for z in range(planes):
            total = total + dot32(attn_ref[z], w_ref[z * part : (z + 1) * part, :width])
        mid_ref, sent_ref = refs[-2:] if grads is None else refs[-3:-1]
        mid_ref[...] = total
        hn = (total * unit_scale(total) * small_ref[base + 1 : base + 2]).astype(jnp.bfloat16)
        sent_ref[...] = dot32(picks_ref[...], hn, FIRST).astype(jnp.bfloat16)
        if grads is not None:
            refs[-1][...] = gate_slots(gates_ref[...], picks_ref[...], [refs[0][...]])

    outs = [make((rows, width)), make((slots, width), jnp.bfloat16)]
    more = []
    if grads is not None:
        outs.append(make((slots, width), jnp.bfloat16))
        more.append(grads)
    return alone(body, outs, 3, attn, x, pack, smalls, picks, slot_gates, *more)


def combine(back, weights, mid, other, smalls, base, following):
    rows, width = mid.shape

    def body(back_ref, weights_ref, mid_ref, other_ref, small_ref, x_ref, *refs):
        mid_value, gate = mid_ref[...], other_ref[...]
        hn = (mid_value * unit_scale(mid_value) * small_ref[base + 1 : base + 2]).astype(
            jnp.bfloat16
        )
        alphas = const_alphas(hn, small_ref, base)
        wide = hn.astype(jnp.float32)
        total = mid_value + exact_dot(
            split(weights_ref[...]), back_ref[...], (((1,), (0,)), ((), ()))
        )
        factor = gate[:, NE + 1 : NE + 2]
        for c in range(2):
            weight = gate[:, NE + 2 + c : NE + 3 + c]
            factor = factor + weight * alphas[c][0]
            total = total + (weight * alphas[c][1]) * small_ref[base + 6 + c : base + 7 + c]
        total = total + factor * wide
        x_ref[...] = total
        if following:
            refs[0][...] = (total * unit_scale(total) * small_ref[base + 8 : base + 9]).astype(
                jnp.bfloat16
            )

    outs = [make((rows, width))]
    if following:
        outs.append(make((rows, width), jnp.bfloat16))
    return alone(body, outs, 3, back, weights, mid, other, smalls)


def experts_back(dback, picks, upstream, mid, other, smalls, base):
    rows, width = mid.shape

    def body(dback_ref, picks_ref, up_ref, mid_ref, other_ref, small_ref, dmid_ref, dy_ref, row_ref):
        mid_value, gate = mid_ref[...], other_ref[...]
        g = up_ref[...].astype(jnp.float32)
        scale = unit_scale(mid_value)
        unit = mid_value * scale
        gain = small_ref[base + 1 : base + 2]
        hn = (unit * gain).astype(jnp.bfloat16)
        alphas = const_alphas(hn, small_ref, base)
        wide = hn.astype(jnp.float32)
        dhn = dot32(picks_ref[...], dback_ref[...])
        g_hn = jnp.sum(g * wide, axis=1, keepdims=True)
        factor = gate[:, NE + 1 : NE + 2]
        row_ref[0:1] = jnp.zeros((1, width), jnp.float32)
        for c in range(2):
            weight = gate[:, NE + 2 + c : NE + 3 + c]
            vector = small_ref[base + 6 + c : base + 7 + c]
            first, second = alphas[c]
            factor = factor + weight * first
            row_ref[6 + c : 7 + c] = jnp.sum((weight * second) * g, axis=0, keepdims=True)
            da_first = weight * g_hn
            da_second = weight * jnp.sum(g * vector, axis=1, keepdims=True)
            mean = first * da_first + second * da_second
            for j, dlog in enumerate((first * (da_first - mean), second * (da_second - mean))):
                at = 2 + 2 * c + j
                dhn = dhn + dlog * small_ref[base + at : base + at + 1]
                row_ref[at : at + 1] = jnp.sum(dlog * wide, axis=0, keepdims=True)
        dhn = dhn + factor * g
        row_ref[1:2] = jnp.sum(dhn * unit, axis=0, keepdims=True)
        through = dhn * gain
        inner = jnp.mean(through * unit, axis=1, keepdims=True)
        dmid = g + scale * (through - unit * inner)
        dmid_ref[...] = dmid
        dy_ref[...] = dmid.astype(jnp.bfloat16)

    return alone(
        body,
        [make((rows, width)), make((rows, width), jnp.bfloat16), make((8, width))],
        4,
        dback,
        picks,
        upstream,
        mid,
        other,
        smalls,
    )


def finish(dxn, x, dmid, rows_in, smalls, base, picks, slot_gates):
    planes, rows, width = dxn.shape

    def body(dxn_ref, x_ref, dmid_ref, row_ref, small_ref, *refs):
        grad = dxn_ref[0].astype(jnp.float32)
        for z in range(1, planes):
            grad = grad + dxn_ref[z].astype(jnp.float32)
        value = x_ref[...].astype(jnp.float32)
        scale = unit_scale(value)
        unit = value * scale
        out_rows = refs[-1 if picks is None else -2]
        out_rows[...] = row_ref[...]
        out_rows[0:1] = jnp.sum(grad * unit, axis=0, keepdims=True)
        through = grad * small_ref[base : base + 1]
        inner = jnp.mean(through * unit, axis=1, keepdims=True)
        g = dmid_ref[...] + scale * (through - unit * inner)
        refs[-2 if picks is None else -3][...] = g
        if picks is not None:
            refs[-1][...] = gate_slots(refs[1][...], refs[0][...], split(g))

    outs = [make((rows, width)), make((8, width))]
    more = []
    if picks is not None:
        outs.append(make((picks.shape[1], width), jnp.bfloat16))
        more = [picks, slot_gates]
    return alone(body, outs, 3, dxn, x, dmid, rows_in, smalls, *more)


def pack_grads(column, dq, dkv, attn, dy, small):
    width = column.shape[1]
    kv_cols, own_out = dkv.shape[1], attn.shape[1]
    tail = own_out + LANES // 2
    rows, cols = own_out // 2, width // 2

    def body(column_ref, dq_ref, dkv_ref, attn_ref, dy_ref, small_ref, one, two):
        one[:, :kv_cols] = dot32(column_ref[...], dkv_ref[...], FIRST).astype(jnp.bfloat16)
        source = lax.broadcasted_iota(jnp.int32, (kv_cols, tail), 0)
        target = lax.broadcasted_iota(jnp.int32, (kv_cols, tail), 1)
        dim = LANES // 2
        goal = lax.div(target, dim) * LANES + lax.rem(target, dim)
        compact = ((goal == source) & (target < own_out)).astype(jnp.bfloat16)
        narrow = dot32(dq_ref[...], compact).astype(jnp.bfloat16)
        placed = jnp.concatenate(
            [
                jnp.zeros((own_out, width), jnp.float32),
                small_ref[...],
                jnp.zeros((tail - own_out - 8, width), jnp.float32),
            ],
            axis=0,
        ).T
        one[:, kv_cols:] = (dot32(column_ref[...], narrow, FIRST) + placed).astype(jnp.bfloat16)
        out = dot32(attn_ref[...], dy_ref[...], FIRST).astype(jnp.bfloat16)
        for a in range(2):
            for b in range(2):
                two[a, b] = out[a * rows : (a + 1) * rows, b * cols : (b + 1) * cols]

    return alone(
        body,
        [make((width, kv_cols + tail), jnp.bfloat16), make((2, 2, rows, cols), jnp.bfloat16)],
        4,
        column,
        dq,
        dkv,
        attn,
        dy,
        small,
    )


def per_device(
    tokens,
    segments,
    routes,
    gates,
    w_qkv,
    w_out,
    gain_attn,
    gain_moe,
    const_gate,
    const_vec,
    w_gate,
    w_up,
    w_down,
    cotangent,
):
    blocks = lax.axis_size("blk")
    head_index, blk_index = lax.axis_index("head"), lax.axis_index("blk")
    span = blocks // COLUMNS
    plane, rest = lax.div(blk_index, span), lax.rem(blk_index, span)
    shards = 2 * blocks
    token_rows, width = tokens.shape
    shard_rows = width // shards
    head_dim = width // HEADS
    heads = HEADS // COLUMNS
    scale = head_dim ** (-0.5)
    half_length = blocks * token_rows
    positions = 2 * half_length
    copies = blocks // NE
    own_out = heads * head_dim
    wide = heads * LANES

    swap = [(0, 1), (1, 0)]
    head_scalar = head_index.reshape((1,)).astype(jnp.int32)

    seg_own = lax.dynamic_index_in_dim(segments, head_index, 0, keepdims=True)
    seg_rows = jnp.concatenate([lax.rem(seg_own, 128), lax.div(seg_own, 128)], axis=0)
    seg_rows = jnp.pad(seg_rows, ((0, 14), (0, 0))).astype(jnp.bfloat16)
    seg_rows = jnp.broadcast_to(seg_rows[None], (COLUMNS,) + seg_rows.shape)
    smalls = [
        jnp.concatenate(
            [gain_attn[n][:, None], gain_moe[n][:, None], const_gate[n], const_vec[n]], axis=1
        )
        for n in range(LAYERS)
    ]
    smalls.append(jnp.zeros((shard_rows, LANES // 2 - 8 * LAYERS), jnp.bfloat16))
    smalls = jnp.concatenate(smalls, axis=1)
    packs = []
    for layer in range(LAYERS):
        parts = w_qkv[layer].reshape((shard_rows, 3, COLUMNS, heads, head_dim))
        kv_part = jnp.concatenate([parts[:, 1], parts[:, 2]], axis=3)
        kv_part = kv_part.transpose((1, 0, 2, 3)).reshape((COLUMNS, shard_rows, wide))
        query_part = parts[:, 0].transpose((1, 0, 2, 3)).reshape((COLUMNS, shard_rows, own_out))
        packs.append(
            jnp.concatenate(
                [
                    jnp.broadcast_to(w_out[layer][None], (COLUMNS, shard_rows, width)),
                    kv_part,
                    query_part,
                    jnp.broadcast_to(smalls[None], (COLUMNS,) + smalls.shape),
                ],
                axis=2,
            )
        )
    (seg_all, *packs), column_tokens = start_gather([seg_rows] + packs, tokens, blocks, 1)
    packs = [pack.reshape((width, -1)) for pack in packs]
    picks, pick_gates, slot_gates, other_gates = route_tables(routes, gates)

    def send_expert(weight, layer, after):
        own, _ = lax.optimization_barrier((weight[layer], after))
        return own, lax.ppermute(own, "head", swap)

    experts = [None] * LAYERS
    seg_all = seg_all[..., :2, :].astype(jnp.int32)
    seg_all = seg_all[..., 0, :] + 128 * seg_all[..., 1, :]
    seg_query = lax.dynamic_index_in_dim(seg_all, head_index, 0, keepdims=False)
    seg_query = lax.dynamic_index_in_dim(seg_query, rest, 1, keepdims=False)
    starts = jnp.sum(
        (seg_all.reshape((1, 1, -1)) < seg_query[:, :, None]).astype(jnp.int32), axis=2
    )
    bases = (
        head_index * half_length
        + (jnp.arange(COLUMNS, dtype=jnp.int32) * span + rest) * token_rows
    )
    bounds = block_bounds(starts, bases, token_rows)
    starts = starts[:, None, :]

    values = tokens
    column, small_rows = column_tokens, None
    kept = []
    for layer in range(LAYERS):
        base = 8 * layer
        last = layer + 1 == LAYERS
        column, queries, query_w, out_rows, kv_all, small_rows = project_gather(
            column, packs[layer], small_rows, heads, scale, blocks, 4 if layer == 0 else 2
        )
        kv_all = kv_all.reshape((positions, wide))
        if layer == 0:
            experts[layer] = [send_expert(w, layer, kv_all) for w in (w_gate, w_up, w_down)]
        else:
            experts[layer] += [send_expert(w, layer, kv_all) for w in (w_up, w_down)]
        attended, attn_col = attend(bounds, queries, kv_all, starts)
        (attn,) = column_exchange([attn_col], [False], blocks, 5, 9)
        mid, *sent = middle(
            attn,
            values,
            packs[layer],
            small_rows,
            base,
            picks[layer],
            slot_gates[layer],
            cotangent if last else None,
        )
        sent = [rows.reshape((NE, CAP, width)) for rows in sent]
        arrived = expert_dispatch(sent, blocks, 7 if last else 6, 24 if last else 15)
        flat_in, *dz_in = [rows.reshape((-1, width)) for rows in arrived]
        if last:
            *wgrads, dparts, parts = expert_backward(
                head_scalar, flat_in, dz_in[0], *zip(*experts[layer]), True
            )
            back, dback = expert_return(
                [rows.reshape((copies, NE, CAP, width)) for rows in (parts, dparts)],
                blocks,
                9,
                24,
            )
        else:
            experts[layer + 1] = [send_expert(w_gate, layer + 1, flat_in)]
            parts = expert_forward(head_scalar, flat_in, *zip(*experts[layer]))
            (back,) = expert_return([parts.reshape((copies, NE, CAP, width))], blocks, 8)
        kept.append(
            (values, column, queries, kv_all, attended, attn_col, query_w, out_rows, mid, flat_in)
        )
        values, *normed = combine(
            back.reshape((NE * CAP, width)),
            pick_gates[layer],
            mid,
            other_gates[layer],
            small_rows,
            base,
            not last,
        )
        if not last:
            (column,) = normed
    output = values

    upstream = cotangent
    shared_grads = [None] * LAYERS
    expert_grads = [None] * LAYERS
    for layer in reversed(range(LAYERS)):
        base = 8 * layer
        values, column, queries, kv_all, attended, attn_col, query_w, out_rows, mid, flat_in = (
            kept[layer]
        )
        if layer + 1 < LAYERS:
            (dz_in,) = expert_dispatch([dz.reshape((NE, CAP, width))], blocks, 6)
            *wgrads, dparts = expert_backward(
                head_scalar,
                flat_in,
                dz_in.reshape((-1, width)),
                *zip(*experts[layer]),
                False,
            )
            (dback,) = expert_return([dparts.reshape((copies, NE, CAP, width))], blocks, 8)
        got = [lax.ppermute(away, "head", swap) for away in wgrads[3:]]
        dback, got[0] = lax.optimization_barrier((dback, got[0]))
        dmid, dy, rows = experts_back(
            dback.reshape((NE * CAP, width)),
            picks[layer],
            upstream,
            mid,
            other_gates[layer],
            small_rows,
            base,
        )
        dy = column_gather(dy, blocks, 3)
        dy, got[1] = lax.optimization_barrier((dy, got[1]))
        dq, dkv_all = attend_back(
            bounds, queries, dy, out_rows, attended, kv_all, starts, scale
        )
        dkv_all, got[2] = lax.optimization_barrier((dkv_all, got[2]))
        dkv, dxn = reduce_project(
            dkv_all.reshape((2, COLUMNS, span, token_rows, wide)),
            dq,
            query_w,
            packs[layer],
            blocks,
            10,
        )
        before = layer > 0
        upstream, rows, *dz = finish(
            dxn,
            values,
            dmid,
            rows,
            small_rows,
            base,
            picks[layer - 1] if before else None,
            slot_gates[layer - 1] if before else None,
        )
        if before:
            (dz,) = dz
        expert_grads[layer] = [
            own + other.astype(jnp.float32) for own, other in zip(wgrads[:3], got)
        ]
        qkv_part, out_part = pack_grads(
            column.reshape((-1, width)),
            dq.reshape((-1, wide)),
            dkv.reshape((-1, wide)),
            attn_col.reshape((-1, own_out)),
            dy.reshape((-1, width)),
            rows,
        )
        shared_grads[layer] = [
            qkv_part.reshape((2, COLUMNS, span, shard_rows, -1)),
            out_part.reshape((2, 2, span, shard_rows, width // 2)),
        ]

    packed = [part for layer in range(LAYERS) for part in shared_grads[layer]]
    reduced = plane_reduce(packed, blocks, 12, 20)
    from_planes = column_exchange(reduced[::2], [False] * LAYERS, blocks, 13, 10)
    from_planes = jnp.stack(from_planes, axis=1).astype(jnp.float32)
    kv_out = from_planes[..., :wide].reshape((COLUMNS, LAYERS, shard_rows, heads, 2, head_dim))
    query_out = from_planes[..., wide : wide + own_out].reshape(
        (COLUMNS, LAYERS, shard_rows, heads, 1, head_dim)
    )
    qkv_out = jnp.concatenate([query_out, kv_out], axis=4)
    qkv_out = qkv_out.transpose((1, 2, 4, 0, 3, 5)).reshape((LAYERS, shard_rows, 3 * width))
    small_out = jnp.sum(from_planes[..., wide + own_out : wide + own_out + 8], axis=0)
    out_grads = jnp.stack(reduced[1::2]).transpose((0, 2, 1, 3))
    out_grads = out_grads.reshape((LAYERS, shard_rows, width))
    owners = [
        (y * blocks + z * span + r, (z * 2 + y) * span + r)
        for y in range(2)
        for z in range(COLUMNS)
        for r in range(span)
    ]
    out_grads = lax.ppermute(out_grads, ("head", "blk"), owners).astype(jnp.float32)
    stacked = [jnp.stack(group) for group in zip(*expert_grads)]
    return (
        output,
        upstream,
        qkv_out,
        out_grads,
        small_out[..., 0],
        small_out[..., 1],
        small_out[..., 2:6],
        small_out[..., 6:8],
        stacked[0],
        stacked[1],
        stacked[2],
    )


def solution(mesh):
    tokens = P(("head", "blk"), None)
    by_layer = P(None, ("head", "blk"), None)
    gains = P(None, ("head", "blk"))
    experts = P(None, "blk", "head")
    return jax.shard_map(
        per_device,
        mesh=mesh,
        in_specs=(
            tokens,
            P(None, "blk"),
            by_layer,
            by_layer,
            by_layer,
            by_layer,
            gains,
            gains,
            by_layer,
            by_layer,
            experts,
            experts,
            experts,
            tokens,
        ),
        out_specs=(
            tokens,
            tokens,
            by_layer,
            by_layer,
            gains,
            gains,
            by_layer,
            by_layer,
            experts,
            experts,
            experts,
        ),
        check_vma=False,
    )
```

```python
import jax
import jax.numpy as jnp
from jax import lax
from jax.experimental import pallas as pl
from jax.experimental.pallas import tpu as pltpu
from jax.sharding import PartitionSpec as P

HEADS = 12
NE = 8
LAYERS = 2
CAP = 40
COLUMNS = 4
MESH = pl.DeviceIdType.MESH
ANY = pl.BlockSpec(memory_space=pl.ANY)
VMEM = pl.BlockSpec(memory_space=pltpu.VMEM)
DMA = pltpu.SemaphoreType.DMA
VMEM_BYTES = 60 * 1024 * 1024


def greet(peers, line=()):
    barrier = pltpu.get_barrier_semaphore()
    count = len(peers)
    for peer in peers:
        pl.semaphore_signal(barrier, inc=1, device_id=peer, device_id_type=MESH)
    for there, peer in line:

        @pl.when(there)
        def _():
            pl.semaphore_signal(barrier, inc=1, device_id=peer, device_id_type=MESH)

        count = count + there.astype(jnp.int32)
    pl.semaphore_wait(barrier, count)


def remote(src, dst, send_sem, recv_sem, peer):
    return pltpu.make_async_remote_copy(
        src_ref=src,
        dst_ref=dst,
        send_sem=send_sem,
        recv_sem=recv_sem,
        device_id=peer,
        device_id_type=MESH,
    )


def comm_params(collective_id):
    return pltpu.CompilerParams(
        collective_id=collective_id, has_side_effects=True, vmem_limit_bytes=VMEM_BYTES
    )


def lasting(microseconds):
    return pl.CostEstimate(
        flops=0, bytes_accessed=int(microseconds * 3_500_000), transcendentals=0
    )


def column_place(blocks):
    span = blocks // COLUMNS
    head, blk = lax.axis_index("head"), lax.axis_index("blk")
    plane, rest = lax.div(blk, span), lax.rem(blk, span)
    planes = [lax.rem(plane + d, COLUMNS) for d in range(COLUMNS)]
    return plane, planes, [(head, p * span + rest) for p in planes]


class Chain:
    def __init__(self, source, dst, send_sems, recv_sems, blocks):
        span = blocks // COLUMNS
        head, blk = lax.axis_index("head"), lax.axis_index("blk")
        plane, rest = lax.div(blk, span), lax.rem(blk, span)
        self.source, self.dst, self.plane = source, dst, plane
        self.send_sems, self.recv_sems = send_sems, recv_sems
        after = jnp.minimum(plane + 1, COLUMNS - 1)
        before = jnp.maximum(plane - 1, 0)
        self.line = [
            (plane < COLUMNS - 1, (head, after * span + rest)),
            (plane > 0, (head, before * span + rest)),
        ]
        lower = plane < COLUMNS // 2
        self.slabs = [
            plane,
            plane + 1 - 2 * lax.rem(plane, 2),
            jnp.where(lower, 2, 1),
            jnp.where(lower, 3, 0),
        ]

    def copy(self, k, way):
        slab = self.slabs[k]
        place = self.dst.at[slab]
        return remote(
            self.source if k == 0 else place,
            place,
            self.send_sems.at[k, way],
            self.recv_sems.at[slab],
            self.line[way][1],
        )

    def onward(self, k):
        if k == 0:
            return [self.line[0][0], self.line[1][0]]
        from_before = self.slabs[k] < self.plane
        return [
            from_before & self.line[0][0],
            jnp.logical_not(from_before) & self.line[1][0],
        ]

    def pass_on(self, k):
        for way, there in enumerate(self.onward(k)):

            @pl.when(there)
            def _():
                self.copy(k, way).start()

    def arrive(self, k):
        self.copy(k, 0).wait_recv()
        self.pass_on(k)

    def finish(self):
        for k in range(COLUMNS):
            for way, there in enumerate(self.onward(k)):

                @pl.when(there)
                def _():
                    self.copy(k, way).wait_send()


def column_start(src, gather, dst, own_sem, send_sems, recv_sems, where):
    plane, planes, peers = where
    own = pltpu.make_async_copy(src if gather else src.at[plane], dst.at[plane], own_sem)
    own.start()
    copies = [own]
    for d in (2, 1, 3):
        copy = remote(
            src if gather else src.at[planes[d]],
            dst.at[plane],
            send_sems.at[d],
            recv_sems.at[d],
            peers[d],
        )
        copy.start()
        copies.append(copy)
    return copies


def column_exchange(arrays, gathers, blocks, collective_id, cost=16):
    count = len(arrays)
    slabs = [
        tuple(values.shape if gather else values.shape[1:])
        for values, gather in zip(arrays, gathers)
    ]

    def body(*refs):
        srcs, dsts = refs[:count], refs[count : 2 * count]
        own_sems, send_sems, recv_sems = refs[2 * count :]
        where = column_place(blocks)
        greet(where[2][1:])
        copies = []
        for n in range(count):
            copies += column_start(
                srcs[n],
                gathers[n],
                dsts[n],
                own_sems.at[n],
                send_sems.at[n],
                recv_sems.at[n],
                where,
            )
        for copy in copies:
            copy.wait()

    return pl.pallas_call(
        body,
        out_shape=[
            jax.ShapeDtypeStruct((COLUMNS,) + slab, values.dtype)
            for values, slab in zip(arrays, slabs)
        ],
        in_specs=[ANY] * count,
        out_specs=[ANY] * count,
        scratch_shapes=[DMA((count,)), DMA((count, COLUMNS)), DMA((count, COLUMNS))],
        compiler_params=comm_params(collective_id),
        cost_estimate=lasting(cost),
    )(*arrays)


def column_gather(values, blocks, collective_id, cost=14):
    def body(src, dst, own_sem, send_sems, recv_sems):
        chain = Chain(src, dst, send_sems, recv_sems, blocks)
        greet([], chain.line)
        chain.pass_on(0)
        own = pltpu.make_async_copy(src, dst.at[chain.plane], own_sem)
        own.start()
        for k in range(1, COLUMNS):
            chain.arrive(k)
        own.wait()
        chain.finish()

    return pl.pallas_call(
        body,
        out_shape=jax.ShapeDtypeStruct((COLUMNS,) + tuple(values.shape), values.dtype),
        in_specs=[ANY],
        out_specs=ANY,
        scratch_shapes=[DMA, DMA((COLUMNS, 2)), DMA((COLUMNS,))],
        compiler_params=comm_params(collective_id),
        cost_estimate=lasting(cost),
    )(values)


def plane_place(blocks):
    span = blocks // COLUMNS
    width = span // 2
    head, blk = lax.axis_index("head"), lax.axis_index("blk")
    plane, rest = lax.div(blk, span), lax.rem(blk, span)
    x, core = lax.div(rest, 2), lax.rem(rest, 2)
    first = plane * span
    right = [lax.rem(x + d, width) for d in range(width)]
    left = [lax.rem(x - d + width, width) for d in range(width)]
    x_peers = [(head, first + right[d] * 2 + core) for d in range(width)]
    y_peer = (1 - head, blk)
    core_peer = (head, first + x * 2 + 1 - core)
    return head, rest, core, left, x_peers, y_peer, core_peer


class PlaneRun:
    def __init__(self, srcs, dsts, own_sems, send_sems, recv_sems, pass_sems, land_sems, where):
        self.srcs, self.dsts = srcs, dsts
        self.own_sems, self.send_sems, self.recv_sems = own_sems, send_sems, recv_sems
        self.pass_sems, self.land_sems = pass_sems, land_sems
        self.head, self.rest, self.core, self.left, self.x_peers, self.y_peer, self.core_peer = (
            where
        )
        self.width = len(self.x_peers)
        self.sends, self.passes, self.owns = [], [], []

    def place(self, n, h, dy, d):
        half = self.srcs[n].shape[0] // 2
        row = self.head if dy == 0 else 1 - self.head
        return self.dsts[n].at[row, pl.ds(h * half, half), self.left[d] * 2 + self.core]

    def held(self, n, h, dy, d):
        half = self.srcs[n].shape[0] // 2
        if dy == 0 and d == 0:
            return self.srcs[n].at[pl.ds(h * half, half)]
        return self.place(n, h, dy, d)

    def send(self, n, h, dy, d, peer, to_dy, to_d):
        copy = remote(
            self.held(n, h, dy, d),
            self.place(n, h, dy, d),
            self.send_sems.at[len(self.sends)],
            self.recv_sems.at[n, h, to_dy, to_d],
            peer,
        )
        copy.start()
        self.sends.append(copy)

    def hand_over(self, n, h, dy, d):
        copy = remote(
            self.held(n, h, dy, d),
            self.place(n, h, dy, d),
            self.pass_sems.at[n, h, dy, d],
            self.land_sems.at[n, h, dy, d],
            self.core_peer,
        )
        copy.start()
        self.passes.append(copy)

    def arrived(self, n, h, dy, d):
        at = self.place(n, h, dy, d)
        remote(
            at, at, self.send_sems.at[0], self.recv_sems.at[n, h, dy, d], self.y_peer
        ).wait_recv()

    def first(self, n):
        own = pltpu.make_async_copy(
            self.srcs[n], self.dsts[n].at[self.head, :, self.rest], self.own_sems.at[n]
        )
        own.start()
        self.owns.append(own)
        for d in range(1, self.width):
            self.send(n, 0, 0, 0, self.x_peers[d], 0, d)
        self.send(n, 1, 0, 0, self.y_peer, 1, 0)
        self.send(n, 0, 0, 0, self.y_peer, 1, 0)
        for d in range(1, self.width):
            self.send(n, 1, 0, 0, self.x_peers[d], 0, d)
        self.hand_over(n, 0, 0, 0)
        self.hand_over(n, 1, 0, 0)

    def second(self, n):
        for d in range(1, self.width):
            self.arrived(n, 0, 0, d)
            self.send(n, 0, 0, d, self.y_peer, 1, d)
            self.hand_over(n, 0, 0, d)
        self.arrived(n, 1, 1, 0)
        for d in range(1, self.width):
            self.send(n, 1, 1, 0, self.x_peers[d], 1, d)
        self.hand_over(n, 1, 1, 0)

    def third(self, n):
        self.arrived(n, 0, 1, 0)
        self.hand_over(n, 0, 1, 0)
        for d in range(1, self.width):
            self.arrived(n, 1, 0, d)
            self.hand_over(n, 1, 0, d)
        for d in range(1, self.width):
            self.arrived(n, 0, 1, d)
            self.hand_over(n, 0, 1, d)
            self.arrived(n, 1, 1, d)
            self.hand_over(n, 1, 1, d)

    def last(self):
        for own in self.owns:
            own.wait()
        for copy in self.passes:
            copy.wait()
        for copy in self.sends:
            copy.wait_send()


def plane_scratch(count, blocks):
    width = blocks // COLUMNS // 2
    links = 4 * (width - 1) + 2
    return [DMA((count,)), DMA((count * links,))] + [DMA((count, 2, 2, width))] * 3


def plane_shapes(arrays, blocks):
    return [
        jax.ShapeDtypeStruct(
            (2, values.shape[0], blocks // COLUMNS) + tuple(values.shape[1:]), values.dtype
        )
        for values in arrays
    ]


def start_gather(packs, tokens, blocks, collective_id, cost=28):
    count = len(packs)

    def body(*refs):
        srcs, refs = refs[: count + 1], refs[count + 1 :]
        wholes, refs = refs[:count], refs[count:]
        columns, refs = refs[: count + 1], refs[count + 1 :]
        own_sems, send_sems, recv_sems, *plane_sems = refs
        column, plane = column_place(blocks), plane_place(blocks)
        greet(column[2][1:] + plane[4][1:] + [plane[5], plane[6]])
        run = PlaneRun(columns[:count], wholes, *plane_sems, plane)

        def begin(n):
            return column_start(
                srcs[n],
                n == count,
                columns[n],
                own_sems.at[n],
                send_sems.at[n],
                recv_sems.at[n],
                column,
            )

        waits = [begin(0), begin(1)]
        for n in range(count):
            for copy in waits[n]:
                copy.wait()
            if n + 2 <= count:
                waits.append(begin(n + 2))
            run.first(n)
        for n in range(count):
            run.second(n)
        for n in range(count):
            run.third(n)
        run.last()
        for copy in waits[count]:
            copy.wait()

    results = pl.pallas_call(
        body,
        out_shape=plane_shapes(packs, blocks)
        + [jax.ShapeDtypeStruct(pack.shape, pack.dtype) for pack in packs]
        + [jax.ShapeDtypeStruct((COLUMNS,) + tokens.shape, tokens.dtype)],
        in_specs=[ANY] * (count + 1),
        out_specs=[ANY] * (2 * count + 1),
        scratch_shapes=[
            DMA((count + 1,)),
            DMA((count + 1, COLUMNS)),
            DMA((count + 1, COLUMNS)),
        ]
        + plane_scratch(count, blocks),
        compiler_params=comm_params(collective_id),
        cost_estimate=lasting(cost),
    )(*packs, tokens)
    return results[:count], results[-1]


def project_gather(source, pack, smalls, heads, scale, blocks, collective_id, cost=22):
    span = blocks // COLUMNS
    width = span // 2
    chained = smalls is not None
    rows, features = source.shape[-2:]
    wide = heads * LANES
    kv_at, tail_at = features, features + wide
    tail_cols = pack.shape[1] - tail_at
    own_out = tail_cols - LANES // 2
    dim = LANES // 2
    half = rows // 2
    small_rows = 8 * LAYERS
    links = 4 * (width - 1) + 2

    def body(*refs):
        if chained:
            source_ref, pack_ref, small_ref = refs[:3]
            refs = refs[3:]
            small_out = None
        else:
            source_ref, pack_ref = refs[:2]
            small_out, refs = refs[2], refs[3:]
        column_ref, query_ref, query_w_ref, out_w_ref, kv_ref = refs[:5]
        kv_own, own_sems, send_sems, recv_sems, pass_sems, land_sems, z_send, z_recv = refs[5:]
        head, rest, core, left, x_peers, y_peer, core_peer = plane_place(blocks)
        plane = lax.div(lax.axis_index("blk"), span)
        sends, passes, owns = [], [], []
        near = x_peers[1:] + [y_peer, core_peer]
        if chained:
            chain = Chain(source_ref, column_ref, z_send, z_recv, blocks)
            slabs = chain.slabs
            greet(near, chain.line)
            chain.pass_on(0)
        else:
            slabs = list(range(COLUMNS))
            greet(near)

        tail = pack_ref[:, tail_at:]
        low = lax.broadcasted_iota(jnp.int32, (tail_cols, wide), 0)
        target = lax.broadcasted_iota(jnp.int32, (tail_cols, wide), 1)
        goal = lax.div(low, dim) * LANES + lax.rem(low, dim)
        to_low = ((goal == target) & (low < own_out)).astype(jnp.bfloat16)
        query_w = dot32(tail, to_low).astype(jnp.bfloat16)
        query_w_ref[...] = query_w
        out_rows = pack_ref[pl.ds(pl.multiple_of(plane * own_out, 64), own_out), :features]
        pieces = []
        for h in range(heads):
            pieces += [jnp.zeros((dim, features), jnp.bfloat16), out_rows[h * dim : (h + 1) * dim]]
        out_w_ref[...] = jnp.concatenate(pieces, axis=0)
        if not chained:
            small = tail[:, tail_cols - LANES :].astype(jnp.float32).T
            at = own_out - (tail_cols - LANES)
            small = small[at : at + small_rows]
            small_out[...] = small

        def place(k, h, dy, d):
            row = head if dy == 0 else 1 - head
            return kv_ref.at[row, slabs[k], left[d] * 2 + core, pl.ds(h * half, half)]

        def held(k, h, dy, d):
            if dy == 0 and d == 0:
                return kv_own.at[k, pl.ds(h * half, half)]
            return place(k, h, dy, d)

        def send(k, h, dy, d, peer, to_dy, to_d):
            copy = remote(
                held(k, h, dy, d),
                place(k, h, dy, d),
                send_sems.at[len(sends)],
                recv_sems.at[k, h, to_dy, to_d],
                peer,
            )
            copy.start()
            sends.append(copy)

        def hand_over(k, h, dy, d):
            copy = remote(
                held(k, h, dy, d),
                place(k, h, dy, d),
                pass_sems.at[k, h, dy, d],
                land_sems.at[k, h, dy, d],
                core_peer,
            )
            copy.start()
            passes.append(copy)

        def arrived(k, h, dy, d):
            at = place(k, h, dy, d)
            remote(at, at, send_sems.at[0], recv_sems.at[k, h, dy, d], y_peer).wait_recv()

        def first(k):
            slab = slabs[k]
            if not chained:
                x = source_ref[slab].astype(jnp.float32)
                xn = (x * unit_scale(x) * small[0:1]).astype(jnp.bfloat16)
                column_ref[slab] = xn
            elif k == 0:
                xn = source_ref[...]
                column_ref[slab] = xn
            else:
                chain.arrive(k)
                xn = column_ref[slab]
            kv = dot32(xn, pack_ref[:, kv_at:tail_at])
            kv_own[k] = kv.astype(jnp.bfloat16)
            own = pltpu.make_async_copy(
                kv_own.at[k], kv_ref.at[head, slab, rest], own_sems.at[k]
            )
            own.start()
            owns.append(own)
            for d in range(1, width):
                send(k, 0, 0, 0, x_peers[d], 0, d)
            send(k, 1, 0, 0, y_peer, 1, 0)
            send(k, 0, 0, 0, y_peer, 1, 0)
            for d in range(1, width):
                send(k, 1, 0, 0, x_peers[d], 0, d)
            hand_over(k, 0, 0, 0)
            hand_over(k, 1, 0, 0)
            query = dot32(xn, query_w).astype(jnp.bfloat16).astype(jnp.float32) * scale
            query_ref[slab] = query.astype(jnp.bfloat16)

        def second(k):
            for d in range(1, width):
                arrived(k, 0, 0, d)
                send(k, 0, 0, d, y_peer, 1, d)
                hand_over(k, 0, 0, d)
            arrived(k, 1, 1, 0)
            for d in range(1, width):
                send(k, 1, 1, 0, x_peers[d], 1, d)
            hand_over(k, 1, 1, 0)

        def third(k):
            arrived(k, 0, 1, 0)
            hand_over(k, 0, 1, 0)
            for d in range(1, width):
                arrived(k, 1, 0, d)
                hand_over(k, 1, 0, d)
            for d in range(1, width):
                arrived(k, 0, 1, d)
                hand_over(k, 0, 1, d)
                arrived(k, 1, 1, d)
                hand_over(k, 1, 1, d)

        for t in range(COLUMNS + 2):
            if t < COLUMNS:
                first(t)
            if 0 <= t - 1 < COLUMNS:
                second(t - 1)
            if 0 <= t - 2 < COLUMNS:
                third(t - 2)
        for copy in owns + passes:
            copy.wait()
        for copy in sends:
            copy.wait_send()
        if chained:
            chain.finish()

    shapes = [
        jax.ShapeDtypeStruct((COLUMNS, rows, features), jnp.bfloat16),
        jax.ShapeDtypeStruct((COLUMNS, rows, wide), jnp.bfloat16),
        jax.ShapeDtypeStruct((features, wide), jnp.bfloat16),
        jax.ShapeDtypeStruct((wide, features), jnp.bfloat16),
        jax.ShapeDtypeStruct((2, COLUMNS, span, rows, wide), jnp.bfloat16),
    ]
    operands = [source, pack]
    if chained:
        operands.append(smalls)
    else:
        shapes = [jax.ShapeDtypeStruct((small_rows, features), jnp.float32)] + shapes
    results = pl.pallas_call(
        body,
        out_shape=shapes,
        in_specs=[VMEM] * len(operands),
        out_specs=[VMEM] * (len(shapes) - 1) + [ANY],
        scratch_shapes=[
            pltpu.VMEM((COLUMNS, rows, wide), jnp.bfloat16),
            DMA((COLUMNS,)),
            DMA((COLUMNS * links,)),
            DMA((COLUMNS, 2, 2, width)),
            DMA((COLUMNS, 2, 2, width)),
            DMA((COLUMNS, 2, 2, width)),
            DMA((COLUMNS, 2)),
            DMA((COLUMNS,)),
        ],
        compiler_params=comm_params(collective_id),
        cost_estimate=lasting(cost),
    )(*operands)
    return list(results) + [smalls] if chained else list(results[1:]) + [results[0]]


def plane_reduce(arrays, blocks, collective_id, cost=25):
    span = blocks // COLUMNS
    width = span // 2
    count = len(arrays)
    shapes = [(values.shape[1],) + tuple(values.shape[3:]) for values in arrays]

    def body(*refs):
        srcs, outs, refs = refs[:count], refs[count : 2 * count], refs[2 * count :]
        scratch = [refs[8 * n : 8 * n + 8] for n in range(count)]
        core_send, core_recv, link_send, link_recv = refs[8 * count :]
        head, blk = lax.axis_index("head"), lax.axis_index("blk")
        plane, rest = lax.div(blk, span), lax.rem(blk, span)
        x, core = lax.div(rest, 2), lax.rem(rest, 2)
        first = plane * span
        right = [lax.rem(x + d, width) for d in range(width)]
        x_peers = [(head, first + right[d] * 2 + core) for d in range(width)]
        y_peer = (1 - head, blk)
        core_peer = (head, first + x * 2 + 1 - core)
        greet(x_peers[1:] + [y_peer, core_peer])

        def wide(ref, *at):
            return ref[at].astype(jnp.float32)

        starts = {}
        for n in range(count):
            half = shapes[n][0] // 2
            for h in range(2):
                copy = remote(
                    srcs[n].at[:, pl.ds(h * half, half), :, 1 - core],
                    scratch[n][0].at[:, pl.ds(h * half, half)],
                    core_send.at[n, h],
                    core_recv.at[n, h],
                    core_peer,
                )
                copy.start()
                starts[n, h] = copy

        sends, yas, ybs, xbs = {}, {}, {}, {}
        for n in range(count):
            src, half, kind = srcs[n], shapes[n][0] // 2, arrays[n].dtype
            core_in, summed, xa_in, _, _, yb_in, _, _ = scratch[n]

            def core_sum(h):
                def step(i, _):
                    yy = lax.div(i, half * width)
                    zz = lax.div(lax.rem(i, half * width), width) + h * half
                    xx = lax.rem(i, width)
                    total = wide(src, yy, zz, xx, core) + wide(core_in, yy, zz, xx)
                    summed[yy, zz, xx] = total.astype(kind)
                    return 0

                lax.fori_loop(0, 2 * half * width, step, 0)

            starts[n, 0].wait_recv()
            core_sum(0)
            for d in range(1, width):
                copy = remote(
                    summed.at[:, pl.ds(0, half), right[d]],
                    xa_in.at[d],
                    link_send.at[n, 0, d],
                    link_recv.at[n, 0, d],
                    x_peers[d],
                )
                copy.start()
                sends[n, d] = copy
            starts[n, 1].wait_recv()
            core_sum(1)
            ybs[n] = remote(
                summed.at[1 - head, pl.ds(half, half)],
                yb_in,
                link_send.at[n, 1, 0],
                link_recv.at[n, 1, 0],
                y_peer,
            )
            ybs[n].start()
        for n in range(count):
            half, kind = shapes[n][0] // 2, arrays[n].dtype
            _, summed, xa_in, ya_out, ya_in, yb_in, xb_out, xb_in = scratch[n]
            for d in range(1, width):
                sends[n, d].wait_recv()

            def a_step(zz, _):
                total = wide(summed, 1 - head, zz, x)
                for d in range(1, width):
                    total = total + wide(xa_in, d, 1 - head, zz)
                ya_out[zz] = total.astype(kind)
                return 0

            lax.fori_loop(0, half, a_step, 0)
            yas[n] = remote(
                ya_out, ya_in, link_send.at[n, 0, 0], link_recv.at[n, 0, 0], y_peer
            )
            yas[n].start()
            ybs[n].wait_recv()
            for d in range(1, width):

                def b_step(zz, _):
                    total = wide(summed, head, half + zz, right[d]) + wide(yb_in, zz, right[d])
                    xb_out[d, zz] = total.astype(kind)
                    return 0

                lax.fori_loop(0, half, b_step, 0)
                xbs[n, d] = remote(
                    xb_out.at[d],
                    xb_in.at[d],
                    link_send.at[n, 1, d],
                    link_recv.at[n, 1, d],
                    x_peers[d],
                )
                xbs[n, d].start()
        for n in range(count):
            out, half, kind = outs[n], shapes[n][0] // 2, arrays[n].dtype
            _, summed, xa_in, _, ya_in, yb_in, _, xb_in = scratch[n]
            yas[n].wait_recv()

            def a_last(zz, _):
                total = wide(summed, head, zz, x) + wide(ya_in, zz)
                for d in range(1, width):
                    total = total + wide(xa_in, d, head, zz)
                out[zz] = total.astype(kind)
                return 0

            lax.fori_loop(0, half, a_last, 0)
            for d in range(1, width):
                xbs[n, d].wait_recv()

            def b_last(zz, _):
                total = wide(summed, head, half + zz, x) + wide(yb_in, zz, x)
                for d in range(1, width):
                    total = total + wide(xb_in, d, zz)
                out[half + zz] = total.astype(kind)
                return 0

            lax.fori_loop(0, half, b_last, 0)
        for group in (starts, sends, yas, ybs, xbs):
            for copy in group.values():
                copy.wait_send()

    scratch = []
    for (slabs, *tile), values in zip(shapes, arrays):
        tile, half, kind = tuple(tile), slabs // 2, values.dtype
        scratch += [
            pltpu.VMEM((2, slabs, width) + tile, kind),
            pltpu.VMEM((2, slabs, width) + tile, kind),
            pltpu.VMEM((width, 2, half) + tile, kind),
            pltpu.VMEM((half,) + tile, kind),
            pltpu.VMEM((half,) + tile, kind),
            pltpu.VMEM((half, width) + tile, kind),
            pltpu.VMEM((width, half) + tile, kind),
            pltpu.VMEM((width, half) + tile, kind),
        ]
    return pl.pallas_call(
        body,
        out_shape=[
            jax.ShapeDtypeStruct(shape, values.dtype) for shape, values in zip(shapes, arrays)
        ],
        in_specs=[VMEM] * count,
        out_specs=[VMEM] * count,
        scratch_shapes=scratch
        + [DMA((count, 2)), DMA((count, 2)), DMA((count, 2, width)), DMA((count, 2, width))],
        compiler_params=comm_params(collective_id),
        cost_estimate=lasting(cost),
    )(
        *[
            values.reshape((2, values.shape[1], width, 2) + tuple(values.shape[3:]))
            for values in arrays
        ]
    )


def reduce_project(dkv_all, dq, query_w, pack, blocks, collective_id, cost=26):
    span = blocks // COLUMNS
    width = span // 2
    rows, wide = dkv_all.shape[3:]
    half = rows // 2
    features = query_w.shape[0]
    kind = dkv_all.dtype

    def body(
        src,
        dq_ref,
        w_ref,
        pack_ref,
        dkv_ref,
        dxn_ref,
        core_in,
        summed,
        xa_in,
        ya_out,
        ya_in,
        yb_in,
        xb_out,
        xb_in,
        share,
        core_send,
        core_recv,
        link_send,
        link_recv,
        z_send,
        z_recv,
    ):
        head, _, core, _, x_peers, y_peer, core_peer = plane_place(blocks)
        plane, planes, z_peers = column_place(blocks)
        x = lax.div(lax.rem(lax.axis_index("blk"), span), 2)
        right = [lax.rem(x + d, width) for d in range(width)]
        greet(x_peers[1:] + [y_peer, core_peer] + z_peers[1:])
        order = (2, 1, 3, 0)
        copies = []

        def begin(copy):
            copy.start()
            copies.append(copy)
            return copy

        def wide_of(ref, *at):
            return ref[at].astype(jnp.float32)

        top, low = pl.ds(0, half), pl.ds(half, half)
        starts = [
            begin(
                remote(
                    src.at[:, planes[d], :, 1 - core],
                    core_in.at[k],
                    core_send.at[k],
                    core_recv.at[k],
                    core_peer,
                )
            )
            for k, d in enumerate(order)
        ]
        xas, yas, ybs, xbs, z_copies = {}, {}, {}, {}, []

        def first(k):
            starts[k].wait_recv()

            def step(i, _):
                yy, xx = lax.div(i, width), lax.rem(i, width)
                total = wide_of(src, yy, planes[order[k]], xx, core) + wide_of(core_in, k, yy, xx)
                summed[k, yy, xx] = total.astype(kind)
                return 0

            lax.fori_loop(0, 2 * width, step, 0)
            for d in range(1, width):
                xas[k, d] = begin(
                    remote(
                        summed.at[k, :, right[d], top],
                        xa_in.at[k, d],
                        link_send.at[k, 0, d],
                        link_recv.at[k, 0, d],
                        x_peers[d],
                    )
                )
            ybs[k] = begin(
                remote(
                    summed.at[k, 1 - head, :, low],
                    yb_in.at[k],
                    link_send.at[k, 1, 0],
                    link_recv.at[k, 1, 0],
                    y_peer,
                )
            )

        def second(k):
            total = wide_of(summed, k, 1 - head, x, top)
            for d in range(1, width):
                xas[k, d].wait_recv()
                total = total + wide_of(xa_in, k, d, 1 - head)
            ya_out[k] = total.astype(kind)
            yas[k] = begin(
                remote(
                    ya_out.at[k],
                    ya_in.at[k],
                    link_send.at[k, 0, 0],
                    link_recv.at[k, 0, 0],
                    y_peer,
                )
            )
            ybs[k].wait_recv()
            for d in range(1, width):
                total = wide_of(summed, k, head, right[d], low) + wide_of(yb_in, k, right[d])
                xb_out[k, d] = total.astype(kind)
                xbs[k, d] = begin(
                    remote(
                        xb_out.at[k, d],
                        xb_in.at[k, d],
                        link_send.at[k, 1, d],
                        link_recv.at[k, 1, d],
                        x_peers[d],
                    )
                )

        def third(k):
            slab = planes[order[k]]
            yas[k].wait_recv()
            total = wide_of(summed, k, head, x, top) + wide_of(ya_in, k)
            for d in range(1, width):
                total = total + wide_of(xa_in, k, d, head)
            dkv_ref[slab, top] = total.astype(kind)
            total = wide_of(summed, k, head, x, low) + wide_of(yb_in, k, x)
            for d in range(1, width):
                xbs[k, d].wait_recv()
                total = total + wide_of(xb_in, k, d)
            dkv_ref[slab, low] = total.astype(kind)
            part = (
                dot32(dq_ref[slab], w_ref[...], LAST)
                + dot32(dkv_ref[slab], pack_ref[:, features : features + wide], LAST)
            ).astype(kind)
            if order[k] == 0:
                dxn_ref[plane] = part
            else:
                share[k] = part
                z_copies.append(
                    begin(
                        remote(
                            share.at[k],
                            dxn_ref.at[plane],
                            z_send.at[order[k]],
                            z_recv.at[order[k]],
                            z_peers[order[k]],
                        )
                    )
                )

        for t in range(COLUMNS + 2):
            if t < COLUMNS:
                first(t)
            if 0 <= t - 1 < COLUMNS:
                second(t - 1)
            if 0 <= t - 2 < COLUMNS:
                third(t - 2)
        for copy in z_copies:
            copy.wait_recv()
        for copy in copies:
            copy.wait_send()

    tile = (rows, wide)
    part = (half, wide)
    return pl.pallas_call(
        body,
        out_shape=[
            jax.ShapeDtypeStruct((COLUMNS,) + tile, kind),
            jax.ShapeDtypeStruct((COLUMNS, rows, features), kind),
        ],
        in_specs=[VMEM] * 4,
        out_specs=[VMEM] * 2,
        scratch_shapes=[
            pltpu.VMEM((COLUMNS, 2, width) + tile, kind),
            pltpu.VMEM((COLUMNS, 2, width) + tile, kind),
            pltpu.VMEM((COLUMNS, width, 2) + part, kind),
            pltpu.VMEM((COLUMNS,) + part, kind),
            pltpu.VMEM((COLUMNS,) + part, kind),
            pltpu.VMEM((COLUMNS, width) + part, kind),
            pltpu.VMEM((COLUMNS, width) + part, kind),
            pltpu.VMEM((COLUMNS, width) + part, kind),
            pltpu.VMEM((COLUMNS, rows, features), kind),
            DMA((COLUMNS,)),
            DMA((COLUMNS,)),
            DMA((COLUMNS, 2, width)),
            DMA((COLUMNS, 2, width)),
            DMA((COLUMNS,)),
            DMA((COLUMNS,)),
        ],
        compiler_params=comm_params(collective_id),
        cost_estimate=lasting(cost),
    )(dkv_all.reshape((2, COLUMNS, width, 2) + tile), dq, query_w, pack)


NEGATIVE = -1e30
EPSILON = 1e-06
KEYS = 1024
LANES = 128
LAST = (((1,), (1,)), ((), ()))
FIRST = (((0,), (0,)), ((), ()))


def dot32(a, b, dims=(((1,), (0,)), ((), ()))):
    return lax.dot_general(a, b, dims, preferred_element_type=jnp.float32)


def visible(key_base, query_base, keys, queries, starts):
    key_pos = key_base + lax.broadcasted_iota(jnp.int32, (keys, queries), 0)
    query_pos = query_base + lax.broadcasted_iota(jnp.int32, (keys, queries), 1)
    return (key_pos <= query_pos) & (key_pos >= starts)


def block_bounds(starts, bases, rows):
    return jnp.stack(
        [
            lax.div(starts[:, 0], KEYS),
            lax.div(bases + rows - 1, KEYS),
            bases,
            lax.div(starts[:, rows - 1], KEYS),
        ],
        axis=1,
    )


def over_chunks(bounds_ref, i, step, carry):
    low, high, edge = bounds_ref[i, 0], bounds_ref[i, 1], bounds_ref[i, 3]
    carry = step(high, True, carry)
    inner = jnp.maximum(high - 1 - edge, 0)
    carry = lax.fori_loop(0, inner, lambda t, c: step(high - 1 - t, False, c), carry)
    below = high - 1 - inner
    return lax.fori_loop(0, below - low + 1, lambda t, c: step(below - t, True, c), carry)


def attend(bounds, queries, kv_all, starts):
    count, rows, width = queries.shape
    heads = width // LANES

    def body(bounds_ref, q_ref, kv_ref, start_ref, out_ref, attn_ref):
        i = pl.program_id(0)
        base = bounds_ref[i, 2]
        start_row = start_ref[0]
        q = [q_ref[0, :, h * LANES : (h + 1) * LANES] for h in range(heads)]

        def step(chunk, masked, carry):
            at = pl.multiple_of(chunk * KEYS, KEYS)
            if masked:
                ok = visible(chunk * KEYS, base, KEYS, rows, start_row)
            kvs = [kv_ref[pl.ds(at, KEYS), h * LANES : (h + 1) * LANES] for h in range(heads)]
            scores = [dot32(kvs[h], q[h], LAST) for h in range(heads)]
            if masked:
                scores = [jnp.where(ok, s, NEGATIVE) for s in scores]
            tops = [
                jnp.maximum(carry[h][0], jnp.max(scores[h], axis=0, keepdims=True))
                for h in range(heads)
            ]
            weights = [jnp.exp(scores[h] - tops[h]) for h in range(heads)]
            shrinks = [jnp.exp(carry[h][0] - tops[h]) for h in range(heads)]
            totals = [
                carry[h][1] * shrinks[h] + jnp.sum(weights[h], axis=0, keepdims=True)
                for h in range(heads)
            ]
            accs = [
                carry[h][2] * shrinks[h] + dot32(kvs[h], weights[h].astype(jnp.bfloat16), FIRST)
                for h in range(heads)
            ]
            return tuple(zip(tops, totals, accs))

        empty = tuple(
            (
                jnp.full((1, rows), NEGATIVE, jnp.float32),
                jnp.zeros((1, rows), jnp.float32),
                jnp.zeros((LANES, rows), jnp.float32),
            )
            for h in range(heads)
        )
        done = over_chunks(bounds_ref, i, step, empty)
        lane = lax.broadcasted_iota(jnp.int32, (LANES, rows), 0)
        narrow = []
        for h in range(heads):
            top, total, acc = done[h]
            value = jnp.where(lane < LANES // 2, top + jnp.log(total), acc / total)
            out_ref[0, :, h * LANES : (h + 1) * LANES] = value.T
            narrow.append(value[LANES // 2 :])
        attn_ref[0] = jnp.concatenate(narrow, axis=0).T.astype(jnp.bfloat16)

    return pl.pallas_call(
        body,
        out_shape=(
            jax.ShapeDtypeStruct((count, rows, width), jnp.float32),
            jax.ShapeDtypeStruct((count, rows, width // 2), jnp.bfloat16),
        ),
        grid_spec=pltpu.PrefetchScalarGridSpec(
            num_scalar_prefetch=1,
            grid=(count,),
            in_specs=[
                pl.BlockSpec((1, rows, width), lambda i, b: (i, 0, 0)),
                pl.BlockSpec(kv_all.shape, lambda i, b: (0, 0)),
                pl.BlockSpec((1, 1, rows), lambda i, b: (i, 0, 0)),
            ],
            out_specs=(
                pl.BlockSpec((1, rows, width), lambda i, b: (i, 0, 0)),
                pl.BlockSpec((1, rows, width // 2), lambda i, b: (i, 0, 0)),
            ),
        ),
        compiler_params=pltpu.CompilerParams(vmem_limit_bytes=VMEM_BYTES),
        cost_estimate=lasting(13),
    )(bounds, queries, kv_all, starts)


def attend_back(bounds, queries, dy, out_rows, kept, kv_all, starts, scale):
    count, rows, width = queries.shape
    total_keys = kv_all.shape[0]
    heads = width // LANES
    if total_keys * width * 14 > VMEM_BYTES:
        heads = 1
    wide = heads * LANES

    def body(bounds_ref, q_ref, dy_ref, w_ref, kept_ref, kv_ref, start_ref, dq_ref, dkv_ref, acc_ref):
        i = pl.program_id(1)
        base = bounds_ref[i, 2]
        start_row = start_ref[0]

        @pl.when(i == 0)
        def _():
            def clear(c, _):
                acc_ref[pl.ds(pl.multiple_of(c * KEYS, KEYS), KEYS), :] = jnp.zeros(
                    (KEYS, wide), jnp.float32
                )
                return 0

            lax.fori_loop(0, total_keys // KEYS, clear, 0)

        q = [q_ref[0, :, h * LANES : (h + 1) * LANES] for h in range(heads)]
        grads = dot32(dy_ref[0], w_ref[...], LAST).astype(jnp.bfloat16)
        g = [grads[:, h * LANES : (h + 1) * LANES] for h in range(heads)]
        qg = [jnp.concatenate([q[h], g[h]], axis=0) for h in range(heads)]
        lse, delta = [], []
        for h in range(heads):
            kept_t = kept_ref[0, :, h * LANES : (h + 1) * LANES].T
            lse.append(kept_t[0:1])
            delta.append(jnp.sum(kept_t * g[h].astype(jnp.float32).T, axis=0, keepdims=True))

        def step(chunk, masked, carry):
            at = pl.multiple_of(chunk * KEYS, KEYS)
            if masked:
                ok = visible(chunk * KEYS, base, KEYS, rows, start_row)
            lanes = [slice(h * LANES, (h + 1) * LANES) for h in range(heads)]
            kvs = [kv_ref[pl.ds(at, KEYS), lanes[h]] for h in range(heads)]
            pairs = [dot32(kvs[h], qg[h], LAST) for h in range(heads)]
            scores = [p[:, :rows] for p in pairs]
            dprobs = [p[:, rows:] for p in pairs]
            if masked:
                scores = [jnp.where(ok, s, NEGATIVE) for s in scores]
            probs = [jnp.exp(scores[h] - lse[h]) for h in range(heads)]
            dscores = [
                (probs[h] * (dprobs[h] - delta[h])).astype(jnp.bfloat16) for h in range(heads)
            ]
            both = [
                jnp.concatenate([dscores[h], probs[h].astype(jnp.bfloat16)], axis=1)
                for h in range(heads)
            ]
            for h in range(heads):
                acc_ref[pl.ds(at, KEYS), lanes[h]] += dot32(both[h], qg[h])
            return tuple(carry[h] + dot32(kvs[h], dscores[h], FIRST) for h in range(heads))

        done = over_chunks(
            bounds_ref,
            i,
            step,
            tuple(jnp.zeros((LANES, rows), jnp.float32) for h in range(heads)),
        )
        lane = lax.broadcasted_iota(jnp.int32, (LANES, rows), 0)
        for h in range(heads):
            value = jnp.where(lane < LANES // 2, done[h] * scale, 0.0)
            dq_ref[0, :, h * LANES : (h + 1) * LANES] = value.T.astype(jnp.bfloat16)

        @pl.when(i == count - 1)
        def _():
            def store(c, _):
                at = pl.ds(pl.multiple_of(c * KEYS, KEYS), KEYS)
                dkv_ref[at, :] = acc_ref[at, :].astype(jnp.bfloat16)
                return 0

            lax.fori_loop(0, total_keys // KEYS, store, 0)

    block = pl.BlockSpec((1, rows, wide), lambda h, i, b: (i, 0, h))
    whole = pl.BlockSpec((total_keys, wide), lambda h, i, b: (0, h))
    return pl.pallas_call(
        body,
        out_shape=(
            jax.ShapeDtypeStruct((count, rows, width), jnp.bfloat16),
            jax.ShapeDtypeStruct(kv_all.shape, jnp.bfloat16),
        ),
        grid_spec=pltpu.PrefetchScalarGridSpec(
            num_scalar_prefetch=1,
            grid=(width // wide, count),
            in_specs=[
                block,
                pl.BlockSpec((1,) + tuple(dy.shape[1:]), lambda h, i, b: (i, 0, 0)),
                pl.BlockSpec((wide, out_rows.shape[1]), lambda h, i, b: (h, 0)),
                block,
                whole,
                pl.BlockSpec((1, 1, rows), lambda h, i, b: (i, 0, 0)),
            ],
            out_specs=(block, whole),
            scratch_shapes=[pltpu.VMEM((total_keys, wide), jnp.float32)],
        ),
        compiler_params=pltpu.CompilerParams(vmem_limit_bytes=VMEM_BYTES),
        cost_estimate=lasting(20),
    )(bounds, queries, dy, out_rows, kept, kv_all, starts)


def experts_exchange(sent, saved, own, other, blocks, collective_id, forward, backward, cost):
    copies = blocks // NE
    half = NE // 2
    slots, width = sent[0].shape[1:]
    hidden, features = own[0].shape
    tile = min(hidden, 256)
    tiles = hidden // tile
    count = len(sent)
    homes_count = int(forward) + int(backward)
    total_rows = copies * NE * slots
    kind = sent[0].dtype
    sizes = (half // 2, half // 2, half)
    first_rows = [copies * slots * at for at in (0, half // 2, half)]
    most_rows = copies * slots * half
    plain = (((1,), (0,)), ((), ()))

    def body(*refs):
        refs = list(refs)

        def take(n):
            taken = refs[:n]
            del refs[:n]
            return taken

        srcs = take(count)
        saved_ref = take(1)[0] if not forward else None
        weight_refs = take(6)
        homes = take(homes_count)
        lands = take(1) if not backward else []
        keeps, aways = (take(3), take(3)) if backward else ([], [])
        if backward:
            lands = lands + take(count)
        weights = take(6)
        parts, sib_ins, totals = take(homes_count), take(homes_count), take(homes_count)
        accs = take(homes_count)
        rows_x = take(1)[0]
        if backward:
            rows_z, act_ref, dgate_ref, dup_ref, keep_ref, away_ref = take(6)
            if not forward:
                gate_ref, up_ref = take(2)
            out_sems = take(1)[0]
        load_sems, own_sems, send_sems, recv_sems, pass_sems, land_sems = take(6)
        home_own, home_send, home_recv, part_send, part_recv = take(5)

        head, blk = lax.axis_index("head"), lax.axis_index("blk")
        expert, piece = lax.div(blk, copies), lax.rem(blk, copies)
        near = lax.div(expert, half) * half
        far = half - near
        places = [lax.rem(piece + k, copies) for k in range(copies)]
        siblings = [(head, expert * copies + places[k]) for k in range(copies)]
        others = [lax.rem(expert + d, NE) for d in range(NE)]
        greet([(head, e * copies + piece) for e in others[1:]] + siblings[1:])
        mine = pl.ds(pl.multiple_of(head * features, LANES), features)
        rest = pl.ds(pl.multiple_of((1 - head) * features, LANES), features)
        steps = [(far, sizes[0]), (far + sizes[0], sizes[1]), (near, sizes[2])]

        def sending(n, e):
            return remote(
                srcs[n].at[e],
                lands[n].at[piece, expert],
                send_sems.at[n, e],
                recv_sems.at[n, expert],
                (head, e * copies + piece),
            )

        owns = []
        for n in range(count):
            copy = pltpu.make_async_copy(
                srcs[n].at[expert], lands[n].at[piece, expert], own_sems.at[n]
            )
            copy.start()
            owns.append(copy)
        def each(t, copy_of, arrays, act):
            first, size = steps[t]
            for j in range(size):
                for n in range(arrays):
                    if t < 2:
                        act(copy_of(n, first + j))
                    else:

                        @pl.when(first + j != expert)
                        def _():
                            act(copy_of(n, first + j))

        def send(t):
            each(t, sending, count, lambda copy: copy.start())

        def sent_out(t):
            each(t, sending, count, lambda copy: copy.wait_send())

        for t in range(3):
            send(t)
        loads = []
        for n in range(6):
            copy = pltpu.make_async_copy(weight_refs[n], weights[n], load_sems.at[n])
            copy.start()
            loads.append(copy)
        go, gx, uo, ux, do, dx = weights
        passes, exchanges = [], {}

        def arrive(t):
            first, size = steps[t]
            waits = []
            if t == 2:
                for copy in owns:
                    copy.wait()
            for j in range(size):
                e = first + j
                for n in range(count):
                    place = lands[n].at[piece, e]

                    @pl.when(e != expert)
                    def _():
                        remote(
                            place, place, send_sems.at[n, e], recv_sems.at[n, e], siblings[0]
                        ).wait_recv()

                    for k in range(1, copies):
                        copy = remote(
                            place,
                            place,
                            pass_sems.at[n, k, e],
                            land_sems.at[n, k, e],
                            siblings[k],
                        )
                        copy.start()
                        waits.append(copy)
            for copy in waits:
                copy.wait_recv()
            passes.extend(waits)

        def flat(ref, t):
            first, size = steps[t]
            value = ref[:, pl.ds(first, size)].astype(jnp.float32)
            return value.reshape((copies * size * slots, width)).astype(kind)

        def span_of(t):
            return slice(first_rows[t], first_rows[t] + copies * steps[t][1] * slots)

        def gate_up(t, j):
            at = pl.ds(pl.multiple_of(j * tile, tile), tile)
            xo, xx = rows_x[span_of(t), mine], rows_x[span_of(t), rest]
            gate = dot32(xo, go[at], LAST) + dot32(xx, gx[at], LAST)
            return gate, dot32(xo, uo[at], LAST) + dot32(xx, ux[at], LAST)

        def early(t):
            rows_x[span_of(t)] = flat(saved_ref, t)
            size = copies * steps[t][1] * slots

            def step(j, _):
                at = pl.ds(pl.multiple_of(j * tile, tile), tile)
                gate_ref[:size, at], up_ref[:size, at] = gate_up(t, j)
                return 0

            lax.fori_loop(0, tiles, step, 0)

        def work(t):
            size = copies * steps[t][1] * slots
            span = span_of(t)
            if forward:
                rows_x[span] = flat(lands[0], t)
            if backward:
                rows_z[span] = flat(lands[-1], t)
            for acc in accs:
                acc[:size] = jnp.zeros((size, width), jnp.float32)

            def step(j, _):
                at = pl.ds(pl.multiple_of(j * tile, tile), tile)
                if forward:
                    gate, up = gate_up(t, j)
                else:
                    gate, up = gate_ref[:size, at], up_ref[:size, at]
                sigmoid = jax.nn.sigmoid(gate)
                silu = gate * sigmoid
                act = (silu * up).astype(kind)
                if forward:
                    accs[0][:size, mine] += dot32(act, do[at])
                    accs[0][:size, rest] += dot32(act, dx[at])
                if backward:
                    zo, zx = rows_z[span, mine], rows_z[span, rest]
                    dact = dot32(zo, do[at], LAST) + dot32(zx, dx[at], LAST)
                    dgate = (dact * up * sigmoid * (1.0 + gate * (1.0 - sigmoid))).astype(kind)
                    dup = (dact * silu).astype(kind)
                    act_ref[span, at] = act
                    dgate_ref[span, at] = dgate
                    dup_ref[span, at] = dup
                    accs[-1][:size, mine] += dot32(dgate, go[at]) + dot32(dup, uo[at])
                    accs[-1][:size, rest] += dot32(dgate, gx[at]) + dot32(dup, ux[at])
                return 0

            lax.fori_loop(0, tiles, step, 0)
            first, size_e = steps[t]
            for n in range(homes_count):
                value = accs[n][:size].reshape((copies, size_e, slots, width))
                parts[n][:, pl.ds(first, size_e)] = value.astype(kind)
                for j in range(size_e):
                    for k in range(1, copies):
                        copy = remote(
                            parts[n].at[places[k], first + j],
                            sib_ins[n].at[k - 1, first + j],
                            part_send.at[n, k, first + j],
                            part_recv.at[n, k, first + j],
                            siblings[k],
                        )
                        copy.start()
                        exchanges[n, t, j, k] = copy

        def homeward(n, e):
            return remote(
                totals[n].at[e],
                homes[n].at[expert],
                home_send.at[n, e],
                home_recv.at[n, expert],
                (head, e * copies + piece),
            )

        def give_back(t):
            first, size = steps[t]
            for j in range(size):
                e = first + j
                for n in range(homes_count):
                    value = parts[n][piece, e].astype(jnp.float32)
                    for k in range(1, copies):
                        exchanges[n, t, j, k].wait_recv()
                        value = value + sib_ins[n][k - 1, e].astype(jnp.float32)
                    totals[n][e] = value.astype(kind)
                    if t < 2:
                        homeward(n, e).start()
                    else:

                        @pl.when(e != expert)
                        def _():
                            homeward(n, e).start()

        for copy in loads:
            copy.wait()
        if not forward:
            early(0)
        for t in range(len(steps)):
            arrive(t)
            work(t)
            if t > 0:
                give_back(t - 1)
            if not forward and t + 1 < len(steps):
                early(t + 1)
        give_back(len(steps) - 1)
        stays = []
        for n in range(homes_count):
            copy = pltpu.make_async_copy(
                totals[n].at[expert], homes[n].at[expert], home_own.at[n]
            )
            copy.start()
            stays.append(copy)

        if backward:

            def saving(n, j, which):
                at = pl.ds(pl.multiple_of(j * tile, tile), tile)
                src, dst = ((keep_ref, keeps), (away_ref, aways))[which]
                return pltpu.make_async_copy(src.at[n, at], dst[n].at[at], out_sems.at[n, j, which])

            def grads(j, _):
                at = pl.ds(pl.multiple_of(j * tile, tile), tile)
                for n, (left, right) in enumerate(
                    ((dgate_ref, rows_x), (dup_ref, rows_x), (act_ref, rows_z))
                ):
                    value = left[:, at]
                    away_ref[n, at] = dot32(value, right[:, rest], FIRST).astype(kind)
                    saving(n, j, 1).start()
                    keep_ref[n, at] = dot32(value, right[:, mine], FIRST)
                    saving(n, j, 0).start()
                return 0

            lax.fori_loop(0, tiles, grads, 0)

        for n in range(homes_count):
            for e in others[1:]:
                place = homes[n].at[e]
                remote(
                    place, place, home_send.at[n, e], home_recv.at[n, e], siblings[0]
                ).wait_recv()
        for t in range(len(steps)):
            sent_out(t)
            each(t, homeward, homes_count, lambda copy: copy.wait_send())
        for copy in passes + list(exchanges.values()):
            copy.wait_send()
        for copy in stays:
            copy.wait()
        if backward:

            def settle(j, _):
                for n in range(3):
                    saving(n, j, 0).wait()
                    saving(n, j, 1).wait()
                return 0

            lax.fori_loop(0, tiles, settle, 0)

    slab = (copies, NE, slots, width)
    shapes = [make((NE, slots, width), kind)] * homes_count
    specs = [ANY] * homes_count
    if not backward:
        shapes.append(make(slab, kind))
        specs.append(VMEM)
    else:
        shapes += [make((hidden, features))] * 3 + [make((hidden, features), kind)] * 3
        specs += [ANY] * 6
    scratch = []
    if backward:
        scratch += [pltpu.VMEM(slab, kind)] * count
    scratch += [pltpu.VMEM((hidden, features), kind)] * 6
    scratch += [pltpu.VMEM(slab, kind)] * homes_count
    scratch += [pltpu.VMEM((copies - 1,) + slab[1:], kind)] * homes_count
    scratch += [pltpu.VMEM((NE, slots, width), kind)] * homes_count
    scratch += [pltpu.VMEM((most_rows, width), jnp.float32)] * homes_count
    scratch.append(pltpu.VMEM((total_rows, width), kind))
    if backward:
        scratch.append(pltpu.VMEM((total_rows, width), kind))
        scratch += [pltpu.VMEM((total_rows, hidden), kind)] * 3
        scratch.append(pltpu.VMEM((3, hidden, features), jnp.float32))
        scratch.append(pltpu.VMEM((3, hidden, features), kind))
        if not forward:
            scratch += [pltpu.VMEM((most_rows, hidden), jnp.float32)] * 2
        scratch.append(DMA((3, tiles, 2)))
    scratch += [DMA((6,)), DMA((count,)), DMA((count, NE)), DMA((count, NE))]
    scratch += [DMA((count, copies, NE))] * 2
    scratch += [DMA((homes_count,)), DMA((homes_count, NE)), DMA((homes_count, NE))]
    scratch += [DMA((homes_count, copies, NE))] * 2
    operands = list(sent)
    in_specs = [ANY] * count
    if not forward:
        operands.append(saved)
        in_specs.append(VMEM)
    operands += [w for pair in zip(own, other) for w in pair]
    in_specs += [ANY] * 6
    return pl.pallas_call(
        body,
        out_shape=shapes,
        in_specs=in_specs,
        out_specs=specs,
        scratch_shapes=scratch,
        compiler_params=comm_params(collective_id),
        cost_estimate=lasting(cost),
    )(*operands)


def split(values, terms=2):
    parts = []
    for _ in range(terms):
        part = values.astype(jnp.bfloat16)
        parts.append(part)
        values = values - part.astype(jnp.float32)
    return parts


def exact_dot(pieces, values, dims):
    total = dot32(pieces[0], values, dims)
    for piece in pieces[1:]:
        total = total + dot32(piece, values, dims)
    return total


def unit_scale(values):
    return lax.rsqrt(jnp.mean(values * values, axis=-1, keepdims=True) + EPSILON)


def alone(body, out_shape, cost, *operands, scalars=0):
    specs = [pl.BlockSpec(memory_space=pltpu.SMEM)] * scalars + [VMEM] * (len(operands) - scalars)
    results = pl.pallas_call(
        body,
        out_shape=out_shape,
        in_specs=specs,
        out_specs=jax.tree.map(lambda _: VMEM, out_shape),
        compiler_params=pltpu.CompilerParams(vmem_limit_bytes=VMEM_BYTES),
        cost_estimate=lasting(cost),
    )(*operands)
    return list(results) if isinstance(out_shape, (list, tuple)) else results


def make(shape, kind=jnp.float32):
    return jax.ShapeDtypeStruct(tuple(shape), kind)


def route_tables(routes, gates):
    count, rows, _ = routes.shape
    slots = NE * CAP

    def body(routes_ref, gates_ref, picks_ref, weights_ref, slot_ref, other_ref):
        row = lax.broadcasted_iota(jnp.int32, (rows, rows), 0)
        col = lax.broadcasted_iota(jnp.int32, (rows, rows), 1)
        before = (col < row).astype(jnp.bfloat16)
        expert = lax.broadcasted_iota(jnp.int32, (rows, LANES), 1)
        slot = lax.broadcasted_iota(jnp.int32, (rows, slots), 1)
        source = lax.broadcasted_iota(jnp.int32, (LANES, slots), 0)
        target = lax.broadcasted_iota(jnp.int32, (LANES, slots), 1)
        spread = (
            (target >= source * CAP) & (target < source * CAP + CAP) & (source < NE)
        ).astype(jnp.bfloat16)
        ones = jnp.ones((rows, LANES), jnp.bfloat16)
        for n in range(count):
            gate = jnp.zeros((rows, LANES), jnp.float32)
            named = jnp.zeros((rows, LANES), jnp.float32)
            for k in range(2):
                hit = routes_ref[n, :, k : k + 1] == expert
                named = named + jnp.where(hit, 1.0, 0.0)
                gate = gate + jnp.where(hit, gates_ref[n, :, k : k + 1], 0.0)
            rank = dot32(before, named.astype(jnp.bfloat16)) + expert.astype(jnp.float32) * CAP
            rank = jnp.where(expert < NE, rank, 0.0)
            goal = exact_dot(split(rank, 2), spread, (((1,), (0,)), ((), ())))
            member = dot32(named.astype(jnp.bfloat16), spread)
            pick = jnp.where(goal == slot.astype(jnp.float32), member, 0.0)
            weight = pick * exact_dot(split(gate, 3), spread, (((1,), (0,)), ((), ())))
            picks_ref[n] = pick.astype(jnp.bfloat16)
            weights_ref[n] = weight
            slot_ref[n] = exact_dot(split(weight, 3), ones, FIRST)
            other_ref[n] = gate

    return alone(
        body,
        (
            make((count, rows, slots), jnp.bfloat16),
            make((count, rows, slots)),
            make((count, slots, LANES)),
            make((count, rows, LANES)),
        ),
        3,
        routes,
        gates,
    )


def gate_slots(slot_gates, picks, grads):
    picked = dot32(picks, grads[0], FIRST)
    for part in grads[1:]:
        picked = picked + dot32(picks, part, FIRST)
    lanes = [
        (picked[:, at : at + LANES] * slot_gates).astype(jnp.bfloat16)
        for at in range(0, picked.shape[1], LANES)
    ]
    return jnp.concatenate(lanes, axis=1)


def const_alphas(hn, smalls, base):
    logits = dot32(hn, smalls[base + 2 : base + 6].astype(jnp.bfloat16), LAST)
    alphas = []
    for c in range(2):
        first, second = logits[:, 2 * c : 2 * c + 1], logits[:, 2 * c + 1 : 2 * c + 2]
        top = jnp.maximum(first, second)
        first, second = jnp.exp(first - top), jnp.exp(second - top)
        total = first + second
        alphas.append((first / total, second / total))
    return alphas


def middle(attn, x, pack, smalls, base, picks, slot_gates, grads):
    planes, rows, part = attn.shape
    width = x.shape[1]
    slots = picks.shape[1]

    def body(attn_ref, x_ref, w_ref, small_ref, picks_ref, gates_ref, *refs):
        total = x_ref[...].astype(jnp.float32)
        for z in range(planes):
            total = total + dot32(attn_ref[z], w_ref[z * part : (z + 1) * part, :width])
        mid_ref, sent_ref = refs[-2:] if grads is None else refs[-3:-1]
        mid_ref[...] = total
        hn = (total * unit_scale(total) * small_ref[base + 1 : base + 2]).astype(jnp.bfloat16)
        sent_ref[...] = dot32(picks_ref[...], hn, FIRST).astype(jnp.bfloat16)
        if grads is not None:
            refs[-1][...] = gate_slots(gates_ref[...], picks_ref[...], [refs[0][...]])

    outs = [make((rows, width)), make((slots, width), jnp.bfloat16)]
    more = []
    if grads is not None:
        outs.append(make((slots, width), jnp.bfloat16))
        more.append(grads)
    return alone(body, outs, 3, attn, x, pack, smalls, picks, slot_gates, *more)


def combine(back, weights, mid, other, smalls, base, following):
    rows, width = mid.shape

    def body(back_ref, weights_ref, mid_ref, other_ref, small_ref, x_ref, *refs):
        mid_value, gate = mid_ref[...], other_ref[...]
        hn = (mid_value * unit_scale(mid_value) * small_ref[base + 1 : base + 2]).astype(
            jnp.bfloat16
        )
        alphas = const_alphas(hn, small_ref, base)
        wide = hn.astype(jnp.float32)
        total = mid_value + exact_dot(
            split(weights_ref[...]), back_ref[...], (((1,), (0,)), ((), ()))
        )
        factor = gate[:, NE + 1 : NE + 2]
        for c in range(2):
            weight = gate[:, NE + 2 + c : NE + 3 + c]
            factor = factor + weight * alphas[c][0]
            total = total + (weight * alphas[c][1]) * small_ref[base + 6 + c : base + 7 + c]
        total = total + factor * wide
        x_ref[...] = total
        if following:
            refs[0][...] = (total * unit_scale(total) * small_ref[base + 8 : base + 9]).astype(
                jnp.bfloat16
            )

    outs = [make((rows, width))]
    if following:
        outs.append(make((rows, width), jnp.bfloat16))
    return alone(body, outs, 3, back, weights, mid, other, smalls)


def experts_back(dback, picks, upstream, mid, other, smalls, base):
    rows, width = mid.shape

    def body(dback_ref, picks_ref, up_ref, mid_ref, other_ref, small_ref, dmid_ref, dy_ref, row_ref):
        mid_value, gate = mid_ref[...], other_ref[...]
        g = up_ref[...].astype(jnp.float32)
        scale = unit_scale(mid_value)
        unit = mid_value * scale
        gain = small_ref[base + 1 : base + 2]
        hn = (unit * gain).astype(jnp.bfloat16)
        alphas = const_alphas(hn, small_ref, base)
        wide = hn.astype(jnp.float32)
        dhn = dot32(picks_ref[...], dback_ref[...])
        g_hn = jnp.sum(g * wide, axis=1, keepdims=True)
        factor = gate[:, NE + 1 : NE + 2]
        row_ref[0:1] = jnp.zeros((1, width), jnp.float32)
        for c in range(2):
            weight = gate[:, NE + 2 + c : NE + 3 + c]
            vector = small_ref[base + 6 + c : base + 7 + c]
            first, second = alphas[c]
            factor = factor + weight * first
            row_ref[6 + c : 7 + c] = jnp.sum((weight * second) * g, axis=0, keepdims=True)
            da_first = weight * g_hn
            da_second = weight * jnp.sum(g * vector, axis=1, keepdims=True)
            mean = first * da_first + second * da_second
            for j, dlog in enumerate((first * (da_first - mean), second * (da_second - mean))):
                at = 2 + 2 * c + j
                dhn = dhn + dlog * small_ref[base + at : base + at + 1]
                row_ref[at : at + 1] = jnp.sum(dlog * wide, axis=0, keepdims=True)
        dhn = dhn + factor * g
        row_ref[1:2] = jnp.sum(dhn * unit, axis=0, keepdims=True)
        through = dhn * gain
        inner = jnp.mean(through * unit, axis=1, keepdims=True)
        dmid = g + scale * (through - unit * inner)
        dmid_ref[...] = dmid
        dy_ref[...] = dmid.astype(jnp.bfloat16)

    return alone(
        body,
        [make((rows, width)), make((rows, width), jnp.bfloat16), make((8, width))],
        4,
        dback,
        picks,
        upstream,
        mid,
        other,
        smalls,
    )


def finish(dxn, x, dmid, rows_in, smalls, base, picks, slot_gates):
    planes, rows, width = dxn.shape

    def body(dxn_ref, x_ref, dmid_ref, row_ref, small_ref, *refs):
        grad = dxn_ref[0].astype(jnp.float32)
        for z in range(1, planes):
            grad = grad + dxn_ref[z].astype(jnp.float32)
        value = x_ref[...].astype(jnp.float32)
        scale = unit_scale(value)
        unit = value * scale
        out_rows = refs[-1 if picks is None else -2]
        out_rows[...] = row_ref[...]
        out_rows[0:1] = jnp.sum(grad * unit, axis=0, keepdims=True)
        through = grad * small_ref[base : base + 1]
        inner = jnp.mean(through * unit, axis=1, keepdims=True)
        g = dmid_ref[...] + scale * (through - unit * inner)
        refs[-2 if picks is None else -3][...] = g
        if picks is not None:
            refs[-1][...] = gate_slots(refs[1][...], refs[0][...], split(g))

    outs = [make((rows, width)), make((8, width))]
    more = []
    if picks is not None:
        outs.append(make((picks.shape[1], width), jnp.bfloat16))
        more = [picks, slot_gates]
    return alone(body, outs, 3, dxn, x, dmid, rows_in, smalls, *more)


def pack_grads(column, dq, dkv, attn, dy, small):
    width = column.shape[1]
    kv_cols, own_out = dkv.shape[1], attn.shape[1]
    tail = own_out + LANES // 2
    rows, cols = own_out // 2, width // 2

    def body(column_ref, dq_ref, dkv_ref, attn_ref, dy_ref, small_ref, one, two):
        one[:, :kv_cols] = dot32(column_ref[...], dkv_ref[...], FIRST).astype(jnp.bfloat16)
        source = lax.broadcasted_iota(jnp.int32, (kv_cols, tail), 0)
        target = lax.broadcasted_iota(jnp.int32, (kv_cols, tail), 1)
        dim = LANES // 2
        goal = lax.div(target, dim) * LANES + lax.rem(target, dim)
        compact = ((goal == source) & (target < own_out)).astype(jnp.bfloat16)
        narrow = dot32(dq_ref[...], compact).astype(jnp.bfloat16)
        placed = jnp.concatenate(
            [
                jnp.zeros((own_out, width), jnp.float32),
                small_ref[...],
                jnp.zeros((tail - own_out - 8, width), jnp.float32),
            ],
            axis=0,
        ).T
        one[:, kv_cols:] = (dot32(column_ref[...], narrow, FIRST) + placed).astype(jnp.bfloat16)
        out = dot32(attn_ref[...], dy_ref[...], FIRST).astype(jnp.bfloat16)
        for a in range(2):
            for b in range(2):
                two[a, b] = out[a * rows : (a + 1) * rows, b * cols : (b + 1) * cols]

    return alone(
        body,
        [make((width, kv_cols + tail), jnp.bfloat16), make((2, 2, rows, cols), jnp.bfloat16)],
        4,
        column,
        dq,
        dkv,
        attn,
        dy,
        small,
    )


def per_device(
    tokens,
    segments,
    routes,
    gates,
    w_qkv,
    w_out,
    gain_attn,
    gain_moe,
    const_gate,
    const_vec,
    w_gate,
    w_up,
    w_down,
    cotangent,
):
    blocks = lax.axis_size("blk")
    head_index, blk_index = lax.axis_index("head"), lax.axis_index("blk")
    span = blocks // COLUMNS
    plane, rest = lax.div(blk_index, span), lax.rem(blk_index, span)
    shards = 2 * blocks
    token_rows, width = tokens.shape
    shard_rows = width // shards
    head_dim = width // HEADS
    heads = HEADS // COLUMNS
    scale = head_dim ** (-0.5)
    half_length = blocks * token_rows
    positions = 2 * half_length
    own_out = heads * head_dim
    wide = heads * LANES

    swap = [(0, 1), (1, 0)]

    seg_own = lax.dynamic_index_in_dim(segments, head_index, 0, keepdims=True)
    seg_rows = jnp.concatenate([lax.rem(seg_own, 128), lax.div(seg_own, 128)], axis=0)
    seg_rows = jnp.pad(seg_rows, ((0, 14), (0, 0))).astype(jnp.bfloat16)
    seg_rows = jnp.broadcast_to(seg_rows[None], (COLUMNS,) + seg_rows.shape)
    smalls = [
        jnp.concatenate(
            [gain_attn[n][:, None], gain_moe[n][:, None], const_gate[n], const_vec[n]], axis=1
        )
        for n in range(LAYERS)
    ]
    smalls.append(jnp.zeros((shard_rows, LANES // 2 - 8 * LAYERS), jnp.bfloat16))
    smalls = jnp.concatenate(smalls, axis=1)
    packs = []
    for layer in range(LAYERS):
        parts = w_qkv[layer].reshape((shard_rows, 3, COLUMNS, heads, head_dim))
        kv_part = jnp.concatenate([parts[:, 1], parts[:, 2]], axis=3)
        kv_part = kv_part.transpose((1, 0, 2, 3)).reshape((COLUMNS, shard_rows, wide))
        query_part = parts[:, 0].transpose((1, 0, 2, 3)).reshape((COLUMNS, shard_rows, own_out))
        packs.append(
            jnp.concatenate(
                [
                    jnp.broadcast_to(w_out[layer][None], (COLUMNS, shard_rows, width)),
                    kv_part,
                    query_part,
                    jnp.broadcast_to(smalls[None], (COLUMNS,) + smalls.shape),
                ],
                axis=2,
            )
        )
    (seg_all, *packs), column_tokens = start_gather([seg_rows] + packs, tokens, blocks, 1)
    packs = [pack.reshape((width, -1)) for pack in packs]
    picks, pick_gates, slot_gates, other_gates = route_tables(routes, gates)

    def send_expert(weight, layer, after):
        own, _ = lax.optimization_barrier((weight[layer], after))
        return own, lax.ppermute(own, "head", swap)

    experts = [[send_expert(w_gate, 0, tokens)]] + [None] * (LAYERS - 1)
    seg_all = seg_all[..., :2, :].astype(jnp.int32)
    seg_all = seg_all[..., 0, :] + 128 * seg_all[..., 1, :]
    seg_query = lax.dynamic_index_in_dim(seg_all, head_index, 0, keepdims=False)
    seg_query = lax.dynamic_index_in_dim(seg_query, rest, 1, keepdims=False)
    starts = jnp.sum(
        (seg_all.reshape((1, 1, -1)) < seg_query[:, :, None]).astype(jnp.int32), axis=2
    )
    bases = (
        head_index * half_length
        + (jnp.arange(COLUMNS, dtype=jnp.int32) * span + rest) * token_rows
    )
    bounds = block_bounds(starts, bases, token_rows)
    starts = starts[:, None, :]

    values = tokens
    column, small_rows = column_tokens, None
    kept = []
    for layer in range(LAYERS):
        base = 8 * layer
        last = layer + 1 == LAYERS
        column, queries, query_w, out_rows, kv_all, small_rows = project_gather(
            column, packs[layer], small_rows, heads, scale, blocks, 4 if layer == 0 else 2
        )
        kv_all = kv_all.reshape((positions, wide))
        if layer == 0:
            experts[layer] += [send_expert(w, layer, kv_all) for w in (w_up, w_down)]
        else:
            experts[layer].append(send_expert(w_down, layer, kv_all))
        attended, attn_col = attend(bounds, queries, kv_all, starts)
        (attn,) = column_exchange([attn_col], [False], blocks, 5, 9)
        mid, *sent = middle(
            attn,
            values,
            packs[layer],
            small_rows,
            base,
            picks[layer],
            slot_gates[layer],
            cotangent if last else None,
        )
        sent = [rows.reshape((NE, CAP, width)) for rows in sent]
        if last:
            back, dback, *wgrads = experts_exchange(
                sent, None, *zip(*experts[layer]), blocks, 7, True, True, 55
            )
            rows_in = None
        else:
            experts[layer + 1] = [send_expert(w, layer + 1, sent[0]) for w in (w_gate, w_up)]
            back, rows_in = experts_exchange(
                sent, None, *zip(*experts[layer]), blocks, 6, True, False, 28
            )
        kept.append(
            (values, column, queries, kv_all, attended, attn_col, query_w, out_rows, mid, rows_in)
        )
        values, *normed = combine(
            back.reshape((NE * CAP, width)),
            pick_gates[layer],
            mid,
            other_gates[layer],
            small_rows,
            base,
            not last,
        )
        if not last:
            (column,) = normed
    output = values

    upstream = cotangent
    shared_grads = [None] * LAYERS
    expert_grads = [None] * LAYERS
    for layer in reversed(range(LAYERS)):
        base = 8 * layer
        values, column, queries, kv_all, attended, attn_col, query_w, out_rows, mid, rows_in = (
            kept[layer]
        )
        if layer + 1 < LAYERS:
            dback, *wgrads = experts_exchange(
                [dz.reshape((NE, CAP, width))],
                rows_in,
                *zip(*experts[layer]),
                blocks,
                8,
                False,
                True,
                36,
            )
            dback, held[2] = lax.optimization_barrier((dback, held[2]))
        got = [lax.ppermute(away, "head", swap) for away in wgrads[3:]]
        dmid, dy, rows = experts_back(
            dback.reshape((NE * CAP, width)),
            picks[layer],
            upstream,
            mid,
            other_gates[layer],
            small_rows,
            base,
        )
        dy = column_gather(dy, blocks, 3)
        dy, got[0] = lax.optimization_barrier((dy, got[0]))
        dq, dkv_all = attend_back(
            bounds, queries, dy, out_rows, attended, kv_all, starts, scale
        )
        dkv_all, got[1] = lax.optimization_barrier((dkv_all, got[1]))
        dkv, dxn = reduce_project(
            dkv_all.reshape((2, COLUMNS, span, token_rows, wide)),
            dq,
            query_w,
            packs[layer],
            blocks,
            10,
        )
        before = layer > 0
        if not before:
            dxn, got[2] = lax.optimization_barrier((dxn, got[2]))
        upstream, rows, *dz = finish(
            dxn,
            values,
            dmid,
            rows,
            small_rows,
            base,
            picks[layer - 1] if before else None,
            slot_gates[layer - 1] if before else None,
        )
        if before:
            (dz,) = dz
        expert_grads[layer] = wgrads[:3], got
        held = got
        qkv_part, out_part = pack_grads(
            column.reshape((-1, width)),
            dq.reshape((-1, wide)),
            dkv.reshape((-1, wide)),
            attn_col.reshape((-1, own_out)),
            dy.reshape((-1, width)),
            rows,
        )
        shared_grads[layer] = [
            qkv_part.reshape((2, COLUMNS, span, shard_rows, -1)),
            out_part.reshape((2, 2, span, shard_rows, width // 2)),
        ]

    packed = [part for layer in range(LAYERS) for part in shared_grads[layer]]
    reduced = plane_reduce(packed, blocks, 12, 20)
    from_planes = column_exchange(reduced[::2], [False] * LAYERS, blocks, 13, 10)
    from_planes = jnp.stack(from_planes, axis=1).astype(jnp.float32)
    kv_out = from_planes[..., :wide].reshape((COLUMNS, LAYERS, shard_rows, heads, 2, head_dim))
    query_out = from_planes[..., wide : wide + own_out].reshape(
        (COLUMNS, LAYERS, shard_rows, heads, 1, head_dim)
    )
    qkv_out = jnp.concatenate([query_out, kv_out], axis=4)
    qkv_out = qkv_out.transpose((1, 2, 4, 0, 3, 5)).reshape((LAYERS, shard_rows, 3 * width))
    small_out = jnp.sum(from_planes[..., wide + own_out : wide + own_out + 8], axis=0)
    out_grads = jnp.stack(reduced[1::2]).transpose((0, 2, 1, 3))
    out_grads = out_grads.reshape((LAYERS, shard_rows, width))
    owners = [
        (y * blocks + z * span + r, (z * 2 + y) * span + r)
        for y in range(2)
        for z in range(COLUMNS)
        for r in range(span)
    ]
    out_grads = lax.ppermute(out_grads, ("head", "blk"), owners).astype(jnp.float32)
    stacked = [
        jnp.stack([owns[n] + gots[n].astype(jnp.float32) for owns, gots in expert_grads])
        for n in range(3)
    ]
    return (
        output,
        upstream,
        qkv_out,
        out_grads,
        small_out[..., 0],
        small_out[..., 1],
        small_out[..., 2:6],
        small_out[..., 6:8],
        stacked[0],
        stacked[1],
        stacked[2],
    )


def solution(mesh):
    tokens = P(("head", "blk"), None)
    by_layer = P(None, ("head", "blk"), None)
    gains = P(None, ("head", "blk"))
    experts = P(None, "blk", "head")
    return jax.shard_map(
        per_device,
        mesh=mesh,
        in_specs=(
            tokens,
            P(None, "blk"),
            by_layer,
            by_layer,
            by_layer,
            by_layer,
            gains,
            gains,
            by_layer,
            by_layer,
            experts,
            experts,
            experts,
            tokens,
        ),
        out_specs=(
            tokens,
            tokens,
            by_layer,
            by_layer,
            gains,
            gains,
            by_layer,
            by_layer,
            experts,
            experts,
            experts,
        ),
        check_vma=False,
    )
```

```python
import jax
import jax.numpy as jnp
from jax import lax
from jax.experimental import pallas as pl
from jax.experimental.pallas import tpu as pltpu
from jax.sharding import PartitionSpec as P

HEADS = 12
NE = 8
LAYERS = 2
CAP = 40
COLUMNS = 4
MESH = pl.DeviceIdType.MESH
ANY = pl.BlockSpec(memory_space=pl.ANY)
VMEM = pl.BlockSpec(memory_space=pltpu.VMEM)
HBM = pl.BlockSpec(memory_space=pltpu.HBM)
DMA = pltpu.SemaphoreType.DMA
VMEM_BYTES = 60 * 1024 * 1024
SPARE_BYTES = 4 * 1024 * 1024


def make(shape, kind=jnp.float32):
    return jax.ShapeDtypeStruct(tuple(shape), kind)


def greet(peers, line=()):
    barrier = pltpu.get_barrier_semaphore()
    count = len(peers)
    for peer in peers:
        pl.semaphore_signal(barrier, inc=1, device_id=peer, device_id_type=MESH)
    for there, peer in line:

        @pl.when(there)
        def _():
            pl.semaphore_signal(barrier, inc=1, device_id=peer, device_id_type=MESH)

        count = count + there.astype(jnp.int32)
    pl.semaphore_wait(barrier, count)


def remote(src, dst, send_sem, recv_sem, peer):
    return pltpu.make_async_remote_copy(
        src_ref=src,
        dst_ref=dst,
        send_sem=send_sem,
        recv_sem=recv_sem,
        device_id=peer,
        device_id_type=MESH,
    )


def room(things, spare=SPARE_BYTES):
    total = spare
    for thing in things:
        if hasattr(thing, "dtype") and hasattr(thing, "shape"):
            if not jnp.issubdtype(thing.dtype, jnp.number):
                continue
            size = jnp.dtype(thing.dtype).itemsize
            for extent in thing.shape:
                size *= extent
            total += size
    return min(total, VMEM_BYTES)


def comm_params(collective_id, things=(), spare=SPARE_BYTES):
    return pltpu.CompilerParams(
        collective_id=collective_id,
        has_side_effects=True,
        vmem_limit_bytes=room(things, spare),
    )


def lasting(microseconds):
    return pl.CostEstimate(
        flops=0, bytes_accessed=int(microseconds * 3_500_000), transcendentals=0
    )


def column_place(blocks):
    span = blocks // COLUMNS
    head, blk = lax.axis_index("head"), lax.axis_index("blk")
    plane, rest = lax.div(blk, span), lax.rem(blk, span)
    planes = [lax.rem(plane + d, COLUMNS) for d in range(COLUMNS)]
    return plane, planes, [(head, p * span + rest) for p in planes]


class Chain:
    def __init__(self, source, dst, send_sems, recv_sems, blocks):
        span = blocks // COLUMNS
        head, blk = lax.axis_index("head"), lax.axis_index("blk")
        plane, rest = lax.div(blk, span), lax.rem(blk, span)
        self.source, self.dst, self.plane = source, dst, plane
        self.send_sems, self.recv_sems = send_sems, recv_sems
        after = jnp.minimum(plane + 1, COLUMNS - 1)
        before = jnp.maximum(plane - 1, 0)
        self.line = [
            (plane < COLUMNS - 1, (head, after * span + rest)),
            (plane > 0, (head, before * span + rest)),
        ]
        lower = plane < COLUMNS // 2
        self.slabs = [
            plane,
            plane + 1 - 2 * lax.rem(plane, 2),
            jnp.where(lower, 2, 1),
            jnp.where(lower, 3, 0),
        ]

    def copy(self, k, way):
        slab = self.slabs[k]
        place = self.dst.at[slab]
        return remote(
            self.source if k == 0 else place,
            place,
            self.send_sems.at[k, way],
            self.recv_sems.at[slab],
            self.line[way][1],
        )

    def onward(self, k):
        if k == 0:
            return [self.line[0][0], self.line[1][0]]
        from_before = self.slabs[k] < self.plane
        return [
            from_before & self.line[0][0],
            jnp.logical_not(from_before) & self.line[1][0],
        ]

    def pass_on(self, k):
        for way, there in enumerate(self.onward(k)):

            @pl.when(there)
            def _():
                self.copy(k, way).start()

    def arrive(self, k):
        self.copy(k, 0).wait_recv()
        self.pass_on(k)

    def finish(self):
        for k in range(COLUMNS):
            for way, there in enumerate(self.onward(k)):

                @pl.when(there)
                def _():
                    self.copy(k, way).wait_send()


def column_start(src, gather, dst, own_sem, send_sems, recv_sems, where):
    plane, planes, peers = where
    own = pltpu.make_async_copy(src if gather else src.at[plane], dst.at[plane], own_sem)
    own.start()
    copies = [own]
    for d in (2, 1, 3):
        copy = remote(
            src if gather else src.at[planes[d]],
            dst.at[plane],
            send_sems.at[d],
            recv_sems.at[d],
            peers[d],
        )
        copy.start()
        copies.append(copy)
    return copies


def column_exchange(arrays, gathers, blocks, collective_id, cost=16):
    count = len(arrays)
    slabs = [
        tuple(values.shape if gather else values.shape[1:])
        for values, gather in zip(arrays, gathers)
    ]

    def body(*refs):
        srcs, dsts = refs[:count], refs[count : 2 * count]
        own_sems, send_sems, recv_sems = refs[2 * count :]
        where = column_place(blocks)
        greet(where[2][1:])
        copies = []
        for n in range(count):
            copies += column_start(
                srcs[n],
                gathers[n],
                dsts[n],
                own_sems.at[n],
                send_sems.at[n],
                recv_sems.at[n],
                where,
            )
        for copy in copies:
            copy.wait()

    return pl.pallas_call(
        body,
        out_shape=[
            jax.ShapeDtypeStruct((COLUMNS,) + slab, values.dtype)
            for values, slab in zip(arrays, slabs)
        ],
        in_specs=[ANY] * count,
        out_specs=[ANY] * count,
        scratch_shapes=[DMA((count,)), DMA((count, COLUMNS)), DMA((count, COLUMNS))],
        compiler_params=comm_params(collective_id),
        cost_estimate=lasting(cost),
    )(*arrays)


def column_gather(values, blocks, collective_id, cost=14):
    def body(src, dst, own_sem, send_sems, recv_sems):
        chain = Chain(src, dst, send_sems, recv_sems, blocks)
        greet([], chain.line)
        chain.pass_on(0)
        own = pltpu.make_async_copy(src, dst.at[chain.plane], own_sem)
        own.start()
        for k in range(1, COLUMNS):
            chain.arrive(k)
        own.wait()
        chain.finish()

    return pl.pallas_call(
        body,
        out_shape=jax.ShapeDtypeStruct((COLUMNS,) + tuple(values.shape), values.dtype),
        in_specs=[ANY],
        out_specs=ANY,
        scratch_shapes=[DMA, DMA((COLUMNS, 2)), DMA((COLUMNS,))],
        compiler_params=comm_params(collective_id),
        cost_estimate=lasting(cost),
    )(values)


def final_exchange(shares, rows, blocks, collective_id, cost=9):
    span = blocks // COLUMNS
    count = len(shares)
    total = 2 * count

    def body(*refs):
        srcs, dsts = refs[:total], refs[total : 2 * total]
        own_sems, send_sems, recv_sems, row_send, row_recv = refs[2 * total :]
        where = column_place(blocks)
        head, blk = lax.axis_index("head"), lax.axis_index("blk")
        plane, rest = lax.div(blk, span), lax.rem(blk, span)
        flat = head * blocks + blk
        goal = (plane * 2 + head) * span + rest
        from_plane = lax.div(flat, span)
        origin = (lax.rem(from_plane, 2), lax.div(from_plane, 2) * span + lax.rem(flat, span))
        goal_place = (lax.div(goal, blocks), lax.rem(goal, blocks))
        away = goal != flat
        greet(where[2][1:], [(away, goal_place), (away, origin)])
        copies = []
        for n in range(count):
            copies += column_start(
                srcs[n],
                False,
                dsts[n],
                own_sems.at[n],
                send_sems.at[n],
                recv_sems.at[n],
                where,
            )

        def row_copy(n):
            return remote(
                srcs[n], dsts[n], row_send.at[n - count], row_recv.at[n - count], goal_place
            )

        def row_stay(n):
            return pltpu.make_async_copy(srcs[n], dsts[n], own_sems.at[n])

        for n in range(count, total):

            @pl.when(away)
            def _():
                row_copy(n).start()

            @pl.when(jnp.logical_not(away))
            def _():
                row_stay(n).start()

        for copy in copies:
            copy.wait()
        for n in range(count, total):

            @pl.when(away)
            def _():
                row_copy(n).wait()

            @pl.when(jnp.logical_not(away))
            def _():
                row_stay(n).wait()

    arrays = list(shares) + list(rows)
    return pl.pallas_call(
        body,
        out_shape=[make(values.shape, values.dtype) for values in arrays],
        in_specs=[ANY] * total,
        out_specs=[ANY] * total,
        scratch_shapes=[
            DMA((total,)),
            DMA((count, COLUMNS)),
            DMA((count, COLUMNS)),
            DMA((count,)),
            DMA((count,)),
        ],
        compiler_params=comm_params(collective_id),
        cost_estimate=lasting(cost),
    )(*arrays)


def plane_place(blocks):
    span = blocks // COLUMNS
    width = span // 2
    head, blk = lax.axis_index("head"), lax.axis_index("blk")
    plane, rest = lax.div(blk, span), lax.rem(blk, span)
    x, core = lax.div(rest, 2), lax.rem(rest, 2)
    first = plane * span
    right = [lax.rem(x + d, width) for d in range(width)]
    left = [lax.rem(x - d + width, width) for d in range(width)]
    x_peers = [(head, first + right[d] * 2 + core) for d in range(width)]
    y_peer = (1 - head, blk)
    core_peer = (head, first + x * 2 + 1 - core)
    return head, rest, core, left, x_peers, y_peer, core_peer


class PlaneRun:
    def __init__(self, srcs, dsts, own_sems, send_sems, recv_sems, pass_sems, land_sems, where):
        self.srcs, self.dsts = srcs, dsts
        self.own_sems, self.send_sems, self.recv_sems = own_sems, send_sems, recv_sems
        self.pass_sems, self.land_sems = pass_sems, land_sems
        self.head, self.rest, self.core, self.left, self.x_peers, self.y_peer, self.core_peer = (
            where
        )
        self.width = len(self.x_peers)
        self.sends, self.passes, self.owns = [], [], []

    def place(self, n, h, dy, d):
        half = self.srcs[n].shape[0] // 2
        row = self.head if dy == 0 else 1 - self.head
        return self.dsts[n].at[row, pl.ds(h * half, half), self.left[d] * 2 + self.core]

    def held(self, n, h, dy, d):
        half = self.srcs[n].shape[0] // 2
        if dy == 0 and d == 0:
            return self.srcs[n].at[pl.ds(h * half, half)]
        return self.place(n, h, dy, d)

    def send(self, n, h, dy, d, peer, to_dy, to_d):
        copy = remote(
            self.held(n, h, dy, d),
            self.place(n, h, dy, d),
            self.send_sems.at[len(self.sends)],
            self.recv_sems.at[n, h, to_dy, to_d],
            peer,
        )
        copy.start()
        self.sends.append(copy)

    def hand_over(self, n, h, dy, d):
        copy = remote(
            self.held(n, h, dy, d),
            self.place(n, h, dy, d),
            self.pass_sems.at[n, h, dy, d],
            self.land_sems.at[n, h, dy, d],
            self.core_peer,
        )
        copy.start()
        self.passes.append(copy)

    def arrived(self, n, h, dy, d):
        at = self.place(n, h, dy, d)
        remote(
            at, at, self.send_sems.at[0], self.recv_sems.at[n, h, dy, d], self.y_peer
        ).wait_recv()

    def first(self, n):
        own = pltpu.make_async_copy(
            self.srcs[n], self.dsts[n].at[self.head, :, self.rest], self.own_sems.at[n]
        )
        own.start()
        self.owns.append(own)
        for d in range(1, self.width):
            self.send(n, 0, 0, 0, self.x_peers[d], 0, d)
        self.send(n, 1, 0, 0, self.y_peer, 1, 0)
        self.send(n, 0, 0, 0, self.y_peer, 1, 0)
        for d in range(1, self.width):
            self.send(n, 1, 0, 0, self.x_peers[d], 0, d)
        self.hand_over(n, 0, 0, 0)
        self.hand_over(n, 1, 0, 0)

    def second(self, n):
        for d in range(1, self.width):
            self.arrived(n, 0, 0, d)
            self.send(n, 0, 0, d, self.y_peer, 1, d)
            self.hand_over(n, 0, 0, d)
        self.arrived(n, 1, 1, 0)
        for d in range(1, self.width):
            self.send(n, 1, 1, 0, self.x_peers[d], 1, d)
        self.hand_over(n, 1, 1, 0)

    def third(self, n):
        self.arrived(n, 0, 1, 0)
        self.hand_over(n, 0, 1, 0)
        for d in range(1, self.width):
            self.arrived(n, 1, 0, d)
            self.hand_over(n, 1, 0, d)
        for d in range(1, self.width):
            self.arrived(n, 0, 1, d)
            self.hand_over(n, 0, 1, d)
            self.arrived(n, 1, 1, d)
            self.hand_over(n, 1, 1, d)

    def last(self):
        for own in self.owns:
            own.wait()
        for copy in self.passes:
            copy.wait()
        for copy in self.sends:
            copy.wait_send()


def plane_scratch(count, blocks):
    width = blocks // COLUMNS // 2
    links = 4 * (width - 1) + 2
    return [DMA((count,)), DMA((count * links,))] + [DMA((count, 2, 2, width))] * 3


def plane_shapes(arrays, blocks):
    return [
        jax.ShapeDtypeStruct(
            (2, values.shape[0], blocks // COLUMNS) + tuple(values.shape[1:]), values.dtype
        )
        for values in arrays
    ]


def start_gather(packs, tokens, blocks, collective_id, cost=28):
    count = len(packs)

    def body(*refs):
        srcs, refs = refs[: count + 1], refs[count + 1 :]
        wholes, refs = refs[:count], refs[count:]
        columns, refs = refs[: count + 1], refs[count + 1 :]
        own_sems, send_sems, recv_sems, chain_send, chain_recv, *plane_sems = refs
        column, plane = column_place(blocks), plane_place(blocks)
        greet(column[2][1:] + plane[4][1:] + [plane[5], plane[6]])
        run = PlaneRun(columns[:count], wholes, *plane_sems, plane)
        chain = Chain(srcs[count], columns[count], chain_send, chain_recv, blocks)
        stay = pltpu.make_async_copy(
            srcs[count], columns[count].at[chain.plane], own_sems.at[count]
        )

        def begin(n):
            return column_start(
                srcs[n],
                False,
                columns[n],
                own_sems.at[n],
                send_sems.at[n],
                recv_sems.at[n],
                column,
            )

        waits = [begin(0), begin(1)]
        for n in range(count):
            for copy in waits[n]:
                copy.wait()
            if n + 2 < count:
                waits.append(begin(n + 2))
            elif n + 2 == count:
                chain.pass_on(0)
                stay.start()
            run.first(n)
        run.second(0)
        run.second(1)
        chain.arrive(1)
        for n in range(2, count):
            run.second(n)
        run.third(0)
        run.third(1)
        chain.arrive(2)
        for n in range(2, count):
            run.third(n)
        chain.arrive(3)
        run.last()
        stay.wait()
        chain.finish()

    results = pl.pallas_call(
        body,
        out_shape=plane_shapes(packs, blocks)
        + [jax.ShapeDtypeStruct(pack.shape, pack.dtype) for pack in packs]
        + [jax.ShapeDtypeStruct((COLUMNS,) + tokens.shape, tokens.dtype)],
        in_specs=[ANY] * (count + 1),
        out_specs=[ANY] * (2 * count + 1),
        scratch_shapes=[
            DMA((count + 1,)),
            DMA((count, COLUMNS)),
            DMA((count, COLUMNS)),
            DMA((COLUMNS, 2)),
            DMA((COLUMNS,)),
        ]
        + plane_scratch(count, blocks),
        compiler_params=comm_params(collective_id),
        cost_estimate=lasting(cost),
    )(*packs, tokens)
    return results[:count], results[-1]


def project_gather(source, pack, smalls, heads, scale, blocks, collective_id, cost=22):
    span = blocks // COLUMNS
    width = span // 2
    chained = smalls is not None
    rows, features = source.shape[-2:]
    wide = heads * LANES
    kv_at, tail_at = features, features + wide
    tail_cols = pack.shape[1] - tail_at
    own_out = tail_cols - LANES // 2
    dim = LANES // 2
    half = rows // 2
    small_rows = 8 * LAYERS
    links = 4 * (width - 1) + 2

    def body(*refs):
        if chained:
            source_ref, pack_ref, small_ref = refs[:3]
            refs = refs[3:]
            small_out = None
        else:
            source_ref, pack_ref = refs[:2]
            small_out, refs = refs[2], refs[3:]
        column_out, query_ref, query_w_out, out_w_out, kv_ref = refs[:5]
        column_ref, query_w_ref, out_w_ref, kv_own, own_sems, send_sems, recv_sems = refs[5:12]
        pass_sems, land_sems, z_send, z_recv, keep_sems = refs[12:]
        head, rest, core, left, x_peers, y_peer, core_peer = plane_place(blocks)
        plane = lax.div(lax.axis_index("blk"), span)
        sends, passes, owns = [], [], []
        near = x_peers[1:] + [y_peer, core_peer]
        if chained:
            chain = Chain(source_ref, column_ref, z_send, z_recv, blocks)
            slabs = chain.slabs
            greet(near, chain.line)
            chain.pass_on(0)
        else:
            slabs = list(range(COLUMNS))
            greet(near)

        tail = pack_ref[:, tail_at:]
        if not chained:
            small = tail[:, tail_cols - LANES :].astype(jnp.float32).T
            at = own_out - (tail_cols - LANES)
            small = small[at : at + small_rows]
            small_out[...] = small

        def place(k, h, dy, d):
            row = head if dy == 0 else 1 - head
            return kv_ref.at[row, slabs[k], left[d] * 2 + core, pl.ds(h * half, half)]

        def held(k, h, dy, d):
            if dy == 0 and d == 0:
                return kv_own.at[k, pl.ds(h * half, half)]
            return place(k, h, dy, d)

        def send(k, h, dy, d, peer, to_dy, to_d):
            copy = remote(
                held(k, h, dy, d),
                place(k, h, dy, d),
                send_sems.at[len(sends)],
                recv_sems.at[k, h, to_dy, to_d],
                peer,
            )
            copy.start()
            sends.append(copy)

        def hand_over(k, h, dy, d):
            copy = remote(
                held(k, h, dy, d),
                place(k, h, dy, d),
                pass_sems.at[k, h, dy, d],
                land_sems.at[k, h, dy, d],
                core_peer,
            )
            copy.start()
            passes.append(copy)

        def arrived(k, h, dy, d):
            at = place(k, h, dy, d)
            remote(at, at, send_sems.at[0], recv_sems.at[k, h, dy, d], y_peer).wait_recv()

        def first(k):
            slab = slabs[k]
            if not chained:
                x = source_ref[slab].astype(jnp.float32)
                xn = (x * unit_scale(x) * small[0:1]).astype(jnp.bfloat16)
                column_ref[slab] = xn
            elif k == 0:
                xn = source_ref[...]
                column_ref[slab] = xn
            else:
                chain.arrive(k)
                xn = column_ref[slab]
            kv = dot32(xn, pack_ref[:, kv_at:tail_at])
            kv_own[k] = kv.astype(jnp.bfloat16)
            own = pltpu.make_async_copy(
                kv_own.at[k], kv_ref.at[head, slab, rest], own_sems.at[k]
            )
            own.start()
            owns.append(own)
            for d in range(1, width):
                send(k, 0, 0, 0, x_peers[d], 0, d)
            send(k, 1, 0, 0, y_peer, 1, 0)
            send(k, 0, 0, 0, y_peer, 1, 0)
            for d in range(1, width):
                send(k, 1, 0, 0, x_peers[d], 0, d)
            hand_over(k, 0, 0, 0)
            hand_over(k, 1, 0, 0)

        def second(k):
            for d in range(1, width):
                arrived(k, 0, 0, d)
                send(k, 0, 0, d, y_peer, 1, d)
                hand_over(k, 0, 0, d)
            arrived(k, 1, 1, 0)
            for d in range(1, width):
                send(k, 1, 1, 0, x_peers[d], 1, d)
            hand_over(k, 1, 1, 0)

        def third(k):
            arrived(k, 0, 1, 0)
            hand_over(k, 0, 1, 0)
            for d in range(1, width):
                arrived(k, 1, 0, d)
                hand_over(k, 1, 0, d)
            for d in range(1, width):
                arrived(k, 0, 1, d)
                hand_over(k, 0, 1, d)
                arrived(k, 1, 1, d)
                hand_over(k, 1, 1, d)

        def queries():
            low = lax.broadcasted_iota(jnp.int32, (tail_cols, wide), 0)
            target = lax.broadcasted_iota(jnp.int32, (tail_cols, wide), 1)
            goal = lax.div(low, dim) * LANES + lax.rem(low, dim)
            to_low = ((goal == target) & (low < own_out)).astype(jnp.bfloat16)
            query_w = dot32(tail, to_low).astype(jnp.bfloat16)
            query_w_ref[...] = query_w
            out_rows = pack_ref[pl.ds(pl.multiple_of(plane * own_out, 64), own_out), :features]
            pieces = []
            for h in range(heads):
                pieces += [jnp.zeros((dim, features), jnp.bfloat16), out_rows[h * dim : (h + 1) * dim]]
            out_w_ref[...] = jnp.concatenate(pieces, axis=0)
            for k in range(COLUMNS):
                slab = slabs[k]
                query = dot32(column_ref[slab], query_w).astype(jnp.bfloat16)
                query = query.astype(jnp.float32) * scale
                query_ref[slab] = query.astype(jnp.bfloat16)
            for n, (src, dst) in enumerate(
                (
                    (column_ref, column_out),
                    (query_w_ref, query_w_out),
                    (out_w_ref, out_w_out),
                )
            ):
                copy = pltpu.make_async_copy(src, dst, keep_sems.at[n])
                copy.start()
                owns.append(copy)

        for t in range(COLUMNS + 2):
            if t < COLUMNS:
                first(t)
            elif t == COLUMNS:
                queries()
            if 0 <= t - 1 < COLUMNS:
                second(t - 1)
            if 0 <= t - 2 < COLUMNS:
                third(t - 2)
        for copy in owns + passes:
            copy.wait()
        for copy in sends:
            copy.wait_send()
        if chained:
            chain.finish()

    shapes = [
        jax.ShapeDtypeStruct((COLUMNS, rows, features), jnp.bfloat16),
        jax.ShapeDtypeStruct((COLUMNS, rows, wide), jnp.bfloat16),
        jax.ShapeDtypeStruct((features, wide), jnp.bfloat16),
        jax.ShapeDtypeStruct((wide, features), jnp.bfloat16),
        jax.ShapeDtypeStruct((2, COLUMNS, span, rows, wide), jnp.bfloat16),
    ]
    operands = [source, pack]
    if chained:
        operands.append(smalls)
    else:
        shapes = [jax.ShapeDtypeStruct((small_rows, features), jnp.float32)] + shapes
    results = pl.pallas_call(
        body,
        out_shape=shapes,
        in_specs=[VMEM] * len(operands),
        out_specs=([] if chained else [VMEM]) + [HBM, VMEM, HBM, HBM, ANY],
        scratch_shapes=[
            pltpu.VMEM((COLUMNS, rows, features), jnp.bfloat16),
            pltpu.VMEM((features, wide), jnp.bfloat16),
            pltpu.VMEM((wide, features), jnp.bfloat16),
            pltpu.VMEM((COLUMNS, rows, wide), jnp.bfloat16),
            DMA((COLUMNS,)),
            DMA((COLUMNS * links,)),
            DMA((COLUMNS, 2, 2, width)),
            DMA((COLUMNS, 2, 2, width)),
            DMA((COLUMNS, 2, 2, width)),
            DMA((COLUMNS, 2)),
            DMA((COLUMNS,)),
            DMA((3,)),
        ],
        compiler_params=comm_params(
            collective_id,
            operands + shapes[:-1] + [make((COLUMNS, rows, wide), jnp.bfloat16)],
            3 * SPARE_BYTES,
        ),
        cost_estimate=lasting(cost),
    )(*operands)
    return list(results) + [smalls] if chained else list(results[1:]) + [results[0]]


def plane_reduce(arrays, blocks, collective_id, cost=25):
    span = blocks // COLUMNS
    width = span // 2
    count = len(arrays)
    shapes = [(values.shape[1],) + tuple(values.shape[3:]) for values in arrays]

    def body(*refs):
        srcs, outs, refs = refs[:count], refs[count : 2 * count], refs[2 * count :]
        scratch = [refs[8 * n : 8 * n + 8] for n in range(count)]
        core_send, core_recv, link_send, link_recv = refs[8 * count :]
        head, blk = lax.axis_index("head"), lax.axis_index("blk")
        plane, rest = lax.div(blk, span), lax.rem(blk, span)
        x, core = lax.div(rest, 2), lax.rem(rest, 2)
        first = plane * span
        right = [lax.rem(x + d, width) for d in range(width)]
        x_peers = [(head, first + right[d] * 2 + core) for d in range(width)]
        y_peer = (1 - head, blk)
        core_peer = (head, first + x * 2 + 1 - core)
        greet(x_peers[1:] + [y_peer, core_peer])

        def wide(ref, *at):
            return ref[at].astype(jnp.float32)

        starts = {}
        for n in range(count):
            half = shapes[n][0] // 2
            for h in range(2):
                copy = remote(
                    srcs[n].at[:, pl.ds(h * half, half), :, 1 - core],
                    scratch[n][0].at[:, pl.ds(h * half, half)],
                    core_send.at[n, h],
                    core_recv.at[n, h],
                    core_peer,
                )
                copy.start()
                starts[n, h] = copy

        sends, yas, ybs, xbs = {}, {}, {}, {}
        for n in range(count):
            src, half, kind = srcs[n], shapes[n][0] // 2, arrays[n].dtype
            core_in, summed, xa_in, _, _, yb_in, _, _ = scratch[n]

            def core_sum(h):
                def step(i, _):
                    yy = lax.div(i, half * width)
                    zz = lax.div(lax.rem(i, half * width), width) + h * half
                    xx = lax.rem(i, width)
                    total = wide(src, yy, zz, xx, core) + wide(core_in, yy, zz, xx)
                    summed[yy, zz, xx] = total.astype(kind)
                    return 0

                lax.fori_loop(0, 2 * half * width, step, 0)

            starts[n, 0].wait_recv()
            core_sum(0)
            for d in range(1, width):
                copy = remote(
                    summed.at[:, pl.ds(0, half), right[d]],
                    xa_in.at[d],
                    link_send.at[n, 0, d],
                    link_recv.at[n, 0, d],
                    x_peers[d],
                )
                copy.start()
                sends[n, d] = copy
            starts[n, 1].wait_recv()
            core_sum(1)
            ybs[n] = remote(
                summed.at[1 - head, pl.ds(half, half)],
                yb_in,
                link_send.at[n, 1, 0],
                link_recv.at[n, 1, 0],
                y_peer,
            )
            ybs[n].start()
        for n in range(count):
            half, kind = shapes[n][0] // 2, arrays[n].dtype
            _, summed, xa_in, ya_out, ya_in, yb_in, xb_out, xb_in = scratch[n]
            for d in range(1, width):
                sends[n, d].wait_recv()

            def a_step(zz, _):
                total = wide(summed, 1 - head, zz, x)
                for d in range(1, width):
                    total = total + wide(xa_in, d, 1 - head, zz)
                ya_out[zz] = total.astype(kind)
                return 0

            lax.fori_loop(0, half, a_step, 0)
            yas[n] = remote(
                ya_out, ya_in, link_send.at[n, 0, 0], link_recv.at[n, 0, 0], y_peer
            )
            yas[n].start()
            ybs[n].wait_recv()
            for d in range(1, width):

                def b_step(zz, _):
                    total = wide(summed, head, half + zz, right[d]) + wide(yb_in, zz, right[d])
                    xb_out[d, zz] = total.astype(kind)
                    return 0

                lax.fori_loop(0, half, b_step, 0)
                xbs[n, d] = remote(
                    xb_out.at[d],
                    xb_in.at[d],
                    link_send.at[n, 1, d],
                    link_recv.at[n, 1, d],
                    x_peers[d],
                )
                xbs[n, d].start()
        for n in range(count):
            out, half, kind = outs[n], shapes[n][0] // 2, arrays[n].dtype
            _, summed, xa_in, _, ya_in, yb_in, _, xb_in = scratch[n]
            yas[n].wait_recv()

            def a_last(zz, _):
                total = wide(summed, head, zz, x) + wide(ya_in, zz)
                for d in range(1, width):
                    total = total + wide(xa_in, d, head, zz)
                out[zz] = total.astype(kind)
                return 0

            lax.fori_loop(0, half, a_last, 0)
            for d in range(1, width):
                xbs[n, d].wait_recv()

            def b_last(zz, _):
                total = wide(summed, head, half + zz, x) + wide(yb_in, zz, x)
                for d in range(1, width):
                    total = total + wide(xb_in, d, zz)
                out[half + zz] = total.astype(kind)
                return 0

            lax.fori_loop(0, half, b_last, 0)
        for group in (starts, sends, yas, ybs, xbs):
            for copy in group.values():
                copy.wait_send()

    scratch = []
    for (slabs, *tile), values in zip(shapes, arrays):
        tile, half, kind = tuple(tile), slabs // 2, values.dtype
        scratch += [
            pltpu.VMEM((2, slabs, width) + tile, kind),
            pltpu.VMEM((2, slabs, width) + tile, kind),
            pltpu.VMEM((width, 2, half) + tile, kind),
            pltpu.VMEM((half,) + tile, kind),
            pltpu.VMEM((half,) + tile, kind),
            pltpu.VMEM((half, width) + tile, kind),
            pltpu.VMEM((width, half) + tile, kind),
            pltpu.VMEM((width, half) + tile, kind),
        ]
    return pl.pallas_call(
        body,
        out_shape=[
            jax.ShapeDtypeStruct(shape, values.dtype) for shape, values in zip(shapes, arrays)
        ],
        in_specs=[VMEM] * count,
        out_specs=[VMEM] * count,
        scratch_shapes=scratch
        + [DMA((count, 2)), DMA((count, 2)), DMA((count, 2, width)), DMA((count, 2, width))],
        compiler_params=comm_params(
            collective_id, scratch + 2 * [make(a.shape, a.dtype) for a in arrays]
        ),
        cost_estimate=lasting(cost),
    )(
        *[
            values.reshape((2, values.shape[1], width, 2) + tuple(values.shape[3:]))
            for values in arrays
        ]
    )


def reduce_project(dkv_all, dq, query_w, pack, blocks, collective_id, cost=26):
    span = blocks // COLUMNS
    width = span // 2
    rows, wide = dkv_all.shape[3:]
    half = rows // 2
    features = query_w.shape[0]
    kind = dkv_all.dtype

    def body(
        src,
        dq_ref,
        w_ref,
        pack_ref,
        dkv_ref,
        dxn_ref,
        core_in,
        summed,
        xa_in,
        ya_out,
        ya_in,
        yb_in,
        xb_out,
        xb_in,
        share,
        core_send,
        core_recv,
        link_send,
        link_recv,
        z_send,
        z_recv,
    ):
        head, _, core, _, x_peers, y_peer, core_peer = plane_place(blocks)
        plane, planes, z_peers = column_place(blocks)
        x = lax.div(lax.rem(lax.axis_index("blk"), span), 2)
        right = [lax.rem(x + d, width) for d in range(width)]
        greet(x_peers[1:] + [y_peer, core_peer] + z_peers[1:])
        order = (2, 1, 3, 0)
        copies = []

        def begin(copy):
            copy.start()
            copies.append(copy)
            return copy

        def wide_of(ref, *at):
            return ref[at].astype(jnp.float32)

        top, low = pl.ds(0, half), pl.ds(half, half)
        starts = []

        def cross(k):
            starts.append(
                begin(
                    remote(
                        src.at[:, planes[order[k]], :, 1 - core],
                        core_in.at[k],
                        core_send.at[k],
                        core_recv.at[k],
                        core_peer,
                    )
                )
            )

        cross(0)
        cross(1)
        xas, yas, ybs, xbs, z_copies = {}, {}, {}, {}, []

        def first(k):
            starts[k].wait_recv()
            if k + 2 < COLUMNS:
                cross(k + 2)

            def step(i, _):
                yy, xx = lax.div(i, width), lax.rem(i, width)
                total = wide_of(src, yy, planes[order[k]], xx, core) + wide_of(core_in, k, yy, xx)
                summed[k, yy, xx] = total.astype(kind)
                return 0

            lax.fori_loop(0, 2 * width, step, 0)
            for d in range(1, width):
                xas[k, d] = begin(
                    remote(
                        summed.at[k, :, right[d], top],
                        xa_in.at[k, d],
                        link_send.at[k, 0, d],
                        link_recv.at[k, 0, d],
                        x_peers[d],
                    )
                )
            ybs[k] = begin(
                remote(
                    summed.at[k, 1 - head, :, low],
                    yb_in.at[k],
                    link_send.at[k, 1, 0],
                    link_recv.at[k, 1, 0],
                    y_peer,
                )
            )

        def second(k):
            total = wide_of(summed, k, 1 - head, x, top)
            for d in range(1, width):
                xas[k, d].wait_recv()
                total = total + wide_of(xa_in, k, d, 1 - head)
            ya_out[k] = total.astype(kind)
            yas[k] = begin(
                remote(
                    ya_out.at[k],
                    ya_in.at[k],
                    link_send.at[k, 0, 0],
                    link_recv.at[k, 0, 0],
                    y_peer,
                )
            )
            ybs[k].wait_recv()
            for d in range(1, width):
                total = wide_of(summed, k, head, right[d], low) + wide_of(yb_in, k, right[d])
                xb_out[k, d] = total.astype(kind)
                xbs[k, d] = begin(
                    remote(
                        xb_out.at[k, d],
                        xb_in.at[k, d],
                        link_send.at[k, 1, d],
                        link_recv.at[k, 1, d],
                        x_peers[d],
                    )
                )

        def third(k):
            slab = planes[order[k]]
            yas[k].wait_recv()
            total = wide_of(summed, k, head, x, top) + wide_of(ya_in, k)
            for d in range(1, width):
                total = total + wide_of(xa_in, k, d, head)
            dkv_ref[slab, top] = total.astype(kind)
            total = wide_of(summed, k, head, x, low) + wide_of(yb_in, k, x)
            for d in range(1, width):
                xbs[k, d].wait_recv()
                total = total + wide_of(xb_in, k, d)
            dkv_ref[slab, low] = total.astype(kind)
            part = (
                dot32(dq_ref[slab], w_ref[...], LAST)
                + dot32(dkv_ref[slab], pack_ref[:, features : features + wide], LAST)
            ).astype(kind)
            if order[k] == 0:
                dxn_ref[plane] = part
            else:
                share[k] = part
                z_copies.append(
                    begin(
                        remote(
                            share.at[k],
                            dxn_ref.at[plane],
                            z_send.at[order[k]],
                            z_recv.at[order[k]],
                            z_peers[order[k]],
                        )
                    )
                )

        for t in range(COLUMNS + 2):
            if t < COLUMNS:
                first(t)
            if 0 <= t - 1 < COLUMNS:
                second(t - 1)
            if 0 <= t - 2 < COLUMNS:
                third(t - 2)
        for copy in z_copies:
            copy.wait_recv()
        for copy in copies:
            copy.wait_send()

    tile = (rows, wide)
    part = (half, wide)
    scratch = [
        pltpu.VMEM((COLUMNS, 2, width) + tile, kind),
        pltpu.VMEM((COLUMNS, 2, width) + tile, kind),
        pltpu.VMEM((COLUMNS, width, 2) + part, kind),
        pltpu.VMEM((COLUMNS,) + part, kind),
        pltpu.VMEM((COLUMNS,) + part, kind),
        pltpu.VMEM((COLUMNS, width) + part, kind),
        pltpu.VMEM((COLUMNS, width) + part, kind),
        pltpu.VMEM((COLUMNS, width) + part, kind),
        pltpu.VMEM((COLUMNS, rows, features), kind),
    ]
    shapes = [make((COLUMNS,) + tile, kind), make((COLUMNS, rows, features), kind)]
    return pl.pallas_call(
        body,
        out_shape=shapes,
        in_specs=[VMEM] * 4,
        out_specs=[VMEM] * 2,
        scratch_shapes=scratch
        + [
            DMA((COLUMNS,)),
            DMA((COLUMNS,)),
            DMA((COLUMNS, 2, width)),
            DMA((COLUMNS, 2, width)),
            DMA((COLUMNS,)),
            DMA((COLUMNS,)),
        ],
        compiler_params=comm_params(
            collective_id, scratch + shapes + [dkv_all, dq, query_w, pack]
        ),
        cost_estimate=lasting(cost),
    )(dkv_all.reshape((2, COLUMNS, width, 2) + tile), dq, query_w, pack)


NEGATIVE = -1e30
EPSILON = 1e-06
KEYS = 1024
LANES = 128
LAST = (((1,), (1,)), ((), ()))
FIRST = (((0,), (0,)), ((), ()))


def dot32(a, b, dims=(((1,), (0,)), ((), ()))):
    return lax.dot_general(a, b, dims, preferred_element_type=jnp.float32)


def visible(key_base, query_base, keys, queries, starts):
    key_pos = key_base + lax.broadcasted_iota(jnp.int32, (keys, queries), 0)
    query_pos = query_base + lax.broadcasted_iota(jnp.int32, (keys, queries), 1)
    return (key_pos <= query_pos) & (key_pos >= starts)


def block_bounds(starts, bases, rows):
    return jnp.stack(
        [
            lax.div(starts[:, 0], KEYS),
            lax.div(bases + rows - 1, KEYS),
            bases,
            lax.div(starts[:, rows - 1], KEYS),
        ],
        axis=1,
    )


def over_chunks(bounds_ref, i, step, carry):
    low, high, edge = bounds_ref[i, 0], bounds_ref[i, 1], bounds_ref[i, 3]
    carry = step(high, True, carry)
    inner = jnp.maximum(high - 1 - edge, 0)
    carry = lax.fori_loop(0, inner, lambda t, c: step(high - 1 - t, False, c), carry)
    below = high - 1 - inner
    return lax.fori_loop(0, below - low + 1, lambda t, c: step(below - t, True, c), carry)


def attend(bounds, queries, kv_all, starts):
    count, rows, width = queries.shape
    heads = width // LANES

    def body(bounds_ref, q_ref, kv_ref, start_ref, out_ref, attn_ref):
        i = pl.program_id(0)
        base = bounds_ref[i, 2]
        start_row = start_ref[0]
        q = [q_ref[0, :, h * LANES : (h + 1) * LANES] for h in range(heads)]

        def step(chunk, masked, carry):
            at = pl.multiple_of(chunk * KEYS, KEYS)
            if masked:
                ok = visible(chunk * KEYS, base, KEYS, rows, start_row)
            kvs = [kv_ref[pl.ds(at, KEYS), h * LANES : (h + 1) * LANES] for h in range(heads)]
            scores = [dot32(kvs[h], q[h], LAST) for h in range(heads)]
            if masked:
                scores = [jnp.where(ok, s, NEGATIVE) for s in scores]
            tops = [
                jnp.maximum(carry[h][0], jnp.max(scores[h], axis=0, keepdims=True))
                for h in range(heads)
            ]
            weights = [jnp.exp(scores[h] - tops[h]) for h in range(heads)]
            shrinks = [jnp.exp(carry[h][0] - tops[h]) for h in range(heads)]
            totals = [
                carry[h][1] * shrinks[h] + jnp.sum(weights[h], axis=0, keepdims=True)
                for h in range(heads)
            ]
            accs = [
                carry[h][2] * shrinks[h] + dot32(kvs[h], weights[h].astype(jnp.bfloat16), FIRST)
                for h in range(heads)
            ]
            return tuple(zip(tops, totals, accs))

        empty = tuple(
            (
                jnp.full((1, rows), NEGATIVE, jnp.float32),
                jnp.zeros((1, rows), jnp.float32),
                jnp.zeros((LANES, rows), jnp.float32),
            )
            for h in range(heads)
        )
        done = over_chunks(bounds_ref, i, step, empty)
        lane = lax.broadcasted_iota(jnp.int32, (LANES, rows), 0)
        narrow = []
        for h in range(heads):
            top, total, acc = done[h]
            value = jnp.where(lane < LANES // 2, top + jnp.log(total), acc / total)
            out_ref[0, :, h * LANES : (h + 1) * LANES] = value.T
            narrow.append(value[LANES // 2 :])
        attn_ref[0] = jnp.concatenate(narrow, axis=0).T.astype(jnp.bfloat16)

    return pl.pallas_call(
        body,
        out_shape=(
            jax.ShapeDtypeStruct((count, rows, width), jnp.float32),
            jax.ShapeDtypeStruct((count, rows, width // 2), jnp.bfloat16),
        ),
        grid_spec=pltpu.PrefetchScalarGridSpec(
            num_scalar_prefetch=1,
            grid=(count,),
            in_specs=[
                pl.BlockSpec((1, rows, width), lambda i, b: (i, 0, 0)),
                pl.BlockSpec(kv_all.shape, lambda i, b: (0, 0)),
                pl.BlockSpec((1, 1, rows), lambda i, b: (i, 0, 0)),
            ],
            out_specs=(
                pl.BlockSpec((1, rows, width), lambda i, b: (i, 0, 0)),
                pl.BlockSpec((1, rows, width // 2), lambda i, b: (i, 0, 0)),
            ),
        ),
        compiler_params=pltpu.CompilerParams(
            vmem_limit_bytes=room([kv_all] * 2, 4 * SPARE_BYTES)
        ),
        cost_estimate=lasting(13),
    )(bounds, queries, kv_all, starts)


def attend_back(bounds, queries, dy, out_rows, kept, kv_all, starts, scale):
    count, rows, width = queries.shape
    total_keys = kv_all.shape[0]
    heads = width // LANES
    if total_keys * width * 14 > VMEM_BYTES:
        heads = 1
    wide = heads * LANES

    def body(bounds_ref, q_ref, dy_ref, w_ref, kept_ref, kv_ref, start_ref, dq_ref, dkv_ref, acc_ref):
        i = pl.program_id(1)
        base = bounds_ref[i, 2]
        start_row = start_ref[0]

        @pl.when(i == 0)
        def _():
            def clear(c, _):
                acc_ref[pl.ds(pl.multiple_of(c * KEYS, KEYS), KEYS), :] = jnp.zeros(
                    (KEYS, wide), jnp.float32
                )
                return 0

            lax.fori_loop(0, total_keys // KEYS, clear, 0)

        q = [q_ref[0, :, h * LANES : (h + 1) * LANES] for h in range(heads)]
        grads = dot32(dy_ref[0], w_ref[...], LAST).astype(jnp.bfloat16)
        g = [grads[:, h * LANES : (h + 1) * LANES] for h in range(heads)]
        qg = [jnp.concatenate([q[h], g[h]], axis=0) for h in range(heads)]
        lse, delta = [], []
        for h in range(heads):
            kept_t = kept_ref[0, :, h * LANES : (h + 1) * LANES].T
            lse.append(kept_t[0:1])
            delta.append(jnp.sum(kept_t * g[h].astype(jnp.float32).T, axis=0, keepdims=True))

        def step(chunk, masked, carry):
            at = pl.multiple_of(chunk * KEYS, KEYS)
            if masked:
                ok = visible(chunk * KEYS, base, KEYS, rows, start_row)
            lanes = [slice(h * LANES, (h + 1) * LANES) for h in range(heads)]
            kvs = [kv_ref[pl.ds(at, KEYS), lanes[h]] for h in range(heads)]
            pairs = [dot32(kvs[h], qg[h], LAST) for h in range(heads)]
            scores = [p[:, :rows] for p in pairs]
            dprobs = [p[:, rows:] for p in pairs]
            if masked:
                scores = [jnp.where(ok, s, NEGATIVE) for s in scores]
            probs = [jnp.exp(scores[h] - lse[h]) for h in range(heads)]
            dscores = [
                (probs[h] * (dprobs[h] - delta[h])).astype(jnp.bfloat16) for h in range(heads)
            ]
            both = [
                jnp.concatenate([dscores[h], probs[h].astype(jnp.bfloat16)], axis=1)
                for h in range(heads)
            ]
            for h in range(heads):
                acc_ref[pl.ds(at, KEYS), lanes[h]] += dot32(both[h], qg[h])
            return tuple(carry[h] + dot32(kvs[h], dscores[h], FIRST) for h in range(heads))

        done = over_chunks(
            bounds_ref,
            i,
            step,
            tuple(jnp.zeros((LANES, rows), jnp.float32) for h in range(heads)),
        )
        lane = lax.broadcasted_iota(jnp.int32, (LANES, rows), 0)
        for h in range(heads):
            value = jnp.where(lane < LANES // 2, done[h] * scale, 0.0)
            dq_ref[0, :, h * LANES : (h + 1) * LANES] = value.T.astype(jnp.bfloat16)

        @pl.when(i == count - 1)
        def _():
            def store(c, _):
                at = pl.ds(pl.multiple_of(c * KEYS, KEYS), KEYS)
                dkv_ref[at, :] = acc_ref[at, :].astype(jnp.bfloat16)
                return 0

            lax.fori_loop(0, total_keys // KEYS, store, 0)

    block = pl.BlockSpec((1, rows, wide), lambda h, i, b: (i, 0, h))
    whole = pl.BlockSpec((total_keys, wide), lambda h, i, b: (0, h))
    return pl.pallas_call(
        body,
        out_shape=(
            jax.ShapeDtypeStruct((count, rows, width), jnp.bfloat16),
            jax.ShapeDtypeStruct(kv_all.shape, jnp.bfloat16),
        ),
        grid_spec=pltpu.PrefetchScalarGridSpec(
            num_scalar_prefetch=1,
            grid=(width // wide, count),
            in_specs=[
                block,
                pl.BlockSpec((1,) + tuple(dy.shape[1:]), lambda h, i, b: (i, 0, 0)),
                pl.BlockSpec((wide, out_rows.shape[1]), lambda h, i, b: (h, 0)),
                block,
                whole,
                pl.BlockSpec((1, 1, rows), lambda h, i, b: (i, 0, 0)),
            ],
            out_specs=(block, whole),
            scratch_shapes=[pltpu.VMEM((total_keys, wide), jnp.float32)],
        ),
        compiler_params=pltpu.CompilerParams(
            vmem_limit_bytes=room([make((total_keys, wide), jnp.bfloat16)] * 6, 5 * SPARE_BYTES)
        ),
        cost_estimate=lasting(20),
    )(bounds, queries, dy, out_rows, kept, kv_all, starts)


def experts_exchange(
    sent, saved, own, other, layer, blocks, collective_id, forward, backward, cost
):
    copies = blocks // NE
    half = NE // 2
    slots, width = sent[0].shape[1:]
    hidden, features = other[0].shape
    tile = min(hidden, 256)
    tiles = hidden // tile
    count = len(sent)
    homes_count = int(forward) + int(backward)
    total_rows = copies * NE * slots
    kind = sent[0].dtype
    sizes = (half // 2, half // 2, half)
    first_rows = [copies * slots * at for at in (0, half // 2, half)]
    most_rows = copies * slots * half
    plain = (((1,), (0,)), ((), ()))

    def body(*refs):
        refs = list(refs)

        def take(n):
            taken = refs[:n]
            del refs[:n]
            return taken

        srcs = take(count)
        saved_ref = take(1)[0] if not forward else None
        weight_refs = take(6)
        homes = take(homes_count)
        arrived_ref = take(1)[0] if not backward else None
        keeps, aways = (take(3), take(3)) if backward else ([], [])
        lands = take(count)
        weights = take(6)
        parts, sib_ins, totals = take(homes_count), take(homes_count), take(homes_count)
        accs = take(homes_count)
        rows_x = take(1)[0]
        if backward:
            rows_z, act_ref, dgate_ref, dup_ref, keep_ref, away_ref = take(6)
            if not forward:
                gate_ref, up_ref = take(2)
            out_sems = take(1)[0]
        load_sems, own_sems, send_sems, recv_sems, pass_sems, land_sems = take(6)
        home_own, home_send, home_recv, part_send, part_recv, arrived_sem = take(6)

        head, blk = lax.axis_index("head"), lax.axis_index("blk")
        expert, piece = lax.div(blk, copies), lax.rem(blk, copies)
        near = lax.div(expert, half) * half
        far = half - near
        places = [lax.rem(piece + k, copies) for k in range(copies)]
        siblings = [(head, expert * copies + places[k]) for k in range(copies)]
        others = [lax.rem(expert + d, NE) for d in range(NE)]
        greet([(head, e * copies + piece) for e in others[1:]] + siblings[1:])
        mine = pl.ds(pl.multiple_of(head * features, LANES), features)
        rest = pl.ds(pl.multiple_of((1 - head) * features, LANES), features)
        steps = [(far, sizes[0]), (far + sizes[0], sizes[1]), (near, sizes[2])]

        def sending(n, e):
            return remote(
                srcs[n].at[e],
                lands[n].at[piece, expert],
                send_sems.at[n, e],
                recv_sems.at[n, expert],
                (head, e * copies + piece),
            )

        owns = []
        for n in range(count):
            copy = pltpu.make_async_copy(
                srcs[n].at[expert], lands[n].at[piece, expert], own_sems.at[n]
            )
            copy.start()
            owns.append(copy)
        def each(t, copy_of, arrays, act):
            first, size = steps[t]
            for j in range(size):
                for n in range(arrays):
                    if t < 2:
                        act(copy_of(n, first + j))
                    else:

                        @pl.when(first + j != expert)
                        def _():
                            act(copy_of(n, first + j))

        def send(t):
            each(t, sending, count, lambda copy: copy.start())

        def sent_out(t):
            each(t, sending, count, lambda copy: copy.wait_send())

        for t in range(3):
            send(t)
        loads = []
        for n in range(6):
            weight = weight_refs[n] if n % 2 else weight_refs[n].at[layer]
            copy = pltpu.make_async_copy(weight, weights[n], load_sems.at[n])
            copy.start()
            loads.append(copy)
        go, gx, uo, ux, do, dx = weights
        passes, exchanges = [], {}

        def arrive(t):
            first, size = steps[t]
            waits = []
            if t == 2:
                for copy in owns:
                    copy.wait()
            for j in range(size):
                e = first + j
                for n in range(count):
                    place = lands[n].at[piece, e]

                    @pl.when(e != expert)
                    def _():
                        remote(
                            place, place, send_sems.at[n, e], recv_sems.at[n, e], siblings[0]
                        ).wait_recv()

                    for k in range(1, copies):
                        copy = remote(
                            place,
                            place,
                            pass_sems.at[n, k, e],
                            land_sems.at[n, k, e],
                            siblings[k],
                        )
                        copy.start()
                        waits.append(copy)
            for copy in waits:
                copy.wait_recv()
            passes.extend(waits)

        def flat(ref, t):
            first, size = steps[t]
            value = ref[:, pl.ds(first, size)].astype(jnp.float32)
            return value.reshape((copies * size * slots, width)).astype(kind)

        def span_of(t):
            return slice(first_rows[t], first_rows[t] + copies * steps[t][1] * slots)

        def gate_up(t, j):
            at = pl.ds(pl.multiple_of(j * tile, tile), tile)
            xo, xx = rows_x[span_of(t), mine], rows_x[span_of(t), rest]
            gate = dot32(xo, go[at], LAST) + dot32(xx, gx[at], LAST)
            return gate, dot32(xo, uo[at], LAST) + dot32(xx, ux[at], LAST)

        def early(t):
            rows_x[span_of(t)] = flat(saved_ref, t)
            size = copies * steps[t][1] * slots

            def step(j, _):
                at = pl.ds(pl.multiple_of(j * tile, tile), tile)
                gate_ref[:size, at], up_ref[:size, at] = gate_up(t, j)
                return 0

            lax.fori_loop(0, tiles, step, 0)

        def work(t):
            size = copies * steps[t][1] * slots
            span = span_of(t)
            if forward:
                rows_x[span] = flat(lands[0], t)
            if backward:
                rows_z[span] = flat(lands[-1], t)
            for acc in accs:
                acc[:size] = jnp.zeros((size, width), jnp.float32)

            def step(j, _):
                at = pl.ds(pl.multiple_of(j * tile, tile), tile)
                if forward:
                    gate, up = gate_up(t, j)
                else:
                    gate, up = gate_ref[:size, at], up_ref[:size, at]
                sigmoid = jax.nn.sigmoid(gate)
                silu = gate * sigmoid
                act = (silu * up).astype(kind)
                if forward:
                    accs[0][:size, mine] += dot32(act, do[at])
                    accs[0][:size, rest] += dot32(act, dx[at])
                if backward:
                    zo, zx = rows_z[span, mine], rows_z[span, rest]
                    dact = dot32(zo, do[at], LAST) + dot32(zx, dx[at], LAST)
                    dgate = (dact * up * sigmoid * (1.0 + gate * (1.0 - sigmoid))).astype(kind)
                    dup = (dact * silu).astype(kind)
                    act_ref[span, at] = act
                    dgate_ref[span, at] = dgate
                    dup_ref[span, at] = dup
                    accs[-1][:size, mine] += dot32(dgate, go[at]) + dot32(dup, uo[at])
                    accs[-1][:size, rest] += dot32(dgate, gx[at]) + dot32(dup, ux[at])
                return 0

            lax.fori_loop(0, tiles, step, 0)
            first, size_e = steps[t]
            for n in range(homes_count):
                value = accs[n][:size].reshape((copies, size_e, slots, width))
                parts[n][:, pl.ds(first, size_e)] = value.astype(kind)
                for j in range(size_e):
                    for k in range(1, copies):
                        copy = remote(
                            parts[n].at[places[k], first + j],
                            sib_ins[n].at[k - 1, first + j],
                            part_send.at[n, k, first + j],
                            part_recv.at[n, k, first + j],
                            siblings[k],
                        )
                        copy.start()
                        exchanges[n, t, j, k] = copy

        def homeward(n, e):
            return remote(
                totals[n].at[e],
                homes[n].at[expert],
                home_send.at[n, e],
                home_recv.at[n, expert],
                (head, e * copies + piece),
            )

        def give_back(t):
            first, size = steps[t]
            for j in range(size):
                e = first + j
                for n in range(homes_count):
                    value = parts[n][piece, e].astype(jnp.float32)
                    for k in range(1, copies):
                        exchanges[n, t, j, k].wait_recv()
                        value = value + sib_ins[n][k - 1, e].astype(jnp.float32)
                    totals[n][e] = value.astype(kind)
                    if t < 2:
                        homeward(n, e).start()
                    else:

                        @pl.when(e != expert)
                        def _():
                            homeward(n, e).start()

        for copy in loads:
            copy.wait()
        if not forward:
            early(0)
        for t in range(len(steps)):
            arrive(t)
            work(t)
            if t > 0:
                give_back(t - 1)
            if not forward and t + 1 < len(steps):
                early(t + 1)
        give_back(len(steps) - 1)
        stays = []
        for n in range(homes_count):
            copy = pltpu.make_async_copy(
                totals[n].at[expert], homes[n].at[expert], home_own.at[n]
            )
            copy.start()
            stays.append(copy)

        if backward:

            def saving(n, j, which):
                at = pl.ds(pl.multiple_of(j * tile, tile), tile)
                src, dst = ((keep_ref, keeps), (away_ref, aways))[which]
                return pltpu.make_async_copy(src.at[n, at], dst[n].at[at], out_sems.at[n, j, which])

            def grads(j, _):
                at = pl.ds(pl.multiple_of(j * tile, tile), tile)
                for n, (left, right) in enumerate(
                    ((dgate_ref, rows_x), (dup_ref, rows_x), (act_ref, rows_z))
                ):
                    value = left[:, at]
                    away_ref[n, at] = dot32(value, right[:, rest], FIRST).astype(kind)
                    saving(n, j, 1).start()
                    keep_ref[n, at] = dot32(value, right[:, mine], FIRST).astype(kind)
                    saving(n, j, 0).start()
                return 0

            lax.fori_loop(0, tiles, grads, 0)

        if not backward:
            copy = pltpu.make_async_copy(lands[0], arrived_ref, arrived_sem)
            copy.start()
            stays.append(copy)
        for n in range(homes_count):
            for e in others[1:]:
                place = homes[n].at[e]
                remote(
                    place, place, home_send.at[n, e], home_recv.at[n, e], siblings[0]
                ).wait_recv()
        for t in range(len(steps)):
            sent_out(t)
            each(t, homeward, homes_count, lambda copy: copy.wait_send())
        for copy in passes + list(exchanges.values()):
            copy.wait_send()
        for copy in stays:
            copy.wait()
        if backward:

            def settle(j, _):
                for n in range(3):
                    saving(n, j, 0).wait()
                    saving(n, j, 1).wait()
                return 0

            lax.fori_loop(0, tiles, settle, 0)

    slab = (copies, NE, slots, width)
    shapes = [make((NE, slots, width), kind)] * homes_count
    specs = [ANY] * homes_count
    if not backward:
        shapes.append(make(slab, kind))
        specs.append(HBM)
    else:
        shapes += [make((hidden, features), kind)] * 6
        specs += [HBM] * 6
    scratch = [pltpu.VMEM(slab, kind)] * count
    scratch += [pltpu.VMEM((hidden, features), kind)] * 6
    scratch += [pltpu.VMEM(slab, kind)] * homes_count
    scratch += [pltpu.VMEM((copies - 1,) + slab[1:], kind)] * homes_count
    scratch += [pltpu.VMEM((NE, slots, width), kind)] * homes_count
    scratch += [pltpu.VMEM((most_rows, width), jnp.float32)] * homes_count
    scratch.append(pltpu.VMEM((total_rows, width), kind))
    if backward:
        scratch.append(pltpu.VMEM((total_rows, width), kind))
        scratch += [pltpu.VMEM((total_rows, hidden), kind)] * 3
        scratch += [pltpu.VMEM((3, hidden, features), kind)] * 2
        if not forward:
            scratch += [pltpu.VMEM((most_rows, hidden), jnp.float32)] * 2
        scratch.append(DMA((3, tiles, 2)))
    scratch += [DMA((6,)), DMA((count,)), DMA((count, NE)), DMA((count, NE))]
    scratch += [DMA((count, copies, NE))] * 2
    scratch += [DMA((homes_count,)), DMA((homes_count, NE)), DMA((homes_count, NE))]
    scratch += [DMA((homes_count, copies, NE))] * 2 + [DMA]
    operands = list(sent)
    in_specs = [ANY] * count
    if not forward:
        operands.append(saved)
        in_specs.append(VMEM)
    operands += [w for pair in zip(own, other) for w in pair]
    in_specs += [HBM] * 6
    return pl.pallas_call(
        body,
        out_shape=shapes,
        in_specs=in_specs,
        out_specs=specs,
        scratch_shapes=scratch,
        compiler_params=comm_params(
            collective_id,
            scratch + ([saved] if not forward else []),
            (11 if backward else 2) * SPARE_BYTES,
        ),
        cost_estimate=lasting(cost),
    )(*operands)


def split(values, terms=2):
    parts = []
    for _ in range(terms):
        part = values.astype(jnp.bfloat16)
        parts.append(part)
        values = values - part.astype(jnp.float32)
    return parts


def exact_dot(pieces, values, dims):
    total = dot32(pieces[0], values, dims)
    for piece in pieces[1:]:
        total = total + dot32(piece, values, dims)
    return total


def unit_scale(values):
    return lax.rsqrt(jnp.mean(values * values, axis=-1, keepdims=True) + EPSILON)


def alone(body, out_shape, cost, *operands, scalars=0):
    specs = [pl.BlockSpec(memory_space=pltpu.SMEM)] * scalars + [VMEM] * (len(operands) - scalars)
    results = pl.pallas_call(
        body,
        out_shape=out_shape,
        in_specs=specs,
        out_specs=jax.tree.map(lambda _: VMEM, out_shape),
        compiler_params=pltpu.CompilerParams(
            vmem_limit_bytes=room(list(operands) + jax.tree.leaves(out_shape), 2 * SPARE_BYTES)
        ),
        cost_estimate=lasting(cost),
    )(*operands)
    return list(results) if isinstance(out_shape, (list, tuple)) else results


def route_tables(routes, gates):
    count, rows, _ = routes.shape
    slots = NE * CAP

    def body(routes_ref, gates_ref, picks_ref, weights_ref, slot_ref, other_ref):
        row = lax.broadcasted_iota(jnp.int32, (rows, rows), 0)
        col = lax.broadcasted_iota(jnp.int32, (rows, rows), 1)
        before = (col < row).astype(jnp.bfloat16)
        expert = lax.broadcasted_iota(jnp.int32, (rows, LANES), 1)
        slot = lax.broadcasted_iota(jnp.int32, (rows, slots), 1)
        source = lax.broadcasted_iota(jnp.int32, (LANES, slots), 0)
        target = lax.broadcasted_iota(jnp.int32, (LANES, slots), 1)
        spread = (
            (target >= source * CAP) & (target < source * CAP + CAP) & (source < NE)
        ).astype(jnp.bfloat16)
        ones = jnp.ones((rows, LANES), jnp.bfloat16)
        for n in range(count):
            gate = jnp.zeros((rows, LANES), jnp.float32)
            named = jnp.zeros((rows, LANES), jnp.float32)
            for k in range(2):
                hit = routes_ref[n, :, k : k + 1] == expert
                named = named + jnp.where(hit, 1.0, 0.0)
                gate = gate + jnp.where(hit, gates_ref[n, :, k : k + 1], 0.0)
            rank = dot32(before, named.astype(jnp.bfloat16)) + expert.astype(jnp.float32) * CAP
            rank = jnp.where(expert < NE, rank, 0.0)
            goal = exact_dot(split(rank, 2), spread, (((1,), (0,)), ((), ())))
            member = dot32(named.astype(jnp.bfloat16), spread)
            pick = jnp.where(goal == slot.astype(jnp.float32), member, 0.0)
            weight = pick * exact_dot(split(gate, 3), spread, (((1,), (0,)), ((), ())))
            picks_ref[n] = pick.astype(jnp.bfloat16)
            weights_ref[n] = weight
            slot_ref[n] = exact_dot(split(weight, 3), ones, FIRST)
            other_ref[n] = gate

    return alone(
        body,
        (
            make((count, rows, slots), jnp.bfloat16),
            make((count, rows, slots)),
            make((count, slots, LANES)),
            make((count, rows, LANES)),
        ),
        3,
        routes,
        gates,
    )


def gate_slots(slot_gates, picks, grads):
    picked = dot32(picks, grads[0], FIRST)
    for part in grads[1:]:
        picked = picked + dot32(picks, part, FIRST)
    lanes = [
        (picked[:, at : at + LANES] * slot_gates).astype(jnp.bfloat16)
        for at in range(0, picked.shape[1], LANES)
    ]
    return jnp.concatenate(lanes, axis=1)


def const_alphas(hn, smalls, base):
    logits = dot32(hn, smalls[base + 2 : base + 6].astype(jnp.bfloat16), LAST)
    alphas = []
    for c in range(2):
        first, second = logits[:, 2 * c : 2 * c + 1], logits[:, 2 * c + 1 : 2 * c + 2]
        top = jnp.maximum(first, second)
        first, second = jnp.exp(first - top), jnp.exp(second - top)
        total = first + second
        alphas.append((first / total, second / total))
    return alphas


def middle(attn, x, pack, smalls, base, picks, slot_gates, grads):
    planes, rows, part = attn.shape
    width = x.shape[1]
    slots = picks.shape[1]

    def body(attn_ref, x_ref, w_ref, small_ref, picks_ref, gates_ref, *refs):
        total = x_ref[...].astype(jnp.float32)
        for z in range(planes):
            total = total + dot32(attn_ref[z], w_ref[z * part : (z + 1) * part, :width])
        mid_ref, sent_ref = refs[-2:] if grads is None else refs[-3:-1]
        mid_ref[...] = total
        hn = (total * unit_scale(total) * small_ref[base + 1 : base + 2]).astype(jnp.bfloat16)
        sent_ref[...] = dot32(picks_ref[...], hn, FIRST).astype(jnp.bfloat16)
        if grads is not None:
            refs[-1][...] = gate_slots(gates_ref[...], picks_ref[...], [refs[0][...]])

    outs = [make((rows, width)), make((slots, width), jnp.bfloat16)]
    more = []
    if grads is not None:
        outs.append(make((slots, width), jnp.bfloat16))
        more.append(grads)
    return alone(body, outs, 3, attn, x, pack, smalls, picks, slot_gates, *more)


def combine(back, weights, mid, other, smalls, base, following):
    rows, width = mid.shape

    def body(back_ref, weights_ref, mid_ref, other_ref, small_ref, x_ref, *refs):
        mid_value, gate = mid_ref[...], other_ref[...]
        hn = (mid_value * unit_scale(mid_value) * small_ref[base + 1 : base + 2]).astype(
            jnp.bfloat16
        )
        alphas = const_alphas(hn, small_ref, base)
        wide = hn.astype(jnp.float32)
        total = mid_value + exact_dot(
            split(weights_ref[...]), back_ref[...], (((1,), (0,)), ((), ()))
        )
        factor = gate[:, NE + 1 : NE + 2]
        for c in range(2):
            weight = gate[:, NE + 2 + c : NE + 3 + c]
            factor = factor + weight * alphas[c][0]
            total = total + (weight * alphas[c][1]) * small_ref[base + 6 + c : base + 7 + c]
        total = total + factor * wide
        x_ref[...] = total
        if following:
            refs[0][...] = (total * unit_scale(total) * small_ref[base + 8 : base + 9]).astype(
                jnp.bfloat16
            )

    outs = [make((rows, width))]
    if following:
        outs.append(make((rows, width), jnp.bfloat16))
    return alone(body, outs, 3, back, weights, mid, other, smalls)


def experts_back(dback, picks, upstream, mid, other, smalls, base):
    rows, width = mid.shape

    def body(dback_ref, picks_ref, up_ref, mid_ref, other_ref, small_ref, dmid_ref, dy_ref, row_ref):
        mid_value, gate = mid_ref[...], other_ref[...]
        g = up_ref[...].astype(jnp.float32)
        scale = unit_scale(mid_value)
        unit = mid_value * scale
        gain = small_ref[base + 1 : base + 2]
        hn = (unit * gain).astype(jnp.bfloat16)
        alphas = const_alphas(hn, small_ref, base)
        wide = hn.astype(jnp.float32)
        dhn = dot32(picks_ref[...], dback_ref[...])
        g_hn = jnp.sum(g * wide, axis=1, keepdims=True)
        factor = gate[:, NE + 1 : NE + 2]
        row_ref[0:1] = jnp.zeros((1, width), jnp.float32)
        for c in range(2):
            weight = gate[:, NE + 2 + c : NE + 3 + c]
            vector = small_ref[base + 6 + c : base + 7 + c]
            first, second = alphas[c]
            factor = factor + weight * first
            row_ref[6 + c : 7 + c] = jnp.sum((weight * second) * g, axis=0, keepdims=True)
            da_first = weight * g_hn
            da_second = weight * jnp.sum(g * vector, axis=1, keepdims=True)
            mean = first * da_first + second * da_second
            for j, dlog in enumerate((first * (da_first - mean), second * (da_second - mean))):
                at = 2 + 2 * c + j
                dhn = dhn + dlog * small_ref[base + at : base + at + 1]
                row_ref[at : at + 1] = jnp.sum(dlog * wide, axis=0, keepdims=True)
        dhn = dhn + factor * g
        row_ref[1:2] = jnp.sum(dhn * unit, axis=0, keepdims=True)
        through = dhn * gain
        inner = jnp.mean(through * unit, axis=1, keepdims=True)
        dmid = g + scale * (through - unit * inner)
        dmid_ref[...] = dmid
        dy_ref[...] = dmid.astype(jnp.bfloat16)

    return alone(
        body,
        [make((rows, width)), make((rows, width), jnp.bfloat16), make((8, width))],
        4,
        dback,
        picks,
        upstream,
        mid,
        other,
        smalls,
    )


def finish(dxn, x, dmid, rows_in, smalls, base, picks, slot_gates):
    planes, rows, width = dxn.shape

    def body(dxn_ref, x_ref, dmid_ref, row_ref, small_ref, *refs):
        grad = dxn_ref[0].astype(jnp.float32)
        for z in range(1, planes):
            grad = grad + dxn_ref[z].astype(jnp.float32)
        value = x_ref[...].astype(jnp.float32)
        scale = unit_scale(value)
        unit = value * scale
        out_rows = refs[-1 if picks is None else -2]
        out_rows[...] = row_ref[...]
        out_rows[0:1] = jnp.sum(grad * unit, axis=0, keepdims=True)
        through = grad * small_ref[base : base + 1]
        inner = jnp.mean(through * unit, axis=1, keepdims=True)
        g = dmid_ref[...] + scale * (through - unit * inner)
        refs[-2 if picks is None else -3][...] = g
        if picks is not None:
            refs[-1][...] = gate_slots(refs[1][...], refs[0][...], split(g))

    outs = [make((rows, width)), make((8, width))]
    more = []
    if picks is not None:
        outs.append(make((picks.shape[1], width), jnp.bfloat16))
        more = [picks, slot_gates]
    return alone(body, outs, 3, dxn, x, dmid, rows_in, smalls, *more)


def sum_expert_grads(owns, gots):
    layers, kinds = len(owns), len(owns[0])
    hidden, features = owns[0][0].shape
    tile = min(hidden, 256)

    def body(*refs):
        outs = refs[2 * layers * kinds :]
        for n in range(kinds):
            for layer in range(layers):
                own, got = refs[2 * (layer * kinds + n) : 2 * (layer * kinds + n) + 2]
                outs[n][layer] = own[...].astype(jnp.float32) + got[...].astype(jnp.float32)

    piece = pl.BlockSpec((tile, features), lambda i: (i, 0))
    operands = [
        w for layer in range(layers) for pair in zip(owns[layer], gots[layer]) for w in pair
    ]
    return pl.pallas_call(
        body,
        out_shape=[make((layers, hidden, features))] * kinds,
        grid=(hidden // tile,),
        in_specs=[piece] * len(operands),
        out_specs=[pl.BlockSpec((layers, tile, features), lambda i: (0, i, 0))] * kinds,
        compiler_params=pltpu.CompilerParams(vmem_limit_bytes=VMEM_BYTES),
        cost_estimate=lasting(7),
    )(*operands)


def pack_grads(column, dq, dkv, attn, dy, small):
    width = column.shape[1]
    kv_cols, own_out = dkv.shape[1], attn.shape[1]
    tail = own_out + LANES // 2
    rows, cols = own_out // 2, width // 2

    def body(column_ref, dq_ref, dkv_ref, attn_ref, dy_ref, small_ref, one, two):
        one[:, :kv_cols] = dot32(column_ref[...], dkv_ref[...], FIRST).astype(jnp.bfloat16)
        source = lax.broadcasted_iota(jnp.int32, (kv_cols, tail), 0)
        target = lax.broadcasted_iota(jnp.int32, (kv_cols, tail), 1)
        dim = LANES // 2
        goal = lax.div(target, dim) * LANES + lax.rem(target, dim)
        compact = ((goal == source) & (target < own_out)).astype(jnp.bfloat16)
        narrow = dot32(dq_ref[...], compact).astype(jnp.bfloat16)
        placed = jnp.concatenate(
            [
                jnp.zeros((own_out, width), jnp.float32),
                small_ref[...],
                jnp.zeros((tail - own_out - 8, width), jnp.float32),
            ],
            axis=0,
        ).T
        one[:, kv_cols:] = (dot32(column_ref[...], narrow, FIRST) + placed).astype(jnp.bfloat16)
        out = dot32(attn_ref[...], dy_ref[...], FIRST).astype(jnp.bfloat16)
        for a in range(2):
            for b in range(2):
                two[a, b] = out[a * rows : (a + 1) * rows, b * cols : (b + 1) * cols]

    return alone(
        body,
        [make((width, kv_cols + tail), jnp.bfloat16), make((2, 2, rows, cols), jnp.bfloat16)],
        4,
        column,
        dq,
        dkv,
        attn,
        dy,
        small,
    )


def per_device(
    tokens,
    segments,
    routes,
    gates,
    w_qkv,
    w_out,
    gain_attn,
    gain_moe,
    const_gate,
    const_vec,
    w_gate,
    w_up,
    w_down,
    cotangent,
):
    blocks = lax.axis_size("blk")
    head_index, blk_index = lax.axis_index("head"), lax.axis_index("blk")
    span = blocks // COLUMNS
    plane, rest = lax.div(blk_index, span), lax.rem(blk_index, span)
    shards = 2 * blocks
    token_rows, width = tokens.shape
    shard_rows = width // shards
    head_dim = width // HEADS
    heads = HEADS // COLUMNS
    scale = head_dim ** (-0.5)
    half_length = blocks * token_rows
    positions = 2 * half_length
    own_out = heads * head_dim
    wide = heads * LANES

    swap = [(0, 1), (1, 0)]

    seg_own = lax.dynamic_index_in_dim(segments, head_index, 0, keepdims=True)
    seg_rows = jnp.concatenate([lax.rem(seg_own, 128), lax.div(seg_own, 128)], axis=0)
    seg_rows = jnp.pad(seg_rows, ((0, 14), (0, 0))).astype(jnp.bfloat16)
    seg_rows = jnp.broadcast_to(seg_rows[None], (COLUMNS,) + seg_rows.shape)
    smalls = [
        jnp.concatenate(
            [gain_attn[n][:, None], gain_moe[n][:, None], const_gate[n], const_vec[n]], axis=1
        )
        for n in range(LAYERS)
    ]
    smalls.append(jnp.zeros((shard_rows, LANES // 2 - 8 * LAYERS), jnp.bfloat16))
    smalls = jnp.concatenate(smalls, axis=1)
    packs = []
    for layer in range(LAYERS):
        parts = w_qkv[layer].reshape((shard_rows, 3, COLUMNS, heads, head_dim))
        kv_part = jnp.concatenate([parts[:, 1], parts[:, 2]], axis=3)
        kv_part = kv_part.transpose((1, 0, 2, 3)).reshape((COLUMNS, shard_rows, wide))
        query_part = parts[:, 0].transpose((1, 0, 2, 3)).reshape((COLUMNS, shard_rows, own_out))
        packs.append(
            jnp.concatenate(
                [
                    jnp.broadcast_to(w_out[layer][None], (COLUMNS, shard_rows, width)),
                    kv_part,
                    query_part,
                    jnp.broadcast_to(smalls[None], (COLUMNS,) + smalls.shape),
                ],
                axis=2,
            )
        )
    (seg_all, *packs), column_tokens = start_gather([seg_rows] + packs, tokens, blocks, 1)
    packs = [pack.reshape((width, -1)) for pack in packs]
    picks, pick_gates, slot_gates, other_gates = route_tables(routes, gates)

    def send_expert(weight, layer, after):
        away, _ = lax.optimization_barrier((weight[layer], after))
        return lax.ppermute(away, "head", swap)

    own_experts = (w_gate, w_up, w_down)

    experts = [[send_expert(w_gate, 0, tokens)]] + [None] * (LAYERS - 1)
    seg_all = seg_all[..., :2, :].astype(jnp.int32)
    seg_all = seg_all[..., 0, :] + 128 * seg_all[..., 1, :]
    seg_query = lax.dynamic_index_in_dim(seg_all, head_index, 0, keepdims=False)
    seg_query = lax.dynamic_index_in_dim(seg_query, rest, 1, keepdims=False)
    starts = jnp.sum(
        (seg_all.reshape((1, 1, -1)) < seg_query[:, :, None]).astype(jnp.int32), axis=2
    )
    bases = (
        head_index * half_length
        + (jnp.arange(COLUMNS, dtype=jnp.int32) * span + rest) * token_rows
    )
    bounds = block_bounds(starts, bases, token_rows)
    starts = starts[:, None, :]

    values = tokens
    column, small_rows = column_tokens, None
    kept = []
    for layer in range(LAYERS):
        base = 8 * layer
        last = layer + 1 == LAYERS
        column, queries, query_w, out_rows, kv_all, small_rows = project_gather(
            column, packs[layer], small_rows, heads, scale, blocks, 4 if layer == 0 else 2
        )
        kv_all = kv_all.reshape((positions, wide))
        if layer == 0:
            experts[layer] += [send_expert(w, layer, kv_all) for w in (w_up, w_down)]
        else:
            experts[layer].append(send_expert(w_down, layer, kv_all))
        attended, attn_col = attend(bounds, queries, kv_all, starts)
        (attn,) = column_exchange([attn_col], [False], blocks, 5, 9)
        mid, *sent = middle(
            attn,
            values,
            packs[layer],
            small_rows,
            base,
            picks[layer],
            slot_gates[layer],
            cotangent if last else None,
        )
        sent = [rows.reshape((NE, CAP, width)) for rows in sent]
        if last:
            back, dback, *wgrads = experts_exchange(
                sent, None, own_experts, experts[layer], layer, blocks, 7, True, True, 55
            )
            rows_in = None
        else:
            experts[layer + 1] = [send_expert(w, layer + 1, sent[0]) for w in (w_gate, w_up)]
            back, rows_in = experts_exchange(
                sent, None, own_experts, experts[layer], layer, blocks, 6, True, False, 28
            )
        kept.append(
            (values, column, queries, kv_all, attended, attn_col, query_w, out_rows, mid, rows_in)
        )
        values, *normed = combine(
            back.reshape((NE * CAP, width)),
            pick_gates[layer],
            mid,
            other_gates[layer],
            small_rows,
            base,
            not last,
        )
        if not last:
            (column,) = normed
    output = values

    upstream = cotangent
    shared_grads = [None] * LAYERS
    expert_grads = [None] * LAYERS
    for layer in reversed(range(LAYERS)):
        base = 8 * layer
        values, column, queries, kv_all, attended, attn_col, query_w, out_rows, mid, rows_in = (
            kept[layer]
        )
        if layer + 1 < LAYERS:
            dback, *wgrads = experts_exchange(
                [dz.reshape((NE, CAP, width))],
                rows_in,
                own_experts,
                experts[layer],
                layer,
                blocks,
                8,
                False,
                True,
                36,
            )
            dback, held[2] = lax.optimization_barrier((dback, held[2]))
        got = [lax.ppermute(away, "head", swap) for away in wgrads[3:]]
        dmid, dy, rows = experts_back(
            dback.reshape((NE * CAP, width)),
            picks[layer],
            upstream,
            mid,
            other_gates[layer],
            small_rows,
            base,
        )
        dy = column_gather(dy, blocks, 3)
        dy, got[0] = lax.optimization_barrier((dy, got[0]))
        dq, dkv_all = attend_back(
            bounds, queries, dy, out_rows, attended, kv_all, starts, scale
        )
        dkv_all, got[1] = lax.optimization_barrier((dkv_all, got[1]))
        dkv, dxn = reduce_project(
            dkv_all.reshape((2, COLUMNS, span, token_rows, wide)),
            dq,
            query_w,
            packs[layer],
            blocks,
            10,
        )
        before = layer > 0
        if not before:
            dxn, got[2] = lax.optimization_barrier((dxn, got[2]))
        upstream, rows, *dz = finish(
            dxn,
            values,
            dmid,
            rows,
            small_rows,
            base,
            picks[layer - 1] if before else None,
            slot_gates[layer - 1] if before else None,
        )
        if before:
            (dz,) = dz
        expert_grads[layer] = wgrads[:3], got
        held = got
        qkv_part, out_part = pack_grads(
            column.reshape((-1, width)),
            dq.reshape((-1, wide)),
            dkv.reshape((-1, wide)),
            attn_col.reshape((-1, own_out)),
            dy.reshape((-1, width)),
            rows,
        )
        shared_grads[layer] = [
            qkv_part.reshape((2, COLUMNS, span, shard_rows, -1)),
            out_part.reshape((2, 2, span, shard_rows, width // 2)),
        ]

    packed = [part for layer in range(LAYERS) for part in shared_grads[layer]]
    reduced = plane_reduce(packed, blocks, 12, 20)
    exchanged = final_exchange(reduced[::2], reduced[1::2], blocks, 13)
    from_planes, out_grads = exchanged[:LAYERS], exchanged[LAYERS:]
    from_planes = jnp.stack(from_planes, axis=1).astype(jnp.float32)
    kv_out = from_planes[..., :wide].reshape((COLUMNS, LAYERS, shard_rows, heads, 2, head_dim))
    query_out = from_planes[..., wide : wide + own_out].reshape(
        (COLUMNS, LAYERS, shard_rows, heads, 1, head_dim)
    )
    qkv_out = jnp.concatenate([query_out, kv_out], axis=4)
    qkv_out = qkv_out.transpose((1, 2, 4, 0, 3, 5)).reshape((LAYERS, shard_rows, 3 * width))
    small_out = jnp.sum(from_planes[..., wide + own_out : wide + own_out + 8], axis=0)
    out_grads = jnp.stack(out_grads).astype(jnp.float32).transpose((0, 2, 1, 3))
    out_grads = out_grads.reshape((LAYERS, shard_rows, width))
    stacked = sum_expert_grads(*zip(*expert_grads))
    return (
        output,
        upstream,
        qkv_out,
        out_grads,
        small_out[..., 0],
        small_out[..., 1],
        small_out[..., 2:6],
        small_out[..., 6:8],
        stacked[0],
        stacked[1],
        stacked[2],
    )


def solution(mesh):
    tokens = P(("head", "blk"), None)
    by_layer = P(None, ("head", "blk"), None)
    gains = P(None, ("head", "blk"))
    experts = P(None, "blk", "head")
    return jax.shard_map(
        per_device,
        mesh=mesh,
        in_specs=(
            tokens,
            P(None, "blk"),
            by_layer,
            by_layer,
            by_layer,
            by_layer,
            gains,
            gains,
            by_layer,
            by_layer,
            experts,
            experts,
            experts,
            tokens,
        ),
        out_specs=(
            tokens,
            tokens,
            by_layer,
            by_layer,
            gains,
            gains,
            by_layer,
            by_layer,
            experts,
            experts,
            experts,
        ),
        check_vma=False,
    )
```

```python
import jax
import jax.numpy as jnp
from jax import lax
from jax.experimental import pallas as pl
from jax.experimental.pallas import tpu as pltpu
from jax.sharding import PartitionSpec as P

HEADS = 12
NE = 8
LAYERS = 2
CAP = 40
COLUMNS = 4
MESH = pl.DeviceIdType.MESH
ANY = pl.BlockSpec(memory_space=pl.ANY)
VMEM = pl.BlockSpec(memory_space=pltpu.VMEM)
HBM = pl.BlockSpec(memory_space=pltpu.HBM)
DMA = pltpu.SemaphoreType.DMA
VMEM_BYTES = 60 * 1024 * 1024
SPARE_BYTES = 4 * 1024 * 1024


def make(shape, kind=jnp.float32):
    return jax.ShapeDtypeStruct(tuple(shape), kind)


def greet(peers, line=()):
    barrier = pltpu.get_barrier_semaphore()
    count = len(peers)
    for peer in peers:
        pl.semaphore_signal(barrier, inc=1, device_id=peer, device_id_type=MESH)
    for there, peer in line:

        @pl.when(there)
        def _():
            pl.semaphore_signal(barrier, inc=1, device_id=peer, device_id_type=MESH)

        count = count + there.astype(jnp.int32)
    pl.semaphore_wait(barrier, count)


def remote(src, dst, send_sem, recv_sem, peer):
    return pltpu.make_async_remote_copy(
        src_ref=src,
        dst_ref=dst,
        send_sem=send_sem,
        recv_sem=recv_sem,
        device_id=peer,
        device_id_type=MESH,
    )


def room(things, spare=SPARE_BYTES):
    total = spare
    for thing in things:
        if hasattr(thing, "dtype") and hasattr(thing, "shape"):
            if not jnp.issubdtype(thing.dtype, jnp.number):
                continue
            size = jnp.dtype(thing.dtype).itemsize
            for extent in thing.shape:
                size *= extent
            total += size
    return min(total, VMEM_BYTES)


def comm_params(collective_id, things=(), spare=SPARE_BYTES):
    return pltpu.CompilerParams(
        collective_id=collective_id,
        has_side_effects=True,
        vmem_limit_bytes=room(things, spare),
    )


def lasting(microseconds):
    return pl.CostEstimate(
        flops=0, bytes_accessed=int(microseconds * 3_500_000), transcendentals=0
    )


def column_place(blocks):
    span = blocks // COLUMNS
    head, blk = lax.axis_index("head"), lax.axis_index("blk")
    plane, rest = lax.div(blk, span), lax.rem(blk, span)
    planes = [lax.rem(plane + d, COLUMNS) for d in range(COLUMNS)]
    return plane, planes, [(head, p * span + rest) for p in planes]


class Chain:
    def __init__(self, source, dst, send_sems, recv_sems, blocks):
        span = blocks // COLUMNS
        head, blk = lax.axis_index("head"), lax.axis_index("blk")
        plane, rest = lax.div(blk, span), lax.rem(blk, span)
        self.source, self.dst, self.plane = source, dst, plane
        self.send_sems, self.recv_sems = send_sems, recv_sems
        after = jnp.minimum(plane + 1, COLUMNS - 1)
        before = jnp.maximum(plane - 1, 0)
        self.line = [
            (plane < COLUMNS - 1, (head, after * span + rest)),
            (plane > 0, (head, before * span + rest)),
        ]
        lower = plane < COLUMNS // 2
        self.slabs = [
            plane,
            plane + 1 - 2 * lax.rem(plane, 2),
            jnp.where(lower, 2, 1),
            jnp.where(lower, 3, 0),
        ]

    def copy(self, k, way):
        slab = self.slabs[k]
        place = self.dst.at[slab]
        return remote(
            self.source if k == 0 else place,
            place,
            self.send_sems.at[k, way],
            self.recv_sems.at[slab],
            self.line[way][1],
        )

    def onward(self, k):
        if k == 0:
            return [self.line[0][0], self.line[1][0]]
        from_before = self.slabs[k] < self.plane
        return [
            from_before & self.line[0][0],
            jnp.logical_not(from_before) & self.line[1][0],
        ]

    def pass_on(self, k):
        for way, there in enumerate(self.onward(k)):

            @pl.when(there)
            def _():
                self.copy(k, way).start()

    def arrive(self, k):
        self.copy(k, 0).wait_recv()
        self.pass_on(k)

    def finish(self):
        for k in range(COLUMNS):
            for way, there in enumerate(self.onward(k)):

                @pl.when(there)
                def _():
                    self.copy(k, way).wait_send()


def column_start(src, gather, dst, own_sem, send_sems, recv_sems, where):
    plane, planes, peers = where
    own = pltpu.make_async_copy(src if gather else src.at[plane], dst.at[plane], own_sem)
    own.start()
    copies = [own]
    for d in (2, 1, 3):
        copy = remote(
            src if gather else src.at[planes[d]],
            dst.at[plane],
            send_sems.at[d],
            recv_sems.at[d],
            peers[d],
        )
        copy.start()
        copies.append(copy)
    return copies


def column_exchange(arrays, gathers, blocks, collective_id, cost=16):
    count = len(arrays)
    slabs = [
        tuple(values.shape if gather else values.shape[1:])
        for values, gather in zip(arrays, gathers)
    ]

    def body(*refs):
        srcs, dsts = refs[:count], refs[count : 2 * count]
        own_sems, send_sems, recv_sems = refs[2 * count :]
        where = column_place(blocks)
        greet(where[2][1:])
        copies = []
        for n in range(count):
            copies += column_start(
                srcs[n],
                gathers[n],
                dsts[n],
                own_sems.at[n],
                send_sems.at[n],
                recv_sems.at[n],
                where,
            )
        for copy in copies:
            copy.wait()

    return pl.pallas_call(
        body,
        out_shape=[
            jax.ShapeDtypeStruct((COLUMNS,) + slab, values.dtype)
            for values, slab in zip(arrays, slabs)
        ],
        in_specs=[ANY] * count,
        out_specs=[ANY] * count,
        scratch_shapes=[DMA((count,)), DMA((count, COLUMNS)), DMA((count, COLUMNS))],
        compiler_params=comm_params(collective_id),
        cost_estimate=lasting(cost),
    )(*arrays)


def column_gather(values, blocks, collective_id, cost=14):
    def body(src, dst, own_sem, send_sems, recv_sems):
        chain = Chain(src, dst, send_sems, recv_sems, blocks)
        greet([], chain.line)
        chain.pass_on(0)
        own = pltpu.make_async_copy(src, dst.at[chain.plane], own_sem)
        own.start()
        for k in range(1, COLUMNS):
            chain.arrive(k)
        own.wait()
        chain.finish()

    return pl.pallas_call(
        body,
        out_shape=jax.ShapeDtypeStruct((COLUMNS,) + tuple(values.shape), values.dtype),
        in_specs=[ANY],
        out_specs=ANY,
        scratch_shapes=[DMA, DMA((COLUMNS, 2)), DMA((COLUMNS,))],
        compiler_params=comm_params(collective_id),
        cost_estimate=lasting(cost),
    )(values)


def final_exchange(shares, rows, blocks, collective_id, cost=9):
    span = blocks // COLUMNS
    count = len(shares)
    total = 2 * count

    def body(*refs):
        srcs, dsts = refs[:total], refs[total : 2 * total]
        own_sems, send_sems, recv_sems, row_send, row_recv = refs[2 * total :]
        where = column_place(blocks)
        head, blk = lax.axis_index("head"), lax.axis_index("blk")
        plane, rest = lax.div(blk, span), lax.rem(blk, span)
        flat = head * blocks + blk
        goal = (plane * 2 + head) * span + rest
        from_plane = lax.div(flat, span)
        origin = (lax.rem(from_plane, 2), lax.div(from_plane, 2) * span + lax.rem(flat, span))
        goal_place = (lax.div(goal, blocks), lax.rem(goal, blocks))
        away = goal != flat
        greet(where[2][1:], [(away, goal_place), (away, origin)])
        copies = []
        for n in range(count):
            copies += column_start(
                srcs[n],
                False,
                dsts[n],
                own_sems.at[n],
                send_sems.at[n],
                recv_sems.at[n],
                where,
            )

        def row_copy(n):
            return remote(
                srcs[n], dsts[n], row_send.at[n - count], row_recv.at[n - count], goal_place
            )

        def row_stay(n):
            return pltpu.make_async_copy(srcs[n], dsts[n], own_sems.at[n])

        for n in range(count, total):

            @pl.when(away)
            def _():
                row_copy(n).start()

            @pl.when(jnp.logical_not(away))
            def _():
                row_stay(n).start()

        for copy in copies:
            copy.wait()
        for n in range(count, total):

            @pl.when(away)
            def _():
                row_copy(n).wait()

            @pl.when(jnp.logical_not(away))
            def _():
                row_stay(n).wait()

    arrays = list(shares) + list(rows)
    return pl.pallas_call(
        body,
        out_shape=[make(values.shape, values.dtype) for values in arrays],
        in_specs=[ANY] * total,
        out_specs=[ANY] * total,
        scratch_shapes=[
            DMA((total,)),
            DMA((count, COLUMNS)),
            DMA((count, COLUMNS)),
            DMA((count,)),
            DMA((count,)),
        ],
        compiler_params=comm_params(collective_id),
        cost_estimate=lasting(cost),
    )(*arrays)


def plane_place(blocks):
    span = blocks // COLUMNS
    width = span // 2
    head, blk = lax.axis_index("head"), lax.axis_index("blk")
    plane, rest = lax.div(blk, span), lax.rem(blk, span)
    x, core = lax.div(rest, 2), lax.rem(rest, 2)
    first = plane * span
    right = [lax.rem(x + d, width) for d in range(width)]
    left = [lax.rem(x - d + width, width) for d in range(width)]
    x_peers = [(head, first + right[d] * 2 + core) for d in range(width)]
    y_peer = (1 - head, blk)
    core_peer = (head, first + x * 2 + 1 - core)
    return head, rest, core, left, x_peers, y_peer, core_peer


class PlaneRun:
    def __init__(self, srcs, dsts, own_sems, send_sems, recv_sems, pass_sems, land_sems, where):
        self.srcs, self.dsts = srcs, dsts
        self.own_sems, self.send_sems, self.recv_sems = own_sems, send_sems, recv_sems
        self.pass_sems, self.land_sems = pass_sems, land_sems
        self.head, self.rest, self.core, self.left, self.x_peers, self.y_peer, self.core_peer = (
            where
        )
        self.width = len(self.x_peers)
        self.sends, self.passes, self.owns = [], [], []

    def place(self, n, h, dy, d):
        half = self.srcs[n].shape[0] // 2
        row = self.head if dy == 0 else 1 - self.head
        return self.dsts[n].at[row, pl.ds(h * half, half), self.left[d] * 2 + self.core]

    def held(self, n, h, dy, d):
        half = self.srcs[n].shape[0] // 2
        if dy == 0 and d == 0:
            return self.srcs[n].at[pl.ds(h * half, half)]
        return self.place(n, h, dy, d)

    def send(self, n, h, dy, d, peer, to_dy, to_d):
        copy = remote(
            self.held(n, h, dy, d),
            self.place(n, h, dy, d),
            self.send_sems.at[len(self.sends)],
            self.recv_sems.at[n, h, to_dy, to_d],
            peer,
        )
        copy.start()
        self.sends.append(copy)

    def hand_over(self, n, h, dy, d):
        copy = remote(
            self.held(n, h, dy, d),
            self.place(n, h, dy, d),
            self.pass_sems.at[n, h, dy, d],
            self.land_sems.at[n, h, dy, d],
            self.core_peer,
        )
        copy.start()
        self.passes.append(copy)

    def arrived(self, n, h, dy, d):
        at = self.place(n, h, dy, d)
        remote(
            at, at, self.send_sems.at[0], self.recv_sems.at[n, h, dy, d], self.y_peer
        ).wait_recv()

    def first(self, n):
        own = pltpu.make_async_copy(
            self.srcs[n], self.dsts[n].at[self.head, :, self.rest], self.own_sems.at[n]
        )
        own.start()
        self.owns.append(own)
        for d in range(1, self.width):
            self.send(n, 0, 0, 0, self.x_peers[d], 0, d)
        self.send(n, 1, 0, 0, self.y_peer, 1, 0)
        self.send(n, 0, 0, 0, self.y_peer, 1, 0)
        for d in range(1, self.width):
            self.send(n, 1, 0, 0, self.x_peers[d], 0, d)
        self.hand_over(n, 0, 0, 0)
        self.hand_over(n, 1, 0, 0)

    def second(self, n):
        for d in range(1, self.width):
            self.arrived(n, 0, 0, d)
            self.send(n, 0, 0, d, self.y_peer, 1, d)
            self.hand_over(n, 0, 0, d)
        self.arrived(n, 1, 1, 0)
        for d in range(1, self.width):
            self.send(n, 1, 1, 0, self.x_peers[d], 1, d)
        self.hand_over(n, 1, 1, 0)

    def third(self, n):
        self.arrived(n, 0, 1, 0)
        self.hand_over(n, 0, 1, 0)
        for d in range(1, self.width):
            self.arrived(n, 1, 0, d)
            self.hand_over(n, 1, 0, d)
        for d in range(1, self.width):
            self.arrived(n, 0, 1, d)
            self.hand_over(n, 0, 1, d)
            self.arrived(n, 1, 1, d)
            self.hand_over(n, 1, 1, d)

    def last(self):
        for own in self.owns:
            own.wait()
        for copy in self.passes:
            copy.wait()
        for copy in self.sends:
            copy.wait_send()


def plane_scratch(count, blocks):
    width = blocks // COLUMNS // 2
    links = 4 * (width - 1) + 2
    return [DMA((count,)), DMA((count * links,))] + [DMA((count, 2, 2, width))] * 3


def plane_shapes(arrays, blocks):
    return [
        jax.ShapeDtypeStruct(
            (2, values.shape[0], blocks // COLUMNS) + tuple(values.shape[1:]), values.dtype
        )
        for values in arrays
    ]


def start_gather(packs, tokens, blocks, collective_id, cost=28):
    count = len(packs)

    def body(*refs):
        srcs, refs = refs[: count + 1], refs[count + 1 :]
        wholes, refs = refs[:count], refs[count:]
        columns, refs = refs[: count + 1], refs[count + 1 :]
        own_sems, send_sems, recv_sems, chain_send, chain_recv, *plane_sems = refs
        column, plane = column_place(blocks), plane_place(blocks)
        greet(column[2][1:] + plane[4][1:] + [plane[5], plane[6]])
        run = PlaneRun(columns[:count], wholes, *plane_sems, plane)
        chain = Chain(srcs[count], columns[count], chain_send, chain_recv, blocks)
        stay = pltpu.make_async_copy(
            srcs[count], columns[count].at[chain.plane], own_sems.at[count]
        )

        def begin(n):
            return column_start(
                srcs[n],
                False,
                columns[n],
                own_sems.at[n],
                send_sems.at[n],
                recv_sems.at[n],
                column,
            )

        waits = [begin(0), begin(1)]
        for n in range(count):
            for copy in waits[n]:
                copy.wait()
            if n + 2 < count:
                waits.append(begin(n + 2))
            elif n + 2 == count:
                chain.pass_on(0)
                stay.start()
            run.first(n)
        run.second(0)
        run.second(1)
        chain.arrive(1)
        for n in range(2, count):
            run.second(n)
        run.third(0)
        run.third(1)
        chain.arrive(2)
        for n in range(2, count):
            run.third(n)
        chain.arrive(3)
        run.last()
        stay.wait()
        chain.finish()

    results = pl.pallas_call(
        body,
        out_shape=plane_shapes(packs, blocks)
        + [jax.ShapeDtypeStruct(pack.shape, pack.dtype) for pack in packs]
        + [jax.ShapeDtypeStruct((COLUMNS,) + tokens.shape, tokens.dtype)],
        in_specs=[ANY] * (count + 1),
        out_specs=[ANY] * (2 * count + 1),
        scratch_shapes=[
            DMA((count + 1,)),
            DMA((count, COLUMNS)),
            DMA((count, COLUMNS)),
            DMA((COLUMNS, 2)),
            DMA((COLUMNS,)),
        ]
        + plane_scratch(count, blocks),
        compiler_params=comm_params(collective_id),
        cost_estimate=lasting(cost),
    )(*packs, tokens)
    return results[:count], results[-1]


def project_gather(source, pack, smalls, heads, scale, blocks, collective_id, cost=22):
    span = blocks // COLUMNS
    width = span // 2
    chained = smalls is not None
    rows, features = source.shape[-2:]
    wide = heads * LANES
    kv_at, tail_at = features, features + wide
    tail_cols = pack.shape[1] - tail_at
    own_out = tail_cols - LANES // 2
    dim = LANES // 2
    half = rows // 2
    small_rows = 8 * LAYERS
    links = 4 * (width - 1) + 2

    def body(*refs):
        if chained:
            source_ref, pack_ref, small_ref = refs[:3]
            refs = refs[3:]
            small_out = None
        else:
            source_ref, pack_ref = refs[:2]
            small_out, refs = refs[2], refs[3:]
        column_out, query_ref, query_w_out, out_w_out, kv_ref = refs[:5]
        column_ref, query_w_ref, out_w_ref, kv_own, own_sems, send_sems, recv_sems = refs[5:12]
        pass_sems, land_sems, z_send, z_recv, keep_sems = refs[12:]
        head, rest, core, left, x_peers, y_peer, core_peer = plane_place(blocks)
        plane = lax.div(lax.axis_index("blk"), span)
        sends, passes, owns = [], [], []
        near = x_peers[1:] + [y_peer, core_peer]
        if chained:
            chain = Chain(source_ref, column_ref, z_send, z_recv, blocks)
            slabs = chain.slabs
            greet(near, chain.line)
            chain.pass_on(0)
        else:
            slabs = list(range(COLUMNS))
            greet(near)

        tail = pack_ref[:, tail_at:]
        if not chained:
            small = tail[:, tail_cols - LANES :].astype(jnp.float32).T
            at = own_out - (tail_cols - LANES)
            small = small[at : at + small_rows]
            small_out[...] = small

        def place(k, h, dy, d):
            row = head if dy == 0 else 1 - head
            return kv_ref.at[row, slabs[k], left[d] * 2 + core, pl.ds(h * half, half)]

        def held(k, h, dy, d):
            if dy == 0 and d == 0:
                return kv_own.at[k, pl.ds(h * half, half)]
            return place(k, h, dy, d)

        def send(k, h, dy, d, peer, to_dy, to_d):
            copy = remote(
                held(k, h, dy, d),
                place(k, h, dy, d),
                send_sems.at[len(sends)],
                recv_sems.at[k, h, to_dy, to_d],
                peer,
            )
            copy.start()
            sends.append(copy)

        def hand_over(k, h, dy, d):
            copy = remote(
                held(k, h, dy, d),
                place(k, h, dy, d),
                pass_sems.at[k, h, dy, d],
                land_sems.at[k, h, dy, d],
                core_peer,
            )
            copy.start()
            passes.append(copy)

        def arrived(k, h, dy, d):
            at = place(k, h, dy, d)
            remote(at, at, send_sems.at[0], recv_sems.at[k, h, dy, d], y_peer).wait_recv()

        def first(k):
            slab = slabs[k]
            if not chained:
                x = source_ref[slab].astype(jnp.float32)
                xn = (x * unit_scale(x) * small[0:1]).astype(jnp.bfloat16)
                column_ref[slab] = xn
            elif k == 0:
                xn = source_ref[...]
                column_ref[slab] = xn
            else:
                chain.arrive(k)
                xn = column_ref[slab]
            kv = dot32(xn, pack_ref[:, kv_at:tail_at])
            kv_own[k] = kv.astype(jnp.bfloat16)
            own = pltpu.make_async_copy(
                kv_own.at[k], kv_ref.at[head, slab, rest], own_sems.at[k]
            )
            own.start()
            owns.append(own)
            for d in range(1, width):
                send(k, 0, 0, 0, x_peers[d], 0, d)
            send(k, 1, 0, 0, y_peer, 1, 0)
            send(k, 0, 0, 0, y_peer, 1, 0)
            for d in range(1, width):
                send(k, 1, 0, 0, x_peers[d], 0, d)
            hand_over(k, 0, 0, 0)
            hand_over(k, 1, 0, 0)

        def second(k):
            for d in range(1, width):
                arrived(k, 0, 0, d)
                send(k, 0, 0, d, y_peer, 1, d)
                hand_over(k, 0, 0, d)
            arrived(k, 1, 1, 0)
            for d in range(1, width):
                send(k, 1, 1, 0, x_peers[d], 1, d)
            hand_over(k, 1, 1, 0)

        def third(k):
            arrived(k, 0, 1, 0)
            hand_over(k, 0, 1, 0)
            for d in range(1, width):
                arrived(k, 1, 0, d)
                hand_over(k, 1, 0, d)
            for d in range(1, width):
                arrived(k, 0, 1, d)
                hand_over(k, 0, 1, d)
                arrived(k, 1, 1, d)
                hand_over(k, 1, 1, d)

        def queries():
            low = lax.broadcasted_iota(jnp.int32, (tail_cols, wide), 0)
            target = lax.broadcasted_iota(jnp.int32, (tail_cols, wide), 1)
            goal = lax.div(low, dim) * LANES + lax.rem(low, dim)
            to_low = ((goal == target) & (low < own_out)).astype(jnp.bfloat16)
            query_w = dot32(tail, to_low).astype(jnp.bfloat16)
            query_w_ref[...] = query_w
            out_rows = pack_ref[pl.ds(pl.multiple_of(plane * own_out, 64), own_out), :features]
            pieces = []
            for h in range(heads):
                pieces += [jnp.zeros((dim, features), jnp.bfloat16), out_rows[h * dim : (h + 1) * dim]]
            out_w_ref[...] = jnp.concatenate(pieces, axis=0)
            for k in range(COLUMNS):
                slab = slabs[k]
                query = dot32(column_ref[slab], query_w).astype(jnp.bfloat16)
                query = query.astype(jnp.float32) * scale
                query_ref[slab] = query.astype(jnp.bfloat16)
            for n, (src, dst) in enumerate(
                (
                    (column_ref, column_out),
                    (query_w_ref, query_w_out),
                    (out_w_ref, out_w_out),
                )
            ):
                copy = pltpu.make_async_copy(src, dst, keep_sems.at[n])
                copy.start()
                owns.append(copy)

        for t in range(COLUMNS + 2):
            if t < COLUMNS:
                first(t)
            elif t == COLUMNS:
                queries()
            if 0 <= t - 1 < COLUMNS:
                second(t - 1)
            if 0 <= t - 2 < COLUMNS:
                third(t - 2)
        for copy in owns + passes:
            copy.wait()
        for copy in sends:
            copy.wait_send()
        if chained:
            chain.finish()

    shapes = [
        pltpu.HBM((COLUMNS, rows, features), jnp.bfloat16),
        make((COLUMNS, rows, wide), jnp.bfloat16),
        pltpu.HBM((features, wide), jnp.bfloat16),
        pltpu.HBM((wide, features), jnp.bfloat16),
        make((2, COLUMNS, span, rows, wide), jnp.bfloat16),
    ]
    operands = [source, pack]
    if chained:
        operands.append(smalls)
    else:
        shapes = [jax.ShapeDtypeStruct((small_rows, features), jnp.float32)] + shapes
    results = pl.pallas_call(
        body,
        out_shape=shapes,
        in_specs=[VMEM] * len(operands),
        out_specs=([] if chained else [VMEM]) + [HBM, VMEM, HBM, HBM, ANY],
        scratch_shapes=[
            pltpu.VMEM((COLUMNS, rows, features), jnp.bfloat16),
            pltpu.VMEM((features, wide), jnp.bfloat16),
            pltpu.VMEM((wide, features), jnp.bfloat16),
            pltpu.VMEM((COLUMNS, rows, wide), jnp.bfloat16),
            DMA((COLUMNS,)),
            DMA((COLUMNS * links,)),
            DMA((COLUMNS, 2, 2, width)),
            DMA((COLUMNS, 2, 2, width)),
            DMA((COLUMNS, 2, 2, width)),
            DMA((COLUMNS, 2)),
            DMA((COLUMNS,)),
            DMA((3,)),
        ],
        compiler_params=comm_params(
            collective_id,
            operands
            + [make(shape.shape, shape.dtype) for shape in shapes[:-1]]
            + [make((COLUMNS, rows, wide), jnp.bfloat16)],
            3 * SPARE_BYTES,
        ),
        cost_estimate=lasting(cost),
    )(*operands)
    return list(results) + [smalls] if chained else list(results[1:]) + [results[0]]


def plane_reduce(arrays, blocks, collective_id, cost=25):
    span = blocks // COLUMNS
    width = span // 2
    count = len(arrays)
    shapes = [(values.shape[1],) + tuple(values.shape[3:]) for values in arrays]

    def body(*refs):
        srcs, outs, refs = refs[:count], refs[count : 2 * count], refs[2 * count :]
        scratch = [refs[8 * n : 8 * n + 8] for n in range(count)]
        core_send, core_recv, link_send, link_recv = refs[8 * count :]
        head, blk = lax.axis_index("head"), lax.axis_index("blk")
        plane, rest = lax.div(blk, span), lax.rem(blk, span)
        x, core = lax.div(rest, 2), lax.rem(rest, 2)
        first = plane * span
        right = [lax.rem(x + d, width) for d in range(width)]
        x_peers = [(head, first + right[d] * 2 + core) for d in range(width)]
        y_peer = (1 - head, blk)
        core_peer = (head, first + x * 2 + 1 - core)
        greet(x_peers[1:] + [y_peer, core_peer])

        def wide(ref, *at):
            return ref[at].astype(jnp.float32)

        starts = {}
        for n in range(count):
            half = shapes[n][0] // 2
            for h in range(2):
                copy = remote(
                    srcs[n].at[:, pl.ds(h * half, half), :, 1 - core],
                    scratch[n][0].at[:, pl.ds(h * half, half)],
                    core_send.at[n, h],
                    core_recv.at[n, h],
                    core_peer,
                )
                copy.start()
                starts[n, h] = copy

        sends, yas, ybs, xbs = {}, {}, {}, {}
        for n in range(count):
            src, half, kind = srcs[n], shapes[n][0] // 2, arrays[n].dtype
            core_in, summed, xa_in, _, _, yb_in, _, _ = scratch[n]

            def core_sum(h):
                def step(i, _):
                    yy = lax.div(i, half * width)
                    zz = lax.div(lax.rem(i, half * width), width) + h * half
                    xx = lax.rem(i, width)
                    total = wide(src, yy, zz, xx, core) + wide(core_in, yy, zz, xx)
                    summed[yy, zz, xx] = total.astype(kind)
                    return 0

                lax.fori_loop(0, 2 * half * width, step, 0)

            starts[n, 0].wait_recv()
            core_sum(0)
            for d in range(1, width):
                copy = remote(
                    summed.at[:, pl.ds(0, half), right[d]],
                    xa_in.at[d],
                    link_send.at[n, 0, d],
                    link_recv.at[n, 0, d],
                    x_peers[d],
                )
                copy.start()
                sends[n, d] = copy
            starts[n, 1].wait_recv()
            core_sum(1)
            ybs[n] = remote(
                summed.at[1 - head, pl.ds(half, half)],
                yb_in,
                link_send.at[n, 1, 0],
                link_recv.at[n, 1, 0],
                y_peer,
            )
            ybs[n].start()
        for n in range(count):
            half, kind = shapes[n][0] // 2, arrays[n].dtype
            _, summed, xa_in, ya_out, ya_in, yb_in, xb_out, xb_in = scratch[n]
            for d in range(1, width):
                sends[n, d].wait_recv()

            def a_step(zz, _):
                total = wide(summed, 1 - head, zz, x)
                for d in range(1, width):
                    total = total + wide(xa_in, d, 1 - head, zz)
                ya_out[zz] = total.astype(kind)
                return 0

            lax.fori_loop(0, half, a_step, 0)
            yas[n] = remote(
                ya_out, ya_in, link_send.at[n, 0, 0], link_recv.at[n, 0, 0], y_peer
            )
            yas[n].start()
            ybs[n].wait_recv()
            for d in range(1, width):

                def b_step(zz, _):
                    total = wide(summed, head, half + zz, right[d]) + wide(yb_in, zz, right[d])
                    xb_out[d, zz] = total.astype(kind)
                    return 0

                lax.fori_loop(0, half, b_step, 0)
                xbs[n, d] = remote(
                    xb_out.at[d],
                    xb_in.at[d],
                    link_send.at[n, 1, d],
                    link_recv.at[n, 1, d],
                    x_peers[d],
                )
                xbs[n, d].start()
        for n in range(count):
            out, half, kind = outs[n], shapes[n][0] // 2, arrays[n].dtype
            _, summed, xa_in, _, ya_in, yb_in, _, xb_in = scratch[n]
            yas[n].wait_recv()

            def a_last(zz, _):
                total = wide(summed, head, zz, x) + wide(ya_in, zz)
                for d in range(1, width):
                    total = total + wide(xa_in, d, head, zz)
                out[zz] = total.astype(kind)
                return 0

            lax.fori_loop(0, half, a_last, 0)
            for d in range(1, width):
                xbs[n, d].wait_recv()

            def b_last(zz, _):
                total = wide(summed, head, half + zz, x) + wide(yb_in, zz, x)
                for d in range(1, width):
                    total = total + wide(xb_in, d, zz)
                out[half + zz] = total.astype(kind)
                return 0

            lax.fori_loop(0, half, b_last, 0)
        for group in (starts, sends, yas, ybs, xbs):
            for copy in group.values():
                copy.wait_send()

    scratch = []
    for (slabs, *tile), values in zip(shapes, arrays):
        tile, half, kind = tuple(tile), slabs // 2, values.dtype
        scratch += [
            pltpu.VMEM((2, slabs, width) + tile, kind),
            pltpu.VMEM((2, slabs, width) + tile, kind),
            pltpu.VMEM((width, 2, half) + tile, kind),
            pltpu.VMEM((half,) + tile, kind),
            pltpu.VMEM((half,) + tile, kind),
            pltpu.VMEM((half, width) + tile, kind),
            pltpu.VMEM((width, half) + tile, kind),
            pltpu.VMEM((width, half) + tile, kind),
        ]
    return pl.pallas_call(
        body,
        out_shape=[
            jax.ShapeDtypeStruct(shape, values.dtype) for shape, values in zip(shapes, arrays)
        ],
        in_specs=[VMEM] * count,
        out_specs=[VMEM] * count,
        scratch_shapes=scratch
        + [DMA((count, 2)), DMA((count, 2)), DMA((count, 2, width)), DMA((count, 2, width))],
        compiler_params=comm_params(
            collective_id, scratch + 2 * [make(a.shape, a.dtype) for a in arrays]
        ),
        cost_estimate=lasting(cost),
    )(
        *[
            values.reshape((2, values.shape[1], width, 2) + tuple(values.shape[3:]))
            for values in arrays
        ]
    )


def reduce_project(dkv_all, dq, query_w, pack, blocks, collective_id, cost=26):
    span = blocks // COLUMNS
    width = span // 2
    rows, wide = dkv_all.shape[3:]
    half = rows // 2
    features = query_w.shape[0]
    kind = dkv_all.dtype

    def body(
        src,
        dq_ref,
        w_ref,
        pack_ref,
        dkv_ref,
        dxn_ref,
        core_in,
        summed,
        xa_in,
        ya_out,
        ya_in,
        yb_in,
        xb_out,
        xb_in,
        share,
        core_send,
        core_recv,
        link_send,
        link_recv,
        z_send,
        z_recv,
    ):
        head, _, core, _, x_peers, y_peer, core_peer = plane_place(blocks)
        plane, planes, z_peers = column_place(blocks)
        x = lax.div(lax.rem(lax.axis_index("blk"), span), 2)
        right = [lax.rem(x + d, width) for d in range(width)]
        greet(x_peers[1:] + [y_peer, core_peer] + z_peers[1:])
        order = (2, 1, 3, 0)
        copies = []

        def begin(copy):
            copy.start()
            copies.append(copy)
            return copy

        def wide_of(ref, *at):
            return ref[at].astype(jnp.float32)

        top, low = pl.ds(0, half), pl.ds(half, half)
        starts = []

        def cross(k):
            starts.append(
                begin(
                    remote(
                        src.at[:, planes[order[k]], :, 1 - core],
                        core_in.at[k],
                        core_send.at[k],
                        core_recv.at[k],
                        core_peer,
                    )
                )
            )

        cross(0)
        cross(1)
        xas, yas, ybs, xbs, z_copies = {}, {}, {}, {}, []

        def first(k):
            starts[k].wait_recv()
            if k + 2 < COLUMNS:
                cross(k + 2)

            def step(i, _):
                yy, xx = lax.div(i, width), lax.rem(i, width)
                total = wide_of(src, yy, planes[order[k]], xx, core) + wide_of(core_in, k, yy, xx)
                summed[k, yy, xx] = total.astype(kind)
                return 0

            lax.fori_loop(0, 2 * width, step, 0)
            for d in range(1, width):
                xas[k, d] = begin(
                    remote(
                        summed.at[k, :, right[d], top],
                        xa_in.at[k, d],
                        link_send.at[k, 0, d],
                        link_recv.at[k, 0, d],
                        x_peers[d],
                    )
                )
            ybs[k] = begin(
                remote(
                    summed.at[k, 1 - head, :, low],
                    yb_in.at[k],
                    link_send.at[k, 1, 0],
                    link_recv.at[k, 1, 0],
                    y_peer,
                )
            )

        def second(k):
            total = wide_of(summed, k, 1 - head, x, top)
            for d in range(1, width):
                xas[k, d].wait_recv()
                total = total + wide_of(xa_in, k, d, 1 - head)
            ya_out[k] = total.astype(kind)
            yas[k] = begin(
                remote(
                    ya_out.at[k],
                    ya_in.at[k],
                    link_send.at[k, 0, 0],
                    link_recv.at[k, 0, 0],
                    y_peer,
                )
            )
            ybs[k].wait_recv()
            for d in range(1, width):
                total = wide_of(summed, k, head, right[d], low) + wide_of(yb_in, k, right[d])
                xb_out[k, d] = total.astype(kind)
                xbs[k, d] = begin(
                    remote(
                        xb_out.at[k, d],
                        xb_in.at[k, d],
                        link_send.at[k, 1, d],
                        link_recv.at[k, 1, d],
                        x_peers[d],
                    )
                )

        def third(k):
            slab = planes[order[k]]
            yas[k].wait_recv()
            total = wide_of(summed, k, head, x, top) + wide_of(ya_in, k)
            for d in range(1, width):
                total = total + wide_of(xa_in, k, d, head)
            dkv_ref[slab, top] = total.astype(kind)
            total = wide_of(summed, k, head, x, low) + wide_of(yb_in, k, x)
            for d in range(1, width):
                xbs[k, d].wait_recv()
                total = total + wide_of(xb_in, k, d)
            dkv_ref[slab, low] = total.astype(kind)
            part = (
                dot32(dq_ref[slab], w_ref[...], LAST)
                + dot32(dkv_ref[slab], pack_ref[:, features : features + wide], LAST)
            ).astype(kind)
            if order[k] == 0:
                dxn_ref[plane] = part
            else:
                share[k] = part
                z_copies.append(
                    begin(
                        remote(
                            share.at[k],
                            dxn_ref.at[plane],
                            z_send.at[order[k]],
                            z_recv.at[order[k]],
                            z_peers[order[k]],
                        )
                    )
                )

        for t in range(COLUMNS + 2):
            if t < COLUMNS:
                first(t)
            if 0 <= t - 1 < COLUMNS:
                second(t - 1)
            if 0 <= t - 2 < COLUMNS:
                third(t - 2)
        for copy in z_copies:
            copy.wait_recv()
        for copy in copies:
            copy.wait_send()

    tile = (rows, wide)
    part = (half, wide)
    scratch = [
        pltpu.VMEM((COLUMNS, 2, width) + tile, kind),
        pltpu.VMEM((COLUMNS, 2, width) + tile, kind),
        pltpu.VMEM((COLUMNS, width, 2) + part, kind),
        pltpu.VMEM((COLUMNS,) + part, kind),
        pltpu.VMEM((COLUMNS,) + part, kind),
        pltpu.VMEM((COLUMNS, width) + part, kind),
        pltpu.VMEM((COLUMNS, width) + part, kind),
        pltpu.VMEM((COLUMNS, width) + part, kind),
        pltpu.VMEM((COLUMNS, rows, features), kind),
    ]
    shapes = [make((COLUMNS,) + tile, kind), make((COLUMNS, rows, features), kind)]
    return pl.pallas_call(
        body,
        out_shape=shapes,
        in_specs=[VMEM] * 4,
        out_specs=[VMEM] * 2,
        scratch_shapes=scratch
        + [
            DMA((COLUMNS,)),
            DMA((COLUMNS,)),
            DMA((COLUMNS, 2, width)),
            DMA((COLUMNS, 2, width)),
            DMA((COLUMNS,)),
            DMA((COLUMNS,)),
        ],
        compiler_params=comm_params(
            collective_id, scratch + shapes + [dkv_all, dq, query_w, pack]
        ),
        cost_estimate=lasting(cost),
    )(dkv_all.reshape((2, COLUMNS, width, 2) + tile), dq, query_w, pack)


NEGATIVE = -1e30
EPSILON = 1e-06
KEYS = 1024
LANES = 128
LAST = (((1,), (1,)), ((), ()))
FIRST = (((0,), (0,)), ((), ()))


def dot32(a, b, dims=(((1,), (0,)), ((), ()))):
    return lax.dot_general(a, b, dims, preferred_element_type=jnp.float32)


def visible(key_base, query_base, keys, queries, starts):
    key_pos = key_base + lax.broadcasted_iota(jnp.int32, (keys, queries), 0)
    query_pos = query_base + lax.broadcasted_iota(jnp.int32, (keys, queries), 1)
    return (key_pos <= query_pos) & (key_pos >= starts)


def block_bounds(starts, bases, rows):
    return jnp.stack(
        [
            lax.div(starts[:, 0], KEYS),
            lax.div(bases + rows - 1, KEYS),
            bases,
            lax.div(starts[:, rows - 1], KEYS),
        ],
        axis=1,
    )


def over_chunks(bounds_ref, i, step, carry):
    low, high, edge = bounds_ref[i, 0], bounds_ref[i, 1], bounds_ref[i, 3]
    carry = step(high, True, carry)
    inner = jnp.maximum(high - 1 - edge, 0)
    carry = lax.fori_loop(0, inner, lambda t, c: step(high - 1 - t, False, c), carry)
    below = high - 1 - inner
    return lax.fori_loop(0, below - low + 1, lambda t, c: step(below - t, True, c), carry)


def attend(bounds, queries, kv_all, starts):
    count, rows, width = queries.shape
    heads = width // LANES

    def body(bounds_ref, q_ref, kv_ref, start_ref, out_ref, attn_ref):
        i = pl.program_id(0)
        base = bounds_ref[i, 2]
        start_row = start_ref[0]
        q = [q_ref[0, :, h * LANES : (h + 1) * LANES] for h in range(heads)]

        def step(chunk, masked, carry):
            at = pl.multiple_of(chunk * KEYS, KEYS)
            if masked:
                ok = visible(chunk * KEYS, base, KEYS, rows, start_row)
            kvs = [kv_ref[pl.ds(at, KEYS), h * LANES : (h + 1) * LANES] for h in range(heads)]
            scores = [dot32(kvs[h], q[h], LAST) for h in range(heads)]
            if masked:
                scores = [jnp.where(ok, s, NEGATIVE) for s in scores]
            tops = [
                jnp.maximum(carry[h][0], jnp.max(scores[h], axis=0, keepdims=True))
                for h in range(heads)
            ]
            weights = [jnp.exp(scores[h] - tops[h]) for h in range(heads)]
            shrinks = [jnp.exp(carry[h][0] - tops[h]) for h in range(heads)]
            totals = [
                carry[h][1] * shrinks[h] + jnp.sum(weights[h], axis=0, keepdims=True)
                for h in range(heads)
            ]
            accs = [
                carry[h][2] * shrinks[h] + dot32(kvs[h], weights[h].astype(jnp.bfloat16), FIRST)
                for h in range(heads)
            ]
            return tuple(zip(tops, totals, accs))

        empty = tuple(
            (
                jnp.full((1, rows), NEGATIVE, jnp.float32),
                jnp.zeros((1, rows), jnp.float32),
                jnp.zeros((LANES, rows), jnp.float32),
            )
            for h in range(heads)
        )
        done = over_chunks(bounds_ref, i, step, empty)
        lane = lax.broadcasted_iota(jnp.int32, (LANES, rows), 0)
        narrow = []
        for h in range(heads):
            top, total, acc = done[h]
            value = jnp.where(lane < LANES // 2, top + jnp.log(total), acc / total)
            out_ref[0, :, h * LANES : (h + 1) * LANES] = value.T
            narrow.append(value[LANES // 2 :])
        attn_ref[0] = jnp.concatenate(narrow, axis=0).T.astype(jnp.bfloat16)

    return pl.pallas_call(
        body,
        out_shape=(
            jax.ShapeDtypeStruct((count, rows, width), jnp.float32),
            jax.ShapeDtypeStruct((count, rows, width // 2), jnp.bfloat16),
        ),
        grid_spec=pltpu.PrefetchScalarGridSpec(
            num_scalar_prefetch=1,
            grid=(count,),
            in_specs=[
                pl.BlockSpec((1, rows, width), lambda i, b: (i, 0, 0)),
                pl.BlockSpec(kv_all.shape, lambda i, b: (0, 0)),
                pl.BlockSpec((1, 1, rows), lambda i, b: (i, 0, 0)),
            ],
            out_specs=(
                pl.BlockSpec((1, rows, width), lambda i, b: (i, 0, 0)),
                pl.BlockSpec((1, rows, width // 2), lambda i, b: (i, 0, 0)),
            ),
        ),
        compiler_params=pltpu.CompilerParams(
            vmem_limit_bytes=room([kv_all] * 2, 4 * SPARE_BYTES)
        ),
        cost_estimate=lasting(13),
    )(bounds, queries, kv_all, starts)


def attend_back(bounds, queries, dy, out_rows, kept, kv_all, starts, scale):
    count, rows, width = queries.shape
    total_keys = kv_all.shape[0]
    heads = width // LANES
    if total_keys * width * 14 > VMEM_BYTES:
        heads = 1
    wide = heads * LANES

    def body(bounds_ref, q_ref, dy_ref, w_ref, kept_ref, kv_ref, start_ref, dq_ref, dkv_ref, acc_ref):
        i = pl.program_id(1)
        base = bounds_ref[i, 2]
        start_row = start_ref[0]

        @pl.when(i == 0)
        def _():
            def clear(c, _):
                acc_ref[pl.ds(pl.multiple_of(c * KEYS, KEYS), KEYS), :] = jnp.zeros(
                    (KEYS, wide), jnp.float32
                )
                return 0

            lax.fori_loop(0, total_keys // KEYS, clear, 0)

        q = [q_ref[0, :, h * LANES : (h + 1) * LANES] for h in range(heads)]
        grads = dot32(dy_ref[0], w_ref[...], LAST).astype(jnp.bfloat16)
        g = [grads[:, h * LANES : (h + 1) * LANES] for h in range(heads)]
        qg = [jnp.concatenate([q[h], g[h]], axis=0) for h in range(heads)]
        lse, delta = [], []
        for h in range(heads):
            kept_t = kept_ref[0, :, h * LANES : (h + 1) * LANES].T
            lse.append(kept_t[0:1])
            delta.append(jnp.sum(kept_t * g[h].astype(jnp.float32).T, axis=0, keepdims=True))

        def step(chunk, masked, carry):
            at = pl.multiple_of(chunk * KEYS, KEYS)
            if masked:
                ok = visible(chunk * KEYS, base, KEYS, rows, start_row)
            lanes = [slice(h * LANES, (h + 1) * LANES) for h in range(heads)]
            kvs = [kv_ref[pl.ds(at, KEYS), lanes[h]] for h in range(heads)]
            pairs = [dot32(kvs[h], qg[h], LAST) for h in range(heads)]
            scores = [p[:, :rows] for p in pairs]
            dprobs = [p[:, rows:] for p in pairs]
            if masked:
                scores = [jnp.where(ok, s, NEGATIVE) for s in scores]
            probs = [jnp.exp(scores[h] - lse[h]) for h in range(heads)]
            dscores = [
                (probs[h] * (dprobs[h] - delta[h])).astype(jnp.bfloat16) for h in range(heads)
            ]
            both = [
                jnp.concatenate([dscores[h], probs[h].astype(jnp.bfloat16)], axis=1)
                for h in range(heads)
            ]
            for h in range(heads):
                acc_ref[pl.ds(at, KEYS), lanes[h]] += dot32(both[h], qg[h])
            return tuple(carry[h] + dot32(kvs[h], dscores[h], FIRST) for h in range(heads))

        done = over_chunks(
            bounds_ref,
            i,
            step,
            tuple(jnp.zeros((LANES, rows), jnp.float32) for h in range(heads)),
        )
        lane = lax.broadcasted_iota(jnp.int32, (LANES, rows), 0)
        for h in range(heads):
            value = jnp.where(lane < LANES // 2, done[h] * scale, 0.0)
            dq_ref[0, :, h * LANES : (h + 1) * LANES] = value.T.astype(jnp.bfloat16)

        @pl.when(i == count - 1)
        def _():
            def store(c, _):
                at = pl.ds(pl.multiple_of(c * KEYS, KEYS), KEYS)
                dkv_ref[at, :] = acc_ref[at, :].astype(jnp.bfloat16)
                return 0

            lax.fori_loop(0, total_keys // KEYS, store, 0)

    block = pl.BlockSpec((1, rows, wide), lambda h, i, b: (i, 0, h))
    whole = pl.BlockSpec((total_keys, wide), lambda h, i, b: (0, h))
    return pl.pallas_call(
        body,
        out_shape=(
            jax.ShapeDtypeStruct((count, rows, width), jnp.bfloat16),
            jax.ShapeDtypeStruct(kv_all.shape, jnp.bfloat16),
        ),
        grid_spec=pltpu.PrefetchScalarGridSpec(
            num_scalar_prefetch=1,
            grid=(width // wide, count),
            in_specs=[
                block,
                pl.BlockSpec((1,) + tuple(dy.shape[1:]), lambda h, i, b: (i, 0, 0)),
                pl.BlockSpec((wide, out_rows.shape[1]), lambda h, i, b: (h, 0)),
                block,
                whole,
                pl.BlockSpec((1, 1, rows), lambda h, i, b: (i, 0, 0)),
            ],
            out_specs=(block, whole),
            scratch_shapes=[pltpu.VMEM((total_keys, wide), jnp.float32)],
        ),
        compiler_params=pltpu.CompilerParams(
            vmem_limit_bytes=room([make((total_keys, wide), jnp.bfloat16)] * 6, 5 * SPARE_BYTES)
        ),
        cost_estimate=lasting(20),
    )(bounds, queries, dy, out_rows, kept, kv_all, starts)


def experts_exchange(
    sent,
    saved,
    own,
    other,
    layer,
    blocks,
    collective_id,
    forward,
    backward,
    cost,
    ahead=None,
    cross=(),
):
    fetch = other[2] is None
    other = [w for w in other if w is not None]
    copies = blocks // NE
    half = NE // 2
    slots, width = sent[0].shape[1:]
    hidden, features = other[0].shape
    tile = min(hidden, 256)
    tiles = hidden // tile
    count = len(sent)
    homes_count = int(forward) + int(backward)
    total_rows = copies * NE * slots
    kind = sent[0].dtype
    sizes = (half // 2, half // 2, half)
    first_rows = [copies * slots * at for at in (0, half // 2, half)]
    most_rows = copies * slots * half
    plain = (((1,), (0,)), ((), ()))

    def body(*refs):
        refs = list(refs)

        def take(n):
            taken = refs[:n]
            del refs[:n]
            return taken

        srcs = take(count)
        saved_ref = take(1)[0] if not forward else None
        weight_refs = take(3 + len(other))
        ahead_ref = take(1)[0] if ahead is not None else None
        cross_refs = take(len(cross))
        homes = take(homes_count)
        arrived_ref = take(1)[0] if not backward else None
        fetched_ref = take(1)[0] if fetch and not backward else None
        next_ref = take(1)[0] if ahead is not None else None
        keeps, aways = (take(3), take(3)) if backward else ([], [])
        crossed = take(len(cross))
        lands = take(count)
        weights = take(6)
        parts, sib_ins, totals = take(homes_count), take(homes_count), take(homes_count)
        accs = take(homes_count)
        rows_x = take(1)[0]
        if backward:
            rows_z, act_ref, dgate_ref, dup_ref, keep_ref, away_ref = take(6)
            if not forward:
                gate_ref, up_ref = take(2)
            out_sems = take(1)[0]
        load_sems, own_sems, send_sems, recv_sems, pass_sems, land_sems = take(6)
        home_own, home_send, home_recv, part_send, part_recv, arrived_sem = take(6)
        swap_send, swap_recv = take(2)

        head, blk = lax.axis_index("head"), lax.axis_index("blk")
        expert, piece = lax.div(blk, copies), lax.rem(blk, copies)
        near = lax.div(expert, half) * half
        far = half - near
        places = [lax.rem(piece + k, copies) for k in range(copies)]
        siblings = [(head, expert * copies + places[k]) for k in range(copies)]
        others = [lax.rem(expert + d, NE) for d in range(NE)]
        swaps = [(1 - head, blk)] if fetch or ahead is not None or cross else []
        greet([(head, e * copies + piece) for e in others[1:]] + siblings[1:] + swaps)
        mine = pl.ds(pl.multiple_of(head * features, LANES), features)
        rest = pl.ds(pl.multiple_of((1 - head) * features, LANES), features)
        steps = [(far, sizes[0]), (far + sizes[0], sizes[1]), (near, sizes[2])]

        def sending(n, e):
            return remote(
                srcs[n].at[e],
                lands[n].at[piece, expert],
                send_sems.at[n, e],
                recv_sems.at[n, expert],
                (head, e * copies + piece),
            )

        owns = []
        for n in range(count):
            copy = pltpu.make_async_copy(
                srcs[n].at[expert], lands[n].at[piece, expert], own_sems.at[n]
            )
            copy.start()
            owns.append(copy)
        def each(t, copy_of, arrays, act):
            first, size = steps[t]
            for j in range(size):
                for n in range(arrays):
                    if t < 2:
                        act(copy_of(n, first + j))
                    else:

                        @pl.when(first + j != expert)
                        def _():
                            act(copy_of(n, first + j))

        def send(t):
            each(t, sending, count, lambda copy: copy.start())

        def sent_out(t):
            each(t, sending, count, lambda copy: copy.wait_send())

        for t in range(3):
            send(t)
        crossing = []
        if fetch:
            crossing.append(
                remote(
                    weight_refs[4].at[layer],
                    weights[5],
                    swap_send.at[0],
                    swap_recv.at[0],
                    swaps[0],
                )
            )
        if ahead is not None:
            crossing.append(
                remote(
                    ahead_ref.at[layer + 1],
                    next_ref,
                    swap_send.at[1],
                    swap_recv.at[1],
                    swaps[0],
                )
            )
        for n in range(len(cross)):
            crossing.append(
                remote(
                    cross_refs[n],
                    crossed[n],
                    swap_send.at[2 + n],
                    swap_recv.at[2 + n],
                    swaps[0],
                )
            )
        for n, copy in enumerate(crossing):
            if ahead is None or n == 0:
                copy.start()
        loads = []
        for n in range(3 + len(other)):
            weight = weight_refs[n] if n % 2 else weight_refs[n].at[layer]
            copy = pltpu.make_async_copy(weight, weights[n], load_sems.at[n])
            copy.start()
            loads.append(copy)
        go, gx, uo, ux, do, dx = weights
        passes, exchanges = [], {}

        def arrive(t):
            first, size = steps[t]
            waits = []
            if t == 2:
                for copy in owns:
                    copy.wait()
            for j in range(size):
                e = first + j
                for n in range(count):
                    place = lands[n].at[piece, e]

                    @pl.when(e != expert)
                    def _():
                        remote(
                            place, place, send_sems.at[n, e], recv_sems.at[n, e], siblings[0]
                        ).wait_recv()

                    for k in range(1, copies):
                        copy = remote(
                            place,
                            place,
                            pass_sems.at[n, k, e],
                            land_sems.at[n, k, e],
                            siblings[k],
                        )
                        copy.start()
                        waits.append(copy)
            for copy in waits:
                copy.wait_recv()
            passes.extend(waits)

        def flat(ref, t):
            first, size = steps[t]
            value = ref[:, pl.ds(first, size)].astype(jnp.float32)
            return value.reshape((copies * size * slots, width)).astype(kind)

        def span_of(t):
            return slice(first_rows[t], first_rows[t] + copies * steps[t][1] * slots)

        def gate_up(t, j):
            at = pl.ds(pl.multiple_of(j * tile, tile), tile)
            xo, xx = rows_x[span_of(t), mine], rows_x[span_of(t), rest]
            gate = dot32(xo, go[at], LAST) + dot32(xx, gx[at], LAST)
            return gate, dot32(xo, uo[at], LAST) + dot32(xx, ux[at], LAST)

        def early(t):
            rows_x[span_of(t)] = flat(saved_ref, t)
            size = copies * steps[t][1] * slots

            def step(j, _):
                at = pl.ds(pl.multiple_of(j * tile, tile), tile)
                gate_ref[:size, at], up_ref[:size, at] = gate_up(t, j)
                return 0

            lax.fori_loop(0, tiles, step, 0)

        def work(t):
            size = copies * steps[t][1] * slots
            span = span_of(t)
            if forward:
                rows_x[span] = flat(lands[0], t)
            if backward:
                rows_z[span] = flat(lands[-1], t)
            for acc in accs:
                acc[:size] = jnp.zeros((size, width), jnp.float32)

            def step(j, _):
                at = pl.ds(pl.multiple_of(j * tile, tile), tile)
                if forward:
                    gate, up = gate_up(t, j)
                else:
                    gate, up = gate_ref[:size, at], up_ref[:size, at]
                sigmoid = jax.nn.sigmoid(gate)
                silu = gate * sigmoid
                act = (silu * up).astype(kind)
                if forward:
                    accs[0][:size, mine] += dot32(act, do[at])
                    accs[0][:size, rest] += dot32(act, dx[at])
                if backward:
                    zo, zx = rows_z[span, mine], rows_z[span, rest]
                    dact = dot32(zo, do[at], LAST) + dot32(zx, dx[at], LAST)
                    dgate = (dact * up * sigmoid * (1.0 + gate * (1.0 - sigmoid))).astype(kind)
                    dup = (dact * silu).astype(kind)
                    act_ref[span, at] = act
                    dgate_ref[span, at] = dgate
                    dup_ref[span, at] = dup
                    accs[-1][:size, mine] += dot32(dgate, go[at]) + dot32(dup, uo[at])
                    accs[-1][:size, rest] += dot32(dgate, gx[at]) + dot32(dup, ux[at])
                return 0

            lax.fori_loop(0, tiles, step, 0)
            first, size_e = steps[t]
            for n in range(homes_count):
                value = accs[n][:size].reshape((copies, size_e, slots, width))
                parts[n][:, pl.ds(first, size_e)] = value.astype(kind)
                for j in range(size_e):
                    for k in range(1, copies):
                        copy = remote(
                            parts[n].at[places[k], first + j],
                            sib_ins[n].at[k - 1, first + j],
                            part_send.at[n, k, first + j],
                            part_recv.at[n, k, first + j],
                            siblings[k],
                        )
                        copy.start()
                        exchanges[n, t, j, k] = copy

        def homeward(n, e):
            return remote(
                totals[n].at[e],
                homes[n].at[expert],
                home_send.at[n, e],
                home_recv.at[n, expert],
                (head, e * copies + piece),
            )

        def give_back(t):
            first, size = steps[t]
            for j in range(size):
                e = first + j
                for n in range(homes_count):
                    value = parts[n][piece, e].astype(jnp.float32)
                    for k in range(1, copies):
                        exchanges[n, t, j, k].wait_recv()
                        value = value + sib_ins[n][k - 1, e].astype(jnp.float32)
                    totals[n][e] = value.astype(kind)
                    if t < 2:
                        homeward(n, e).start()
                    else:

                        @pl.when(e != expert)
                        def _():
                            homeward(n, e).start()

        for copy in loads:
            copy.wait()
        if not forward:
            early(0)
        for t in range(len(steps)):
            arrive(t)
            if t == 0 and fetch:
                crossing[0].wait_recv()
                if ahead is not None:
                    crossing[1].start()
            work(t)
            if t > 0:
                give_back(t - 1)
            if not forward and t + 1 < len(steps):
                early(t + 1)
        give_back(len(steps) - 1)
        stays = []
        for n in range(homes_count):
            copy = pltpu.make_async_copy(
                totals[n].at[expert], homes[n].at[expert], home_own.at[n]
            )
            copy.start()
            stays.append(copy)

        if backward:

            def saving(n, j, which):
                at = pl.ds(pl.multiple_of(j * tile, tile), tile)
                src, dst = ((keep_ref, keeps), (away_ref, aways))[which]
                return pltpu.make_async_copy(src.at[n, at], dst[n].at[at], out_sems.at[n, j, which])

            def grads(j, _):
                at = pl.ds(pl.multiple_of(j * tile, tile), tile)
                for n, (left, right) in enumerate(
                    ((dgate_ref, rows_x), (dup_ref, rows_x), (act_ref, rows_z))
                ):
                    value = left[:, at]
                    away_ref[n, at] = dot32(value, right[:, rest], FIRST).astype(kind)
                    saving(n, j, 1).start()
                    keep_ref[n, at] = dot32(value, right[:, mine], FIRST).astype(kind)
                    saving(n, j, 0).start()
                return 0

            lax.fori_loop(0, tiles, grads, 0)

        if not backward:
            copy = pltpu.make_async_copy(lands[0], arrived_ref, arrived_sem)
            copy.start()
            stays.append(copy)
            if fetch:
                copy = pltpu.make_async_copy(weights[5], fetched_ref, load_sems.at[5])
                copy.start()
                stays.append(copy)
        for n in range(homes_count):
            for e in others[1:]:
                place = homes[n].at[e]
                remote(
                    place, place, home_send.at[n, e], home_recv.at[n, e], siblings[0]
                ).wait_recv()
        for t in range(len(steps)):
            sent_out(t)
            each(t, homeward, homes_count, lambda copy: copy.wait_send())
        for copy in passes + list(exchanges.values()):
            copy.wait_send()
        for copy in stays:
            copy.wait()
        for copy in crossing[int(fetch) :]:
            copy.wait_recv()
        for copy in crossing:
            copy.wait_send()
        if backward:

            def settle(j, _):
                for n in range(3):
                    saving(n, j, 0).wait()
                    saving(n, j, 1).wait()
                return 0

            lax.fori_loop(0, tiles, settle, 0)

    slab = (copies, NE, slots, width)
    shapes = [make((NE, slots, width), kind)] * homes_count
    specs = [ANY] * homes_count
    if not backward:
        shapes.append(pltpu.HBM(slab, kind))
        specs.append(HBM)
        for _ in range(int(fetch) + int(ahead is not None)):
            shapes.append(pltpu.HBM((hidden, features), kind))
            specs.append(HBM)
    else:
        shapes += [pltpu.HBM((hidden, features), kind)] * (6 + len(cross))
        specs += [HBM] * (6 + len(cross))
    scratch = [pltpu.VMEM(slab, kind)] * count
    scratch += [pltpu.VMEM((hidden, features), kind)] * 6
    scratch += [pltpu.VMEM(slab, kind)] * homes_count
    scratch += [pltpu.VMEM((copies - 1,) + slab[1:], kind)] * homes_count
    scratch += [pltpu.VMEM((NE, slots, width), kind)] * homes_count
    scratch += [pltpu.VMEM((most_rows, width), jnp.float32)] * homes_count
    scratch.append(pltpu.VMEM((total_rows, width), kind))
    if backward:
        scratch.append(pltpu.VMEM((total_rows, width), kind))
        scratch += [pltpu.VMEM((total_rows, hidden), kind)] * 3
        scratch += [pltpu.VMEM((3, hidden, features), kind)] * 2
        if not forward:
            scratch += [pltpu.VMEM((most_rows, hidden), jnp.float32)] * 2
        scratch.append(DMA((3, tiles, 2)))
    scratch += [DMA((6,)), DMA((count,)), DMA((count, NE)), DMA((count, NE))]
    scratch += [DMA((count, copies, NE))] * 2
    scratch += [DMA((homes_count,)), DMA((homes_count, NE)), DMA((homes_count, NE))]
    scratch += [DMA((homes_count, copies, NE))] * 2 + [DMA] + [DMA((2 + len(cross),))] * 2
    operands = list(sent)
    in_specs = [ANY] * count
    if not forward:
        operands.append(saved)
        in_specs.append(VMEM)
    for n in range(3):
        operands += [own[n]] + other[n : n + 1]
    if ahead is not None:
        operands.append(ahead)
    operands += list(cross)
    in_specs += [HBM] * (len(operands) - len(in_specs))
    return pl.pallas_call(
        body,
        out_shape=shapes,
        in_specs=in_specs,
        out_specs=specs,
        scratch_shapes=scratch,
        compiler_params=comm_params(
            collective_id,
            scratch + ([saved] if not forward else []),
            (11 if backward else 2) * SPARE_BYTES,
        ),
        cost_estimate=lasting(cost),
    )(*operands)


def split(values, terms=2):
    parts = []
    for _ in range(terms):
        part = values.astype(jnp.bfloat16)
        parts.append(part)
        values = values - part.astype(jnp.float32)
    return parts


def exact_dot(pieces, values, dims):
    total = dot32(pieces[0], values, dims)
    for piece in pieces[1:]:
        total = total + dot32(piece, values, dims)
    return total


def unit_scale(values):
    return lax.rsqrt(jnp.mean(values * values, axis=-1, keepdims=True) + EPSILON)


def alone(body, out_shape, cost, *operands, scalars=0):
    specs = [pl.BlockSpec(memory_space=pltpu.SMEM)] * scalars + [VMEM] * (len(operands) - scalars)
    results = pl.pallas_call(
        body,
        out_shape=out_shape,
        in_specs=specs,
        out_specs=jax.tree.map(lambda _: VMEM, out_shape),
        compiler_params=pltpu.CompilerParams(
            vmem_limit_bytes=room(list(operands) + jax.tree.leaves(out_shape), 2 * SPARE_BYTES)
        ),
        cost_estimate=lasting(cost),
    )(*operands)
    return list(results) if isinstance(out_shape, (list, tuple)) else results


def route_tables(routes, gates):
    count, rows, _ = routes.shape
    slots = NE * CAP

    def body(routes_ref, gates_ref, picks_ref, weights_ref, slot_ref, other_ref):
        row = lax.broadcasted_iota(jnp.int32, (rows, rows), 0)
        col = lax.broadcasted_iota(jnp.int32, (rows, rows), 1)
        before = (col < row).astype(jnp.bfloat16)
        expert = lax.broadcasted_iota(jnp.int32, (rows, LANES), 1)
        slot = lax.broadcasted_iota(jnp.int32, (rows, slots), 1)
        source = lax.broadcasted_iota(jnp.int32, (LANES, slots), 0)
        target = lax.broadcasted_iota(jnp.int32, (LANES, slots), 1)
        spread = (
            (target >= source * CAP) & (target < source * CAP + CAP) & (source < NE)
        ).astype(jnp.bfloat16)
        ones = jnp.ones((rows, LANES), jnp.bfloat16)
        for n in range(count):
            gate = jnp.zeros((rows, LANES), jnp.float32)
            named = jnp.zeros((rows, LANES), jnp.float32)
            for k in range(2):
                hit = routes_ref[n, :, k : k + 1] == expert
                named = named + jnp.where(hit, 1.0, 0.0)
                gate = gate + jnp.where(hit, gates_ref[n, :, k : k + 1], 0.0)
            rank = dot32(before, named.astype(jnp.bfloat16)) + expert.astype(jnp.float32) * CAP
            rank = jnp.where(expert < NE, rank, 0.0)
            goal = exact_dot(split(rank, 2), spread, (((1,), (0,)), ((), ())))
            member = dot32(named.astype(jnp.bfloat16), spread)
            pick = jnp.where(goal == slot.astype(jnp.float32), member, 0.0)
            weight = pick * exact_dot(split(gate, 3), spread, (((1,), (0,)), ((), ())))
            picks_ref[n] = pick.astype(jnp.bfloat16)
            weights_ref[n] = weight
            slot_ref[n] = exact_dot(split(weight, 3), ones, FIRST)
            other_ref[n] = gate

    return alone(
        body,
        (
            make((count, rows, slots), jnp.bfloat16),
            make((count, rows, slots)),
            make((count, slots, LANES)),
            make((count, rows, LANES)),
        ),
        3,
        routes,
        gates,
    )


def gate_slots(slot_gates, picks, grads):
    picked = dot32(picks, grads[0], FIRST)
    for part in grads[1:]:
        picked = picked + dot32(picks, part, FIRST)
    lanes = [
        (picked[:, at : at + LANES] * slot_gates).astype(jnp.bfloat16)
        for at in range(0, picked.shape[1], LANES)
    ]
    return jnp.concatenate(lanes, axis=1)


def const_alphas(hn, smalls, base):
    logits = dot32(hn, smalls[base + 2 : base + 6].astype(jnp.bfloat16), LAST)
    alphas = []
    for c in range(2):
        first, second = logits[:, 2 * c : 2 * c + 1], logits[:, 2 * c + 1 : 2 * c + 2]
        top = jnp.maximum(first, second)
        first, second = jnp.exp(first - top), jnp.exp(second - top)
        total = first + second
        alphas.append((first / total, second / total))
    return alphas


def middle(attn, x, pack, smalls, base, picks, slot_gates, grads):
    planes, rows, part = attn.shape
    width = x.shape[1]
    slots = picks.shape[1]

    def body(attn_ref, x_ref, w_ref, small_ref, picks_ref, gates_ref, *refs):
        total = x_ref[...].astype(jnp.float32)
        for z in range(planes):
            total = total + dot32(attn_ref[z], w_ref[z * part : (z + 1) * part, :width])
        mid_ref, sent_ref = refs[-2:] if grads is None else refs[-3:-1]
        mid_ref[...] = total
        hn = (total * unit_scale(total) * small_ref[base + 1 : base + 2]).astype(jnp.bfloat16)
        sent_ref[...] = dot32(picks_ref[...], hn, FIRST).astype(jnp.bfloat16)
        if grads is not None:
            refs[-1][...] = gate_slots(gates_ref[...], picks_ref[...], [refs[0][...]])

    outs = [make((rows, width)), make((slots, width), jnp.bfloat16)]
    more = []
    if grads is not None:
        outs.append(make((slots, width), jnp.bfloat16))
        more.append(grads)
    return alone(body, outs, 3, attn, x, pack, smalls, picks, slot_gates, *more)


def combine(back, weights, mid, other, smalls, base, following):
    rows, width = mid.shape

    def body(back_ref, weights_ref, mid_ref, other_ref, small_ref, x_ref, *refs):
        mid_value, gate = mid_ref[...], other_ref[...]
        hn = (mid_value * unit_scale(mid_value) * small_ref[base + 1 : base + 2]).astype(
            jnp.bfloat16
        )
        alphas = const_alphas(hn, small_ref, base)
        wide = hn.astype(jnp.float32)
        total = mid_value + exact_dot(
            split(weights_ref[...]), back_ref[...], (((1,), (0,)), ((), ()))
        )
        factor = gate[:, NE + 1 : NE + 2]
        for c in range(2):
            weight = gate[:, NE + 2 + c : NE + 3 + c]
            factor = factor + weight * alphas[c][0]
            total = total + (weight * alphas[c][1]) * small_ref[base + 6 + c : base + 7 + c]
        total = total + factor * wide
        x_ref[...] = total
        if following:
            refs[0][...] = (total * unit_scale(total) * small_ref[base + 8 : base + 9]).astype(
                jnp.bfloat16
            )

    outs = [make((rows, width))]
    if following:
        outs.append(make((rows, width), jnp.bfloat16))
    return alone(body, outs, 3, back, weights, mid, other, smalls)


def experts_back(dback, picks, upstream, mid, other, smalls, base):
    rows, width = mid.shape

    def body(dback_ref, picks_ref, up_ref, mid_ref, other_ref, small_ref, dmid_ref, dy_ref, row_ref):
        mid_value, gate = mid_ref[...], other_ref[...]
        g = up_ref[...].astype(jnp.float32)
        scale = unit_scale(mid_value)
        unit = mid_value * scale
        gain = small_ref[base + 1 : base + 2]
        hn = (unit * gain).astype(jnp.bfloat16)
        alphas = const_alphas(hn, small_ref, base)
        wide = hn.astype(jnp.float32)
        dhn = dot32(picks_ref[...], dback_ref[...])
        g_hn = jnp.sum(g * wide, axis=1, keepdims=True)
        factor = gate[:, NE + 1 : NE + 2]
        row_ref[0:1] = jnp.zeros((1, width), jnp.float32)
        for c in range(2):
            weight = gate[:, NE + 2 + c : NE + 3 + c]
            vector = small_ref[base + 6 + c : base + 7 + c]
            first, second = alphas[c]
            factor = factor + weight * first
            row_ref[6 + c : 7 + c] = jnp.sum((weight * second) * g, axis=0, keepdims=True)
            da_first = weight * g_hn
            da_second = weight * jnp.sum(g * vector, axis=1, keepdims=True)
            mean = first * da_first + second * da_second
            for j, dlog in enumerate((first * (da_first - mean), second * (da_second - mean))):
                at = 2 + 2 * c + j
                dhn = dhn + dlog * small_ref[base + at : base + at + 1]
                row_ref[at : at + 1] = jnp.sum(dlog * wide, axis=0, keepdims=True)
        dhn = dhn + factor * g
        row_ref[1:2] = jnp.sum(dhn * unit, axis=0, keepdims=True)
        through = dhn * gain
        inner = jnp.mean(through * unit, axis=1, keepdims=True)
        dmid = g + scale * (through - unit * inner)
        dmid_ref[...] = dmid
        dy_ref[...] = dmid.astype(jnp.bfloat16)

    return alone(
        body,
        [make((rows, width)), make((rows, width), jnp.bfloat16), make((8, width))],
        4,
        dback,
        picks,
        upstream,
        mid,
        other,
        smalls,
    )


def finish(dxn, x, dmid, rows_in, smalls, base, picks, slot_gates):
    planes, rows, width = dxn.shape

    def body(dxn_ref, x_ref, dmid_ref, row_ref, small_ref, *refs):
        grad = dxn_ref[0].astype(jnp.float32)
        for z in range(1, planes):
            grad = grad + dxn_ref[z].astype(jnp.float32)
        value = x_ref[...].astype(jnp.float32)
        scale = unit_scale(value)
        unit = value * scale
        out_rows = refs[-1 if picks is None else -2]
        out_rows[...] = row_ref[...]
        out_rows[0:1] = jnp.sum(grad * unit, axis=0, keepdims=True)
        through = grad * small_ref[base : base + 1]
        inner = jnp.mean(through * unit, axis=1, keepdims=True)
        g = dmid_ref[...] + scale * (through - unit * inner)
        refs[-2 if picks is None else -3][...] = g
        if picks is not None:
            refs[-1][...] = gate_slots(refs[1][...], refs[0][...], split(g))

    outs = [make((rows, width)), make((8, width))]
    more = []
    if picks is not None:
        outs.append(make((picks.shape[1], width), jnp.bfloat16))
        more = [picks, slot_gates]
    return alone(body, outs, 3, dxn, x, dmid, rows_in, smalls, *more)


def sum_expert_grads(owns, gots):
    layers, kinds = len(owns), len(owns[0])
    hidden, features = owns[0][0].shape
    tile = min(hidden, 256)

    def body(*refs):
        outs = refs[2 * layers * kinds :]
        for n in range(kinds):
            for layer in range(layers):
                own, got = refs[2 * (layer * kinds + n) : 2 * (layer * kinds + n) + 2]
                outs[n][layer] = own[...].astype(jnp.float32) + got[...].astype(jnp.float32)

    piece = pl.BlockSpec((tile, features), lambda i: (i, 0))
    operands = [
        w for layer in range(layers) for pair in zip(owns[layer], gots[layer]) for w in pair
    ]
    return pl.pallas_call(
        body,
        out_shape=[make((layers, hidden, features))] * kinds,
        grid=(hidden // tile,),
        in_specs=[piece] * len(operands),
        out_specs=[pl.BlockSpec((layers, tile, features), lambda i: (0, i, 0))] * kinds,
        compiler_params=pltpu.CompilerParams(vmem_limit_bytes=VMEM_BYTES),
        cost_estimate=lasting(7),
    )(*operands)


def pack_grads(column, dq, dkv, attn, dy, small):
    width = column.shape[1]
    kv_cols, own_out = dkv.shape[1], attn.shape[1]
    tail = own_out + LANES // 2
    rows, cols = own_out // 2, width // 2

    def body(column_ref, dq_ref, dkv_ref, attn_ref, dy_ref, small_ref, one, two):
        one[:, :kv_cols] = dot32(column_ref[...], dkv_ref[...], FIRST).astype(jnp.bfloat16)
        source = lax.broadcasted_iota(jnp.int32, (kv_cols, tail), 0)
        target = lax.broadcasted_iota(jnp.int32, (kv_cols, tail), 1)
        dim = LANES // 2
        goal = lax.div(target, dim) * LANES + lax.rem(target, dim)
        compact = ((goal == source) & (target < own_out)).astype(jnp.bfloat16)
        narrow = dot32(dq_ref[...], compact).astype(jnp.bfloat16)
        placed = jnp.concatenate(
            [
                jnp.zeros((own_out, width), jnp.float32),
                small_ref[...],
                jnp.zeros((tail - own_out - 8, width), jnp.float32),
            ],
            axis=0,
        ).T
        one[:, kv_cols:] = (dot32(column_ref[...], narrow, FIRST) + placed).astype(jnp.bfloat16)
        out = dot32(attn_ref[...], dy_ref[...], FIRST).astype(jnp.bfloat16)
        for a in range(2):
            for b in range(2):
                two[a, b] = out[a * rows : (a + 1) * rows, b * cols : (b + 1) * cols]

    return alone(
        body,
        [make((width, kv_cols + tail), jnp.bfloat16), make((2, 2, rows, cols), jnp.bfloat16)],
        4,
        column,
        dq,
        dkv,
        attn,
        dy,
        small,
    )


def per_device(
    tokens,
    segments,
    routes,
    gates,
    w_qkv,
    w_out,
    gain_attn,
    gain_moe,
    const_gate,
    const_vec,
    w_gate,
    w_up,
    w_down,
    cotangent,
):
    blocks = lax.axis_size("blk")
    head_index, blk_index = lax.axis_index("head"), lax.axis_index("blk")
    span = blocks // COLUMNS
    plane, rest = lax.div(blk_index, span), lax.rem(blk_index, span)
    shards = 2 * blocks
    token_rows, width = tokens.shape
    shard_rows = width // shards
    head_dim = width // HEADS
    heads = HEADS // COLUMNS
    scale = head_dim ** (-0.5)
    half_length = blocks * token_rows
    positions = 2 * half_length
    own_out = heads * head_dim
    wide = heads * LANES

    swap = [(0, 1), (1, 0)]

    seg_own = lax.dynamic_index_in_dim(segments, head_index, 0, keepdims=True)
    seg_rows = jnp.concatenate([lax.rem(seg_own, 128), lax.div(seg_own, 128)], axis=0)
    seg_rows = jnp.pad(seg_rows, ((0, 14), (0, 0))).astype(jnp.bfloat16)
    seg_rows = jnp.broadcast_to(seg_rows[None], (COLUMNS,) + seg_rows.shape)
    smalls = [
        jnp.concatenate(
            [gain_attn[n][:, None], gain_moe[n][:, None], const_gate[n], const_vec[n]], axis=1
        )
        for n in range(LAYERS)
    ]
    smalls.append(jnp.zeros((shard_rows, LANES // 2 - 8 * LAYERS), jnp.bfloat16))
    smalls = jnp.concatenate(smalls, axis=1)
    packs = []
    for layer in range(LAYERS):
        parts = w_qkv[layer].reshape((shard_rows, 3, COLUMNS, heads, head_dim))
        kv_part = jnp.concatenate([parts[:, 1], parts[:, 2]], axis=3)
        kv_part = kv_part.transpose((1, 0, 2, 3)).reshape((COLUMNS, shard_rows, wide))
        query_part = parts[:, 0].transpose((1, 0, 2, 3)).reshape((COLUMNS, shard_rows, own_out))
        packs.append(
            jnp.concatenate(
                [
                    jnp.broadcast_to(w_out[layer][None], (COLUMNS, shard_rows, width)),
                    kv_part,
                    query_part,
                    jnp.broadcast_to(smalls[None], (COLUMNS,) + smalls.shape),
                ],
                axis=2,
            )
        )
    (seg_all, *packs), column_tokens = start_gather([seg_rows] + packs, tokens, blocks, 1)
    packs = [pack.reshape((width, -1)) for pack in packs]
    picks, pick_gates, slot_gates, other_gates = route_tables(routes, gates)

    def send_expert(weight, layer, after):
        away, _ = lax.optimization_barrier((weight[layer], after))
        return lax.ppermute(away, "head", swap)

    own_experts = (w_gate, w_up, w_down)

    experts = [[send_expert(w_gate, 0, tokens)]] + [None] * (LAYERS - 1)
    seg_all = seg_all[..., :2, :].astype(jnp.int32)
    seg_all = seg_all[..., 0, :] + 128 * seg_all[..., 1, :]
    seg_query = lax.dynamic_index_in_dim(seg_all, head_index, 0, keepdims=False)
    seg_query = lax.dynamic_index_in_dim(seg_query, rest, 1, keepdims=False)
    starts = jnp.sum(
        (seg_all.reshape((1, 1, -1)) < seg_query[:, :, None]).astype(jnp.int32), axis=2
    )
    bases = (
        head_index * half_length
        + (jnp.arange(COLUMNS, dtype=jnp.int32) * span + rest) * token_rows
    )
    bounds = block_bounds(starts, bases, token_rows)
    starts = starts[:, None, :]

    values = tokens
    column, small_rows = column_tokens, None
    kept = []
    for layer in range(LAYERS):
        base = 8 * layer
        last = layer + 1 == LAYERS
        column, queries, query_w, out_rows, kv_all, small_rows = project_gather(
            column, packs[layer], small_rows, heads, scale, blocks, 4 if layer == 0 else 2
        )
        kv_all = kv_all.reshape((positions, wide))
        if layer == 0:
            experts[layer] += [send_expert(w, layer, kv_all) for w in (w_up, w_down)]
        else:
            experts[layer].append(send_expert(w_down, layer, kv_all))
        attended, attn_col = attend(bounds, queries, kv_all, starts)
        (attn,) = column_exchange([attn_col], [False], blocks, 5, 9)
        mid, *sent = middle(
            attn,
            values,
            packs[layer],
            small_rows,
            base,
            picks[layer],
            slot_gates[layer],
            cotangent if last else None,
        )
        sent = [rows.reshape((NE, CAP, width)) for rows in sent]
        if last:
            back, dback, *wgrads = experts_exchange(
                sent, None, own_experts, experts[layer], layer, blocks, 7, True, True, 55
            )
            rows_in = None
        else:
            experts[layer + 1] = [send_expert(w, layer + 1, sent[0]) for w in (w_gate, w_up)]
            back, rows_in = experts_exchange(
                sent, None, own_experts, experts[layer], layer, blocks, 6, True, False, 28
            )
        kept.append(
            (values, column, queries, kv_all, attended, attn_col, query_w, out_rows, mid, rows_in)
        )
        values, *normed = combine(
            back.reshape((NE * CAP, width)),
            pick_gates[layer],
            mid,
            other_gates[layer],
            small_rows,
            base,
            not last,
        )
        if not last:
            (column,) = normed
    output = values

    upstream = cotangent
    shared_grads = [None] * LAYERS
    expert_grads = [None] * LAYERS
    for layer in reversed(range(LAYERS)):
        base = 8 * layer
        values, column, queries, kv_all, attended, attn_col, query_w, out_rows, mid, rows_in = (
            kept[layer]
        )
        if layer + 1 < LAYERS:
            dback, *wgrads = experts_exchange(
                [dz.reshape((NE, CAP, width))],
                rows_in,
                own_experts,
                experts[layer],
                layer,
                blocks,
                8,
                False,
                True,
                36,
                None,
                waiting,
            )
            expert_grads[layer + 1][1][1:] = wgrads[6:]
        before = layer > 0
        if before:
            got, waiting = [lax.ppermute(wgrads[3], "head", swap)], wgrads[4:6]
        else:
            got = [lax.ppermute(away, "head", swap) for away in wgrads[3:5]]
        dmid, dy, rows = experts_back(
            dback.reshape((NE * CAP, width)),
            picks[layer],
            upstream,
            mid,
            other_gates[layer],
            small_rows,
            base,
        )
        dy = column_gather(dy, blocks, 3)
        dy, got[0] = lax.optimization_barrier((dy, got[0]))
        dq, dkv_all = attend_back(
            bounds, queries, dy, out_rows, attended, kv_all, starts, scale
        )
        if not before:
            dkv_all, got[1] = lax.optimization_barrier((dkv_all, got[1]))
        dkv, dxn = reduce_project(
            dkv_all.reshape((2, COLUMNS, span, token_rows, wide)),
            dq,
            query_w,
            packs[layer],
            blocks,
            10,
        )
        upstream, rows, *dz = finish(
            dxn,
            values,
            dmid,
            rows,
            small_rows,
            base,
            picks[layer - 1] if before else None,
            slot_gates[layer - 1] if before else None,
        )
        if before:
            (dz,) = dz
        expert_grads[layer] = wgrads[:3], got
        qkv_part, out_part = pack_grads(
            column.reshape((-1, width)),
            dq.reshape((-1, wide)),
            dkv.reshape((-1, wide)),
            attn_col.reshape((-1, own_out)),
            dy.reshape((-1, width)),
            rows,
        )
        shared_grads[layer] = [
            qkv_part.reshape((2, COLUMNS, span, shard_rows, -1)),
            out_part.reshape((2, 2, span, shard_rows, width // 2)),
        ]

    packed = [part for layer in range(LAYERS) for part in shared_grads[layer]]
    reduced = plane_reduce(packed, blocks, 12, 20)
    away, _ = lax.optimization_barrier((wgrads[5], reduced[0]))
    expert_grads[0][1].append(lax.ppermute(away, "head", swap))
    exchanged = final_exchange(reduced[::2], reduced[1::2], blocks, 13)
    from_planes, out_grads = exchanged[:LAYERS], exchanged[LAYERS:]
    from_planes = jnp.stack(from_planes, axis=1).astype(jnp.float32)
    kv_out = from_planes[..., :wide].reshape((COLUMNS, LAYERS, shard_rows, heads, 2, head_dim))
    query_out = from_planes[..., wide : wide + own_out].reshape(
        (COLUMNS, LAYERS, shard_rows, heads, 1, head_dim)
    )
    qkv_out = jnp.concatenate([query_out, kv_out], axis=4)
    qkv_out = qkv_out.transpose((1, 2, 4, 0, 3, 5)).reshape((LAYERS, shard_rows, 3 * width))
    small_out = jnp.sum(from_planes[..., wide + own_out : wide + own_out + 8], axis=0)
    out_grads = jnp.stack(out_grads).astype(jnp.float32).transpose((0, 2, 1, 3))
    out_grads = out_grads.reshape((LAYERS, shard_rows, width))
    stacked = sum_expert_grads(*zip(*expert_grads))
    return (
        output,
        upstream,
        qkv_out,
        out_grads,
        small_out[..., 0],
        small_out[..., 1],
        small_out[..., 2:6],
        small_out[..., 6:8],
        stacked[0],
        stacked[1],
        stacked[2],
    )


def solution(mesh):
    tokens = P(("head", "blk"), None)
    by_layer = P(None, ("head", "blk"), None)
    gains = P(None, ("head", "blk"))
    experts = P(None, "blk", "head")
    return jax.shard_map(
        per_device,
        mesh=mesh,
        in_specs=(
            tokens,
            P(None, "blk"),
            by_layer,
            by_layer,
            by_layer,
            by_layer,
            gains,
            gains,
            by_layer,
            by_layer,
            experts,
            experts,
            experts,
            tokens,
        ),
        out_specs=(
            tokens,
            tokens,
            by_layer,
            by_layer,
            gains,
            gains,
            by_layer,
            by_layer,
            experts,
            experts,
            experts,
        ),
        check_vma=False,
    )
```

```python
import jax
import jax.numpy as jnp
from jax import lax
from jax.experimental import pallas as pl
from jax.experimental.pallas import tpu as pltpu
from jax.sharding import PartitionSpec as P

HEADS = 12
NE = 8
LAYERS = 2
CAP = 40
COLUMNS = 4
MESH = pl.DeviceIdType.MESH
ANY = pl.BlockSpec(memory_space=pl.ANY)
VMEM = pl.BlockSpec(memory_space=pltpu.VMEM)
HBM = pl.BlockSpec(memory_space=pltpu.HBM)
DMA = pltpu.SemaphoreType.DMA
VMEM_BYTES = 60 * 1024 * 1024
SPARE_BYTES = 4 * 1024 * 1024


def make(shape, kind=jnp.float32):
    return jax.ShapeDtypeStruct(tuple(shape), kind)


def greet(peers, line=()):
    barrier = pltpu.get_barrier_semaphore()
    count = len(peers)
    for peer in peers:
        pl.semaphore_signal(barrier, inc=1, device_id=peer, device_id_type=MESH)
    for there, peer in line:

        @pl.when(there)
        def _():
            pl.semaphore_signal(barrier, inc=1, device_id=peer, device_id_type=MESH)

        count = count + there.astype(jnp.int32)
    pl.semaphore_wait(barrier, count)


def remote(src, dst, send_sem, recv_sem, peer):
    return pltpu.make_async_remote_copy(
        src_ref=src,
        dst_ref=dst,
        send_sem=send_sem,
        recv_sem=recv_sem,
        device_id=peer,
        device_id_type=MESH,
    )


def room(things, spare=SPARE_BYTES):
    total = spare
    for thing in things:
        if hasattr(thing, "dtype") and hasattr(thing, "shape"):
            if not jnp.issubdtype(thing.dtype, jnp.number):
                continue
            size = jnp.dtype(thing.dtype).itemsize
            for extent in thing.shape:
                size *= extent
            total += size
    return min(total, VMEM_BYTES)


def comm_params(collective_id, things=(), spare=SPARE_BYTES):
    return pltpu.CompilerParams(
        collective_id=collective_id,
        has_side_effects=True,
        vmem_limit_bytes=room(things, spare),
    )


def lasting(microseconds):
    return pl.CostEstimate(
        flops=0, bytes_accessed=int(microseconds * 3_500_000), transcendentals=0
    )


def column_place(blocks):
    span = blocks // COLUMNS
    head, blk = lax.axis_index("head"), lax.axis_index("blk")
    plane, rest = lax.div(blk, span), lax.rem(blk, span)
    planes = [lax.rem(plane + d, COLUMNS) for d in range(COLUMNS)]
    return plane, planes, [(head, p * span + rest) for p in planes]


class Chain:
    def __init__(self, source, dst, send_sems, recv_sems, blocks):
        span = blocks // COLUMNS
        head, blk = lax.axis_index("head"), lax.axis_index("blk")
        plane, rest = lax.div(blk, span), lax.rem(blk, span)
        self.source, self.dst, self.plane = source, dst, plane
        self.send_sems, self.recv_sems = send_sems, recv_sems
        after = jnp.minimum(plane + 1, COLUMNS - 1)
        before = jnp.maximum(plane - 1, 0)
        self.line = [
            (plane < COLUMNS - 1, (head, after * span + rest)),
            (plane > 0, (head, before * span + rest)),
        ]
        lower = plane < COLUMNS // 2
        self.slabs = [
            plane,
            plane + 1 - 2 * lax.rem(plane, 2),
            jnp.where(lower, 2, 1),
            jnp.where(lower, 3, 0),
        ]

    def copy(self, k, way):
        slab = self.slabs[k]
        place = self.dst.at[slab]
        return remote(
            self.source if k == 0 else place,
            place,
            self.send_sems.at[k, way],
            self.recv_sems.at[slab],
            self.line[way][1],
        )

    def onward(self, k):
        if k == 0:
            return [self.line[0][0], self.line[1][0]]
        from_before = self.slabs[k] < self.plane
        return [
            from_before & self.line[0][0],
            jnp.logical_not(from_before) & self.line[1][0],
        ]

    def pass_on(self, k):
        for way, there in enumerate(self.onward(k)):

            @pl.when(there)
            def _():
                self.copy(k, way).start()

    def arrive(self, k):
        self.copy(k, 0).wait_recv()
        self.pass_on(k)

    def finish(self):
        for k in range(COLUMNS):
            for way, there in enumerate(self.onward(k)):

                @pl.when(there)
                def _():
                    self.copy(k, way).wait_send()


def column_start(src, gather, dst, own_sem, send_sems, recv_sems, where):
    plane, planes, peers = where
    own = pltpu.make_async_copy(src if gather else src.at[plane], dst.at[plane], own_sem)
    own.start()
    copies = [own]
    for d in (2, 1, 3):
        copy = remote(
            src if gather else src.at[planes[d]],
            dst.at[plane],
            send_sems.at[d],
            recv_sems.at[d],
            peers[d],
        )
        copy.start()
        copies.append(copy)
    return copies


def column_exchange(arrays, gathers, blocks, collective_id, cost=16):
    count = len(arrays)
    slabs = [
        tuple(values.shape if gather else values.shape[1:])
        for values, gather in zip(arrays, gathers)
    ]

    def body(*refs):
        srcs, dsts = refs[:count], refs[count : 2 * count]
        own_sems, send_sems, recv_sems = refs[2 * count :]
        where = column_place(blocks)
        greet(where[2][1:])
        copies = []
        for n in range(count):
            copies += column_start(
                srcs[n],
                gathers[n],
                dsts[n],
                own_sems.at[n],
                send_sems.at[n],
                recv_sems.at[n],
                where,
            )
        for copy in copies:
            copy.wait()

    return pl.pallas_call(
        body,
        out_shape=[
            jax.ShapeDtypeStruct((COLUMNS,) + slab, values.dtype)
            for values, slab in zip(arrays, slabs)
        ],
        in_specs=[ANY] * count,
        out_specs=[ANY] * count,
        scratch_shapes=[DMA((count,)), DMA((count, COLUMNS)), DMA((count, COLUMNS))],
        compiler_params=comm_params(collective_id),
        cost_estimate=lasting(cost),
    )(*arrays)


def column_gather(values, blocks, collective_id, cost=14):
    def body(src, dst, own_sem, send_sems, recv_sems):
        chain = Chain(src, dst, send_sems, recv_sems, blocks)
        greet([], chain.line)
        chain.pass_on(0)
        own = pltpu.make_async_copy(src, dst.at[chain.plane], own_sem)
        own.start()
        for k in range(1, COLUMNS):
            chain.arrive(k)
        own.wait()
        chain.finish()

    return pl.pallas_call(
        body,
        out_shape=jax.ShapeDtypeStruct((COLUMNS,) + tuple(values.shape), values.dtype),
        in_specs=[ANY],
        out_specs=ANY,
        scratch_shapes=[DMA, DMA((COLUMNS, 2)), DMA((COLUMNS,))],
        compiler_params=comm_params(collective_id),
        cost_estimate=lasting(cost),
    )(values)


def final_exchange(shares, rows, blocks, collective_id, cost=9):
    span = blocks // COLUMNS
    count = len(shares)
    total = 2 * count

    def body(*refs):
        srcs, dsts = refs[:total], refs[total : 2 * total]
        own_sems, send_sems, recv_sems, row_send, row_recv = refs[2 * total :]
        where = column_place(blocks)
        head, blk = lax.axis_index("head"), lax.axis_index("blk")
        plane, rest = lax.div(blk, span), lax.rem(blk, span)
        flat = head * blocks + blk
        goal = (plane * 2 + head) * span + rest
        from_plane = lax.div(flat, span)
        origin = (lax.rem(from_plane, 2), lax.div(from_plane, 2) * span + lax.rem(flat, span))
        goal_place = (lax.div(goal, blocks), lax.rem(goal, blocks))
        away = goal != flat
        greet(where[2][1:], [(away, goal_place), (away, origin)])
        copies = []
        for n in range(count):
            copies += column_start(
                srcs[n],
                False,
                dsts[n],
                own_sems.at[n],
                send_sems.at[n],
                recv_sems.at[n],
                where,
            )

        def row_copy(n):
            return remote(
                srcs[n], dsts[n], row_send.at[n - count], row_recv.at[n - count], goal_place
            )

        def row_stay(n):
            return pltpu.make_async_copy(srcs[n], dsts[n], own_sems.at[n])

        for n in range(count, total):

            @pl.when(away)
            def _():
                row_copy(n).start()

            @pl.when(jnp.logical_not(away))
            def _():
                row_stay(n).start()

        for copy in copies:
            copy.wait()
        for n in range(count, total):

            @pl.when(away)
            def _():
                row_copy(n).wait()

            @pl.when(jnp.logical_not(away))
            def _():
                row_stay(n).wait()

    arrays = list(shares) + list(rows)
    return pl.pallas_call(
        body,
        out_shape=[make(values.shape, values.dtype) for values in arrays],
        in_specs=[ANY] * total,
        out_specs=[ANY] * total,
        scratch_shapes=[
            DMA((total,)),
            DMA((count, COLUMNS)),
            DMA((count, COLUMNS)),
            DMA((count,)),
            DMA((count,)),
        ],
        compiler_params=comm_params(collective_id),
        cost_estimate=lasting(cost),
    )(*arrays)


def plane_place(blocks):
    span = blocks // COLUMNS
    width = span // 2
    head, blk = lax.axis_index("head"), lax.axis_index("blk")
    plane, rest = lax.div(blk, span), lax.rem(blk, span)
    x, core = lax.div(rest, 2), lax.rem(rest, 2)
    first = plane * span
    right = [lax.rem(x + d, width) for d in range(width)]
    left = [lax.rem(x - d + width, width) for d in range(width)]
    x_peers = [(head, first + right[d] * 2 + core) for d in range(width)]
    y_peer = (1 - head, blk)
    core_peer = (head, first + x * 2 + 1 - core)
    return head, rest, core, left, x_peers, y_peer, core_peer


class PlaneRun:
    def __init__(self, srcs, dsts, own_sems, send_sems, recv_sems, pass_sems, land_sems, where):
        self.srcs, self.dsts = srcs, dsts
        self.own_sems, self.send_sems, self.recv_sems = own_sems, send_sems, recv_sems
        self.pass_sems, self.land_sems = pass_sems, land_sems
        self.head, self.rest, self.core, self.left, self.x_peers, self.y_peer, self.core_peer = (
            where
        )
        self.width = len(self.x_peers)
        self.sends, self.passes, self.owns = [], [], []

    def place(self, n, h, dy, d):
        half = self.srcs[n].shape[0] // 2
        row = self.head if dy == 0 else 1 - self.head
        return self.dsts[n].at[row, pl.ds(h * half, half), self.left[d] * 2 + self.core]

    def held(self, n, h, dy, d):
        half = self.srcs[n].shape[0] // 2
        if dy == 0 and d == 0:
            return self.srcs[n].at[pl.ds(h * half, half)]
        return self.place(n, h, dy, d)

    def send(self, n, h, dy, d, peer, to_dy, to_d):
        copy = remote(
            self.held(n, h, dy, d),
            self.place(n, h, dy, d),
            self.send_sems.at[len(self.sends)],
            self.recv_sems.at[n, h, to_dy, to_d],
            peer,
        )
        copy.start()
        self.sends.append(copy)

    def hand_over(self, n, h, dy, d):
        copy = remote(
            self.held(n, h, dy, d),
            self.place(n, h, dy, d),
            self.pass_sems.at[n, h, dy, d],
            self.land_sems.at[n, h, dy, d],
            self.core_peer,
        )
        copy.start()
        self.passes.append(copy)

    def arrived(self, n, h, dy, d):
        at = self.place(n, h, dy, d)
        remote(
            at, at, self.send_sems.at[0], self.recv_sems.at[n, h, dy, d], self.y_peer
        ).wait_recv()

    def first(self, n):
        own = pltpu.make_async_copy(
            self.srcs[n], self.dsts[n].at[self.head, :, self.rest], self.own_sems.at[n]
        )
        own.start()
        self.owns.append(own)
        for d in range(1, self.width):
            self.send(n, 0, 0, 0, self.x_peers[d], 0, d)
        self.send(n, 1, 0, 0, self.y_peer, 1, 0)
        self.send(n, 0, 0, 0, self.y_peer, 1, 0)
        for d in range(1, self.width):
            self.send(n, 1, 0, 0, self.x_peers[d], 0, d)
        self.hand_over(n, 0, 0, 0)
        self.hand_over(n, 1, 0, 0)

    def second(self, n):
        for d in range(1, self.width):
            self.arrived(n, 0, 0, d)
            self.send(n, 0, 0, d, self.y_peer, 1, d)
            self.hand_over(n, 0, 0, d)
        self.arrived(n, 1, 1, 0)
        for d in range(1, self.width):
            self.send(n, 1, 1, 0, self.x_peers[d], 1, d)
        self.hand_over(n, 1, 1, 0)

    def third(self, n):
        self.arrived(n, 0, 1, 0)
        self.hand_over(n, 0, 1, 0)
        for d in range(1, self.width):
            self.arrived(n, 1, 0, d)
            self.hand_over(n, 1, 0, d)
        for d in range(1, self.width):
            self.arrived(n, 0, 1, d)
            self.hand_over(n, 0, 1, d)
            self.arrived(n, 1, 1, d)
            self.hand_over(n, 1, 1, d)

    def last(self):
        for own in self.owns:
            own.wait()
        for copy in self.passes:
            copy.wait()
        for copy in self.sends:
            copy.wait_send()


def plane_scratch(count, blocks):
    width = blocks // COLUMNS // 2
    links = 4 * (width - 1) + 2
    return [DMA((count,)), DMA((count * links,))] + [DMA((count, 2, 2, width))] * 3


def plane_shapes(arrays, blocks):
    return [
        jax.ShapeDtypeStruct(
            (2, values.shape[0], blocks // COLUMNS) + tuple(values.shape[1:]), values.dtype
        )
        for values in arrays
    ]


def start_gather(packs, tokens, blocks, collective_id, cost=28):
    count = len(packs)

    def body(*refs):
        srcs, refs = refs[: count + 1], refs[count + 1 :]
        wholes, refs = refs[:count], refs[count:]
        columns, refs = refs[: count + 1], refs[count + 1 :]
        own_sems, send_sems, recv_sems, chain_send, chain_recv, *plane_sems = refs
        column, plane = column_place(blocks), plane_place(blocks)
        greet(column[2][1:] + plane[4][1:] + [plane[5], plane[6]])
        run = PlaneRun(columns[:count], wholes, *plane_sems, plane)
        chain = Chain(srcs[count], columns[count], chain_send, chain_recv, blocks)
        stay = pltpu.make_async_copy(
            srcs[count], columns[count].at[chain.plane], own_sems.at[count]
        )

        def begin(n):
            return column_start(
                srcs[n],
                False,
                columns[n],
                own_sems.at[n],
                send_sems.at[n],
                recv_sems.at[n],
                column,
            )

        waits = [begin(0), begin(1)]
        for n in range(count):
            for copy in waits[n]:
                copy.wait()
            if n + 2 < count:
                waits.append(begin(n + 2))
            elif n + 2 == count:
                chain.pass_on(0)
                stay.start()
            run.first(n)
        run.second(0)
        run.second(1)
        chain.arrive(1)
        for n in range(2, count):
            run.second(n)
        run.third(0)
        run.third(1)
        chain.arrive(2)
        for n in range(2, count):
            run.third(n)
        chain.arrive(3)
        run.last()
        stay.wait()
        chain.finish()

    results = pl.pallas_call(
        body,
        out_shape=plane_shapes(packs, blocks)
        + [jax.ShapeDtypeStruct(pack.shape, pack.dtype) for pack in packs]
        + [jax.ShapeDtypeStruct((COLUMNS,) + tokens.shape, tokens.dtype)],
        in_specs=[ANY] * (count + 1),
        out_specs=[ANY] * (2 * count + 1),
        scratch_shapes=[
            DMA((count + 1,)),
            DMA((count, COLUMNS)),
            DMA((count, COLUMNS)),
            DMA((COLUMNS, 2)),
            DMA((COLUMNS,)),
        ]
        + plane_scratch(count, blocks),
        compiler_params=comm_params(collective_id),
        cost_estimate=lasting(cost),
    )(*packs, tokens)
    return results[:count], results[-1]


def project_gather(source, pack, smalls, heads, scale, blocks, collective_id, cost=22):
    span = blocks // COLUMNS
    width = span // 2
    chained = smalls is not None
    rows, features = source.shape[-2:]
    wide = heads * LANES
    kv_at, tail_at = features, features + wide
    tail_cols = pack.shape[1] - tail_at
    own_out = tail_cols - LANES // 2
    dim = LANES // 2
    half = rows // 2
    small_rows = 8 * LAYERS
    links = 4 * (width - 1) + 2

    def body(*refs):
        if chained:
            source_ref, pack_ref, small_ref = refs[:3]
            refs = refs[3:]
            small_out = None
        else:
            source_ref, pack_ref = refs[:2]
            small_out, refs = refs[2], refs[3:]
        column_out, query_ref, query_w_out, out_w_out, kv_ref = refs[:5]
        column_ref, query_w_ref, out_w_ref, kv_own, own_sems, send_sems, recv_sems = refs[5:12]
        pass_sems, land_sems, z_send, z_recv, keep_sems = refs[12:]
        head, rest, core, left, x_peers, y_peer, core_peer = plane_place(blocks)
        plane = lax.div(lax.axis_index("blk"), span)
        sends, passes, owns = [], [], []
        near = x_peers[1:] + [y_peer, core_peer]
        if chained:
            chain = Chain(source_ref, column_ref, z_send, z_recv, blocks)
            slabs = chain.slabs
            greet(near, chain.line)
            chain.pass_on(0)
        else:
            slabs = list(range(COLUMNS))
            greet(near)

        tail = pack_ref[:, tail_at:]
        if not chained:
            small = tail[:, tail_cols - LANES :].astype(jnp.float32).T
            at = own_out - (tail_cols - LANES)
            small = small[at : at + small_rows]
            small_out[...] = small

        def place(k, h, dy, d):
            row = head if dy == 0 else 1 - head
            return kv_ref.at[row, slabs[k], left[d] * 2 + core, pl.ds(h * half, half)]

        def held(k, h, dy, d):
            if dy == 0 and d == 0:
                return kv_own.at[k, pl.ds(h * half, half)]
            return place(k, h, dy, d)

        def send(k, h, dy, d, peer, to_dy, to_d):
            copy = remote(
                held(k, h, dy, d),
                place(k, h, dy, d),
                send_sems.at[len(sends)],
                recv_sems.at[k, h, to_dy, to_d],
                peer,
            )
            copy.start()
            sends.append(copy)

        def hand_over(k, h, dy, d):
            copy = remote(
                held(k, h, dy, d),
                place(k, h, dy, d),
                pass_sems.at[k, h, dy, d],
                land_sems.at[k, h, dy, d],
                core_peer,
            )
            copy.start()
            passes.append(copy)

        def arrived(k, h, dy, d):
            at = place(k, h, dy, d)
            remote(at, at, send_sems.at[0], recv_sems.at[k, h, dy, d], y_peer).wait_recv()

        def first(k):
            slab = slabs[k]
            if not chained:
                x = source_ref[slab].astype(jnp.float32)
                xn = (x * unit_scale(x) * small[0:1]).astype(jnp.bfloat16)
                column_ref[slab] = xn
            elif k == 0:
                xn = source_ref[...]
                column_ref[slab] = xn
            else:
                chain.arrive(k)
                xn = column_ref[slab]
            kv = dot32(xn, pack_ref[:, kv_at:tail_at])
            kv_own[k] = kv.astype(jnp.bfloat16)
            own = pltpu.make_async_copy(
                kv_own.at[k], kv_ref.at[head, slab, rest], own_sems.at[k]
            )
            own.start()
            owns.append(own)
            for d in range(1, width):
                send(k, 0, 0, 0, x_peers[d], 0, d)
            send(k, 1, 0, 0, y_peer, 1, 0)
            send(k, 0, 0, 0, y_peer, 1, 0)
            for d in range(1, width):
                send(k, 1, 0, 0, x_peers[d], 0, d)
            hand_over(k, 0, 0, 0)
            hand_over(k, 1, 0, 0)

        def second(k):
            for d in range(1, width):
                arrived(k, 0, 0, d)
                send(k, 0, 0, d, y_peer, 1, d)
                hand_over(k, 0, 0, d)
            arrived(k, 1, 1, 0)
            for d in range(1, width):
                send(k, 1, 1, 0, x_peers[d], 1, d)
            hand_over(k, 1, 1, 0)

        def third(k):
            arrived(k, 0, 1, 0)
            hand_over(k, 0, 1, 0)
            for d in range(1, width):
                arrived(k, 1, 0, d)
                hand_over(k, 1, 0, d)
            for d in range(1, width):
                arrived(k, 0, 1, d)
                hand_over(k, 0, 1, d)
                arrived(k, 1, 1, d)
                hand_over(k, 1, 1, d)

        def queries():
            low = lax.broadcasted_iota(jnp.int32, (tail_cols, wide), 0)
            target = lax.broadcasted_iota(jnp.int32, (tail_cols, wide), 1)
            goal = lax.div(low, dim) * LANES + lax.rem(low, dim)
            to_low = ((goal == target) & (low < own_out)).astype(jnp.bfloat16)
            query_w = dot32(tail, to_low).astype(jnp.bfloat16)
            query_w_ref[...] = query_w
            out_rows = pack_ref[pl.ds(pl.multiple_of(plane * own_out, 64), own_out), :features]
            pieces = []
            for h in range(heads):
                pieces += [jnp.zeros((dim, features), jnp.bfloat16), out_rows[h * dim : (h + 1) * dim]]
            out_w_ref[...] = jnp.concatenate(pieces, axis=0)
            for k in range(COLUMNS):
                slab = slabs[k]
                query = dot32(column_ref[slab], query_w).astype(jnp.bfloat16)
                query = query.astype(jnp.float32) * scale
                query_ref[slab] = query.astype(jnp.bfloat16)
            for n, (src, dst) in enumerate(
                (
                    (column_ref, column_out),
                    (query_w_ref, query_w_out),
                    (out_w_ref, out_w_out),
                )
            ):
                copy = pltpu.make_async_copy(src, dst, keep_sems.at[n])
                copy.start()
                owns.append(copy)

        for t in range(COLUMNS + 2):
            if t < COLUMNS:
                first(t)
            elif t == COLUMNS:
                queries()
            if 0 <= t - 1 < COLUMNS:
                second(t - 1)
            if 0 <= t - 2 < COLUMNS:
                third(t - 2)
        for copy in owns + passes:
            copy.wait()
        for copy in sends:
            copy.wait_send()
        if chained:
            chain.finish()

    shapes = [
        pltpu.HBM((COLUMNS, rows, features), jnp.bfloat16),
        make((COLUMNS, rows, wide), jnp.bfloat16),
        pltpu.HBM((features, wide), jnp.bfloat16),
        pltpu.HBM((wide, features), jnp.bfloat16),
        make((2, COLUMNS, span, rows, wide), jnp.bfloat16),
    ]
    operands = [source, pack]
    if chained:
        operands.append(smalls)
    else:
        shapes = [jax.ShapeDtypeStruct((small_rows, features), jnp.float32)] + shapes
    results = pl.pallas_call(
        body,
        out_shape=shapes,
        in_specs=[VMEM] * len(operands),
        out_specs=([] if chained else [VMEM]) + [HBM, VMEM, HBM, HBM, ANY],
        scratch_shapes=[
            pltpu.VMEM((COLUMNS, rows, features), jnp.bfloat16),
            pltpu.VMEM((features, wide), jnp.bfloat16),
            pltpu.VMEM((wide, features), jnp.bfloat16),
            pltpu.VMEM((COLUMNS, rows, wide), jnp.bfloat16),
            DMA((COLUMNS,)),
            DMA((COLUMNS * links,)),
            DMA((COLUMNS, 2, 2, width)),
            DMA((COLUMNS, 2, 2, width)),
            DMA((COLUMNS, 2, 2, width)),
            DMA((COLUMNS, 2)),
            DMA((COLUMNS,)),
            DMA((3,)),
        ],
        compiler_params=comm_params(
            collective_id,
            operands
            + [make(shape.shape, shape.dtype) for shape in shapes[:-1]]
            + [make((COLUMNS, rows, wide), jnp.bfloat16)],
            3 * SPARE_BYTES,
        ),
        cost_estimate=lasting(cost),
    )(*operands)
    return list(results) + [smalls] if chained else list(results[1:]) + [results[0]]


def plane_reduce(arrays, blocks, collective_id, cost=25):
    span = blocks // COLUMNS
    width = span // 2
    count = len(arrays)
    shapes = [(values.shape[1],) + tuple(values.shape[3:]) for values in arrays]

    def body(*refs):
        srcs, outs, refs = refs[:count], refs[count : 2 * count], refs[2 * count :]
        scratch = [refs[8 * n : 8 * n + 8] for n in range(count)]
        core_send, core_recv, link_send, link_recv = refs[8 * count :]
        head, blk = lax.axis_index("head"), lax.axis_index("blk")
        plane, rest = lax.div(blk, span), lax.rem(blk, span)
        x, core = lax.div(rest, 2), lax.rem(rest, 2)
        first = plane * span
        right = [lax.rem(x + d, width) for d in range(width)]
        x_peers = [(head, first + right[d] * 2 + core) for d in range(width)]
        y_peer = (1 - head, blk)
        core_peer = (head, first + x * 2 + 1 - core)
        greet(x_peers[1:] + [y_peer, core_peer])

        def wide(ref, *at):
            return ref[at].astype(jnp.float32)

        starts = {}
        for n in range(count):
            half = shapes[n][0] // 2
            for h in range(2):
                copy = remote(
                    srcs[n].at[:, pl.ds(h * half, half), :, 1 - core],
                    scratch[n][0].at[:, pl.ds(h * half, half)],
                    core_send.at[n, h],
                    core_recv.at[n, h],
                    core_peer,
                )
                copy.start()
                starts[n, h] = copy

        sends, yas, ybs, xbs = {}, {}, {}, {}
        for n in range(count):
            src, half, kind = srcs[n], shapes[n][0] // 2, arrays[n].dtype
            core_in, summed, xa_in, _, _, yb_in, _, _ = scratch[n]

            def core_sum(h):
                def step(i, _):
                    yy = lax.div(i, half * width)
                    zz = lax.div(lax.rem(i, half * width), width) + h * half
                    xx = lax.rem(i, width)
                    total = wide(src, yy, zz, xx, core) + wide(core_in, yy, zz, xx)
                    summed[yy, zz, xx] = total.astype(kind)
                    return 0

                lax.fori_loop(0, 2 * half * width, step, 0)

            starts[n, 0].wait_recv()
            core_sum(0)
            for d in range(1, width):
                copy = remote(
                    summed.at[:, pl.ds(0, half), right[d]],
                    xa_in.at[d],
                    link_send.at[n, 0, d],
                    link_recv.at[n, 0, d],
                    x_peers[d],
                )
                copy.start()
                sends[n, d] = copy
            starts[n, 1].wait_recv()
            core_sum(1)
            ybs[n] = remote(
                summed.at[1 - head, pl.ds(half, half)],
                yb_in,
                link_send.at[n, 1, 0],
                link_recv.at[n, 1, 0],
                y_peer,
            )
            ybs[n].start()
        for n in range(count):
            half, kind = shapes[n][0] // 2, arrays[n].dtype
            _, summed, xa_in, ya_out, ya_in, yb_in, xb_out, xb_in = scratch[n]
            for d in range(1, width):
                sends[n, d].wait_recv()

            def a_step(zz, _):
                total = wide(summed, 1 - head, zz, x)
                for d in range(1, width):
                    total = total + wide(xa_in, d, 1 - head, zz)
                ya_out[zz] = total.astype(kind)
                return 0

            lax.fori_loop(0, half, a_step, 0)
            yas[n] = remote(
                ya_out, ya_in, link_send.at[n, 0, 0], link_recv.at[n, 0, 0], y_peer
            )
            yas[n].start()
            ybs[n].wait_recv()
            for d in range(1, width):

                def b_step(zz, _):
                    total = wide(summed, head, half + zz, right[d]) + wide(yb_in, zz, right[d])
                    xb_out[d, zz] = total.astype(kind)
                    return 0

                lax.fori_loop(0, half, b_step, 0)
                xbs[n, d] = remote(
                    xb_out.at[d],
                    xb_in.at[d],
                    link_send.at[n, 1, d],
                    link_recv.at[n, 1, d],
                    x_peers[d],
                )
                xbs[n, d].start()
        for n in range(count):
            out, half, kind = outs[n], shapes[n][0] // 2, arrays[n].dtype
            _, summed, xa_in, _, ya_in, yb_in, _, xb_in = scratch[n]
            yas[n].wait_recv()

            def a_last(zz, _):
                total = wide(summed, head, zz, x) + wide(ya_in, zz)
                for d in range(1, width):
                    total = total + wide(xa_in, d, head, zz)
                out[zz] = total.astype(kind)
                return 0

            lax.fori_loop(0, half, a_last, 0)
            for d in range(1, width):
                xbs[n, d].wait_recv()

            def b_last(zz, _):
                total = wide(summed, head, half + zz, x) + wide(yb_in, zz, x)
                for d in range(1, width):
                    total = total + wide(xb_in, d, zz)
                out[half + zz] = total.astype(kind)
                return 0

            lax.fori_loop(0, half, b_last, 0)
        for group in (starts, sends, yas, ybs, xbs):
            for copy in group.values():
                copy.wait_send()

    scratch = []
    for (slabs, *tile), values in zip(shapes, arrays):
        tile, half, kind = tuple(tile), slabs // 2, values.dtype
        scratch += [
            pltpu.VMEM((2, slabs, width) + tile, kind),
            pltpu.VMEM((2, slabs, width) + tile, kind),
            pltpu.VMEM((width, 2, half) + tile, kind),
            pltpu.VMEM((half,) + tile, kind),
            pltpu.VMEM((half,) + tile, kind),
            pltpu.VMEM((half, width) + tile, kind),
            pltpu.VMEM((width, half) + tile, kind),
            pltpu.VMEM((width, half) + tile, kind),
        ]
    return pl.pallas_call(
        body,
        out_shape=[
            jax.ShapeDtypeStruct(shape, values.dtype) for shape, values in zip(shapes, arrays)
        ],
        in_specs=[VMEM] * count,
        out_specs=[VMEM] * count,
        scratch_shapes=scratch
        + [DMA((count, 2)), DMA((count, 2)), DMA((count, 2, width)), DMA((count, 2, width))],
        compiler_params=comm_params(
            collective_id, scratch + 2 * [make(a.shape, a.dtype) for a in arrays]
        ),
        cost_estimate=lasting(cost),
    )(
        *[
            values.reshape((2, values.shape[1], width, 2) + tuple(values.shape[3:]))
            for values in arrays
        ]
    )


def reduce_project(dkv_all, dq, query_w, pack, blocks, collective_id, cost=26):
    span = blocks // COLUMNS
    width = span // 2
    rows, wide = dkv_all.shape[3:]
    half = rows // 2
    features = query_w.shape[0]
    kind = dkv_all.dtype

    def body(
        src,
        dq_ref,
        w_ref,
        pack_ref,
        dkv_ref,
        dxn_ref,
        core_in,
        summed,
        xa_in,
        ya_out,
        ya_in,
        yb_in,
        xb_out,
        xb_in,
        share,
        core_send,
        core_recv,
        link_send,
        link_recv,
        z_send,
        z_recv,
    ):
        head, _, core, _, x_peers, y_peer, core_peer = plane_place(blocks)
        plane, planes, z_peers = column_place(blocks)
        x = lax.div(lax.rem(lax.axis_index("blk"), span), 2)
        right = [lax.rem(x + d, width) for d in range(width)]
        greet(x_peers[1:] + [y_peer, core_peer] + z_peers[1:])
        order = (2, 1, 3, 0)
        copies = []

        def begin(copy):
            copy.start()
            copies.append(copy)
            return copy

        def wide_of(ref, *at):
            return ref[at].astype(jnp.float32)

        top, low = pl.ds(0, half), pl.ds(half, half)
        starts = []

        def cross(k):
            starts.append(
                begin(
                    remote(
                        src.at[:, planes[order[k]], :, 1 - core],
                        core_in.at[k],
                        core_send.at[k],
                        core_recv.at[k],
                        core_peer,
                    )
                )
            )

        cross(0)
        cross(1)
        xas, yas, ybs, xbs, z_copies = {}, {}, {}, {}, []

        def first(k):
            starts[k].wait_recv()
            if k + 2 < COLUMNS:
                cross(k + 2)

            def step(i, _):
                yy, xx = lax.div(i, width), lax.rem(i, width)
                total = wide_of(src, yy, planes[order[k]], xx, core) + wide_of(core_in, k, yy, xx)
                summed[k, yy, xx] = total.astype(kind)
                return 0

            lax.fori_loop(0, 2 * width, step, 0)
            for d in range(1, width):
                xas[k, d] = begin(
                    remote(
                        summed.at[k, :, right[d], top],
                        xa_in.at[k, d],
                        link_send.at[k, 0, d],
                        link_recv.at[k, 0, d],
                        x_peers[d],
                    )
                )
            ybs[k] = begin(
                remote(
                    summed.at[k, 1 - head, :, low],
                    yb_in.at[k],
                    link_send.at[k, 1, 0],
                    link_recv.at[k, 1, 0],
                    y_peer,
                )
            )

        def second(k):
            total = wide_of(summed, k, 1 - head, x, top)
            for d in range(1, width):
                xas[k, d].wait_recv()
                total = total + wide_of(xa_in, k, d, 1 - head)
            ya_out[k] = total.astype(kind)
            yas[k] = begin(
                remote(
                    ya_out.at[k],
                    ya_in.at[k],
                    link_send.at[k, 0, 0],
                    link_recv.at[k, 0, 0],
                    y_peer,
                )
            )
            ybs[k].wait_recv()
            for d in range(1, width):
                total = wide_of(summed, k, head, right[d], low) + wide_of(yb_in, k, right[d])
                xb_out[k, d] = total.astype(kind)
                xbs[k, d] = begin(
                    remote(
                        xb_out.at[k, d],
                        xb_in.at[k, d],
                        link_send.at[k, 1, d],
                        link_recv.at[k, 1, d],
                        x_peers[d],
                    )
                )

        def third(k):
            slab = planes[order[k]]
            yas[k].wait_recv()
            total = wide_of(summed, k, head, x, top) + wide_of(ya_in, k)
            for d in range(1, width):
                total = total + wide_of(xa_in, k, d, head)
            dkv_ref[slab, top] = total.astype(kind)
            total = wide_of(summed, k, head, x, low) + wide_of(yb_in, k, x)
            for d in range(1, width):
                xbs[k, d].wait_recv()
                total = total + wide_of(xb_in, k, d)
            dkv_ref[slab, low] = total.astype(kind)
            part = (
                dot32(dq_ref[slab], w_ref[...], LAST)
                + dot32(dkv_ref[slab], pack_ref[:, features : features + wide], LAST)
            ).astype(kind)
            if order[k] == 0:
                dxn_ref[plane] = part
            else:
                share[k] = part
                z_copies.append(
                    begin(
                        remote(
                            share.at[k],
                            dxn_ref.at[plane],
                            z_send.at[order[k]],
                            z_recv.at[order[k]],
                            z_peers[order[k]],
                        )
                    )
                )

        for t in range(COLUMNS + 2):
            if t < COLUMNS:
                first(t)
            if 0 <= t - 1 < COLUMNS:
                second(t - 1)
            if 0 <= t - 2 < COLUMNS:
                third(t - 2)
        for copy in z_copies:
            copy.wait_recv()
        for copy in copies:
            copy.wait_send()

    tile = (rows, wide)
    part = (half, wide)
    scratch = [
        pltpu.VMEM((COLUMNS, 2, width) + tile, kind),
        pltpu.VMEM((COLUMNS, 2, width) + tile, kind),
        pltpu.VMEM((COLUMNS, width, 2) + part, kind),
        pltpu.VMEM((COLUMNS,) + part, kind),
        pltpu.VMEM((COLUMNS,) + part, kind),
        pltpu.VMEM((COLUMNS, width) + part, kind),
        pltpu.VMEM((COLUMNS, width) + part, kind),
        pltpu.VMEM((COLUMNS, width) + part, kind),
        pltpu.VMEM((COLUMNS, rows, features), kind),
    ]
    shapes = [make((COLUMNS,) + tile, kind), make((COLUMNS, rows, features), kind)]
    return pl.pallas_call(
        body,
        out_shape=shapes,
        in_specs=[VMEM] * 4,
        out_specs=[VMEM] * 2,
        scratch_shapes=scratch
        + [
            DMA((COLUMNS,)),
            DMA((COLUMNS,)),
            DMA((COLUMNS, 2, width)),
            DMA((COLUMNS, 2, width)),
            DMA((COLUMNS,)),
            DMA((COLUMNS,)),
        ],
        compiler_params=comm_params(
            collective_id, scratch + shapes + [dkv_all, dq, query_w, pack], 7 * SPARE_BYTES
        ),
        cost_estimate=lasting(cost),
    )(dkv_all.reshape((2, COLUMNS, width, 2) + tile), dq, query_w, pack)


NEGATIVE = -1e30
EPSILON = 1e-06
KEYS = 1024
LANES = 128
LAST = (((1,), (1,)), ((), ()))
FIRST = (((0,), (0,)), ((), ()))


def dot32(a, b, dims=(((1,), (0,)), ((), ()))):
    return lax.dot_general(a, b, dims, preferred_element_type=jnp.float32)


def visible(key_base, query_base, keys, queries, starts):
    key_pos = key_base + lax.broadcasted_iota(jnp.int32, (keys, queries), 0)
    query_pos = query_base + lax.broadcasted_iota(jnp.int32, (keys, queries), 1)
    return (key_pos <= query_pos) & (key_pos >= starts)


def block_bounds(starts, bases, rows):
    return jnp.stack(
        [
            lax.div(starts[:, 0], KEYS),
            lax.div(bases + rows - 1, KEYS),
            bases,
            lax.div(starts[:, rows - 1], KEYS),
        ],
        axis=1,
    )


def over_chunks(bounds_ref, i, step, carry):
    low, high, edge = bounds_ref[i, 0], bounds_ref[i, 1], bounds_ref[i, 3]
    carry = step(high, True, carry)
    inner = jnp.maximum(high - 1 - edge, 0)
    carry = lax.fori_loop(0, inner, lambda t, c: step(high - 1 - t, False, c), carry)
    below = high - 1 - inner
    return lax.fori_loop(0, below - low + 1, lambda t, c: step(below - t, True, c), carry)


def attend(bounds, queries, kv_all, starts):
    count, rows, width = queries.shape
    heads = width // LANES

    def body(bounds_ref, q_ref, kv_ref, start_ref, out_ref, attn_ref):
        i = pl.program_id(0)
        base = bounds_ref[i, 2]
        start_row = start_ref[0]
        q = [q_ref[0, :, h * LANES : (h + 1) * LANES] for h in range(heads)]

        def step(chunk, masked, carry):
            at = pl.multiple_of(chunk * KEYS, KEYS)
            if masked:
                ok = visible(chunk * KEYS, base, KEYS, rows, start_row)
            kvs = [kv_ref[pl.ds(at, KEYS), h * LANES : (h + 1) * LANES] for h in range(heads)]
            scores = [dot32(kvs[h], q[h], LAST) for h in range(heads)]
            if masked:
                scores = [jnp.where(ok, s, NEGATIVE) for s in scores]
            tops = [
                jnp.maximum(carry[h][0], jnp.max(scores[h], axis=0, keepdims=True))
                for h in range(heads)
            ]
            weights = [jnp.exp(scores[h] - tops[h]) for h in range(heads)]
            shrinks = [jnp.exp(carry[h][0] - tops[h]) for h in range(heads)]
            totals = [
                carry[h][1] * shrinks[h] + jnp.sum(weights[h], axis=0, keepdims=True)
                for h in range(heads)
            ]
            accs = [
                carry[h][2] * shrinks[h] + dot32(kvs[h], weights[h].astype(jnp.bfloat16), FIRST)
                for h in range(heads)
            ]
            return tuple(zip(tops, totals, accs))

        empty = tuple(
            (
                jnp.full((1, rows), NEGATIVE, jnp.float32),
                jnp.zeros((1, rows), jnp.float32),
                jnp.zeros((LANES, rows), jnp.float32),
            )
            for h in range(heads)
        )
        done = over_chunks(bounds_ref, i, step, empty)
        lane = lax.broadcasted_iota(jnp.int32, (LANES, rows), 0)
        narrow = []
        for h in range(heads):
            top, total, acc = done[h]
            value = jnp.where(lane < LANES // 2, top + jnp.log(total), acc / total)
            out_ref[0, :, h * LANES : (h + 1) * LANES] = value.T
            narrow.append(value[LANES // 2 :])
        attn_ref[0] = jnp.concatenate(narrow, axis=0).T.astype(jnp.bfloat16)

    return pl.pallas_call(
        body,
        out_shape=(
            jax.ShapeDtypeStruct((count, rows, width), jnp.float32),
            jax.ShapeDtypeStruct((count, rows, width // 2), jnp.bfloat16),
        ),
        grid_spec=pltpu.PrefetchScalarGridSpec(
            num_scalar_prefetch=1,
            grid=(count,),
            in_specs=[
                pl.BlockSpec((1, rows, width), lambda i, b: (i, 0, 0)),
                pl.BlockSpec(kv_all.shape, lambda i, b: (0, 0)),
                pl.BlockSpec((1, 1, rows), lambda i, b: (i, 0, 0)),
            ],
            out_specs=(
                pl.BlockSpec((1, rows, width), lambda i, b: (i, 0, 0)),
                pl.BlockSpec((1, rows, width // 2), lambda i, b: (i, 0, 0)),
            ),
        ),
        compiler_params=pltpu.CompilerParams(
            vmem_limit_bytes=room([kv_all] * 2, 4 * SPARE_BYTES)
        ),
        cost_estimate=lasting(13),
    )(bounds, queries, kv_all, starts)


def attend_back(bounds, queries, dy, out_rows, kept, kv_all, starts, scale):
    count, rows, width = queries.shape
    total_keys = kv_all.shape[0]
    heads = width // LANES
    if total_keys * width * 14 > VMEM_BYTES:
        heads = 1
    wide = heads * LANES

    def body(bounds_ref, q_ref, dy_ref, w_ref, kept_ref, kv_ref, start_ref, dq_ref, dkv_ref, acc_ref):
        i = pl.program_id(1)
        base = bounds_ref[i, 2]
        start_row = start_ref[0]

        @pl.when(i == 0)
        def _():
            def clear(c, _):
                acc_ref[pl.ds(pl.multiple_of(c * KEYS, KEYS), KEYS), :] = jnp.zeros(
                    (KEYS, wide), jnp.float32
                )
                return 0

            lax.fori_loop(0, total_keys // KEYS, clear, 0)

        q = [q_ref[0, :, h * LANES : (h + 1) * LANES] for h in range(heads)]
        grads = dot32(dy_ref[0], w_ref[...], LAST).astype(jnp.bfloat16)
        g = [grads[:, h * LANES : (h + 1) * LANES] for h in range(heads)]
        qg = [jnp.concatenate([q[h], g[h]], axis=0) for h in range(heads)]
        lse, delta = [], []
        for h in range(heads):
            kept_t = kept_ref[0, :, h * LANES : (h + 1) * LANES].T
            lse.append(kept_t[0:1])
            delta.append(jnp.sum(kept_t * g[h].astype(jnp.float32).T, axis=0, keepdims=True))

        def step(chunk, masked, carry):
            at = pl.multiple_of(chunk * KEYS, KEYS)
            if masked:
                ok = visible(chunk * KEYS, base, KEYS, rows, start_row)
            lanes = [slice(h * LANES, (h + 1) * LANES) for h in range(heads)]
            kvs = [kv_ref[pl.ds(at, KEYS), lanes[h]] for h in range(heads)]
            pairs = [dot32(kvs[h], qg[h], LAST) for h in range(heads)]
            scores = [p[:, :rows] for p in pairs]
            dprobs = [p[:, rows:] for p in pairs]
            if masked:
                scores = [jnp.where(ok, s, NEGATIVE) for s in scores]
            probs = [jnp.exp(scores[h] - lse[h]) for h in range(heads)]
            dscores = [
                (probs[h] * (dprobs[h] - delta[h])).astype(jnp.bfloat16) for h in range(heads)
            ]
            both = [
                jnp.concatenate([dscores[h], probs[h].astype(jnp.bfloat16)], axis=1)
                for h in range(heads)
            ]
            for h in range(heads):
                acc_ref[pl.ds(at, KEYS), lanes[h]] += dot32(both[h], qg[h])
            return tuple(carry[h] + dot32(kvs[h], dscores[h], FIRST) for h in range(heads))

        done = over_chunks(
            bounds_ref,
            i,
            step,
            tuple(jnp.zeros((LANES, rows), jnp.float32) for h in range(heads)),
        )
        lane = lax.broadcasted_iota(jnp.int32, (LANES, rows), 0)
        for h in range(heads):
            value = jnp.where(lane < LANES // 2, done[h] * scale, 0.0)
            dq_ref[0, :, h * LANES : (h + 1) * LANES] = value.T.astype(jnp.bfloat16)

        @pl.when(i == count - 1)
        def _():
            def store(c, _):
                at = pl.ds(pl.multiple_of(c * KEYS, KEYS), KEYS)
                dkv_ref[at, :] = acc_ref[at, :].astype(jnp.bfloat16)
                return 0

            lax.fori_loop(0, total_keys // KEYS, store, 0)

    block = pl.BlockSpec((1, rows, wide), lambda h, i, b: (i, 0, h))
    whole = pl.BlockSpec((total_keys, wide), lambda h, i, b: (0, h))
    return pl.pallas_call(
        body,
        out_shape=(
            jax.ShapeDtypeStruct((count, rows, width), jnp.bfloat16),
            jax.ShapeDtypeStruct(kv_all.shape, jnp.bfloat16),
        ),
        grid_spec=pltpu.PrefetchScalarGridSpec(
            num_scalar_prefetch=1,
            grid=(width // wide, count),
            in_specs=[
                block,
                pl.BlockSpec((1,) + tuple(dy.shape[1:]), lambda h, i, b: (i, 0, 0)),
                pl.BlockSpec((wide, out_rows.shape[1]), lambda h, i, b: (h, 0)),
                block,
                whole,
                pl.BlockSpec((1, 1, rows), lambda h, i, b: (i, 0, 0)),
            ],
            out_specs=(block, whole),
            scratch_shapes=[pltpu.VMEM((total_keys, wide), jnp.float32)],
        ),
        compiler_params=pltpu.CompilerParams(
            vmem_limit_bytes=room([make((total_keys, wide), jnp.bfloat16)] * 6, 5 * SPARE_BYTES)
        ),
        cost_estimate=lasting(20),
    )(bounds, queries, dy, out_rows, kept, kv_all, starts)


def experts_exchange(
    sent,
    saved,
    own,
    other,
    layer,
    blocks,
    collective_id,
    forward,
    backward,
    cost,
    ahead=None,
    cross=(),
):
    fetch = other[2] is None
    other = [w for w in other if w is not None]
    copies = blocks // NE
    half = NE // 2
    slots, width = sent[0].shape[1:]
    hidden, features = other[0].shape
    tile = min(hidden, 256)
    tiles = hidden // tile
    count = len(sent)
    homes_count = int(forward) + int(backward)
    total_rows = copies * NE * slots
    kind = sent[0].dtype
    sizes = (half // 2, half // 2, half)
    first_rows = [copies * slots * at for at in (0, half // 2, half)]
    most_rows = copies * slots * half
    plain = (((1,), (0,)), ((), ()))

    def body(*refs):
        refs = list(refs)

        def take(n):
            taken = refs[:n]
            del refs[:n]
            return taken

        srcs = take(count)
        saved_ref = take(1)[0] if not forward else None
        weight_refs = take(3 + len(other))
        ahead_ref = take(1)[0] if ahead is not None else None
        cross_refs = take(len(cross))
        homes = take(homes_count)
        arrived_ref = take(1)[0] if not backward else None
        fetched_ref = take(1)[0] if fetch and not backward else None
        next_ref = take(1)[0] if ahead is not None else None
        keeps, aways = (take(3), take(3)) if backward else ([], [])
        crossed = take(len(cross))
        lands = take(count)
        weights = take(6)
        parts, sib_ins, totals = take(homes_count), take(homes_count), take(homes_count)
        accs = take(homes_count)
        rows_x = take(1)[0]
        if backward:
            rows_z, act_ref, dgate_ref, dup_ref, keep_ref, away_ref = take(6)
            if not forward:
                gate_ref, up_ref = take(2)
            out_sems = take(1)[0]
        load_sems, own_sems, send_sems, recv_sems, pass_sems, land_sems = take(6)
        home_own, home_send, home_recv, part_send, part_recv, arrived_sem = take(6)
        swap_send, swap_recv = take(2)

        head, blk = lax.axis_index("head"), lax.axis_index("blk")
        expert, piece = lax.div(blk, copies), lax.rem(blk, copies)
        near = lax.div(expert, half) * half
        far = half - near
        places = [lax.rem(piece + k, copies) for k in range(copies)]
        siblings = [(head, expert * copies + places[k]) for k in range(copies)]
        others = [lax.rem(expert + d, NE) for d in range(NE)]
        swaps = [(1 - head, blk)] if fetch or ahead is not None or cross else []
        greet([(head, e * copies + piece) for e in others[1:]] + siblings[1:] + swaps)
        mine = pl.ds(pl.multiple_of(head * features, LANES), features)
        rest = pl.ds(pl.multiple_of((1 - head) * features, LANES), features)
        steps = [(far, sizes[0]), (far + sizes[0], sizes[1]), (near, sizes[2])]

        def sending(n, e):
            return remote(
                srcs[n].at[e],
                lands[n].at[piece, expert],
                send_sems.at[n, e],
                recv_sems.at[n, expert],
                (head, e * copies + piece),
            )

        owns = []
        for n in range(count):
            copy = pltpu.make_async_copy(
                srcs[n].at[expert], lands[n].at[piece, expert], own_sems.at[n]
            )
            copy.start()
            owns.append(copy)
        def each(t, copy_of, arrays, act):
            first, size = steps[t]
            for j in range(size):
                for n in range(arrays):
                    if t < 2:
                        act(copy_of(n, first + j))
                    else:

                        @pl.when(first + j != expert)
                        def _():
                            act(copy_of(n, first + j))

        def send(t):
            each(t, sending, count, lambda copy: copy.start())

        def sent_out(t):
            each(t, sending, count, lambda copy: copy.wait_send())

        for t in range(3):
            send(t)
        crossing = []
        if fetch:
            crossing.append(
                remote(
                    weight_refs[4].at[layer],
                    weights[5],
                    swap_send.at[0],
                    swap_recv.at[0],
                    swaps[0],
                )
            )
        if ahead is not None:
            crossing.append(
                remote(
                    ahead_ref.at[layer + 1],
                    next_ref,
                    swap_send.at[1],
                    swap_recv.at[1],
                    swaps[0],
                )
            )
        for n in range(len(cross)):
            crossing.append(
                remote(
                    cross_refs[n],
                    crossed[n],
                    swap_send.at[2 + n],
                    swap_recv.at[2 + n],
                    swaps[0],
                )
            )
        for n, copy in enumerate(crossing):
            if ahead is None or n == 0:
                copy.start()
        loads = []
        for n in range(3 + len(other)):
            weight = weight_refs[n] if n % 2 else weight_refs[n].at[layer]
            copy = pltpu.make_async_copy(weight, weights[n], load_sems.at[n])
            copy.start()
            loads.append(copy)
        go, gx, uo, ux, do, dx = weights
        passes, exchanges = [], {}

        def arrive(t):
            first, size = steps[t]
            waits = []
            if t == 2:
                for copy in owns:
                    copy.wait()
            for j in range(size):
                e = first + j
                for n in range(count):
                    place = lands[n].at[piece, e]

                    @pl.when(e != expert)
                    def _():
                        remote(
                            place, place, send_sems.at[n, e], recv_sems.at[n, e], siblings[0]
                        ).wait_recv()

                    for k in range(1, copies):
                        copy = remote(
                            place,
                            place,
                            pass_sems.at[n, k, e],
                            land_sems.at[n, k, e],
                            siblings[k],
                        )
                        copy.start()
                        waits.append(copy)
            for copy in waits:
                copy.wait_recv()
            passes.extend(waits)

        def flat(ref, t):
            first, size = steps[t]
            value = ref[:, pl.ds(first, size)].astype(jnp.float32)
            return value.reshape((copies * size * slots, width)).astype(kind)

        def span_of(t):
            return slice(first_rows[t], first_rows[t] + copies * steps[t][1] * slots)

        def gate_up(t, j):
            at = pl.ds(pl.multiple_of(j * tile, tile), tile)
            xo, xx = rows_x[span_of(t), mine], rows_x[span_of(t), rest]
            gate = dot32(xo, go[at], LAST) + dot32(xx, gx[at], LAST)
            return gate, dot32(xo, uo[at], LAST) + dot32(xx, ux[at], LAST)

        def early(t):
            rows_x[span_of(t)] = flat(saved_ref, t)
            size = copies * steps[t][1] * slots

            def step(j, _):
                at = pl.ds(pl.multiple_of(j * tile, tile), tile)
                gate_ref[:size, at], up_ref[:size, at] = gate_up(t, j)
                return 0

            lax.fori_loop(0, tiles, step, 0)

        def work(t):
            size = copies * steps[t][1] * slots
            span = span_of(t)
            if forward:
                rows_x[span] = flat(lands[0], t)
            if backward:
                rows_z[span] = flat(lands[-1], t)
            for acc in accs:
                acc[:size] = jnp.zeros((size, width), jnp.float32)

            def step(j, _):
                at = pl.ds(pl.multiple_of(j * tile, tile), tile)
                if forward:
                    gate, up = gate_up(t, j)
                else:
                    gate, up = gate_ref[:size, at], up_ref[:size, at]
                sigmoid = jax.nn.sigmoid(gate)
                silu = gate * sigmoid
                act = (silu * up).astype(kind)
                if forward:
                    accs[0][:size, mine] += dot32(act, do[at])
                    accs[0][:size, rest] += dot32(act, dx[at])
                if backward:
                    zo, zx = rows_z[span, mine], rows_z[span, rest]
                    dact = dot32(zo, do[at], LAST) + dot32(zx, dx[at], LAST)
                    dgate = (dact * up * sigmoid * (1.0 + gate * (1.0 - sigmoid))).astype(kind)
                    dup = (dact * silu).astype(kind)
                    act_ref[span, at] = act
                    dgate_ref[span, at] = dgate
                    dup_ref[span, at] = dup
                    accs[-1][:size, mine] += dot32(dgate, go[at]) + dot32(dup, uo[at])
                    accs[-1][:size, rest] += dot32(dgate, gx[at]) + dot32(dup, ux[at])
                return 0

            lax.fori_loop(0, tiles, step, 0)
            first, size_e = steps[t]
            for n in range(homes_count):
                value = accs[n][:size].reshape((copies, size_e, slots, width))
                parts[n][:, pl.ds(first, size_e)] = value.astype(kind)
                for j in range(size_e):
                    for k in range(1, copies):
                        copy = remote(
                            parts[n].at[places[k], first + j],
                            sib_ins[n].at[k - 1, first + j],
                            part_send.at[n, k, first + j],
                            part_recv.at[n, k, first + j],
                            siblings[k],
                        )
                        copy.start()
                        exchanges[n, t, j, k] = copy

        def homeward(n, e):
            return remote(
                totals[n].at[e],
                homes[n].at[expert],
                home_send.at[n, e],
                home_recv.at[n, expert],
                (head, e * copies + piece),
            )

        def give_back(t):
            first, size = steps[t]
            for j in range(size):
                e = first + j
                for n in range(homes_count):
                    value = parts[n][piece, e].astype(jnp.float32)
                    for k in range(1, copies):
                        exchanges[n, t, j, k].wait_recv()
                        value = value + sib_ins[n][k - 1, e].astype(jnp.float32)
                    totals[n][e] = value.astype(kind)
                    if t < 2:
                        homeward(n, e).start()
                    else:

                        @pl.when(e != expert)
                        def _():
                            homeward(n, e).start()

        for copy in loads:
            copy.wait()
        if not forward:
            early(0)
        for t in range(len(steps)):
            arrive(t)
            if t == 0 and fetch:
                crossing[0].wait_recv()
                if ahead is not None:
                    crossing[1].start()
            work(t)
            if t > 0:
                give_back(t - 1)
            if not forward and t + 1 < len(steps):
                early(t + 1)
        give_back(len(steps) - 1)
        stays = []
        for n in range(homes_count):
            copy = pltpu.make_async_copy(
                totals[n].at[expert], homes[n].at[expert], home_own.at[n]
            )
            copy.start()
            stays.append(copy)

        if backward:

            def saving(n, j, which):
                at = pl.ds(pl.multiple_of(j * tile, tile), tile)
                src, dst = ((keep_ref, keeps), (away_ref, aways))[which]
                return pltpu.make_async_copy(src.at[n, at], dst[n].at[at], out_sems.at[n, j, which])

            def grads(j, _):
                at = pl.ds(pl.multiple_of(j * tile, tile), tile)
                for n, (left, right) in enumerate(
                    ((dgate_ref, rows_x), (dup_ref, rows_x), (act_ref, rows_z))
                ):
                    value = left[:, at]
                    away_ref[n, at] = dot32(value, right[:, rest], FIRST).astype(kind)
                    saving(n, j, 1).start()
                    keep_ref[n, at] = dot32(value, right[:, mine], FIRST).astype(kind)
                    saving(n, j, 0).start()
                return 0

            lax.fori_loop(0, tiles, grads, 0)

        if not backward:
            copy = pltpu.make_async_copy(lands[0], arrived_ref, arrived_sem)
            copy.start()
            stays.append(copy)
            if fetch:
                copy = pltpu.make_async_copy(weights[5], fetched_ref, load_sems.at[5])
                copy.start()
                stays.append(copy)
        for n in range(homes_count):
            for e in others[1:]:
                place = homes[n].at[e]
                remote(
                    place, place, home_send.at[n, e], home_recv.at[n, e], siblings[0]
                ).wait_recv()
        for t in range(len(steps)):
            sent_out(t)
            each(t, homeward, homes_count, lambda copy: copy.wait_send())
        for copy in passes + list(exchanges.values()):
            copy.wait_send()
        for copy in stays:
            copy.wait()
        for copy in crossing[int(fetch) :]:
            copy.wait_recv()
        for copy in crossing:
            copy.wait_send()
        if backward:

            def settle(j, _):
                for n in range(3):
                    saving(n, j, 0).wait()
                    saving(n, j, 1).wait()
                return 0

            lax.fori_loop(0, tiles, settle, 0)

    slab = (copies, NE, slots, width)
    shapes = [make((NE, slots, width), kind)] * homes_count
    specs = [ANY] * homes_count
    if not backward:
        shapes.append(pltpu.HBM(slab, kind))
        specs.append(HBM)
        for _ in range(int(fetch) + int(ahead is not None)):
            shapes.append(pltpu.HBM((hidden, features), kind))
            specs.append(HBM)
    else:
        shapes += [pltpu.HBM((hidden, features), kind)] * (6 + len(cross))
        specs += [HBM] * (6 + len(cross))
    scratch = [pltpu.VMEM(slab, kind)] * count
    scratch += [pltpu.VMEM((hidden, features), kind)] * 6
    scratch += [pltpu.VMEM(slab, kind)] * homes_count
    scratch += [pltpu.VMEM((copies - 1,) + slab[1:], kind)] * homes_count
    scratch += [pltpu.VMEM((NE, slots, width), kind)] * homes_count
    scratch += [pltpu.VMEM((most_rows, width), jnp.float32)] * homes_count
    scratch.append(pltpu.VMEM((total_rows, width), kind))
    if backward:
        scratch.append(pltpu.VMEM((total_rows, width), kind))
        scratch += [pltpu.VMEM((total_rows, hidden), kind)] * 3
        scratch += [pltpu.VMEM((3, hidden, features), kind)] * 2
        if not forward:
            scratch += [pltpu.VMEM((most_rows, hidden), jnp.float32)] * 2
        scratch.append(DMA((3, tiles, 2)))
    scratch += [DMA((6,)), DMA((count,)), DMA((count, NE)), DMA((count, NE))]
    scratch += [DMA((count, copies, NE))] * 2
    scratch += [DMA((homes_count,)), DMA((homes_count, NE)), DMA((homes_count, NE))]
    scratch += [DMA((homes_count, copies, NE))] * 2 + [DMA] + [DMA((2 + len(cross),))] * 2
    operands = list(sent)
    in_specs = [ANY] * count
    if not forward:
        operands.append(saved)
        in_specs.append(VMEM)
    for n in range(3):
        operands += [own[n]] + other[n : n + 1]
    if ahead is not None:
        operands.append(ahead)
    operands += list(cross)
    in_specs += [HBM] * (len(operands) - len(in_specs))
    return pl.pallas_call(
        body,
        out_shape=shapes,
        in_specs=in_specs,
        out_specs=specs,
        scratch_shapes=scratch,
        compiler_params=comm_params(
            collective_id,
            scratch + ([saved] if not forward else []),
            (11 if backward else 2) * SPARE_BYTES,
        ),
        cost_estimate=lasting(cost),
    )(*operands)


def split(values, terms=2):
    parts = []
    for _ in range(terms):
        part = values.astype(jnp.bfloat16)
        parts.append(part)
        values = values - part.astype(jnp.float32)
    return parts


def exact_dot(pieces, values, dims):
    total = dot32(pieces[0], values, dims)
    for piece in pieces[1:]:
        total = total + dot32(piece, values, dims)
    return total


def unit_scale(values):
    return lax.rsqrt(jnp.mean(values * values, axis=-1, keepdims=True) + EPSILON)


def alone(body, out_shape, cost, *operands, scalars=0):
    specs = [pl.BlockSpec(memory_space=pltpu.SMEM)] * scalars + [VMEM] * (len(operands) - scalars)
    results = pl.pallas_call(
        body,
        out_shape=out_shape,
        in_specs=specs,
        out_specs=jax.tree.map(lambda _: VMEM, out_shape),
        compiler_params=pltpu.CompilerParams(
            vmem_limit_bytes=room(list(operands) + jax.tree.leaves(out_shape), 2 * SPARE_BYTES)
        ),
        cost_estimate=lasting(cost),
    )(*operands)
    return list(results) if isinstance(out_shape, (list, tuple)) else results


def route_tables(routes, gates):
    count, rows, _ = routes.shape
    slots = NE * CAP

    def body(routes_ref, gates_ref, picks_ref, weights_ref, slot_ref, other_ref):
        row = lax.broadcasted_iota(jnp.int32, (rows, rows), 0)
        col = lax.broadcasted_iota(jnp.int32, (rows, rows), 1)
        before = (col < row).astype(jnp.bfloat16)
        expert = lax.broadcasted_iota(jnp.int32, (rows, LANES), 1)
        slot = lax.broadcasted_iota(jnp.int32, (rows, slots), 1)
        source = lax.broadcasted_iota(jnp.int32, (LANES, slots), 0)
        target = lax.broadcasted_iota(jnp.int32, (LANES, slots), 1)
        spread = (
            (target >= source * CAP) & (target < source * CAP + CAP) & (source < NE)
        ).astype(jnp.bfloat16)
        ones = jnp.ones((rows, LANES), jnp.bfloat16)
        for n in range(count):
            gate = jnp.zeros((rows, LANES), jnp.float32)
            named = jnp.zeros((rows, LANES), jnp.float32)
            for k in range(2):
                hit = routes_ref[n, :, k : k + 1] == expert
                named = named + jnp.where(hit, 1.0, 0.0)
                gate = gate + jnp.where(hit, gates_ref[n, :, k : k + 1], 0.0)
            rank = dot32(before, named.astype(jnp.bfloat16)) + expert.astype(jnp.float32) * CAP
            rank = jnp.where(expert < NE, rank, 0.0)
            goal = exact_dot(split(rank, 2), spread, (((1,), (0,)), ((), ())))
            member = dot32(named.astype(jnp.bfloat16), spread)
            pick = jnp.where(goal == slot.astype(jnp.float32), member, 0.0)
            weight = pick * exact_dot(split(gate, 3), spread, (((1,), (0,)), ((), ())))
            picks_ref[n] = pick.astype(jnp.bfloat16)
            weights_ref[n] = weight
            slot_ref[n] = exact_dot(split(weight, 3), ones, FIRST)
            other_ref[n] = gate

    return alone(
        body,
        (
            make((count, rows, slots), jnp.bfloat16),
            make((count, rows, slots)),
            make((count, slots, LANES)),
            make((count, rows, LANES)),
        ),
        3,
        routes,
        gates,
    )


def gate_slots(slot_gates, picks, grads):
    picked = dot32(picks, grads[0], FIRST)
    for part in grads[1:]:
        picked = picked + dot32(picks, part, FIRST)
    lanes = [
        (picked[:, at : at + LANES] * slot_gates).astype(jnp.bfloat16)
        for at in range(0, picked.shape[1], LANES)
    ]
    return jnp.concatenate(lanes, axis=1)


def const_alphas(hn, smalls, base):
    logits = dot32(hn, smalls[base + 2 : base + 6].astype(jnp.bfloat16), LAST)
    alphas = []
    for c in range(2):
        first, second = logits[:, 2 * c : 2 * c + 1], logits[:, 2 * c + 1 : 2 * c + 2]
        top = jnp.maximum(first, second)
        first, second = jnp.exp(first - top), jnp.exp(second - top)
        total = first + second
        alphas.append((first / total, second / total))
    return alphas


def middle(attn, x, pack, smalls, base, picks, slot_gates, grads):
    planes, rows, part = attn.shape
    width = x.shape[1]
    slots = picks.shape[1]

    def body(attn_ref, x_ref, w_ref, small_ref, picks_ref, gates_ref, *refs):
        total = x_ref[...].astype(jnp.float32)
        for z in range(planes):
            total = total + dot32(attn_ref[z], w_ref[z * part : (z + 1) * part, :width])
        mid_ref, sent_ref = refs[-2:] if grads is None else refs[-3:-1]
        mid_ref[...] = total
        hn = (total * unit_scale(total) * small_ref[base + 1 : base + 2]).astype(jnp.bfloat16)
        sent_ref[...] = dot32(picks_ref[...], hn, FIRST).astype(jnp.bfloat16)
        if grads is not None:
            refs[-1][...] = gate_slots(gates_ref[...], picks_ref[...], [refs[0][...]])

    outs = [make((rows, width)), make((slots, width), jnp.bfloat16)]
    more = []
    if grads is not None:
        outs.append(make((slots, width), jnp.bfloat16))
        more.append(grads)
    return alone(body, outs, 3, attn, x, pack, smalls, picks, slot_gates, *more)


def combine(back, weights, mid, other, smalls, base, following):
    rows, width = mid.shape

    def body(back_ref, weights_ref, mid_ref, other_ref, small_ref, x_ref, *refs):
        mid_value, gate = mid_ref[...], other_ref[...]
        hn = (mid_value * unit_scale(mid_value) * small_ref[base + 1 : base + 2]).astype(
            jnp.bfloat16
        )
        alphas = const_alphas(hn, small_ref, base)
        wide = hn.astype(jnp.float32)
        total = mid_value + exact_dot(
            split(weights_ref[...]), back_ref[...], (((1,), (0,)), ((), ()))
        )
        factor = gate[:, NE + 1 : NE + 2]
        for c in range(2):
            weight = gate[:, NE + 2 + c : NE + 3 + c]
            factor = factor + weight * alphas[c][0]
            total = total + (weight * alphas[c][1]) * small_ref[base + 6 + c : base + 7 + c]
        total = total + factor * wide
        x_ref[...] = total
        if following:
            refs[0][...] = (total * unit_scale(total) * small_ref[base + 8 : base + 9]).astype(
                jnp.bfloat16
            )

    outs = [make((rows, width))]
    if following:
        outs.append(make((rows, width), jnp.bfloat16))
    return alone(body, outs, 3, back, weights, mid, other, smalls)


def experts_back(dback, picks, upstream, mid, other, smalls, base):
    rows, width = mid.shape

    def body(dback_ref, picks_ref, up_ref, mid_ref, other_ref, small_ref, dmid_ref, dy_ref, row_ref):
        mid_value, gate = mid_ref[...], other_ref[...]
        g = up_ref[...].astype(jnp.float32)
        scale = unit_scale(mid_value)
        unit = mid_value * scale
        gain = small_ref[base + 1 : base + 2]
        hn = (unit * gain).astype(jnp.bfloat16)
        alphas = const_alphas(hn, small_ref, base)
        wide = hn.astype(jnp.float32)
        dhn = dot32(picks_ref[...], dback_ref[...])
        g_hn = jnp.sum(g * wide, axis=1, keepdims=True)
        factor = gate[:, NE + 1 : NE + 2]
        row_ref[0:1] = jnp.zeros((1, width), jnp.float32)
        for c in range(2):
            weight = gate[:, NE + 2 + c : NE + 3 + c]
            vector = small_ref[base + 6 + c : base + 7 + c]
            first, second = alphas[c]
            factor = factor + weight * first
            row_ref[6 + c : 7 + c] = jnp.sum((weight * second) * g, axis=0, keepdims=True)
            da_first = weight * g_hn
            da_second = weight * jnp.sum(g * vector, axis=1, keepdims=True)
            mean = first * da_first + second * da_second
            for j, dlog in enumerate((first * (da_first - mean), second * (da_second - mean))):
                at = 2 + 2 * c + j
                dhn = dhn + dlog * small_ref[base + at : base + at + 1]
                row_ref[at : at + 1] = jnp.sum(dlog * wide, axis=0, keepdims=True)
        dhn = dhn + factor * g
        row_ref[1:2] = jnp.sum(dhn * unit, axis=0, keepdims=True)
        through = dhn * gain
        inner = jnp.mean(through * unit, axis=1, keepdims=True)
        dmid = g + scale * (through - unit * inner)
        dmid_ref[...] = dmid
        dy_ref[...] = dmid.astype(jnp.bfloat16)

    return alone(
        body,
        [make((rows, width)), make((rows, width), jnp.bfloat16), make((8, width))],
        4,
        dback,
        picks,
        upstream,
        mid,
        other,
        smalls,
    )


def finish(dxn, x, dmid, rows_in, smalls, base, picks, slot_gates):
    planes, rows, width = dxn.shape

    def body(dxn_ref, x_ref, dmid_ref, row_ref, small_ref, *refs):
        grad = dxn_ref[0].astype(jnp.float32)
        for z in range(1, planes):
            grad = grad + dxn_ref[z].astype(jnp.float32)
        value = x_ref[...].astype(jnp.float32)
        scale = unit_scale(value)
        unit = value * scale
        out_rows = refs[-1 if picks is None else -2]
        out_rows[...] = row_ref[...]
        out_rows[0:1] = jnp.sum(grad * unit, axis=0, keepdims=True)
        through = grad * small_ref[base : base + 1]
        inner = jnp.mean(through * unit, axis=1, keepdims=True)
        g = dmid_ref[...] + scale * (through - unit * inner)
        refs[-2 if picks is None else -3][...] = g
        if picks is not None:
            refs[-1][...] = gate_slots(refs[1][...], refs[0][...], split(g))

    outs = [make((rows, width)), make((8, width))]
    more = []
    if picks is not None:
        outs.append(make((picks.shape[1], width), jnp.bfloat16))
        more = [picks, slot_gates]
    return alone(body, outs, 3, dxn, x, dmid, rows_in, smalls, *more)


def sum_expert_grads(owns, gots):
    layers, kinds = len(owns), len(owns[0])
    hidden, features = owns[0][0].shape
    tile = min(hidden, 256)

    def body(*refs):
        outs = refs[2 * layers * kinds :]
        for n in range(kinds):
            for layer in range(layers):
                own, got = refs[2 * (layer * kinds + n) : 2 * (layer * kinds + n) + 2]
                outs[n][layer] = own[...].astype(jnp.float32) + got[...].astype(jnp.float32)

    piece = pl.BlockSpec((tile, features), lambda i: (i, 0))
    operands = [
        w for layer in range(layers) for pair in zip(owns[layer], gots[layer]) for w in pair
    ]
    return pl.pallas_call(
        body,
        out_shape=[make((layers, hidden, features))] * kinds,
        grid=(hidden // tile,),
        in_specs=[piece] * len(operands),
        out_specs=[pl.BlockSpec((layers, tile, features), lambda i: (0, i, 0))] * kinds,
        compiler_params=pltpu.CompilerParams(vmem_limit_bytes=VMEM_BYTES),
        cost_estimate=lasting(7),
    )(*operands)


def pack_grads(column, dq, dkv, attn, dy, small):
    width = column.shape[1]
    kv_cols, own_out = dkv.shape[1], attn.shape[1]
    tail = own_out + LANES // 2
    rows, cols = own_out // 2, width // 2

    def body(column_ref, dq_ref, dkv_ref, attn_ref, dy_ref, small_ref, one, two):
        one[:, :kv_cols] = dot32(column_ref[...], dkv_ref[...], FIRST).astype(jnp.bfloat16)
        source = lax.broadcasted_iota(jnp.int32, (kv_cols, tail), 0)
        target = lax.broadcasted_iota(jnp.int32, (kv_cols, tail), 1)
        dim = LANES // 2
        goal = lax.div(target, dim) * LANES + lax.rem(target, dim)
        compact = ((goal == source) & (target < own_out)).astype(jnp.bfloat16)
        narrow = dot32(dq_ref[...], compact).astype(jnp.bfloat16)
        placed = jnp.concatenate(
            [
                jnp.zeros((own_out, width), jnp.float32),
                small_ref[...],
                jnp.zeros((tail - own_out - 8, width), jnp.float32),
            ],
            axis=0,
        ).T
        one[:, kv_cols:] = (dot32(column_ref[...], narrow, FIRST) + placed).astype(jnp.bfloat16)
        out = dot32(attn_ref[...], dy_ref[...], FIRST).astype(jnp.bfloat16)
        for a in range(2):
            for b in range(2):
                two[a, b] = out[a * rows : (a + 1) * rows, b * cols : (b + 1) * cols]

    return alone(
        body,
        [make((width, kv_cols + tail), jnp.bfloat16), make((2, 2, rows, cols), jnp.bfloat16)],
        4,
        column,
        dq,
        dkv,
        attn,
        dy,
        small,
    )


def per_device(
    tokens,
    segments,
    routes,
    gates,
    w_qkv,
    w_out,
    gain_attn,
    gain_moe,
    const_gate,
    const_vec,
    w_gate,
    w_up,
    w_down,
    cotangent,
):
    blocks = lax.axis_size("blk")
    head_index, blk_index = lax.axis_index("head"), lax.axis_index("blk")
    span = blocks // COLUMNS
    plane, rest = lax.div(blk_index, span), lax.rem(blk_index, span)
    shards = 2 * blocks
    token_rows, width = tokens.shape
    shard_rows = width // shards
    head_dim = width // HEADS
    heads = HEADS // COLUMNS
    scale = head_dim ** (-0.5)
    half_length = blocks * token_rows
    positions = 2 * half_length
    own_out = heads * head_dim
    wide = heads * LANES

    swap = [(0, 1), (1, 0)]

    seg_own = lax.dynamic_index_in_dim(segments, head_index, 0, keepdims=True)
    seg_rows = jnp.concatenate([lax.rem(seg_own, 128), lax.div(seg_own, 128)], axis=0)
    seg_rows = jnp.pad(seg_rows, ((0, 14), (0, 0))).astype(jnp.bfloat16)
    seg_rows = jnp.broadcast_to(seg_rows[None], (COLUMNS,) + seg_rows.shape)
    smalls = [
        jnp.concatenate(
            [gain_attn[n][:, None], gain_moe[n][:, None], const_gate[n], const_vec[n]], axis=1
        )
        for n in range(LAYERS)
    ]
    smalls.append(jnp.zeros((shard_rows, LANES // 2 - 8 * LAYERS), jnp.bfloat16))
    smalls = jnp.concatenate(smalls, axis=1)
    packs = []
    for layer in range(LAYERS):
        parts = w_qkv[layer].reshape((shard_rows, 3, COLUMNS, heads, head_dim))
        kv_part = jnp.concatenate([parts[:, 1], parts[:, 2]], axis=3)
        kv_part = kv_part.transpose((1, 0, 2, 3)).reshape((COLUMNS, shard_rows, wide))
        query_part = parts[:, 0].transpose((1, 0, 2, 3)).reshape((COLUMNS, shard_rows, own_out))
        packs.append(
            jnp.concatenate(
                [
                    jnp.broadcast_to(w_out[layer][None], (COLUMNS, shard_rows, width)),
                    kv_part,
                    query_part,
                    jnp.broadcast_to(smalls[None], (COLUMNS,) + smalls.shape),
                ],
                axis=2,
            )
        )
    (seg_all, *packs), column_tokens = start_gather([seg_rows] + packs, tokens, blocks, 1)
    packs = [pack.reshape((width, -1)) for pack in packs]
    picks, pick_gates, slot_gates, other_gates = route_tables(routes, gates)

    def send_expert(weight, layer, after):
        away, _ = lax.optimization_barrier((weight[layer], after))
        return lax.ppermute(away, "head", swap)

    own_experts = (w_gate, w_up, w_down)

    experts = [[send_expert(w_gate, 0, tokens)]] + [None] * (LAYERS - 1)
    seg_all = seg_all[..., :2, :].astype(jnp.int32)
    seg_all = seg_all[..., 0, :] + 128 * seg_all[..., 1, :]
    seg_query = lax.dynamic_index_in_dim(seg_all, head_index, 0, keepdims=False)
    seg_query = lax.dynamic_index_in_dim(seg_query, rest, 1, keepdims=False)
    starts = jnp.sum(
        (seg_all.reshape((1, 1, -1)) < seg_query[:, :, None]).astype(jnp.int32), axis=2
    )
    bases = (
        head_index * half_length
        + (jnp.arange(COLUMNS, dtype=jnp.int32) * span + rest) * token_rows
    )
    bounds = block_bounds(starts, bases, token_rows)
    starts = starts[:, None, :]

    values = tokens
    column, small_rows = column_tokens, None
    kept = []
    for layer in range(LAYERS):
        base = 8 * layer
        last = layer + 1 == LAYERS
        column, queries, query_w, out_rows, kv_all, small_rows = project_gather(
            column, packs[layer], small_rows, heads, scale, blocks, 4 if layer == 0 else 2
        )
        kv_all = kv_all.reshape((positions, wide))
        if layer == 0:
            experts[layer] += [send_expert(w, layer, kv_all) for w in (w_up, w_down)]
        else:
            experts[layer].append(send_expert(w_down, layer, kv_all))
        attended, attn_col = attend(bounds, queries, kv_all, starts)
        (attn,) = column_exchange([attn_col], [False], blocks, 5, 9)
        mid, *sent = middle(
            attn,
            values,
            packs[layer],
            small_rows,
            base,
            picks[layer],
            slot_gates[layer],
            cotangent if last else None,
        )
        sent = [rows.reshape((NE, CAP, width)) for rows in sent]
        if last:
            back, dback, *wgrads = experts_exchange(
                sent, None, own_experts, experts[layer], layer, blocks, 7, True, True, 55
            )
            rows_in = None
        else:
            experts[layer + 1] = [send_expert(w, layer + 1, sent[0]) for w in (w_gate, w_up)]
            back, rows_in = experts_exchange(
                sent, None, own_experts, experts[layer], layer, blocks, 6, True, False, 28
            )
        kept.append(
            (values, column, queries, kv_all, attended, attn_col, query_w, out_rows, mid, rows_in)
        )
        values, *normed = combine(
            back.reshape((NE * CAP, width)),
            pick_gates[layer],
            mid,
            other_gates[layer],
            small_rows,
            base,
            not last,
        )
        if not last:
            (column,) = normed
    output = values

    upstream = cotangent
    shared_grads = [None] * LAYERS
    expert_grads = [None] * LAYERS
    for layer in reversed(range(LAYERS)):
        base = 8 * layer
        values, column, queries, kv_all, attended, attn_col, query_w, out_rows, mid, rows_in = (
            kept[layer]
        )
        if layer + 1 < LAYERS:
            dback, *wgrads = experts_exchange(
                [dz.reshape((NE, CAP, width))],
                rows_in,
                own_experts,
                experts[layer],
                layer,
                blocks,
                8,
                False,
                True,
                36,
                None,
                waiting,
            )
            expert_grads[layer + 1][1][1:] = wgrads[6:]
        before = layer > 0
        if before:
            got, waiting = [lax.ppermute(wgrads[3], "head", swap)], wgrads[4:6]
        else:
            got = [lax.ppermute(away, "head", swap) for away in wgrads[3:5]]
        dmid, dy, rows = experts_back(
            dback.reshape((NE * CAP, width)),
            picks[layer],
            upstream,
            mid,
            other_gates[layer],
            small_rows,
            base,
        )
        dy = column_gather(dy, blocks, 3)
        dy, got[0] = lax.optimization_barrier((dy, got[0]))
        dq, dkv_all = attend_back(
            bounds, queries, dy, out_rows, attended, kv_all, starts, scale
        )
        if not before:
            dkv_all, got[1] = lax.optimization_barrier((dkv_all, got[1]))
        dkv, dxn = reduce_project(
            dkv_all.reshape((2, COLUMNS, span, token_rows, wide)),
            dq,
            query_w,
            packs[layer],
            blocks,
            10,
        )
        upstream, rows, *dz = finish(
            dxn,
            values,
            dmid,
            rows,
            small_rows,
            base,
            picks[layer - 1] if before else None,
            slot_gates[layer - 1] if before else None,
        )
        if before:
            (dz,) = dz
        expert_grads[layer] = wgrads[:3], got
        qkv_part, out_part = pack_grads(
            column.reshape((-1, width)),
            dq.reshape((-1, wide)),
            dkv.reshape((-1, wide)),
            attn_col.reshape((-1, own_out)),
            dy.reshape((-1, width)),
            rows,
        )
        shared_grads[layer] = [
            qkv_part.reshape((2, COLUMNS, span, shard_rows, -1)),
            out_part.reshape((2, 2, span, shard_rows, width // 2)),
        ]

    packed = [part for layer in range(LAYERS) for part in shared_grads[layer]]
    reduced = plane_reduce(packed, blocks, 12, 20)
    away, _ = lax.optimization_barrier((wgrads[5], reduced[0]))
    expert_grads[0][1].append(lax.ppermute(away, "head", swap))
    exchanged = final_exchange(reduced[::2], reduced[1::2], blocks, 13)
    from_planes, out_grads = exchanged[:LAYERS], exchanged[LAYERS:]
    from_planes = jnp.stack(from_planes, axis=1).astype(jnp.float32)
    kv_out = from_planes[..., :wide].reshape((COLUMNS, LAYERS, shard_rows, heads, 2, head_dim))
    query_out = from_planes[..., wide : wide + own_out].reshape(
        (COLUMNS, LAYERS, shard_rows, heads, 1, head_dim)
    )
    qkv_out = jnp.concatenate([query_out, kv_out], axis=4)
    qkv_out = qkv_out.transpose((1, 2, 4, 0, 3, 5)).reshape((LAYERS, shard_rows, 3 * width))
    small_out = jnp.sum(from_planes[..., wide + own_out : wide + own_out + 8], axis=0)
    out_grads = jnp.stack(out_grads).astype(jnp.float32).transpose((0, 2, 1, 3))
    out_grads = out_grads.reshape((LAYERS, shard_rows, width))
    stacked = sum_expert_grads(*zip(*expert_grads))
    return (
        output,
        upstream,
        qkv_out,
        out_grads,
        small_out[..., 0],
        small_out[..., 1],
        small_out[..., 2:6],
        small_out[..., 6:8],
        stacked[0],
        stacked[1],
        stacked[2],
    )


def solution(mesh):
    tokens = P(("head", "blk"), None)
    by_layer = P(None, ("head", "blk"), None)
    gains = P(None, ("head", "blk"))
    experts = P(None, "blk", "head")
    return jax.shard_map(
        per_device,
        mesh=mesh,
        in_specs=(
            tokens,
            P(None, "blk"),
            by_layer,
            by_layer,
            by_layer,
            by_layer,
            gains,
            gains,
            by_layer,
            by_layer,
            experts,
            experts,
            experts,
            tokens,
        ),
        out_specs=(
            tokens,
            tokens,
            by_layer,
            by_layer,
            gains,
            gains,
            by_layer,
            by_layer,
            experts,
            experts,
            experts,
        ),
        check_vma=False,
    )
```

```python
import jax
import jax.numpy as jnp
from jax import lax
from jax.experimental import pallas as pl
from jax.experimental.pallas import tpu as pltpu
from jax.sharding import PartitionSpec as P

HEADS = 12
NE = 8
LAYERS = 2
CAP = 40
COLUMNS = 4
PIECES = 2
MESH = pl.DeviceIdType.MESH
ANY = pl.BlockSpec(memory_space=pl.ANY)
VMEM = pl.BlockSpec(memory_space=pltpu.VMEM)
HBM = pl.BlockSpec(memory_space=pltpu.HBM)
DMA = pltpu.SemaphoreType.DMA
VMEM_BYTES = 60 * 1024 * 1024
SPARE_BYTES = 4 * 1024 * 1024


def make(shape, kind=jnp.float32):
    return jax.ShapeDtypeStruct(tuple(shape), kind)


def greet(peers, line=()):
    barrier = pltpu.get_barrier_semaphore()
    count = len(peers)
    for peer in peers:
        pl.semaphore_signal(barrier, inc=1, device_id=peer, device_id_type=MESH)
    for there, peer in line:

        @pl.when(there)
        def _():
            pl.semaphore_signal(barrier, inc=1, device_id=peer, device_id_type=MESH)

        count = count + there.astype(jnp.int32)
    pl.semaphore_wait(barrier, count)


def remote(src, dst, send_sem, recv_sem, peer):
    return pltpu.make_async_remote_copy(
        src_ref=src,
        dst_ref=dst,
        send_sem=send_sem,
        recv_sem=recv_sem,
        device_id=peer,
        device_id_type=MESH,
    )


def room(things, spare=SPARE_BYTES):
    total = spare
    for thing in things:
        if hasattr(thing, "dtype") and hasattr(thing, "shape"):
            if not jnp.issubdtype(thing.dtype, jnp.number):
                continue
            size = jnp.dtype(thing.dtype).itemsize
            for extent in thing.shape:
                size *= extent
            total += size
    return min(total, VMEM_BYTES)


def comm_params(collective_id, things=(), spare=SPARE_BYTES):
    return pltpu.CompilerParams(
        collective_id=collective_id,
        has_side_effects=True,
        vmem_limit_bytes=room(things, spare),
    )


def lasting(microseconds):
    return pl.CostEstimate(
        flops=0, bytes_accessed=int(microseconds * 3_500_000), transcendentals=0
    )


def column_place(blocks):
    span = blocks // COLUMNS
    head, blk = lax.axis_index("head"), lax.axis_index("blk")
    plane, rest = lax.div(blk, span), lax.rem(blk, span)
    planes = [lax.rem(plane + d, COLUMNS) for d in range(COLUMNS)]
    return plane, planes, [(head, p * span + rest) for p in planes]


class Chain:
    def __init__(self, source, dst, send_sems, recv_sems, blocks):
        span = blocks // COLUMNS
        head, blk = lax.axis_index("head"), lax.axis_index("blk")
        plane, rest = lax.div(blk, span), lax.rem(blk, span)
        self.source, self.dst, self.plane = source, dst, plane
        self.send_sems, self.recv_sems = send_sems, recv_sems
        after = jnp.minimum(plane + 1, COLUMNS - 1)
        before = jnp.maximum(plane - 1, 0)
        self.line = [
            (plane < COLUMNS - 1, (head, after * span + rest)),
            (plane > 0, (head, before * span + rest)),
        ]
        lower = plane < COLUMNS // 2
        self.slabs = [
            plane,
            plane + 1 - 2 * lax.rem(plane, 2),
            jnp.where(lower, 2, 1),
            jnp.where(lower, 3, 0),
        ]

    def copy(self, k, way, piece):
        slab = self.slabs[k]
        rows = self.dst.shape[1] // PIECES
        part = pl.ds(piece * rows, rows)
        place = self.dst.at[slab, part]
        return remote(
            self.source.at[part] if k == 0 else place,
            place,
            self.send_sems.at[k, way, piece],
            self.recv_sems.at[slab, piece],
            self.line[way][1],
        )

    def onward(self, k):
        if k == 0:
            return [self.line[0][0], self.line[1][0]]
        from_before = self.slabs[k] < self.plane
        return [
            from_before & self.line[0][0],
            jnp.logical_not(from_before) & self.line[1][0],
        ]

    def pass_on(self, k, pieces=range(PIECES)):
        for piece in pieces:
            for way, there in enumerate(self.onward(k)):

                @pl.when(there)
                def _():
                    self.copy(k, way, piece).start()

    def arrive(self, k):
        for piece in range(PIECES):
            self.copy(k, 0, piece).wait_recv()
            self.pass_on(k, [piece])

    def finish(self):
        for k in range(COLUMNS):
            for piece in range(PIECES):
                for way, there in enumerate(self.onward(k)):

                    @pl.when(there)
                    def _():
                        self.copy(k, way, piece).wait_send()


def column_start(src, gather, dst, own_sem, send_sems, recv_sems, where):
    plane, planes, peers = where
    own = pltpu.make_async_copy(src if gather else src.at[plane], dst.at[plane], own_sem)
    own.start()
    copies = [own]
    for d in (2, 1, 3):
        copy = remote(
            src if gather else src.at[planes[d]],
            dst.at[plane],
            send_sems.at[d],
            recv_sems.at[d],
            peers[d],
        )
        copy.start()
        copies.append(copy)
    return copies


def column_exchange(arrays, gathers, blocks, collective_id, cost=16):
    count = len(arrays)
    slabs = [
        tuple(values.shape if gather else values.shape[1:])
        for values, gather in zip(arrays, gathers)
    ]

    def body(*refs):
        srcs, dsts = refs[:count], refs[count : 2 * count]
        own_sems, send_sems, recv_sems = refs[2 * count :]
        where = column_place(blocks)
        greet(where[2][1:])
        copies = []
        for n in range(count):
            copies += column_start(
                srcs[n],
                gathers[n],
                dsts[n],
                own_sems.at[n],
                send_sems.at[n],
                recv_sems.at[n],
                where,
            )
        for copy in copies:
            copy.wait()

    return pl.pallas_call(
        body,
        out_shape=[
            jax.ShapeDtypeStruct((COLUMNS,) + slab, values.dtype)
            for values, slab in zip(arrays, slabs)
        ],
        in_specs=[ANY] * count,
        out_specs=[ANY] * count,
        scratch_shapes=[DMA((count,)), DMA((count, COLUMNS)), DMA((count, COLUMNS))],
        compiler_params=comm_params(collective_id),
        cost_estimate=lasting(cost),
    )(*arrays)


def column_gather(values, blocks, collective_id, cost=14):
    def body(src, dst, own_sem, send_sems, recv_sems):
        chain = Chain(src, dst, send_sems, recv_sems, blocks)
        greet([], chain.line)
        chain.pass_on(0)
        own = pltpu.make_async_copy(src, dst.at[chain.plane], own_sem)
        own.start()
        for k in range(1, COLUMNS):
            chain.arrive(k)
        own.wait()
        chain.finish()

    return pl.pallas_call(
        body,
        out_shape=jax.ShapeDtypeStruct((COLUMNS,) + tuple(values.shape), values.dtype),
        in_specs=[ANY],
        out_specs=ANY,
        scratch_shapes=[DMA, DMA((COLUMNS, 2, PIECES)), DMA((COLUMNS, PIECES))],
        compiler_params=comm_params(collective_id),
        cost_estimate=lasting(cost),
    )(values)


def final_exchange(shares, rows, blocks, collective_id, cost=9):
    span = blocks // COLUMNS
    count = len(shares)
    total = 2 * count

    def body(*refs):
        srcs, dsts = refs[:total], refs[total : 2 * total]
        own_sems, send_sems, recv_sems, row_send, row_recv = refs[2 * total :]
        where = column_place(blocks)
        head, blk = lax.axis_index("head"), lax.axis_index("blk")
        plane, rest = lax.div(blk, span), lax.rem(blk, span)
        flat = head * blocks + blk
        goal = (plane * 2 + head) * span + rest
        from_plane = lax.div(flat, span)
        origin = (lax.rem(from_plane, 2), lax.div(from_plane, 2) * span + lax.rem(flat, span))
        goal_place = (lax.div(goal, blocks), lax.rem(goal, blocks))
        away = goal != flat
        greet(where[2][1:], [(away, goal_place), (away, origin)])
        copies = []
        for n in range(count):
            copies += column_start(
                srcs[n],
                False,
                dsts[n],
                own_sems.at[n],
                send_sems.at[n],
                recv_sems.at[n],
                where,
            )

        def row_copy(n):
            return remote(
                srcs[n], dsts[n], row_send.at[n - count], row_recv.at[n - count], goal_place
            )

        def row_stay(n):
            return pltpu.make_async_copy(srcs[n], dsts[n], own_sems.at[n])

        for n in range(count, total):

            @pl.when(away)
            def _():
                row_copy(n).start()

            @pl.when(jnp.logical_not(away))
            def _():
                row_stay(n).start()

        for copy in copies:
            copy.wait()
        for n in range(count, total):

            @pl.when(away)
            def _():
                row_copy(n).wait()

            @pl.when(jnp.logical_not(away))
            def _():
                row_stay(n).wait()

    arrays = list(shares) + list(rows)
    return pl.pallas_call(
        body,
        out_shape=[make(values.shape, values.dtype) for values in arrays],
        in_specs=[ANY] * total,
        out_specs=[ANY] * total,
        scratch_shapes=[
            DMA((total,)),
            DMA((count, COLUMNS)),
            DMA((count, COLUMNS)),
            DMA((count,)),
            DMA((count,)),
        ],
        compiler_params=comm_params(collective_id),
        cost_estimate=lasting(cost),
    )(*arrays)


def plane_place(blocks):
    span = blocks // COLUMNS
    width = span // 2
    head, blk = lax.axis_index("head"), lax.axis_index("blk")
    plane, rest = lax.div(blk, span), lax.rem(blk, span)
    x, core = lax.div(rest, 2), lax.rem(rest, 2)
    first = plane * span
    right = [lax.rem(x + d, width) for d in range(width)]
    left = [lax.rem(x - d + width, width) for d in range(width)]
    x_peers = [(head, first + right[d] * 2 + core) for d in range(width)]
    y_peer = (1 - head, blk)
    core_peer = (head, first + x * 2 + 1 - core)
    return head, rest, core, left, x_peers, y_peer, core_peer


class PlaneRun:
    def __init__(self, srcs, dsts, own_sems, send_sems, recv_sems, pass_sems, land_sems, where):
        self.srcs, self.dsts = srcs, dsts
        self.own_sems, self.send_sems, self.recv_sems = own_sems, send_sems, recv_sems
        self.pass_sems, self.land_sems = pass_sems, land_sems
        self.head, self.rest, self.core, self.left, self.x_peers, self.y_peer, self.core_peer = (
            where
        )
        self.width = len(self.x_peers)
        self.sends, self.passes, self.owns = [], [], []

    def place(self, n, h, dy, d):
        half = self.srcs[n].shape[0] // 2
        row = self.head if dy == 0 else 1 - self.head
        return self.dsts[n].at[row, pl.ds(h * half, half), self.left[d] * 2 + self.core]

    def held(self, n, h, dy, d):
        half = self.srcs[n].shape[0] // 2
        if dy == 0 and d == 0:
            return self.srcs[n].at[pl.ds(h * half, half)]
        return self.place(n, h, dy, d)

    def send(self, n, h, dy, d, peer, to_dy, to_d):
        copy = remote(
            self.held(n, h, dy, d),
            self.place(n, h, dy, d),
            self.send_sems.at[len(self.sends)],
            self.recv_sems.at[n, h, to_dy, to_d],
            peer,
        )
        copy.start()
        self.sends.append(copy)

    def hand_over(self, n, h, dy, d):
        copy = remote(
            self.held(n, h, dy, d),
            self.place(n, h, dy, d),
            self.pass_sems.at[n, h, dy, d],
            self.land_sems.at[n, h, dy, d],
            self.core_peer,
        )
        copy.start()
        self.passes.append(copy)

    def arrived(self, n, h, dy, d):
        at = self.place(n, h, dy, d)
        remote(
            at, at, self.send_sems.at[0], self.recv_sems.at[n, h, dy, d], self.y_peer
        ).wait_recv()

    def first(self, n):
        own = pltpu.make_async_copy(
            self.srcs[n], self.dsts[n].at[self.head, :, self.rest], self.own_sems.at[n]
        )
        own.start()
        self.owns.append(own)
        for d in range(1, self.width):
            self.send(n, 0, 0, 0, self.x_peers[d], 0, d)
        self.send(n, 1, 0, 0, self.y_peer, 1, 0)
        self.send(n, 0, 0, 0, self.y_peer, 1, 0)
        for d in range(1, self.width):
            self.send(n, 1, 0, 0, self.x_peers[d], 0, d)
        self.hand_over(n, 0, 0, 0)
        self.hand_over(n, 1, 0, 0)

    def second(self, n):
        for d in range(1, self.width):
            self.arrived(n, 0, 0, d)
            self.send(n, 0, 0, d, self.y_peer, 1, d)
            self.hand_over(n, 0, 0, d)
        self.arrived(n, 1, 1, 0)
        for d in range(1, self.width):
            self.send(n, 1, 1, 0, self.x_peers[d], 1, d)
        self.hand_over(n, 1, 1, 0)

    def third(self, n):
        self.arrived(n, 0, 1, 0)
        self.hand_over(n, 0, 1, 0)
        for d in range(1, self.width):
            self.arrived(n, 1, 0, d)
            self.hand_over(n, 1, 0, d)
        for d in range(1, self.width):
            self.arrived(n, 0, 1, d)
            self.hand_over(n, 0, 1, d)
            self.arrived(n, 1, 1, d)
            self.hand_over(n, 1, 1, d)

    def last(self):
        for own in self.owns:
            own.wait()
        for copy in self.passes:
            copy.wait()
        for copy in self.sends:
            copy.wait_send()


def plane_scratch(count, blocks):
    width = blocks // COLUMNS // 2
    links = 4 * (width - 1) + 2
    return [DMA((count,)), DMA((count * links,))] + [DMA((count, 2, 2, width))] * 3


def plane_shapes(arrays, blocks):
    return [
        jax.ShapeDtypeStruct(
            (2, values.shape[0], blocks // COLUMNS) + tuple(values.shape[1:]), values.dtype
        )
        for values in arrays
    ]


def start_gather(packs, tokens, blocks, collective_id, cost=28):
    count = len(packs)

    def body(*refs):
        srcs, refs = refs[: count + 1], refs[count + 1 :]
        wholes, refs = refs[:count], refs[count:]
        columns, refs = refs[: count + 1], refs[count + 1 :]
        own_sems, send_sems, recv_sems, chain_send, chain_recv, *plane_sems = refs
        column, plane = column_place(blocks), plane_place(blocks)
        greet(column[2][1:] + plane[4][1:] + [plane[5], plane[6]])
        run = PlaneRun(columns[:count], wholes, *plane_sems, plane)
        chain = Chain(srcs[count], columns[count], chain_send, chain_recv, blocks)
        stay = pltpu.make_async_copy(
            srcs[count], columns[count].at[chain.plane], own_sems.at[count]
        )

        def begin(n):
            return column_start(
                srcs[n],
                False,
                columns[n],
                own_sems.at[n],
                send_sems.at[n],
                recv_sems.at[n],
                column,
            )

        waits = [begin(0), begin(1)]
        for n in range(count):
            for copy in waits[n]:
                copy.wait()
            if n + 2 < count:
                waits.append(begin(n + 2))
            elif n + 2 == count:
                chain.pass_on(0)
                stay.start()
            run.first(n)
        run.second(0)
        run.second(1)
        chain.arrive(1)
        for n in range(2, count):
            run.second(n)
        run.third(0)
        run.third(1)
        chain.arrive(2)
        for n in range(2, count):
            run.third(n)
        chain.arrive(3)
        run.last()
        stay.wait()
        chain.finish()

    results = pl.pallas_call(
        body,
        out_shape=plane_shapes(packs, blocks)
        + [jax.ShapeDtypeStruct(pack.shape, pack.dtype) for pack in packs]
        + [jax.ShapeDtypeStruct((COLUMNS,) + tokens.shape, tokens.dtype)],
        in_specs=[ANY] * (count + 1),
        out_specs=[ANY] * (2 * count + 1),
        scratch_shapes=[
            DMA((count + 1,)),
            DMA((count, COLUMNS)),
            DMA((count, COLUMNS)),
            DMA((COLUMNS, 2, PIECES)),
            DMA((COLUMNS, PIECES)),
        ]
        + plane_scratch(count, blocks),
        compiler_params=comm_params(collective_id),
        cost_estimate=lasting(cost),
    )(*packs, tokens)
    return results[:count], results[-1]


def project_gather(source, pack, smalls, heads, scale, blocks, collective_id, cost=22):
    span = blocks // COLUMNS
    width = span // 2
    chained = smalls is not None
    rows, features = source.shape[-2:]
    wide = heads * LANES
    kv_at, tail_at = features, features + wide
    tail_cols = pack.shape[1] - tail_at
    own_out = tail_cols - LANES // 2
    dim = LANES // 2
    half = rows // 2
    small_rows = 8 * LAYERS
    links = 4 * (width - 1) + 2

    def body(*refs):
        if chained:
            source_ref, pack_ref, small_ref = refs[:3]
            refs = refs[3:]
            small_out = None
        else:
            source_ref, pack_ref = refs[:2]
            small_out, refs = refs[2], refs[3:]
        column_out, query_ref, query_w_out, out_w_out, kv_ref = refs[:5]
        column_ref, query_w_ref, out_w_ref, kv_own, own_sems, send_sems, recv_sems = refs[5:12]
        pass_sems, land_sems, z_send, z_recv, keep_sems = refs[12:]
        head, rest, core, left, x_peers, y_peer, core_peer = plane_place(blocks)
        plane = lax.div(lax.axis_index("blk"), span)
        sends, passes, owns = [], [], []
        near = x_peers[1:] + [y_peer, core_peer]
        if chained:
            chain = Chain(source_ref, column_ref, z_send, z_recv, blocks)
            slabs = chain.slabs
            greet(near, chain.line)
            chain.pass_on(0)
        else:
            slabs = list(range(COLUMNS))
            greet(near)

        tail = pack_ref[:, tail_at:]
        if not chained:
            small = tail[:, tail_cols - LANES :].astype(jnp.float32).T
            at = own_out - (tail_cols - LANES)
            small = small[at : at + small_rows]
            small_out[...] = small

        def place(k, h, dy, d):
            row = head if dy == 0 else 1 - head
            return kv_ref.at[row, slabs[k], left[d] * 2 + core, pl.ds(h * half, half)]

        def held(k, h, dy, d):
            if dy == 0 and d == 0:
                return kv_own.at[k, pl.ds(h * half, half)]
            return place(k, h, dy, d)

        def send(k, h, dy, d, peer, to_dy, to_d):
            copy = remote(
                held(k, h, dy, d),
                place(k, h, dy, d),
                send_sems.at[len(sends)],
                recv_sems.at[k, h, to_dy, to_d],
                peer,
            )
            copy.start()
            sends.append(copy)

        def hand_over(k, h, dy, d):
            copy = remote(
                held(k, h, dy, d),
                place(k, h, dy, d),
                pass_sems.at[k, h, dy, d],
                land_sems.at[k, h, dy, d],
                core_peer,
            )
            copy.start()
            passes.append(copy)

        def arrived(k, h, dy, d):
            at = place(k, h, dy, d)
            remote(at, at, send_sems.at[0], recv_sems.at[k, h, dy, d], y_peer).wait_recv()

        def first(k):
            slab = slabs[k]
            if not chained:
                x = source_ref[slab].astype(jnp.float32)
                xn = (x * unit_scale(x) * small[0:1]).astype(jnp.bfloat16)
                column_ref[slab] = xn
            elif k == 0:
                xn = source_ref[...]
                column_ref[slab] = xn
            else:
                chain.arrive(k)
                xn = column_ref[slab]
            kv = dot32(xn, pack_ref[:, kv_at:tail_at])
            kv_own[k] = kv.astype(jnp.bfloat16)
            own = pltpu.make_async_copy(
                kv_own.at[k], kv_ref.at[head, slab, rest], own_sems.at[k]
            )
            own.start()
            owns.append(own)
            for d in range(1, width):
                send(k, 0, 0, 0, x_peers[d], 0, d)
            send(k, 1, 0, 0, y_peer, 1, 0)
            send(k, 0, 0, 0, y_peer, 1, 0)
            for d in range(1, width):
                send(k, 1, 0, 0, x_peers[d], 0, d)
            hand_over(k, 0, 0, 0)
            hand_over(k, 1, 0, 0)

        def second(k):
            for d in range(1, width):
                arrived(k, 0, 0, d)
                send(k, 0, 0, d, y_peer, 1, d)
                hand_over(k, 0, 0, d)
            arrived(k, 1, 1, 0)
            for d in range(1, width):
                send(k, 1, 1, 0, x_peers[d], 1, d)
            hand_over(k, 1, 1, 0)

        def third(k):
            arrived(k, 0, 1, 0)
            hand_over(k, 0, 1, 0)
            for d in range(1, width):
                arrived(k, 1, 0, d)
                hand_over(k, 1, 0, d)
            for d in range(1, width):
                arrived(k, 0, 1, d)
                hand_over(k, 0, 1, d)
                arrived(k, 1, 1, d)
                hand_over(k, 1, 1, d)

        def queries():
            low = lax.broadcasted_iota(jnp.int32, (tail_cols, wide), 0)
            target = lax.broadcasted_iota(jnp.int32, (tail_cols, wide), 1)
            goal = lax.div(low, dim) * LANES + lax.rem(low, dim)
            to_low = ((goal == target) & (low < own_out)).astype(jnp.bfloat16)
            query_w = dot32(tail, to_low).astype(jnp.bfloat16)
            query_w_ref[...] = query_w
            out_rows = pack_ref[pl.ds(pl.multiple_of(plane * own_out, 64), own_out), :features]
            pieces = []
            for h in range(heads):
                pieces += [jnp.zeros((dim, features), jnp.bfloat16), out_rows[h * dim : (h + 1) * dim]]
            out_w_ref[...] = jnp.concatenate(pieces, axis=0)
            for k in range(COLUMNS):
                slab = slabs[k]
                query = dot32(column_ref[slab], query_w).astype(jnp.bfloat16)
                query = query.astype(jnp.float32) * scale
                query_ref[slab] = query.astype(jnp.bfloat16)
            for n, (src, dst) in enumerate(
                (
                    (column_ref, column_out),
                    (query_w_ref, query_w_out),
                    (out_w_ref, out_w_out),
                )
            ):
                copy = pltpu.make_async_copy(src, dst, keep_sems.at[n])
                copy.start()
                owns.append(copy)

        for t in range(COLUMNS + 2):
            if t < COLUMNS:
                first(t)
            elif t == COLUMNS:
                queries()
            if 0 <= t - 1 < COLUMNS:
                second(t - 1)
            if 0 <= t - 2 < COLUMNS:
                third(t - 2)
        for copy in owns + passes:
            copy.wait()
        for copy in sends:
            copy.wait_send()
        if chained:
            chain.finish()

    shapes = [
        pltpu.HBM((COLUMNS, rows, features), jnp.bfloat16),
        make((COLUMNS, rows, wide), jnp.bfloat16),
        pltpu.HBM((features, wide), jnp.bfloat16),
        pltpu.HBM((wide, features), jnp.bfloat16),
        make((2, COLUMNS, span, rows, wide), jnp.bfloat16),
    ]
    operands = [source, pack]
    if chained:
        operands.append(smalls)
    else:
        shapes = [jax.ShapeDtypeStruct((small_rows, features), jnp.float32)] + shapes
    results = pl.pallas_call(
        body,
        out_shape=shapes,
        in_specs=[VMEM] * len(operands),
        out_specs=([] if chained else [VMEM]) + [HBM, VMEM, HBM, HBM, ANY],
        scratch_shapes=[
            pltpu.VMEM((COLUMNS, rows, features), jnp.bfloat16),
            pltpu.VMEM((features, wide), jnp.bfloat16),
            pltpu.VMEM((wide, features), jnp.bfloat16),
            pltpu.VMEM((COLUMNS, rows, wide), jnp.bfloat16),
            DMA((COLUMNS,)),
            DMA((COLUMNS * links,)),
            DMA((COLUMNS, 2, 2, width)),
            DMA((COLUMNS, 2, 2, width)),
            DMA((COLUMNS, 2, 2, width)),
            DMA((COLUMNS, 2, PIECES)),
            DMA((COLUMNS, PIECES)),
            DMA((3,)),
        ],
        compiler_params=comm_params(
            collective_id,
            operands
            + [make(shape.shape, shape.dtype) for shape in shapes[:-1]]
            + [make((COLUMNS, rows, wide), jnp.bfloat16)],
            3 * SPARE_BYTES,
        ),
        cost_estimate=lasting(cost),
    )(*operands)
    return list(results) + [smalls] if chained else list(results[1:]) + [results[0]]


def plane_reduce(arrays, blocks, collective_id, cost=25):
    span = blocks // COLUMNS
    width = span // 2
    count = len(arrays)
    shapes = [(values.shape[1],) + tuple(values.shape[3:]) for values in arrays]

    def body(*refs):
        srcs, outs, refs = refs[:count], refs[count : 2 * count], refs[2 * count :]
        scratch = [refs[8 * n : 8 * n + 8] for n in range(count)]
        core_send, core_recv, link_send, link_recv = refs[8 * count :]
        head, blk = lax.axis_index("head"), lax.axis_index("blk")
        plane, rest = lax.div(blk, span), lax.rem(blk, span)
        x, core = lax.div(rest, 2), lax.rem(rest, 2)
        first = plane * span
        right = [lax.rem(x + d, width) for d in range(width)]
        x_peers = [(head, first + right[d] * 2 + core) for d in range(width)]
        y_peer = (1 - head, blk)
        core_peer = (head, first + x * 2 + 1 - core)
        greet(x_peers[1:] + [y_peer, core_peer])

        def wide(ref, *at):
            return ref[at].astype(jnp.float32)

        starts = {}
        for n in range(count):
            half = shapes[n][0] // 2
            for h in range(2):
                copy = remote(
                    srcs[n].at[:, pl.ds(h * half, half), :, 1 - core],
                    scratch[n][0].at[:, pl.ds(h * half, half)],
                    core_send.at[n, h],
                    core_recv.at[n, h],
                    core_peer,
                )
                copy.start()
                starts[n, h] = copy

        sends, yas, ybs, xbs = {}, {}, {}, {}
        for n in range(count):
            src, half, kind = srcs[n], shapes[n][0] // 2, arrays[n].dtype
            core_in, summed, xa_in, _, _, yb_in, _, _ = scratch[n]

            def core_sum(h):
                def step(i, _):
                    yy = lax.div(i, half * width)
                    zz = lax.div(lax.rem(i, half * width), width) + h * half
                    xx = lax.rem(i, width)
                    total = wide(src, yy, zz, xx, core) + wide(core_in, yy, zz, xx)
                    summed[yy, zz, xx] = total.astype(kind)
                    return 0

                lax.fori_loop(0, 2 * half * width, step, 0)

            starts[n, 0].wait_recv()
            core_sum(0)
            for d in range(1, width):
                copy = remote(
                    summed.at[:, pl.ds(0, half), right[d]],
                    xa_in.at[d],
                    link_send.at[n, 0, d],
                    link_recv.at[n, 0, d],
                    x_peers[d],
                )
                copy.start()
                sends[n, d] = copy
            starts[n, 1].wait_recv()
            core_sum(1)
            ybs[n] = remote(
                summed.at[1 - head, pl.ds(half, half)],
                yb_in,
                link_send.at[n, 1, 0],
                link_recv.at[n, 1, 0],
                y_peer,
            )
            ybs[n].start()
        for n in range(count):
            half, kind = shapes[n][0] // 2, arrays[n].dtype
            _, summed, xa_in, ya_out, ya_in, yb_in, xb_out, xb_in = scratch[n]
            for d in range(1, width):
                sends[n, d].wait_recv()

            def a_step(zz, _):
                total = wide(summed, 1 - head, zz, x)
                for d in range(1, width):
                    total = total + wide(xa_in, d, 1 - head, zz)
                ya_out[zz] = total.astype(kind)
                return 0

            lax.fori_loop(0, half, a_step, 0)
            yas[n] = remote(
                ya_out, ya_in, link_send.at[n, 0, 0], link_recv.at[n, 0, 0], y_peer
            )
            yas[n].start()
            ybs[n].wait_recv()
            for d in range(1, width):

                def b_step(zz, _):
                    total = wide(summed, head, half + zz, right[d]) + wide(yb_in, zz, right[d])
                    xb_out[d, zz] = total.astype(kind)
                    return 0

                lax.fori_loop(0, half, b_step, 0)
                xbs[n, d] = remote(
                    xb_out.at[d],
                    xb_in.at[d],
                    link_send.at[n, 1, d],
                    link_recv.at[n, 1, d],
                    x_peers[d],
                )
                xbs[n, d].start()
        for n in range(count):
            out, half, kind = outs[n], shapes[n][0] // 2, arrays[n].dtype
            _, summed, xa_in, _, ya_in, yb_in, _, xb_in = scratch[n]
            yas[n].wait_recv()

            def a_last(zz, _):
                total = wide(summed, head, zz, x) + wide(ya_in, zz)
                for d in range(1, width):
                    total = total + wide(xa_in, d, head, zz)
                out[zz] = total.astype(kind)
                return 0

            lax.fori_loop(0, half, a_last, 0)
            for d in range(1, width):
                xbs[n, d].wait_recv()

            def b_last(zz, _):
                total = wide(summed, head, half + zz, x) + wide(yb_in, zz, x)
                for d in range(1, width):
                    total = total + wide(xb_in, d, zz)
                out[half + zz] = total.astype(kind)
                return 0

            lax.fori_loop(0, half, b_last, 0)
        for group in (starts, sends, yas, ybs, xbs):
            for copy in group.values():
                copy.wait_send()

    scratch = []
    for (slabs, *tile), values in zip(shapes, arrays):
        tile, half, kind = tuple(tile), slabs // 2, values.dtype
        scratch += [
            pltpu.VMEM((2, slabs, width) + tile, kind),
            pltpu.VMEM((2, slabs, width) + tile, kind),
            pltpu.VMEM((width, 2, half) + tile, kind),
            pltpu.VMEM((half,) + tile, kind),
            pltpu.VMEM((half,) + tile, kind),
            pltpu.VMEM((half, width) + tile, kind),
            pltpu.VMEM((width, half) + tile, kind),
            pltpu.VMEM((width, half) + tile, kind),
        ]
    return pl.pallas_call(
        body,
        out_shape=[
            jax.ShapeDtypeStruct(shape, values.dtype) for shape, values in zip(shapes, arrays)
        ],
        in_specs=[VMEM] * count,
        out_specs=[VMEM] * count,
        scratch_shapes=scratch
        + [DMA((count, 2)), DMA((count, 2)), DMA((count, 2, width)), DMA((count, 2, width))],
        compiler_params=comm_params(
            collective_id, scratch + 2 * [make(a.shape, a.dtype) for a in arrays]
        ),
        cost_estimate=lasting(cost),
    )(
        *[
            values.reshape((2, values.shape[1], width, 2) + tuple(values.shape[3:]))
            for values in arrays
        ]
    )


def reduce_project(dkv_all, dq, query_w, pack, blocks, collective_id, cost=26):
    span = blocks // COLUMNS
    width = span // 2
    rows, wide = dkv_all.shape[3:]
    half = rows // 2
    features = query_w.shape[0]
    kind = dkv_all.dtype

    def body(
        src,
        dq_ref,
        w_ref,
        pack_ref,
        dkv_ref,
        dxn_ref,
        core_in,
        summed,
        xa_in,
        ya_out,
        ya_in,
        yb_in,
        xb_out,
        xb_in,
        share,
        core_send,
        core_recv,
        link_send,
        link_recv,
        z_send,
        z_recv,
    ):
        head, _, core, _, x_peers, y_peer, core_peer = plane_place(blocks)
        plane, planes, z_peers = column_place(blocks)
        x = lax.div(lax.rem(lax.axis_index("blk"), span), 2)
        right = [lax.rem(x + d, width) for d in range(width)]
        greet(x_peers[1:] + [y_peer, core_peer] + z_peers[1:])
        order = (2, 1, 3, 0)
        copies = []

        def begin(copy):
            copy.start()
            copies.append(copy)
            return copy

        def wide_of(ref, *at):
            return ref[at].astype(jnp.float32)

        top, low = pl.ds(0, half), pl.ds(half, half)
        starts = []

        def cross(k):
            starts.append(
                begin(
                    remote(
                        src.at[:, planes[order[k]], :, 1 - core],
                        core_in.at[k],
                        core_send.at[k],
                        core_recv.at[k],
                        core_peer,
                    )
                )
            )

        cross(0)
        cross(1)
        xas, yas, ybs, xbs, z_copies = {}, {}, {}, {}, []

        def first(k):
            starts[k].wait_recv()
            if k + 2 < COLUMNS:
                cross(k + 2)

            def step(i, _):
                yy, xx = lax.div(i, width), lax.rem(i, width)
                total = wide_of(src, yy, planes[order[k]], xx, core) + wide_of(core_in, k, yy, xx)
                summed[k, yy, xx] = total.astype(kind)
                return 0

            lax.fori_loop(0, 2 * width, step, 0)
            for d in range(1, width):
                xas[k, d] = begin(
                    remote(
                        summed.at[k, :, right[d], top],
                        xa_in.at[k, d],
                        link_send.at[k, 0, d],
                        link_recv.at[k, 0, d],
                        x_peers[d],
                    )
                )
            ybs[k] = begin(
                remote(
                    summed.at[k, 1 - head, :, low],
                    yb_in.at[k],
                    link_send.at[k, 1, 0],
                    link_recv.at[k, 1, 0],
                    y_peer,
                )
            )

        def second(k):
            total = wide_of(summed, k, 1 - head, x, top)
            for d in range(1, width):
                xas[k, d].wait_recv()
                total = total + wide_of(xa_in, k, d, 1 - head)
            ya_out[k] = total.astype(kind)
            yas[k] = begin(
                remote(
                    ya_out.at[k],
                    ya_in.at[k],
                    link_send.at[k, 0, 0],
                    link_recv.at[k, 0, 0],
                    y_peer,
                )
            )
            ybs[k].wait_recv()
            for d in range(1, width):
                total = wide_of(summed, k, head, right[d], low) + wide_of(yb_in, k, right[d])
                xb_out[k, d] = total.astype(kind)
                xbs[k, d] = begin(
                    remote(
                        xb_out.at[k, d],
                        xb_in.at[k, d],
                        link_send.at[k, 1, d],
                        link_recv.at[k, 1, d],
                        x_peers[d],
                    )
                )

        def third(k):
            slab = planes[order[k]]
            yas[k].wait_recv()
            total = wide_of(summed, k, head, x, top) + wide_of(ya_in, k)
            for d in range(1, width):
                total = total + wide_of(xa_in, k, d, head)
            dkv_ref[slab, top] = total.astype(kind)
            total = wide_of(summed, k, head, x, low) + wide_of(yb_in, k, x)
            for d in range(1, width):
                xbs[k, d].wait_recv()
                total = total + wide_of(xb_in, k, d)
            dkv_ref[slab, low] = total.astype(kind)
            part = (
                dot32(dq_ref[slab], w_ref[...], LAST)
                + dot32(dkv_ref[slab], pack_ref[:, features : features + wide], LAST)
            ).astype(kind)
            if order[k] == 0:
                dxn_ref[plane] = part
            else:
                share[k] = part
                z_copies.append(
                    begin(
                        remote(
                            share.at[k],
                            dxn_ref.at[plane],
                            z_send.at[order[k]],
                            z_recv.at[order[k]],
                            z_peers[order[k]],
                        )
                    )
                )

        for t in range(COLUMNS + 2):
            if t < COLUMNS:
                first(t)
            if 0 <= t - 1 < COLUMNS:
                second(t - 1)
            if 0 <= t - 2 < COLUMNS:
                third(t - 2)
        for copy in z_copies:
            copy.wait_recv()
        for copy in copies:
            copy.wait_send()

    tile = (rows, wide)
    part = (half, wide)
    scratch = [
        pltpu.VMEM((COLUMNS, 2, width) + tile, kind),
        pltpu.VMEM((COLUMNS, 2, width) + tile, kind),
        pltpu.VMEM((COLUMNS, width, 2) + part, kind),
        pltpu.VMEM((COLUMNS,) + part, kind),
        pltpu.VMEM((COLUMNS,) + part, kind),
        pltpu.VMEM((COLUMNS, width) + part, kind),
        pltpu.VMEM((COLUMNS, width) + part, kind),
        pltpu.VMEM((COLUMNS, width) + part, kind),
        pltpu.VMEM((COLUMNS, rows, features), kind),
    ]
    shapes = [make((COLUMNS,) + tile, kind), make((COLUMNS, rows, features), kind)]
    return pl.pallas_call(
        body,
        out_shape=shapes,
        in_specs=[VMEM] * 4,
        out_specs=[VMEM] * 2,
        scratch_shapes=scratch
        + [
            DMA((COLUMNS,)),
            DMA((COLUMNS,)),
            DMA((COLUMNS, 2, width)),
            DMA((COLUMNS, 2, width)),
            DMA((COLUMNS,)),
            DMA((COLUMNS,)),
        ],
        compiler_params=comm_params(
            collective_id, scratch + shapes + [dkv_all, dq, query_w, pack], 7 * SPARE_BYTES
        ),
        cost_estimate=lasting(cost),
    )(dkv_all.reshape((2, COLUMNS, width, 2) + tile), dq, query_w, pack)


NEGATIVE = -1e30
EPSILON = 1e-06
KEYS = 1024
LANES = 128
LAST = (((1,), (1,)), ((), ()))
FIRST = (((0,), (0,)), ((), ()))


def dot32(a, b, dims=(((1,), (0,)), ((), ()))):
    return lax.dot_general(a, b, dims, preferred_element_type=jnp.float32)


def visible(key_base, query_base, keys, queries, starts):
    key_pos = key_base + lax.broadcasted_iota(jnp.int32, (keys, queries), 0)
    query_pos = query_base + lax.broadcasted_iota(jnp.int32, (keys, queries), 1)
    return (key_pos <= query_pos) & (key_pos >= starts)


def block_bounds(starts, bases, rows):
    return jnp.stack(
        [
            lax.div(starts[:, 0], KEYS),
            lax.div(bases + rows - 1, KEYS),
            bases,
            lax.div(starts[:, rows - 1], KEYS),
        ],
        axis=1,
    )


def over_chunks(bounds_ref, i, step, carry):
    low, high, edge = bounds_ref[i, 0], bounds_ref[i, 1], bounds_ref[i, 3]
    carry = step(high, True, carry)
    inner = jnp.maximum(high - 1 - edge, 0)
    carry = lax.fori_loop(0, inner, lambda t, c: step(high - 1 - t, False, c), carry)
    below = high - 1 - inner
    return lax.fori_loop(0, below - low + 1, lambda t, c: step(below - t, True, c), carry)


def attend(bounds, queries, kv_all, starts):
    count, rows, width = queries.shape
    heads = width // LANES

    def body(bounds_ref, q_ref, kv_ref, start_ref, out_ref, attn_ref):
        i = pl.program_id(0)
        base = bounds_ref[i, 2]
        start_row = start_ref[0]
        q = [q_ref[0, :, h * LANES : (h + 1) * LANES] for h in range(heads)]

        def step(chunk, masked, carry):
            at = pl.multiple_of(chunk * KEYS, KEYS)
            if masked:
                ok = visible(chunk * KEYS, base, KEYS, rows, start_row)
            kvs = [kv_ref[pl.ds(at, KEYS), h * LANES : (h + 1) * LANES] for h in range(heads)]
            scores = [dot32(kvs[h], q[h], LAST) for h in range(heads)]
            if masked:
                scores = [jnp.where(ok, s, NEGATIVE) for s in scores]
            tops = [
                jnp.maximum(carry[h][0], jnp.max(scores[h], axis=0, keepdims=True))
                for h in range(heads)
            ]
            weights = [jnp.exp(scores[h] - tops[h]) for h in range(heads)]
            shrinks = [jnp.exp(carry[h][0] - tops[h]) for h in range(heads)]
            totals = [
                carry[h][1] * shrinks[h] + jnp.sum(weights[h], axis=0, keepdims=True)
                for h in range(heads)
            ]
            accs = [
                carry[h][2] * shrinks[h] + dot32(kvs[h], weights[h].astype(jnp.bfloat16), FIRST)
                for h in range(heads)
            ]
            return tuple(zip(tops, totals, accs))

        empty = tuple(
            (
                jnp.full((1, rows), NEGATIVE, jnp.float32),
                jnp.zeros((1, rows), jnp.float32),
                jnp.zeros((LANES, rows), jnp.float32),
            )
            for h in range(heads)
        )
        done = over_chunks(bounds_ref, i, step, empty)
        lane = lax.broadcasted_iota(jnp.int32, (LANES, rows), 0)
        narrow = []
        for h in range(heads):
            top, total, acc = done[h]
            value = jnp.where(lane < LANES // 2, top + jnp.log(total), acc / total)
            out_ref[0, :, h * LANES : (h + 1) * LANES] = value.T
            narrow.append(value[LANES // 2 :])
        attn_ref[0] = jnp.concatenate(narrow, axis=0).T.astype(jnp.bfloat16)

    return pl.pallas_call(
        body,
        out_shape=(
            jax.ShapeDtypeStruct((count, rows, width), jnp.float32),
            jax.ShapeDtypeStruct((count, rows, width // 2), jnp.bfloat16),
        ),
        grid_spec=pltpu.PrefetchScalarGridSpec(
            num_scalar_prefetch=1,
            grid=(count,),
            in_specs=[
                pl.BlockSpec((1, rows, width), lambda i, b: (i, 0, 0)),
                pl.BlockSpec(kv_all.shape, lambda i, b: (0, 0)),
                pl.BlockSpec((1, 1, rows), lambda i, b: (i, 0, 0)),
            ],
            out_specs=(
                pl.BlockSpec((1, rows, width), lambda i, b: (i, 0, 0)),
                pl.BlockSpec((1, rows, width // 2), lambda i, b: (i, 0, 0)),
            ),
        ),
        compiler_params=pltpu.CompilerParams(
            vmem_limit_bytes=room([kv_all] * 2, 4 * SPARE_BYTES)
        ),
        cost_estimate=lasting(13),
    )(bounds, queries, kv_all, starts)


def attend_back(bounds, queries, dy, out_rows, kept, kv_all, starts, scale):
    count, rows, width = queries.shape
    total_keys = kv_all.shape[0]
    heads = width // LANES
    if total_keys * width * 14 > VMEM_BYTES:
        heads = 1
    wide = heads * LANES

    def body(bounds_ref, q_ref, dy_ref, w_ref, kept_ref, kv_ref, start_ref, dq_ref, dkv_ref, acc_ref):
        i = pl.program_id(1)
        base = bounds_ref[i, 2]
        start_row = start_ref[0]

        @pl.when(i == 0)
        def _():
            def clear(c, _):
                acc_ref[pl.ds(pl.multiple_of(c * KEYS, KEYS), KEYS), :] = jnp.zeros(
                    (KEYS, wide), jnp.float32
                )
                return 0

            lax.fori_loop(0, total_keys // KEYS, clear, 0)

        q = [q_ref[0, :, h * LANES : (h + 1) * LANES] for h in range(heads)]
        grads = dot32(dy_ref[0], w_ref[...], LAST).astype(jnp.bfloat16)
        g = [grads[:, h * LANES : (h + 1) * LANES] for h in range(heads)]
        qg = [jnp.concatenate([q[h], g[h]], axis=0) for h in range(heads)]
        lse, delta = [], []
        for h in range(heads):
            kept_t = kept_ref[0, :, h * LANES : (h + 1) * LANES].T
            lse.append(kept_t[0:1])
            delta.append(jnp.sum(kept_t * g[h].astype(jnp.float32).T, axis=0, keepdims=True))

        def step(chunk, masked, carry):
            at = pl.multiple_of(chunk * KEYS, KEYS)
            if masked:
                ok = visible(chunk * KEYS, base, KEYS, rows, start_row)
            lanes = [slice(h * LANES, (h + 1) * LANES) for h in range(heads)]
            kvs = [kv_ref[pl.ds(at, KEYS), lanes[h]] for h in range(heads)]
            pairs = [dot32(kvs[h], qg[h], LAST) for h in range(heads)]
            scores = [p[:, :rows] for p in pairs]
            dprobs = [p[:, rows:] for p in pairs]
            if masked:
                scores = [jnp.where(ok, s, NEGATIVE) for s in scores]
            probs = [jnp.exp(scores[h] - lse[h]) for h in range(heads)]
            dscores = [
                (probs[h] * (dprobs[h] - delta[h])).astype(jnp.bfloat16) for h in range(heads)
            ]
            both = [
                jnp.concatenate([dscores[h], probs[h].astype(jnp.bfloat16)], axis=1)
                for h in range(heads)
            ]
            for h in range(heads):
                acc_ref[pl.ds(at, KEYS), lanes[h]] += dot32(both[h], qg[h])
            return tuple(carry[h] + dot32(kvs[h], dscores[h], FIRST) for h in range(heads))

        done = over_chunks(
            bounds_ref,
            i,
            step,
            tuple(jnp.zeros((LANES, rows), jnp.float32) for h in range(heads)),
        )
        lane = lax.broadcasted_iota(jnp.int32, (LANES, rows), 0)
        for h in range(heads):
            value = jnp.where(lane < LANES // 2, done[h] * scale, 0.0)
            dq_ref[0, :, h * LANES : (h + 1) * LANES] = value.T.astype(jnp.bfloat16)

        @pl.when(i == count - 1)
        def _():
            def store(c, _):
                at = pl.ds(pl.multiple_of(c * KEYS, KEYS), KEYS)
                dkv_ref[at, :] = acc_ref[at, :].astype(jnp.bfloat16)
                return 0

            lax.fori_loop(0, total_keys // KEYS, store, 0)

    block = pl.BlockSpec((1, rows, wide), lambda h, i, b: (i, 0, h))
    whole = pl.BlockSpec((total_keys, wide), lambda h, i, b: (0, h))
    return pl.pallas_call(
        body,
        out_shape=(
            jax.ShapeDtypeStruct((count, rows, width), jnp.bfloat16),
            jax.ShapeDtypeStruct(kv_all.shape, jnp.bfloat16),
        ),
        grid_spec=pltpu.PrefetchScalarGridSpec(
            num_scalar_prefetch=1,
            grid=(width // wide, count),
            in_specs=[
                block,
                pl.BlockSpec((1,) + tuple(dy.shape[1:]), lambda h, i, b: (i, 0, 0)),
                pl.BlockSpec((wide, out_rows.shape[1]), lambda h, i, b: (h, 0)),
                block,
                whole,
                pl.BlockSpec((1, 1, rows), lambda h, i, b: (i, 0, 0)),
            ],
            out_specs=(block, whole),
            scratch_shapes=[pltpu.VMEM((total_keys, wide), jnp.float32)],
        ),
        compiler_params=pltpu.CompilerParams(
            vmem_limit_bytes=room([make((total_keys, wide), jnp.bfloat16)] * 6, 5 * SPARE_BYTES)
        ),
        cost_estimate=lasting(20),
    )(bounds, queries, dy, out_rows, kept, kv_all, starts)


def experts_exchange(
    sent,
    saved,
    own,
    other,
    layer,
    blocks,
    collective_id,
    forward,
    backward,
    cost,
    ahead=None,
    cross=(),
):
    fetch = other[2] is None
    other = [w for w in other if w is not None]
    copies = blocks // NE
    half = NE // 2
    slots, width = sent[0].shape[1:]
    hidden, features = other[0].shape
    tile = min(hidden, 256)
    tiles = hidden // tile
    count = len(sent)
    homes_count = int(forward) + int(backward)
    total_rows = copies * NE * slots
    kind = sent[0].dtype
    sizes = (half // 2, half // 2, half)
    first_rows = [copies * slots * at for at in (0, half // 2, half)]
    most_rows = copies * slots * half
    plain = (((1,), (0,)), ((), ()))

    def body(*refs):
        refs = list(refs)

        def take(n):
            taken = refs[:n]
            del refs[:n]
            return taken

        srcs = take(count)
        saved_ref = take(1)[0] if not forward else None
        weight_refs = take(3 + len(other))
        ahead_ref = take(1)[0] if ahead is not None else None
        cross_refs = take(len(cross))
        homes = take(homes_count)
        arrived_ref = take(1)[0] if not backward else None
        fetched_ref = take(1)[0] if fetch and not backward else None
        next_ref = take(1)[0] if ahead is not None else None
        keeps, aways = (take(3), take(3)) if backward else ([], [])
        crossed = take(len(cross))
        lands = take(count)
        weights = take(6)
        parts, sib_ins, totals = take(homes_count), take(homes_count), take(homes_count)
        accs = take(homes_count)
        rows_x = take(1)[0]
        if backward:
            rows_z, act_ref, dgate_ref, dup_ref, keep_ref, away_ref = take(6)
            if not forward:
                gate_ref, up_ref = take(2)
            out_sems = take(1)[0]
        load_sems, own_sems, send_sems, recv_sems, pass_sems, land_sems = take(6)
        home_own, home_send, home_recv, part_send, part_recv, arrived_sem = take(6)
        swap_send, swap_recv = take(2)

        head, blk = lax.axis_index("head"), lax.axis_index("blk")
        expert, piece = lax.div(blk, copies), lax.rem(blk, copies)
        near = lax.div(expert, half) * half
        far = half - near
        places = [lax.rem(piece + k, copies) for k in range(copies)]
        siblings = [(head, expert * copies + places[k]) for k in range(copies)]
        others = [lax.rem(expert + d, NE) for d in range(NE)]
        swaps = [(1 - head, blk)] if fetch or ahead is not None or cross else []
        greet([(head, e * copies + piece) for e in others[1:]] + siblings[1:] + swaps)
        mine = pl.ds(pl.multiple_of(head * features, LANES), features)
        rest = pl.ds(pl.multiple_of((1 - head) * features, LANES), features)
        steps = [(far, sizes[0]), (far + sizes[0], sizes[1]), (near, sizes[2])]

        def sending(n, e):
            return remote(
                srcs[n].at[e],
                lands[n].at[piece, expert],
                send_sems.at[n, e],
                recv_sems.at[n, expert],
                (head, e * copies + piece),
            )

        owns = []
        for n in range(count):
            copy = pltpu.make_async_copy(
                srcs[n].at[expert], lands[n].at[piece, expert], own_sems.at[n]
            )
            copy.start()
            owns.append(copy)
        def each(t, copy_of, arrays, act):
            first, size = steps[t]
            for j in range(size):
                for n in range(arrays):
                    if t < 2:
                        act(copy_of(n, first + j))
                    else:

                        @pl.when(first + j != expert)
                        def _():
                            act(copy_of(n, first + j))

        def send(t):
            each(t, sending, count, lambda copy: copy.start())

        def sent_out(t):
            each(t, sending, count, lambda copy: copy.wait_send())

        for t in range(3):
            send(t)
        crossing = []
        if fetch:
            crossing.append(
                remote(
                    weight_refs[4].at[layer],
                    weights[5],
                    swap_send.at[0],
                    swap_recv.at[0],
                    swaps[0],
                )
            )
        if ahead is not None:
            crossing.append(
                remote(
                    ahead_ref.at[layer + 1],
                    next_ref,
                    swap_send.at[1],
                    swap_recv.at[1],
                    swaps[0],
                )
            )
        for n in range(len(cross)):
            crossing.append(
                remote(
                    cross_refs[n],
                    crossed[n],
                    swap_send.at[2 + n],
                    swap_recv.at[2 + n],
                    swaps[0],
                )
            )
        for n, copy in enumerate(crossing):
            if ahead is None or n == 0:
                copy.start()
        loads = []
        for n in range(3 + len(other)):
            weight = weight_refs[n] if n % 2 else weight_refs[n].at[layer]
            copy = pltpu.make_async_copy(weight, weights[n], load_sems.at[n])
            copy.start()
            loads.append(copy)
        go, gx, uo, ux, do, dx = weights
        passes, exchanges = [], {}

        def arrive(t):
            first, size = steps[t]
            waits = []
            if t == 2:
                for copy in owns:
                    copy.wait()
            for j in range(size):
                e = first + j
                for n in range(count):
                    place = lands[n].at[piece, e]

                    @pl.when(e != expert)
                    def _():
                        remote(
                            place, place, send_sems.at[n, e], recv_sems.at[n, e], siblings[0]
                        ).wait_recv()

                    for k in range(1, copies):
                        copy = remote(
                            place,
                            place,
                            pass_sems.at[n, k, e],
                            land_sems.at[n, k, e],
                            siblings[k],
                        )
                        copy.start()
                        waits.append(copy)
            for copy in waits:
                copy.wait_recv()
            passes.extend(waits)

        def flat(ref, t):
            first, size = steps[t]
            value = ref[:, pl.ds(first, size)].astype(jnp.float32)
            return value.reshape((copies * size * slots, width)).astype(kind)

        def span_of(t):
            return slice(first_rows[t], first_rows[t] + copies * steps[t][1] * slots)

        def gate_up(t, j):
            at = pl.ds(pl.multiple_of(j * tile, tile), tile)
            xo, xx = rows_x[span_of(t), mine], rows_x[span_of(t), rest]
            gate = dot32(xo, go[at], LAST) + dot32(xx, gx[at], LAST)
            return gate, dot32(xo, uo[at], LAST) + dot32(xx, ux[at], LAST)

        def early(t):
            rows_x[span_of(t)] = flat(saved_ref, t)
            size = copies * steps[t][1] * slots

            def step(j, _):
                at = pl.ds(pl.multiple_of(j * tile, tile), tile)
                gate_ref[:size, at], up_ref[:size, at] = gate_up(t, j)
                return 0

            lax.fori_loop(0, tiles, step, 0)

        def work(t):
            size = copies * steps[t][1] * slots
            span = span_of(t)
            if forward:
                rows_x[span] = flat(lands[0], t)
            if backward:
                rows_z[span] = flat(lands[-1], t)
            for acc in accs:
                acc[:size] = jnp.zeros((size, width), jnp.float32)

            def step(j, _):
                at = pl.ds(pl.multiple_of(j * tile, tile), tile)
                if forward:
                    gate, up = gate_up(t, j)
                else:
                    gate, up = gate_ref[:size, at], up_ref[:size, at]
                sigmoid = jax.nn.sigmoid(gate)
                silu = gate * sigmoid
                act = (silu * up).astype(kind)
                if forward:
                    accs[0][:size, mine] += dot32(act, do[at])
                    accs[0][:size, rest] += dot32(act, dx[at])
                if backward:
                    zo, zx = rows_z[span, mine], rows_z[span, rest]
                    dact = dot32(zo, do[at], LAST) + dot32(zx, dx[at], LAST)
                    dgate = (dact * up * sigmoid * (1.0 + gate * (1.0 - sigmoid))).astype(kind)
                    dup = (dact * silu).astype(kind)
                    act_ref[span, at] = act
                    dgate_ref[span, at] = dgate
                    dup_ref[span, at] = dup
                    accs[-1][:size, mine] += dot32(dgate, go[at]) + dot32(dup, uo[at])
                    accs[-1][:size, rest] += dot32(dgate, gx[at]) + dot32(dup, ux[at])
                return 0

            lax.fori_loop(0, tiles, step, 0)
            first, size_e = steps[t]
            for n in range(homes_count):
                value = accs[n][:size].reshape((copies, size_e, slots, width))
                parts[n][:, pl.ds(first, size_e)] = value.astype(kind)
                for j in range(size_e):
                    for k in range(1, copies):
                        copy = remote(
                            parts[n].at[places[k], first + j],
                            sib_ins[n].at[k - 1, first + j],
                            part_send.at[n, k, first + j],
                            part_recv.at[n, k, first + j],
                            siblings[k],
                        )
                        copy.start()
                        exchanges[n, t, j, k] = copy

        def homeward(n, e):
            return remote(
                totals[n].at[e],
                homes[n].at[expert],
                home_send.at[n, e],
                home_recv.at[n, expert],
                (head, e * copies + piece),
            )

        def give_back(t):
            first, size = steps[t]
            for j in range(size):
                e = first + j
                for n in range(homes_count):
                    value = parts[n][piece, e].astype(jnp.float32)
                    for k in range(1, copies):
                        exchanges[n, t, j, k].wait_recv()
                        value = value + sib_ins[n][k - 1, e].astype(jnp.float32)
                    totals[n][e] = value.astype(kind)
                    if t < 2:
                        homeward(n, e).start()
                    else:

                        @pl.when(e != expert)
                        def _():
                            homeward(n, e).start()

        for copy in loads:
            copy.wait()
        if not forward:
            early(0)
        for t in range(len(steps)):
            arrive(t)
            if t == 0 and fetch:
                crossing[0].wait_recv()
                if ahead is not None:
                    crossing[1].start()
            work(t)
            if t > 0:
                give_back(t - 1)
            if not forward and t + 1 < len(steps):
                early(t + 1)
        give_back(len(steps) - 1)
        stays = []
        for n in range(homes_count):
            copy = pltpu.make_async_copy(
                totals[n].at[expert], homes[n].at[expert], home_own.at[n]
            )
            copy.start()
            stays.append(copy)

        if backward:

            def saving(n, j, which):
                at = pl.ds(pl.multiple_of(j * tile, tile), tile)
                src, dst = ((keep_ref, keeps), (away_ref, aways))[which]
                return pltpu.make_async_copy(src.at[n, at], dst[n].at[at], out_sems.at[n, j, which])

            def grads(j, _):
                at = pl.ds(pl.multiple_of(j * tile, tile), tile)
                for n, (left, right) in enumerate(
                    ((dgate_ref, rows_x), (dup_ref, rows_x), (act_ref, rows_z))
                ):
                    value = left[:, at]
                    away_ref[n, at] = dot32(value, right[:, rest], FIRST).astype(kind)
                    saving(n, j, 1).start()
                    keep_ref[n, at] = dot32(value, right[:, mine], FIRST).astype(kind)
                    saving(n, j, 0).start()
                return 0

            lax.fori_loop(0, tiles, grads, 0)

        if not backward:
            copy = pltpu.make_async_copy(lands[0], arrived_ref, arrived_sem)
            copy.start()
            stays.append(copy)
            if fetch:
                copy = pltpu.make_async_copy(weights[5], fetched_ref, load_sems.at[5])
                copy.start()
                stays.append(copy)
        for n in range(homes_count):
            for e in others[1:]:
                place = homes[n].at[e]
                remote(
                    place, place, home_send.at[n, e], home_recv.at[n, e], siblings[0]
                ).wait_recv()
        for t in range(len(steps)):
            sent_out(t)
            each(t, homeward, homes_count, lambda copy: copy.wait_send())
        for copy in passes + list(exchanges.values()):
            copy.wait_send()
        for copy in stays:
            copy.wait()
        for copy in crossing[int(fetch) :]:
            copy.wait_recv()
        for copy in crossing:
            copy.wait_send()
        if backward:

            def settle(j, _):
                for n in range(3):
                    saving(n, j, 0).wait()
                    saving(n, j, 1).wait()
                return 0

            lax.fori_loop(0, tiles, settle, 0)

    slab = (copies, NE, slots, width)
    shapes = [make((NE, slots, width), kind)] * homes_count
    specs = [ANY] * homes_count
    if not backward:
        shapes.append(pltpu.HBM(slab, kind))
        specs.append(HBM)
        for _ in range(int(fetch) + int(ahead is not None)):
            shapes.append(pltpu.HBM((hidden, features), kind))
            specs.append(HBM)
    else:
        shapes += [pltpu.HBM((hidden, features), kind)] * (6 + len(cross))
        specs += [HBM] * (6 + len(cross))
    scratch = [pltpu.VMEM(slab, kind)] * count
    scratch += [pltpu.VMEM((hidden, features), kind)] * 6
    scratch += [pltpu.VMEM(slab, kind)] * homes_count
    scratch += [pltpu.VMEM((copies - 1,) + slab[1:], kind)] * homes_count
    scratch += [pltpu.VMEM((NE, slots, width), kind)] * homes_count
    scratch += [pltpu.VMEM((most_rows, width), jnp.float32)] * homes_count
    scratch.append(pltpu.VMEM((total_rows, width), kind))
    if backward:
        scratch.append(pltpu.VMEM((total_rows, width), kind))
        scratch += [pltpu.VMEM((total_rows, hidden), kind)] * 3
        scratch += [pltpu.VMEM((3, hidden, features), kind)] * 2
        if not forward:
            scratch += [pltpu.VMEM((most_rows, hidden), jnp.float32)] * 2
        scratch.append(DMA((3, tiles, 2)))
    scratch += [DMA((6,)), DMA((count,)), DMA((count, NE)), DMA((count, NE))]
    scratch += [DMA((count, copies, NE))] * 2
    scratch += [DMA((homes_count,)), DMA((homes_count, NE)), DMA((homes_count, NE))]
    scratch += [DMA((homes_count, copies, NE))] * 2 + [DMA] + [DMA((2 + len(cross),))] * 2
    operands = list(sent)
    in_specs = [ANY] * count
    if not forward:
        operands.append(saved)
        in_specs.append(VMEM)
    for n in range(3):
        operands += [own[n]] + other[n : n + 1]
    if ahead is not None:
        operands.append(ahead)
    operands += list(cross)
    in_specs += [HBM] * (len(operands) - len(in_specs))
    return pl.pallas_call(
        body,
        out_shape=shapes,
        in_specs=in_specs,
        out_specs=specs,
        scratch_shapes=scratch,
        compiler_params=comm_params(
            collective_id,
            scratch + ([saved] if not forward else []),
            (11 if backward else 2) * SPARE_BYTES,
        ),
        cost_estimate=lasting(cost),
    )(*operands)


def split(values, terms=2):
    parts = []
    for _ in range(terms):
        part = values.astype(jnp.bfloat16)
        parts.append(part)
        values = values - part.astype(jnp.float32)
    return parts


def exact_dot(pieces, values, dims):
    total = dot32(pieces[0], values, dims)
    for piece in pieces[1:]:
        total = total + dot32(piece, values, dims)
    return total


def unit_scale(values):
    return lax.rsqrt(jnp.mean(values * values, axis=-1, keepdims=True) + EPSILON)


def alone(body, out_shape, cost, *operands, scalars=0):
    specs = [pl.BlockSpec(memory_space=pltpu.SMEM)] * scalars + [VMEM] * (len(operands) - scalars)
    results = pl.pallas_call(
        body,
        out_shape=out_shape,
        in_specs=specs,
        out_specs=jax.tree.map(lambda _: VMEM, out_shape),
        compiler_params=pltpu.CompilerParams(
            vmem_limit_bytes=room(list(operands) + jax.tree.leaves(out_shape), 2 * SPARE_BYTES)
        ),
        cost_estimate=lasting(cost),
    )(*operands)
    return list(results) if isinstance(out_shape, (list, tuple)) else results


def route_tables(routes, gates):
    count, rows, _ = routes.shape
    slots = NE * CAP

    def body(routes_ref, gates_ref, picks_ref, weights_ref, slot_ref, other_ref):
        row = lax.broadcasted_iota(jnp.int32, (rows, rows), 0)
        col = lax.broadcasted_iota(jnp.int32, (rows, rows), 1)
        before = (col < row).astype(jnp.bfloat16)
        expert = lax.broadcasted_iota(jnp.int32, (rows, LANES), 1)
        slot = lax.broadcasted_iota(jnp.int32, (rows, slots), 1)
        source = lax.broadcasted_iota(jnp.int32, (LANES, slots), 0)
        target = lax.broadcasted_iota(jnp.int32, (LANES, slots), 1)
        spread = (
            (target >= source * CAP) & (target < source * CAP + CAP) & (source < NE)
        ).astype(jnp.bfloat16)
        ones = jnp.ones((rows, LANES), jnp.bfloat16)
        for n in range(count):
            gate = jnp.zeros((rows, LANES), jnp.float32)
            named = jnp.zeros((rows, LANES), jnp.float32)
            for k in range(2):
                hit = routes_ref[n, :, k : k + 1] == expert
                named = named + jnp.where(hit, 1.0, 0.0)
                gate = gate + jnp.where(hit, gates_ref[n, :, k : k + 1], 0.0)
            rank = dot32(before, named.astype(jnp.bfloat16)) + expert.astype(jnp.float32) * CAP
            rank = jnp.where(expert < NE, rank, 0.0)
            goal = exact_dot(split(rank, 2), spread, (((1,), (0,)), ((), ())))
            member = dot32(named.astype(jnp.bfloat16), spread)
            pick = jnp.where(goal == slot.astype(jnp.float32), member, 0.0)
            weight = pick * exact_dot(split(gate, 3), spread, (((1,), (0,)), ((), ())))
            picks_ref[n] = pick.astype(jnp.bfloat16)
            weights_ref[n] = weight
            slot_ref[n] = exact_dot(split(weight, 3), ones, FIRST)
            other_ref[n] = gate

    return alone(
        body,
        (
            make((count, rows, slots), jnp.bfloat16),
            make((count, rows, slots)),
            make((count, slots, LANES)),
            make((count, rows, LANES)),
        ),
        3,
        routes,
        gates,
    )


def gate_slots(slot_gates, picks, grads):
    picked = dot32(picks, grads[0], FIRST)
    for part in grads[1:]:
        picked = picked + dot32(picks, part, FIRST)
    lanes = [
        (picked[:, at : at + LANES] * slot_gates).astype(jnp.bfloat16)
        for at in range(0, picked.shape[1], LANES)
    ]
    return jnp.concatenate(lanes, axis=1)


def const_alphas(hn, smalls, base):
    logits = dot32(hn, smalls[base + 2 : base + 6].astype(jnp.bfloat16), LAST)
    alphas = []
    for c in range(2):
        first, second = logits[:, 2 * c : 2 * c + 1], logits[:, 2 * c + 1 : 2 * c + 2]
        top = jnp.maximum(first, second)
        first, second = jnp.exp(first - top), jnp.exp(second - top)
        total = first + second
        alphas.append((first / total, second / total))
    return alphas


def middle(attn, x, pack, smalls, base, picks, slot_gates, grads):
    planes, rows, part = attn.shape
    width = x.shape[1]
    slots = picks.shape[1]

    def body(attn_ref, x_ref, w_ref, small_ref, picks_ref, gates_ref, *refs):
        total = x_ref[...].astype(jnp.float32)
        for z in range(planes):
            total = total + dot32(attn_ref[z], w_ref[z * part : (z + 1) * part, :width])
        mid_ref, sent_ref = refs[-2:] if grads is None else refs[-3:-1]
        mid_ref[...] = total
        hn = (total * unit_scale(total) * small_ref[base + 1 : base + 2]).astype(jnp.bfloat16)
        sent_ref[...] = dot32(picks_ref[...], hn, FIRST).astype(jnp.bfloat16)
        if grads is not None:
            refs[-1][...] = gate_slots(gates_ref[...], picks_ref[...], [refs[0][...]])

    outs = [make((rows, width)), make((slots, width), jnp.bfloat16)]
    more = []
    if grads is not None:
        outs.append(make((slots, width), jnp.bfloat16))
        more.append(grads)
    return alone(body, outs, 3, attn, x, pack, smalls, picks, slot_gates, *more)


def combine(back, weights, mid, other, smalls, base, following):
    rows, width = mid.shape

    def body(back_ref, weights_ref, mid_ref, other_ref, small_ref, x_ref, *refs):
        mid_value, gate = mid_ref[...], other_ref[...]
        hn = (mid_value * unit_scale(mid_value) * small_ref[base + 1 : base + 2]).astype(
            jnp.bfloat16
        )
        alphas = const_alphas(hn, small_ref, base)
        wide = hn.astype(jnp.float32)
        total = mid_value + exact_dot(
            split(weights_ref[...]), back_ref[...], (((1,), (0,)), ((), ()))
        )
        factor = gate[:, NE + 1 : NE + 2]
        for c in range(2):
            weight = gate[:, NE + 2 + c : NE + 3 + c]
            factor = factor + weight * alphas[c][0]
            total = total + (weight * alphas[c][1]) * small_ref[base + 6 + c : base + 7 + c]
        total = total + factor * wide
        x_ref[...] = total
        if following:
            refs[0][...] = (total * unit_scale(total) * small_ref[base + 8 : base + 9]).astype(
                jnp.bfloat16
            )

    outs = [make((rows, width))]
    if following:
        outs.append(make((rows, width), jnp.bfloat16))
    return alone(body, outs, 3, back, weights, mid, other, smalls)


def experts_back(dback, picks, upstream, mid, other, smalls, base):
    rows, width = mid.shape

    def body(dback_ref, picks_ref, up_ref, mid_ref, other_ref, small_ref, dmid_ref, dy_ref, row_ref):
        mid_value, gate = mid_ref[...], other_ref[...]
        g = up_ref[...].astype(jnp.float32)
        scale = unit_scale(mid_value)
        unit = mid_value * scale
        gain = small_ref[base + 1 : base + 2]
        hn = (unit * gain).astype(jnp.bfloat16)
        alphas = const_alphas(hn, small_ref, base)
        wide = hn.astype(jnp.float32)
        dhn = dot32(picks_ref[...], dback_ref[...])
        g_hn = jnp.sum(g * wide, axis=1, keepdims=True)
        factor = gate[:, NE + 1 : NE + 2]
        row_ref[0:1] = jnp.zeros((1, width), jnp.float32)
        for c in range(2):
            weight = gate[:, NE + 2 + c : NE + 3 + c]
            vector = small_ref[base + 6 + c : base + 7 + c]
            first, second = alphas[c]
            factor = factor + weight * first
            row_ref[6 + c : 7 + c] = jnp.sum((weight * second) * g, axis=0, keepdims=True)
            da_first = weight * g_hn
            da_second = weight * jnp.sum(g * vector, axis=1, keepdims=True)
            mean = first * da_first + second * da_second
            for j, dlog in enumerate((first * (da_first - mean), second * (da_second - mean))):
                at = 2 + 2 * c + j
                dhn = dhn + dlog * small_ref[base + at : base + at + 1]
                row_ref[at : at + 1] = jnp.sum(dlog * wide, axis=0, keepdims=True)
        dhn = dhn + factor * g
        row_ref[1:2] = jnp.sum(dhn * unit, axis=0, keepdims=True)
        through = dhn * gain
        inner = jnp.mean(through * unit, axis=1, keepdims=True)
        dmid = g + scale * (through - unit * inner)
        dmid_ref[...] = dmid
        dy_ref[...] = dmid.astype(jnp.bfloat16)

    return alone(
        body,
        [make((rows, width)), make((rows, width), jnp.bfloat16), make((8, width))],
        4,
        dback,
        picks,
        upstream,
        mid,
        other,
        smalls,
    )


def finish(dxn, x, dmid, rows_in, smalls, base, picks, slot_gates):
    planes, rows, width = dxn.shape

    def body(dxn_ref, x_ref, dmid_ref, row_ref, small_ref, *refs):
        grad = dxn_ref[0].astype(jnp.float32)
        for z in range(1, planes):
            grad = grad + dxn_ref[z].astype(jnp.float32)
        value = x_ref[...].astype(jnp.float32)
        scale = unit_scale(value)
        unit = value * scale
        out_rows = refs[-1 if picks is None else -2]
        out_rows[...] = row_ref[...]
        out_rows[0:1] = jnp.sum(grad * unit, axis=0, keepdims=True)
        through = grad * small_ref[base : base + 1]
        inner = jnp.mean(through * unit, axis=1, keepdims=True)
        g = dmid_ref[...] + scale * (through - unit * inner)
        refs[-2 if picks is None else -3][...] = g
        if picks is not None:
            refs[-1][...] = gate_slots(refs[1][...], refs[0][...], split(g))

    outs = [make((rows, width)), make((8, width))]
    more = []
    if picks is not None:
        outs.append(make((picks.shape[1], width), jnp.bfloat16))
        more = [picks, slot_gates]
    return alone(body, outs, 3, dxn, x, dmid, rows_in, smalls, *more)


def sum_expert_grads(owns, gots):
    layers, kinds = len(owns), len(owns[0])
    hidden, features = owns[0][0].shape
    tile = min(hidden, 256)

    def body(*refs):
        outs = refs[2 * layers * kinds :]
        for n in range(kinds):
            for layer in range(layers):
                own, got = refs[2 * (layer * kinds + n) : 2 * (layer * kinds + n) + 2]
                outs[n][layer] = own[...].astype(jnp.float32) + got[...].astype(jnp.float32)

    piece = pl.BlockSpec((tile, features), lambda i: (i, 0))
    operands = [
        w for layer in range(layers) for pair in zip(owns[layer], gots[layer]) for w in pair
    ]
    return pl.pallas_call(
        body,
        out_shape=[make((layers, hidden, features))] * kinds,
        grid=(hidden // tile,),
        in_specs=[piece] * len(operands),
        out_specs=[pl.BlockSpec((layers, tile, features), lambda i: (0, i, 0))] * kinds,
        compiler_params=pltpu.CompilerParams(vmem_limit_bytes=VMEM_BYTES),
        cost_estimate=lasting(7),
    )(*operands)


def pack_grads(column, dq, dkv, attn, dy, small):
    width = column.shape[1]
    kv_cols, own_out = dkv.shape[1], attn.shape[1]
    tail = own_out + LANES // 2
    rows, cols = own_out // 2, width // 2

    def body(column_ref, dq_ref, dkv_ref, attn_ref, dy_ref, small_ref, one, two):
        one[:, :kv_cols] = dot32(column_ref[...], dkv_ref[...], FIRST).astype(jnp.bfloat16)
        source = lax.broadcasted_iota(jnp.int32, (kv_cols, tail), 0)
        target = lax.broadcasted_iota(jnp.int32, (kv_cols, tail), 1)
        dim = LANES // 2
        goal = lax.div(target, dim) * LANES + lax.rem(target, dim)
        compact = ((goal == source) & (target < own_out)).astype(jnp.bfloat16)
        narrow = dot32(dq_ref[...], compact).astype(jnp.bfloat16)
        placed = jnp.concatenate(
            [
                jnp.zeros((own_out, width), jnp.float32),
                small_ref[...],
                jnp.zeros((tail - own_out - 8, width), jnp.float32),
            ],
            axis=0,
        ).T
        one[:, kv_cols:] = (dot32(column_ref[...], narrow, FIRST) + placed).astype(jnp.bfloat16)
        out = dot32(attn_ref[...], dy_ref[...], FIRST).astype(jnp.bfloat16)
        for a in range(2):
            for b in range(2):
                two[a, b] = out[a * rows : (a + 1) * rows, b * cols : (b + 1) * cols]

    return alone(
        body,
        [make((width, kv_cols + tail), jnp.bfloat16), make((2, 2, rows, cols), jnp.bfloat16)],
        4,
        column,
        dq,
        dkv,
        attn,
        dy,
        small,
    )


def per_device(
    tokens,
    segments,
    routes,
    gates,
    w_qkv,
    w_out,
    gain_attn,
    gain_moe,
    const_gate,
    const_vec,
    w_gate,
    w_up,
    w_down,
    cotangent,
):
    blocks = lax.axis_size("blk")
    head_index, blk_index = lax.axis_index("head"), lax.axis_index("blk")
    span = blocks // COLUMNS
    plane, rest = lax.div(blk_index, span), lax.rem(blk_index, span)
    shards = 2 * blocks
    token_rows, width = tokens.shape
    shard_rows = width // shards
    head_dim = width // HEADS
    heads = HEADS // COLUMNS
    scale = head_dim ** (-0.5)
    half_length = blocks * token_rows
    positions = 2 * half_length
    own_out = heads * head_dim
    wide = heads * LANES

    swap = [(0, 1), (1, 0)]

    seg_own = lax.dynamic_index_in_dim(segments, head_index, 0, keepdims=True)
    seg_rows = jnp.concatenate([lax.rem(seg_own, 128), lax.div(seg_own, 128)], axis=0)
    seg_rows = jnp.pad(seg_rows, ((0, 14), (0, 0))).astype(jnp.bfloat16)
    seg_rows = jnp.broadcast_to(seg_rows[None], (COLUMNS,) + seg_rows.shape)
    smalls = [
        jnp.concatenate(
            [gain_attn[n][:, None], gain_moe[n][:, None], const_gate[n], const_vec[n]], axis=1
        )
        for n in range(LAYERS)
    ]
    smalls.append(jnp.zeros((shard_rows, LANES // 2 - 8 * LAYERS), jnp.bfloat16))
    smalls = jnp.concatenate(smalls, axis=1)
    packs = []
    for layer in range(LAYERS):
        parts = w_qkv[layer].reshape((shard_rows, 3, COLUMNS, heads, head_dim))
        kv_part = jnp.concatenate([parts[:, 1], parts[:, 2]], axis=3)
        kv_part = kv_part.transpose((1, 0, 2, 3)).reshape((COLUMNS, shard_rows, wide))
        query_part = parts[:, 0].transpose((1, 0, 2, 3)).reshape((COLUMNS, shard_rows, own_out))
        packs.append(
            jnp.concatenate(
                [
                    jnp.broadcast_to(w_out[layer][None], (COLUMNS, shard_rows, width)),
                    kv_part,
                    query_part,
                    jnp.broadcast_to(smalls[None], (COLUMNS,) + smalls.shape),
                ],
                axis=2,
            )
        )
    (seg_all, *packs), column_tokens = start_gather([seg_rows] + packs, tokens, blocks, 1)
    packs = [pack.reshape((width, -1)) for pack in packs]
    picks, pick_gates, slot_gates, other_gates = route_tables(routes, gates)

    def send_expert(weight, layer, after):
        away, _ = lax.optimization_barrier((weight[layer], after))
        return lax.ppermute(away, "head", swap)

    own_experts = (w_gate, w_up, w_down)

    experts = [[send_expert(w_gate, 0, tokens)]] + [None] * (LAYERS - 1)
    seg_all = seg_all[..., :2, :].astype(jnp.int32)
    seg_all = seg_all[..., 0, :] + 128 * seg_all[..., 1, :]
    seg_query = lax.dynamic_index_in_dim(seg_all, head_index, 0, keepdims=False)
    seg_query = lax.dynamic_index_in_dim(seg_query, rest, 1, keepdims=False)
    starts = jnp.sum(
        (seg_all.reshape((1, 1, -1)) < seg_query[:, :, None]).astype(jnp.int32), axis=2
    )
    bases = (
        head_index * half_length
        + (jnp.arange(COLUMNS, dtype=jnp.int32) * span + rest) * token_rows
    )
    bounds = block_bounds(starts, bases, token_rows)
    starts = starts[:, None, :]

    values = tokens
    column, small_rows = column_tokens, None
    kept = []
    for layer in range(LAYERS):
        base = 8 * layer
        last = layer + 1 == LAYERS
        column, queries, query_w, out_rows, kv_all, small_rows = project_gather(
            column, packs[layer], small_rows, heads, scale, blocks, 4 if layer == 0 else 2
        )
        kv_all = kv_all.reshape((positions, wide))
        if layer == 0:
            experts[layer] += [send_expert(w, layer, kv_all) for w in (w_up, w_down)]
        else:
            experts[layer].append(send_expert(w_down, layer, kv_all))
        attended, attn_col = attend(bounds, queries, kv_all, starts)
        (attn,) = column_exchange([attn_col], [False], blocks, 5, 9)
        mid, *sent = middle(
            attn,
            values,
            packs[layer],
            small_rows,
            base,
            picks[layer],
            slot_gates[layer],
            cotangent if last else None,
        )
        sent = [rows.reshape((NE, CAP, width)) for rows in sent]
        if last:
            back, dback, *wgrads = experts_exchange(
                sent, None, own_experts, experts[layer], layer, blocks, 7, True, True, 55
            )
            rows_in = None
        else:
            experts[layer + 1] = [send_expert(w, layer + 1, sent[0]) for w in (w_gate, w_up)]
            back, rows_in = experts_exchange(
                sent, None, own_experts, experts[layer], layer, blocks, 6, True, False, 28
            )
        kept.append(
            (values, column, queries, kv_all, attended, attn_col, query_w, out_rows, mid, rows_in)
        )
        values, *normed = combine(
            back.reshape((NE * CAP, width)),
            pick_gates[layer],
            mid,
            other_gates[layer],
            small_rows,
            base,
            not last,
        )
        if not last:
            (column,) = normed
    output = values

    upstream = cotangent
    shared_grads = [None] * LAYERS
    expert_grads = [None] * LAYERS
    for layer in reversed(range(LAYERS)):
        base = 8 * layer
        values, column, queries, kv_all, attended, attn_col, query_w, out_rows, mid, rows_in = (
            kept[layer]
        )
        if layer + 1 < LAYERS:
            dback, *wgrads = experts_exchange(
                [dz.reshape((NE, CAP, width))],
                rows_in,
                own_experts,
                experts[layer],
                layer,
                blocks,
                8,
                False,
                True,
                36,
                None,
                waiting,
            )
            expert_grads[layer + 1][1][1:] = wgrads[6:]
        before = layer > 0
        if before:
            got, waiting = [lax.ppermute(wgrads[3], "head", swap)], wgrads[4:6]
        else:
            got = [lax.ppermute(away, "head", swap) for away in wgrads[3:5]]
        dmid, dy, rows = experts_back(
            dback.reshape((NE * CAP, width)),
            picks[layer],
            upstream,
            mid,
            other_gates[layer],
            small_rows,
            base,
        )
        dy = column_gather(dy, blocks, 3)
        dy, got[0] = lax.optimization_barrier((dy, got[0]))
        dq, dkv_all = attend_back(
            bounds, queries, dy, out_rows, attended, kv_all, starts, scale
        )
        if not before:
            dkv_all, got[1] = lax.optimization_barrier((dkv_all, got[1]))
        dkv, dxn = reduce_project(
            dkv_all.reshape((2, COLUMNS, span, token_rows, wide)),
            dq,
            query_w,
            packs[layer],
            blocks,
            10,
        )
        upstream, rows, *dz = finish(
            dxn,
            values,
            dmid,
            rows,
            small_rows,
            base,
            picks[layer - 1] if before else None,
            slot_gates[layer - 1] if before else None,
        )
        if before:
            (dz,) = dz
        expert_grads[layer] = wgrads[:3], got
        qkv_part, out_part = pack_grads(
            column.reshape((-1, width)),
            dq.reshape((-1, wide)),
            dkv.reshape((-1, wide)),
            attn_col.reshape((-1, own_out)),
            dy.reshape((-1, width)),
            rows,
        )
        shared_grads[layer] = [
            qkv_part.reshape((2, COLUMNS, span, shard_rows, -1)),
            out_part.reshape((2, 2, span, shard_rows, width // 2)),
        ]

    packed = [part for layer in range(LAYERS) for part in shared_grads[layer]]
    reduced = plane_reduce(packed, blocks, 12, 20)
    away, _ = lax.optimization_barrier((wgrads[5], reduced[0]))
    expert_grads[0][1].append(lax.ppermute(away, "head", swap))
    exchanged = final_exchange(reduced[::2], reduced[1::2], blocks, 13)
    from_planes, out_grads = exchanged[:LAYERS], exchanged[LAYERS:]
    from_planes = jnp.stack(from_planes, axis=1).astype(jnp.float32)
    kv_out = from_planes[..., :wide].reshape((COLUMNS, LAYERS, shard_rows, heads, 2, head_dim))
    query_out = from_planes[..., wide : wide + own_out].reshape(
        (COLUMNS, LAYERS, shard_rows, heads, 1, head_dim)
    )
    qkv_out = jnp.concatenate([query_out, kv_out], axis=4)
    qkv_out = qkv_out.transpose((1, 2, 4, 0, 3, 5)).reshape((LAYERS, shard_rows, 3 * width))
    small_out = jnp.sum(from_planes[..., wide + own_out : wide + own_out + 8], axis=0)
    out_grads = jnp.stack(out_grads).astype(jnp.float32).transpose((0, 2, 1, 3))
    out_grads = out_grads.reshape((LAYERS, shard_rows, width))
    stacked = sum_expert_grads(*zip(*expert_grads))
    return (
        output,
        upstream,
        qkv_out,
        out_grads,
        small_out[..., 0],
        small_out[..., 1],
        small_out[..., 2:6],
        small_out[..., 6:8],
        stacked[0],
        stacked[1],
        stacked[2],
    )


def solution(mesh):
    tokens = P(("head", "blk"), None)
    by_layer = P(None, ("head", "blk"), None)
    gains = P(None, ("head", "blk"))
    experts = P(None, "blk", "head")
    return jax.shard_map(
        per_device,
        mesh=mesh,
        in_specs=(
            tokens,
            P(None, "blk"),
            by_layer,
            by_layer,
            by_layer,
            by_layer,
            gains,
            gains,
            by_layer,
            by_layer,
            experts,
            experts,
            experts,
            tokens,
        ),
        out_specs=(
            tokens,
            tokens,
            by_layer,
            by_layer,
            gains,
            gains,
            by_layer,
            by_layer,
            experts,
            experts,
            experts,
        ),
        check_vma=False,
    )
```
